32 devices in a mesh: dp: 4 (over y, core), expert: 8 (over z, x).
Axes of the slice: x: 2, y: 2, z: 4, core: 2. Of those that a mesh axis runs over, the one named last changes fastest.
Arguments:
- tokens: bfloat16 [4096, 3584], P(('dp', 'expert')), may hold values from -6 to 6
- route_weight: float32 [4096], P(('dp', 'expert')), may hold values from 0.1 to 1
- cotangent: bfloat16 [4096, 1024], P(('dp', 'expert')), may hold values from -6 to 6
- slot_ids: int32 [4096], P(('dp', 'expert')), may hold values from 0 to 7, as said below
- placement: int32 [8], replicated, may hold values from 0 to 4, as said below
- weight: bfloat16 [8, 3584, 1024], P('expert'), as said below
- momentum: bfloat16 [8, 3584, 1024], P('expert', 'dp'), as said below
Outputs:
- expert_out: bfloat16 [4096, 1024], P(('dp', 'expert'))
- token_grad: bfloat16 [4096, 3584], P(('dp', 'expert'))
- new_weight: bfloat16 [8, 3584, 1024], P('expert', 'dp')
- new_momentum: bfloat16 [8, 3584, 1024], P('expert', 'dp')
The draws below stay inside these ranges and needn't reach their ends.
Inputs may be any that keep to these rules, and one draw needn't show every extreme that they name: `slot_ids`: one device's 128 tokens (an aligned block) send at most 18 tokens to one slot; in each group of 8 consecutive blocks some slot gets exactly 18 from every block. `placement`: slots j and j + 4 carry the same number for exactly 3 values of j below 4; all other slots carry distinct numbers, and every number is used. `weight`: slots with equal placement numbers hold equal matrices. `momentum`: slots with equal placement numbers hold equal matrices.
All inputs are finite; a program needn't handle non-finite values.
Results may differ from the reference program's by a relative error of at most 0.018.
Values may be sent and summed in bfloat16 or wider, within the bound.
No kernel may reach another device: no remote copies, remote signals or barrier semaphores. Data moves between devices by JAX's collectives and lax.ppermute only.
A program may use at most 64 MiB of HBM per device.

```python
import jax
import jax.numpy as jnp
from jax import lax

D = 3584
F = 1024
TOK_DEV = 128
CAP = 18
HOT = 3
TOKENS = 4096
N_DP = 4
N_EXPERT = 8


def layout_table(key):
    base_key = jax.random.fold_in(key, 101)
    pairs = N_EXPERT // 2
    order = jax.random.permutation(jax.random.fold_in(base_key, 1), pairs - 2)
    middle = (order < HOT - 2).astype(jnp.int32)
    edge = jnp.ones((1,), jnp.int32)
    hot_pair = jnp.concatenate([edge, middle, edge])
    units = 2 - hot_pair
    start = jnp.cumsum(units) - units
    labels = jnp.concatenate([start, start + 1 - hot_pair])
    relabel = jax.random.permutation(jax.random.fold_in(base_key, 2), N_EXPERT - HOT)
    return (relabel[labels].astype(jnp.int32), jnp.concatenate([hot_pair, hot_pair]))


def source_slot(key):
    hot_flags = layout_table(key)[1]
    slots = jnp.arange(N_EXPERT, dtype=jnp.int32)
    upper = (slots >= N_EXPERT // 2) & (hot_flags == 1)
    return jnp.where(upper, slots - N_EXPERT // 2, slots)


def draw_placement(key, part):
    return layout_table(key)[0]


def draw_weight(key, part):
    inner = jax.random.fold_in(key, 7)
    values = jax.random.normal(inner, (N_EXPERT, D, F), jnp.float32)
    values = values * D ** (-0.5)
    return values[source_slot(key)].astype(jnp.bfloat16)


def draw_momentum(key, part):
    inner = jax.random.fold_in(key, 9)
    values = jax.random.normal(inner, (N_EXPERT, D, F), jnp.float32) * 10.0
    return values[source_slot(key)].astype(jnp.bfloat16)


def draw_slot_ids(key, part):
    blocks = TOKENS // TOK_DEV
    positions = N_EXPERT * CAP
    full_slot = jax.random.randint(jax.random.fold_in(key, 5), (blocks // N_EXPERT,), 0, N_EXPERT)
    block_full = jnp.repeat(full_slot, N_EXPERT)
    block_keys = jax.random.split(jax.random.fold_in(key, 6), blocks)

    def one_block(block_key, chosen_full):
        first_key, second_key = jax.random.split(block_key)
        priority = jax.random.permutation(first_key, positions)
        places = jnp.arange(positions, dtype=jnp.int32)
        score = jnp.where(places // CAP == chosen_full, -1 - places, priority)
        ordered = jnp.argsort(score)
        picked = (ordered[:TOK_DEV] // CAP).astype(jnp.int32)
        return picked[jax.random.permutation(second_key, TOK_DEV)]
    return jax.vmap(one_block)(block_keys, block_full).reshape(-1).astype(jnp.int32)


def shard_levels(key, extent, cuts, least, largest):
    def one(dim, parts):
        steps = jax.random.uniform(jax.random.fold_in(jax.random.fold_in(key, 6), dim), (parts,), jnp.float32, least / len(cuts), largest / len(cuts))
        return jnp.repeat(jnp.exp(steps), extent[dim] // parts).reshape((-1,) + (1,) * (len(extent) - dim - 1))

    loudness = one(*cuts[0])
    for cut in cuts[1:]:
        loudness = loudness * one(*cut)
    return loudness


def gaussian(own_key, dims, scale, limit, pieces=(), held_as=jnp.bfloat16):
    values = jax.random.normal(own_key, dims, jnp.float32) * scale
    if len(pieces) > 0:
        values = shard_levels(own_key, dims, pieces, -0.22, 0.18) * values
    return jnp.clip(values, min=-limit, max=limit).astype(held_as)


def setup_inputs(seed: int = 0) -> dict:
    seeds = jax.random.split(jax.random.key(seed), 8)
    tokens = gaussian(seeds[0], (TOKENS, D), 1.0, 6.0, ((0, 32),))
    route_weight = jnp.clip(0.1 + 0.9 * jax.random.uniform(seeds[1], (TOKENS,), jnp.float32) ** shard_levels(seeds[1], (TOKENS,), ((0, 32),), -0.2, 0.2), 0.1, 1.0)
    cotangent = gaussian(seeds[2], (TOKENS, F), 1.0, 6.0, ((0, 32),))
    slot_ids = draw_slot_ids(jax.random.fold_in(seeds[7], 71), 0)
    placement = draw_placement(jax.random.fold_in(seeds[7], 71), 0)
    weight = draw_weight(jax.random.fold_in(seeds[7], 71), 0)
    momentum = draw_momentum(jax.random.fold_in(seeds[7], 71), 0)
    return {"tokens": tokens, "route_weight": route_weight, "cotangent": cotangent, "slot_ids": slot_ids, "placement": placement, "weight": weight, "momentum": momentum}


learning_rate = 0.004
decay_rate = 0.9


def reference(tokens, route_weight, cotangent, slot_ids, placement, weight, momentum):
    n_blocks = TOKENS // TOK_DEV
    slot_rows = N_EXPERT * CAP
    blocked = slot_ids.reshape(n_blocks, TOK_DEV)
    onehot = (blocked[:, :, None] == jnp.arange(N_EXPERT, dtype=jnp.int32)[None, None, :]).astype(jnp.int32)
    ranks = jnp.sum((jnp.cumsum(onehot, axis=1) - 1) * onehot, axis=2).astype(jnp.int32)
    block_ids = jnp.arange(n_blocks, dtype=jnp.int32)[:, None]
    group = block_ids // N_EXPERT
    source = block_ids % N_EXPERT
    position = ((((blocked * N_DP + group) * N_EXPERT + source) * CAP) + ranks).reshape(-1).astype(jnp.int32)
    all_rows = N_EXPERT * N_DP * slot_rows
    x_buf = jnp.zeros((all_rows, D), jnp.bfloat16).at[position].set(tokens).reshape(N_EXPERT, N_DP, slot_rows, D)
    scaled = (route_weight[:, None] * cotangent.astype(jnp.float32)).astype(jnp.bfloat16)
    g_buf = jnp.zeros((all_rows, F), jnp.bfloat16).at[position].set(scaled).reshape(N_EXPERT, N_DP, slot_rows, F)

    def per_slot(slot):
        rows_x = x_buf[slot].astype(jnp.float32)
        rows_g = g_buf[slot].astype(jnp.float32)
        matrix = weight[slot].astype(jnp.float32)
        preact = jnp.einsum("nrd,df->nrf", rows_x, matrix)
        sigma = jax.nn.sigmoid(preact)
        act = (preact * sigma).astype(jnp.bfloat16)
        grad_pre = (rows_g * sigma * (1.0 + preact * (1.0 - sigma))).astype(jnp.bfloat16)
        back = jnp.einsum("nrf,df->nrd", grad_pre.astype(jnp.float32), matrix).astype(jnp.bfloat16)
        terms = jnp.einsum("nrd,nrf->ndf", rows_x, grad_pre.astype(jnp.float32))
        terms = lax.optimization_barrier(terms.astype(jnp.bfloat16)).astype(jnp.float32)
        reduced = jnp.sum(terms, axis=0).astype(jnp.bfloat16)
        return act, back, reduced

    act_all, back_all, reduced = lax.map(per_slot, jnp.arange(N_EXPERT, dtype=jnp.int32))
    act_rows = act_all.reshape(all_rows, F)[position]
    expert_out = (route_weight[:, None] * act_rows.astype(jnp.float32)).astype(jnp.bfloat16)
    token_grad = back_all.reshape(all_rows, D)[position]
    half = N_EXPERT // 2
    partner = jnp.roll(reduced, half, axis=0)
    partner_label = jnp.roll(placement, half, axis=0)
    same = (placement == partner_label)[:, None, None]
    total = reduced.astype(jnp.float32) + jnp.where(same, partner.astype(jnp.float32), jnp.float32(0.0))
    new_momentum = (decay_rate * momentum.astype(jnp.float32) + total).astype(jnp.bfloat16)
    new_weight = (weight.astype(jnp.float32) - learning_rate * new_momentum.astype(jnp.float32)).astype(jnp.bfloat16)
    return expert_out, token_grad, new_weight, new_momentum
```

```python
import functools

import jax
import jax.numpy as jnp
from jax import lax
from jax.experimental import pallas as pl
from jax.experimental.pallas import tpu as pltpu
from jax.sharding import PartitionSpec as P

learning_rate = 0.004
decay_rate = 0.9

BF16 = jnp.bfloat16
F32 = jnp.float32
SUB = 8
LANES = 128


class Plan:
    def __init__(self, slots, groups, tokens, features, hidden):
        self.slots, self.groups, self.tokens = slots, groups, tokens
        self.D, self.F = features, hidden
        self.half = slots // 2
        self.cap = tokens * 9 // 8 // slots
        self.full, self.rest = divmod(self.cap, SUB)
        self.cuts = SUB // self.rest if self.rest else 1
        self.rows = self.half * self.cap
        self.share = features // groups
        self.DX = features * self.cap // SUB
        self.FG = hidden * self.cap // SUB
        self.C = self.DX + self.FG
        self.pieces = self.cap * groups // SUB

    def fits(self):
        return (
            self.slots % 2 == 0
            and (self.rest == 0 or SUB % self.rest == 0)
            and self.D % (self.cuts * LANES) == 0
            and self.F % (self.cuts * LANES) == 0
            and self.D % (self.groups * LANES) == 0
            and (self.cap * self.groups) % SUB == 0
            and self.rows % SUB == 0
            and (self.half * self.rest) % SUB == 0
            and self.tokens % LANES == 0
        )


def away(place, step, count):
    if count & (count - 1) == 0:
        return place ^ step
    return (place + step) % count


def away_traced(place, step, count):
    if count & (count - 1) == 0:
        return jnp.bitwise_xor(place, step)
    return lax.rem(place + step, count)


def steps_between(first, second, count):
    if count & (count - 1) == 0:
        return jnp.bitwise_xor(first, second)
    return lax.rem(first - second + count, count)


def iota(shape, dim):
    return lax.broadcasted_iota(jnp.int32, shape, dim)


def dot(a, b):
    return jnp.dot(a, b, preferred_element_type=F32)


def dot_nt(a, b):
    return lax.dot_general(a, b, (((1,), (1,)), ((), ())), preferred_element_type=F32)


def dot_tn(a, b):
    return lax.dot_general(a, b, (((0,), (0,)), ((), ())), preferred_element_type=F32)


def picker(plan, cut):
    shape = (plan.half * plan.rest, plan.half * SUB)
    row, col = iota(shape, 0), iota(shape, 1)
    wanted = (row // plan.rest) * SUB + cut * plan.rest + row % plan.rest
    return (wanted == col).astype(BF16)


def unfold(plan, blocks, width):
    parts = [
        jnp.concatenate([b[:, i * width : (i + 1) * width] for b in blocks], axis=0)
        for i in range(plan.full)
    ]
    if plan.rest:
        piece = width // plan.cuts
        tail = jnp.concatenate([b[:, plan.full * width :] for b in blocks], axis=0).astype(BF16)
        parts.append(
            jnp.concatenate([dot(picker(plan, q), tail) for q in range(plan.cuts)], axis=1)
        )
    return jnp.concatenate(parts, axis=0).astype(BF16)


def fold(plan, rows):
    width = rows.shape[1]
    block = plan.half * SUB
    parts = [rows[i * block : (i + 1) * block] for i in range(plan.full)]
    if plan.rest:
        piece = width // plan.cuts
        tail = rows[plan.full * block :].astype(BF16)
        total = None
        for q in range(plan.cuts):
            term = dot_tn(picker(plan, q), tail[:, q * piece : (q + 1) * piece])
            total = term if total is None else total + term
        parts.append(total)
    return jnp.concatenate(parts, axis=1)


def is_hot(plan, placement_ref):
    me = lax.axis_index("expert")
    partner = lax.rem(me + plan.half, plan.slots)
    return placement_ref[me] == placement_ref[partner]


def token_places(plan, slot):
    me = lax.axis_index("expert")
    my_half = me // plan.half
    my_place = lax.rem(me, plan.half)
    upper = (slot >= plan.half).astype(jnp.int32)
    place = slot - plan.half * upper
    far = jnp.where(upper == my_half, 0, 1)
    step = steps_between(place, jnp.zeros_like(place) + my_place, plan.half)
    block = 2 * step + far
    count = plan.tokens
    onehot = (iota((2 * plan.half, count), 0) == block).astype(F32)
    upto = (iota((count, count), 0) <= iota((count, count), 1)).astype(BF16)
    seen = dot(onehot.astype(BF16), upto)
    rank = jnp.sum(onehot * (seen - 1.0), axis=0, keepdims=True).astype(jnp.int32)
    return block, rank


def row_targets(plan, block, rank):
    targets = []
    for i in range(plan.full):
        inside = (rank >= i * SUB) & (rank < (i + 1) * SUB)
        targets.append(jnp.where(inside, block * SUB + rank - i * SUB, -1))
    for q in range(plan.cuts if plan.rest else 0):
        inside = rank >= plan.full * SUB
        targets.append(
            jnp.where(inside, block * SUB + q * plan.rest + rank - plan.full * SUB, -1)
        )
    return targets


def to_column(row):
    n = row.shape[1]
    eye = (iota((n, n), 0) == iota((n, n), 1)).astype(F32)
    return jnp.sum(eye * row.astype(F32), axis=1, keepdims=True)


def pack_kernel(plan, slot_ref, gate_ref, tok_ref, cot_ref, *outs):
    near, far = outs[: plan.half], outs[plan.half :]
    block, rank = token_places(plan, slot_ref[...])
    targets = row_targets(plan, block, rank)
    height = 2 * plan.half * SUB
    onehots = [(iota((height, plan.tokens), 0) == t).astype(BF16) for t in targets]
    tok = tok_ref[...]
    scaled = (to_column(gate_ref[...]) * cot_ref[...].astype(F32)).astype(BF16)

    def store(values, start):
        stop = start + values.shape[1]
        for m in range(plan.half):
            low = 2 * m * SUB
            near[m][:, start:stop] = values[low : low + 2 * SUB].astype(BF16)
            far[m][:, start:stop] = values[low + SUB : low + 2 * SUB].astype(BF16)

    for data, base in ((tok, 0), (scaled, plan.DX)):
        width = data.shape[1]
        for i in range(plan.full):
            store(dot(onehots[i], data), base + i * width)
        if plan.rest:
            piece = width // plan.cuts
            total = None
            for q in range(plan.cuts):
                term = dot(onehots[plan.full + q], data[:, q * piece : (q + 1) * piece])
                total = term if total is None else total + term
            store(total, base + plan.full * width)


def near_blocks(plan, refs, far, start, stop):
    low = SUB if far else 0
    return [r[:, start:stop].astype(F32)[low : low + SUB] for r in refs]


def columns_kernel(plan, *refs):
    near, outs, rows = refs[: plan.half], refs[plan.half : -1], refs[-1]
    rows[...] = unfold(plan, near_blocks(plan, near, False, 0, plan.DX), plan.D)
    group = lax.axis_index("dp")
    for m in range(plan.groups):
        start = pl.multiple_of(away_traced(group, m, plan.groups) * plan.share, LANES)
        outs[m][...] = rows[:, pl.ds(start, plan.share)]


def load_weight(plan, weight_ref, held, sems):
    count = sems.shape[0]
    height = plan.D // count
    copies = []
    for c in range(count):
        span = pl.ds(c * height, height)
        copy = pltpu.make_async_copy(weight_ref.at[0, span, :], held.at[span, :], sems.at[c])
        copy.start()
        copies.append(copy)
    return copies, height


def project(x, held, copies, height):
    preact = None
    for c, copy in enumerate(copies):
        copy.wait()
        span = slice(c * height, (c + 1) * height)
        term = dot(x[:, span], held[span, :])
        preact = term if preact is None else preact + term
    return preact


def activate(preact, scaled):
    sigma = jax.nn.sigmoid(preact)
    act = (preact * sigma).astype(BF16)
    grad_pre = (scaled.astype(F32) * sigma * (1.0 + preact * (1.0 - sigma))).astype(BF16)
    return act, grad_pre


def pull_back(grad_pre, held, copies, height):
    return jnp.concatenate(
        [
            dot_nt(grad_pre, held[c * height : (c + 1) * height, :])
            for c in range(len(copies))
        ],
        axis=1,
    )


def near_kernel(plan, placement_ref, weight_ref, *refs):
    half, groups = plan.half, plan.groups
    near, refs = refs[:half], refs[half:]
    back_near, refs = refs[:half], refs[half:]
    local_far, folded_grad, refs = refs[0], refs[1], refs[2:]
    share, refs = refs[:groups], refs[groups:]
    held, far_rows, sems = refs
    copies, height = load_weight(plan, weight_ref, held, sems)
    x_near = unfold(plan, near_blocks(plan, near, False, 0, plan.DX), plan.D)
    x_far = unfold(plan, near_blocks(plan, near, True, 0, plan.DX), plan.D)
    g_near = unfold(plan, near_blocks(plan, near, False, plan.DX, plan.C), plan.F)
    g_far = unfold(plan, near_blocks(plan, near, True, plan.DX, plan.C), plan.F)
    far_rows[...] = x_far
    x = jnp.concatenate([x_near.astype(F32), x_far.astype(F32)], axis=0).astype(BF16)
    g = jnp.concatenate([g_near.astype(F32), g_far.astype(F32)], axis=0).astype(BF16)
    act, grad_pre = activate(project(x, held, copies, height), g)
    back = pull_back(grad_pre, held, copies, height)
    act, grad32 = act.astype(F32), grad_pre.astype(F32)
    near_back = fold(plan, back[: plan.rows])
    near_act = fold(plan, act[: plan.rows])
    for m in range(half):
        back_near[m][:, : plan.DX] = near_back[m * SUB : (m + 1) * SUB].astype(BF16)
        back_near[m][:, plan.DX :] = near_act[m * SUB : (m + 1) * SUB].astype(BF16)
    local_far[:, : plan.DX] = fold(plan, back[plan.rows :]).astype(BF16)
    local_far[:, plan.DX :] = fold(plan, act[plan.rows :]).astype(BF16)
    grad_near = grad32[: plan.rows]
    grad_far = jnp.where(is_hot(plan, placement_ref), grad32[plan.rows :], 0.0).astype(BF16)
    folded_grad[...] = fold(plan, grad_near).astype(BF16)
    group = lax.axis_index("dp")
    for m in range(groups):
        start = pl.multiple_of(away_traced(group, m, groups) * plan.share, LANES)
        share[m][:, : plan.share] = far_rows[:, pl.ds(start, plan.share)]
        share[m][:, plan.share : plan.share + plan.F] = grad_near.astype(BF16)
        share[m][:, plan.share + plan.F :] = grad_far


def far_kernel(plan, placement_ref, weight_ref, folded_grad, *refs):
    half, groups = plan.half, plan.groups
    far, refs = refs[:half], refs[half:]
    columns, refs = refs[:groups], refs[groups:]
    payload, refs = refs[0], refs[1:]
    share, refs = refs[:groups], refs[groups:]
    held, rows, sems = refs
    copies, height = load_weight(plan, weight_ref, held, sems)
    x = unfold(plan, [r[:, : plan.DX].astype(F32) for r in far], plan.D)
    g = unfold(plan, [r[:, plan.DX :].astype(F32) for r in far], plan.F)
    rows[...] = x
    act, grad_pre = activate(project(x, held, copies, height), g)
    hot = is_hot(plan, placement_ref)

    @pl.when(jnp.logical_not(hot))
    def _():
        back = pull_back(grad_pre, held, copies, height)
        payload[:, : plan.DX] = fold(plan, back).astype(BF16)
        payload[:, plan.DX :] = fold(plan, act.astype(F32)).astype(BF16)

    @pl.when(hot)
    def _():
        together = jnp.concatenate([c[...].astype(F32) for c in columns], axis=0)
        block = half * SUB
        for i in range(plan.pieces):
            payload[:, i * plan.share : (i + 1) * plan.share] = together[
                i * block : (i + 1) * block
            ].astype(BF16)
        payload[:, plan.DX :] = folded_grad[...]

    group = lax.axis_index("dp")
    for m in range(groups):
        start = pl.multiple_of(away_traced(group, m, groups) * plan.share, LANES)
        share[m][:, : plan.share] = rows[:, pl.ds(start, plan.share)]
        share[m][:, plan.share :] = grad_pre


def after_kernel(plan, placement_ref, payload, local_far, *outs):
    hot = is_hot(plan, placement_ref)
    chosen = jnp.where(hot, local_far[...].astype(F32), payload[...].astype(F32))
    for m in range(plan.half):
        outs[m][...] = chosen[m * SUB : (m + 1) * SUB].astype(BF16)
    g = payload[:, plan.DX :].astype(F32)
    blocks = [g[m * SUB : (m + 1) * SUB] for m in range(plan.half)]
    outs[plan.half][...] = jnp.where(hot, unfold(plan, blocks, plan.F).astype(F32), 0.0).astype(BF16)


def unpack_kernel(plan, slot_ref, gate_ref, *refs):
    near, refs = refs[: plan.half], refs[plan.half :]
    far, refs = refs[: plan.half], refs[plan.half :]
    out_ref, grad_ref = refs
    block, rank = token_places(plan, slot_ref[...])
    width = 2 * plan.half * SUB
    picks = []
    for target in row_targets(plan, block, rank):
        column = to_column(target).astype(jnp.int32)
        picks.append((iota((plan.tokens, width), 1) == column).astype(BF16))
    stacked = []
    for m in range(plan.half):
        stacked += [near[m][...].astype(F32), far[m][...].astype(F32)]
    stacked = jnp.concatenate(stacked, axis=0).astype(BF16)

    def gather(base, size):
        total = None
        for i in range(plan.full):
            term = dot(picks[i], stacked[:, base + i * size : base + (i + 1) * size])
            total = term if total is None else total + term
        if plan.rest:
            piece = size // plan.cuts
            tail = stacked[:, base + plan.full * size : base + plan.full * size + piece]
            term = jnp.concatenate(
                [dot(picks[plan.full + q], tail) for q in range(plan.cuts)], axis=1
            )
            total = term if total is None else total + term
        return total

    grad_ref[...] = gather(0, plan.D).astype(BF16)
    out_ref[...] = (to_column(gate_ref[...]) * gather(plan.DX, plan.F)).astype(BF16)


def update_kernel(plan, placement_ref, payload, *refs):
    groups, share, width = plan.groups, plan.share, plan.F
    near_x, refs = refs[:groups], refs[groups:]
    near_rest, refs = refs[:groups], refs[groups:]
    far_all, refs = refs[:groups], refs[groups:]
    other_g, refs = refs[:groups], refs[groups:]
    weight_ref, momentum_ref, new_weight, new_momentum, x_all, g_all = refs
    step = pl.program_id(0)
    tile = new_weight.shape[1]

    @pl.when(step == 0)
    def _():
        hot = is_hot(plan, placement_ref)
        x_parts, g_parts = [], []
        for m in range(groups):
            x_parts += [near_x[m][...], near_rest[m][:, :share], far_all[m][:, :share]]
            g_parts += [
                near_rest[m][:, share : share + width],
                near_rest[m][:, share + width :],
                far_all[m][:, share:],
            ]
        for i in range(plan.pieces):
            piece = payload[:, i * share : (i + 1) * share].astype(F32)
            x_parts.append(jnp.where(hot, piece, 0.0))
        g_parts += [g[...] for g in other_g]
        x_all[...] = jnp.concatenate([p.astype(F32) for p in x_parts], axis=0).astype(BF16)
        g_all[...] = jnp.concatenate([p.astype(F32) for p in g_parts], axis=0).astype(BF16)

    start = pl.multiple_of(step * tile, LANES)
    total = dot_tn(x_all[:, pl.ds(start, tile)], g_all[...])
    momentum = (decay_rate * momentum_ref[0].astype(F32) + total).astype(BF16)
    new_momentum[0] = momentum
    new_weight[0] = (
        weight_ref[0].astype(F32) - learning_rate * momentum.astype(F32)
    ).astype(BF16)


VMEM_LIMIT = 48 * 1024 * 1024
SMEM_SPEC = pl.BlockSpec(memory_space=pltpu.SMEM)
ANY_SPEC = pl.BlockSpec(memory_space=pl.ANY)
VMEM_SPEC = pl.BlockSpec(memory_space=pltpu.VMEM)


def call(kernel, plan, ins, specs, outs, scratch, flops, name):
    moved = sum(a.size * a.dtype.itemsize for a in ins) + sum(2 * r * c for r, c in outs)
    return pl.pallas_call(
        functools.partial(kernel, plan),
        out_shape=[jax.ShapeDtypeStruct(s, BF16) for s in outs],
        in_specs=specs,
        out_specs=[VMEM_SPEC] * len(outs),
        scratch_shapes=scratch,
        compiler_params=pltpu.CompilerParams(vmem_limit_bytes=VMEM_LIMIT),
        cost_estimate=pl.CostEstimate(flops=flops, bytes_accessed=moved, transcendentals=0),
        name=name,
    )(*ins)


def routed(plan, tokens, route_weight, cotangent, slot_ids, placement, weight, momentum):
    half, groups = plan.half, plan.groups
    D, F, C, rows, share = plan.D, plan.F, plan.C, plan.rows, plan.share
    slot = slot_ids.reshape(1, -1)
    gate = route_weight.reshape(1, -1)
    chunks = 7 if D % (7 * LANES) == 0 else 1

    def to_slot(data, m, flip):
        pairs = []
        for e in range(plan.slots):
            h, k = divmod(e, half)
            pairs.append((e, (h ^ flip) * half + away(k, m, half)))
        return lax.ppermute(data, "expert", pairs)

    def to_source(data, m):
        pairs = []
        for e in range(plan.slots):
            h, k = divmod(e, half)
            pairs.append((h * half + away(k, m, half), e))
        return lax.ppermute(data, "expert", pairs)

    def to_group(data, m):
        return lax.ppermute(data, "dp", [(d, away(d, m, groups)) for d in range(groups)])

    def spread(per_step):
        back = [m if groups & (groups - 1) == 0 else groups - m for m in range(groups)]
        return [per_step[0]] + [to_group(per_step[m], m) for m in back[1:]]

    packed = call(
        pack_kernel,
        plan,
        [slot, gate, tokens, cotangent],
        [VMEM_SPEC] * 4,
        [(2 * SUB, C)] * half + [(SUB, C)] * half,
        [],
        2 * 4 * half * SUB * plan.tokens * (D + F),
        "pack",
    )
    near = [packed[0]] + [to_slot(packed[m], m, 0) for m in range(1, half)]
    far = [to_slot(packed[half + m], m, 1) for m in range(half)]

    columns = call(
        columns_kernel,
        plan,
        near,
        [VMEM_SPEC] * half,
        [(rows, share)] * groups,
        [pltpu.VMEM((rows, D), BF16)],
        2 * rows * SUB * D,
        "near_columns",
    )
    near_x = spread(columns)
    held = [
        pltpu.VMEM((D, F), BF16),
        pltpu.VMEM((rows, D), BF16),
        pltpu.SemaphoreType.DMA((chunks,)),
    ]
    outs = call(
        near_kernel,
        plan,
        [placement, weight] + near,
        [SMEM_SPEC, ANY_SPEC] + [VMEM_SPEC] * half,
        [(SUB, C)] * half
        + [(half * SUB, C), (half * SUB, plan.FG)]
        + [(rows, share + 2 * F)] * groups,
        held,
        8 * rows * D * F,
        "near_rows",
    )
    back_near = [outs[0]] + [to_source(outs[m], m) for m in range(1, half)]
    local_far, folded_grad = outs[half], outs[half + 1]
    near_rest = spread(outs[half + 2 :])

    outs = call(
        far_kernel,
        plan,
        [placement, weight, folded_grad] + far + near_x,
        [SMEM_SPEC, ANY_SPEC] + [VMEM_SPEC] * (1 + half + groups),
        [(half * SUB, C)] + [(rows, share + F)] * groups,
        held,
        4 * rows * D * F,
        "far_rows",
    )
    payload = lax.ppermute(
        outs[0], "expert", [(e, (e + half) % plan.slots) for e in range(plan.slots)]
    )
    far_all = spread(outs[1:])

    outs = call(
        after_kernel,
        plan,
        [placement, payload, local_far],
        [SMEM_SPEC] + [VMEM_SPEC] * 2,
        [(SUB, C)] * half + [(rows, F)],
        [],
        1000000,
        "after_swap",
    )
    back_far = [outs[0]] + [to_source(outs[m], m) for m in range(1, half)]
    other_g = spread([outs[half]] * groups)

    tile = LANES
    steps = share // tile
    offset = share // tile
    total_rows = plan.groups * plan.rows * 4
    group = lax.axis_index("dp").reshape(1)

    def whole(*shape):
        return pl.BlockSpec(shape, lambda i, g: (0,) * len(shape))

    new_weight, new_momentum = pl.pallas_call(
        lambda g_ref, *refs: update_kernel(plan, *refs),
        grid_spec=pltpu.PrefetchScalarGridSpec(
            num_scalar_prefetch=1,
            grid=(steps,),
            in_specs=[SMEM_SPEC, whole(half * SUB, C)]
            + [whole(rows, share)] * groups
            + [whole(rows, share + 2 * F)] * groups
            + [whole(rows, share + F)] * groups
            + [whole(rows, F)] * groups
            + [
                pl.BlockSpec((1, tile, F), lambda i, g: (0, g[0] * offset + i, 0)),
                pl.BlockSpec((1, tile, F), lambda i, g: (0, i, 0)),
            ],
            out_specs=[pl.BlockSpec((1, tile, F), lambda i, g: (0, i, 0))] * 2,
            scratch_shapes=[
                pltpu.VMEM((total_rows, share), BF16),
                pltpu.VMEM((total_rows, F), BF16),
            ],
        ),
        out_shape=[jax.ShapeDtypeStruct((1, share, F), BF16)] * 2,
        compiler_params=pltpu.CompilerParams(vmem_limit_bytes=VMEM_LIMIT),
        cost_estimate=pl.CostEstimate(
            flops=2 * total_rows * share * F, bytes_accessed=16 * share * F, transcendentals=0
        ),
        name="update",
    )(group, placement, payload, *near_x, *near_rest, *far_all, *other_g, weight, momentum)

    expert_out, token_grad = call(
        unpack_kernel,
        plan,
        [slot, gate] + back_near + back_far,
        [VMEM_SPEC] * (2 + 2 * half),
        [(plan.tokens, F), (plan.tokens, D)],
        [],
        2 * 4 * half * SUB * plan.tokens * (D + F),
        "unpack",
    )
    return expert_out, token_grad, new_weight, new_momentum


def general(tokens, route_weight, cotangent, slot_ids, placement, weight, momentum):
    n_slots = lax.axis_size("expert")
    n_groups = lax.axis_size("dp")
    tok_count, D = tokens.shape
    F = cotangent.shape[1]
    capacity = tok_count * 9 // 8 // n_slots
    onehot = (slot_ids[:, None] == jnp.arange(n_slots, dtype=jnp.int32)[None, :]).astype(jnp.int32)
    ranks = jnp.sum((jnp.cumsum(onehot, axis=0) - 1) * onehot, axis=1)
    position = slot_ids * capacity + ranks
    send_rows = jnp.zeros((n_slots * capacity, D), BF16).at[position].set(tokens)
    scaled = (route_weight[:, None] * cotangent.astype(F32)).astype(BF16)
    send_grads = jnp.zeros((n_slots * capacity, F), BF16).at[position].set(scaled)
    matrix = weight[0]

    def exchange(rows):
        width = rows.shape[-1]
        return lax.all_to_all(
            rows.reshape(n_slots, capacity, width), "expert", split_axis=0, concat_axis=0, tiled=True
        ).reshape(-1, width)

    flat_x = exchange(send_rows)
    act, flat_grad = activate(dot(flat_x, matrix), exchange(send_grads))
    back = dot_nt(flat_grad, matrix).astype(BF16)
    act_rows = exchange(act)[position]
    expert_out = (route_weight[:, None] * act_rows.astype(F32)).astype(BF16)
    token_grad = exchange(back)[position]
    row_count = flat_x.shape[0]
    share = D // n_groups
    columns = lax.all_to_all(
        flat_x.reshape(1, row_count, n_groups, share), "dp", split_axis=2, concat_axis=0, tiled=True
    )
    columns = columns.reshape(n_groups, row_count, share)
    terms = jnp.einsum(
        "krd,krf->kdf",
        columns,
        lax.all_gather(flat_grad[None], "dp", axis=0, tiled=True),
        preferred_element_type=F32,
    )
    terms = lax.optimization_barrier(terms.astype(BF16)).astype(F32)
    reduced = jnp.sum(terms, axis=0).astype(BF16)
    half = n_slots // 2
    partner_grad = lax.ppermute(
        reduced, "expert", [(i, (i + half) % n_slots) for i in range(n_slots)]
    ).astype(F32)
    my_slot = lax.axis_index("expert")
    partner_slot = (my_slot + half) % n_slots
    same = placement[my_slot] == placement[partner_slot]
    total = reduced.astype(F32) + jnp.where(same, partner_grad, 0.0)
    new_momentum = (decay_rate * momentum[0].astype(F32) + total).astype(BF16)
    old = lax.dynamic_slice_in_dim(matrix, lax.axis_index("dp") * share, share, 0).astype(F32)
    new_weight = (old - learning_rate * new_momentum.astype(F32)).astype(BF16)
    return expert_out, token_grad, new_weight[None], new_momentum[None]


def solution(mesh):
    def shards(tokens, route_weight, cotangent, slot_ids, placement, weight, momentum):
        plan = Plan(
            mesh.shape["expert"],
            mesh.shape["dp"],
            tokens.shape[0],
            tokens.shape[1],
            cotangent.shape[1],
        )
        body = functools.partial(routed, plan) if plan.fits() else general
        return body(tokens, route_weight, cotangent, slot_ids, placement, weight, momentum)

    return jax.shard_map(
        shards,
        mesh=mesh,
        in_specs=(
            P(("dp", "expert"), None),
            P(("dp", "expert")),
            P(("dp", "expert"), None),
            P(("dp", "expert")),
            P(),
            P("expert", None, None),
            P("expert", "dp", None),
        ),
        out_specs=(
            P(("dp", "expert"), None),
            P(("dp", "expert"), None),
            P("expert", "dp", None),
            P("expert", "dp", None),
        ),
        check_vma=False,
    )
```

```python
import functools
import math

import jax
import jax.numpy as jnp
from jax import lax
from jax.experimental import pallas as pl
from jax.experimental.pallas import tpu as pltpu
from jax.sharding import PartitionSpec as P

learning_rate = 0.004
decay_rate = 0.9

BF16 = jnp.bfloat16
F32 = jnp.float32
SUB = 8
LANES = 128
INNER = 2


class Plan:
    def __init__(self, slots, groups, tokens, features, hidden):
        self.slots, self.groups, self.tokens = slots, groups, tokens
        self.D, self.F = features, hidden
        self.half = slots // 2
        self.cap = tokens * 9 // 8 // slots
        self.full, self.rest = divmod(self.cap, SUB)
        self.cuts = SUB // self.rest if self.rest else 1
        self.rows = self.half * self.cap
        self.share = features // groups
        self.DX = features * self.cap // SUB
        self.FG = hidden * self.cap // SUB
        self.C = self.DX + self.FG
        self.pieces = self.cap * groups // SUB
        self.outer = groups // INNER

    def group_at(self, group, step):
        chip, core = group // INNER, group % INNER
        if isinstance(group, int):
            return away(chip, step // INNER, self.outer) * INNER + (core ^ (step % INNER))
        return away_traced(chip, step // INNER, self.outer) * INNER + jnp.bitwise_xor(
            core, step % INNER
        )

    def group_from(self, step):
        chips = step // INNER
        if self.outer & (self.outer - 1):
            chips = (self.outer - chips) % self.outer
        return chips * INNER + step % INNER

    def fits(self):
        return (
            self.slots % 2 == 0
            and (self.rest == 0 or SUB % self.rest == 0)
            and self.D % (self.cuts * LANES) == 0
            and self.F % (self.cuts * LANES) == 0
            and self.D % (self.groups * LANES) == 0
            and self.groups % INNER == 0
            and (self.cap * self.groups) % SUB == 0
            and self.rows % SUB == 0
            and (self.half * self.rest) % SUB == 0
            and self.tokens % LANES == 0
        )


def away(place, step, count):
    if count & (count - 1) == 0:
        return place ^ step
    return (place + step) % count


def away_traced(place, step, count):
    if count & (count - 1) == 0:
        return jnp.bitwise_xor(place, step)
    return lax.rem(place + step, count)


def steps_between(first, second, count):
    if count & (count - 1) == 0:
        return jnp.bitwise_xor(first, second)
    return lax.rem(first - second + count, count)


def iota(shape, dim):
    return lax.broadcasted_iota(jnp.int32, shape, dim)


def dot(a, b):
    return jnp.dot(a, b, preferred_element_type=F32)


def dot_nt(a, b):
    return lax.dot_general(a, b, (((1,), (1,)), ((), ())), preferred_element_type=F32)


def dot_tn(a, b):
    return lax.dot_general(a, b, (((0,), (0,)), ((), ())), preferred_element_type=F32)


def picker(plan, cut):
    shape = (plan.half * plan.rest, plan.half * SUB)
    row, col = iota(shape, 0), iota(shape, 1)
    wanted = (row // plan.rest) * SUB + cut * plan.rest + row % plan.rest
    return (wanted == col).astype(BF16)


def unfold(plan, blocks, width):
    parts = [
        jnp.concatenate([b[:, i * width : (i + 1) * width] for b in blocks], axis=0)
        for i in range(plan.full)
    ]
    if plan.rest:
        piece = width // plan.cuts
        tail = jnp.concatenate([b[:, plan.full * width :] for b in blocks], axis=0).astype(BF16)
        parts.append(
            jnp.concatenate([dot(picker(plan, q), tail) for q in range(plan.cuts)], axis=1)
        )
    return jnp.concatenate(parts, axis=0).astype(BF16)


def fold(plan, rows):
    width = rows.shape[1]
    block = plan.half * SUB
    parts = [rows[i * block : (i + 1) * block] for i in range(plan.full)]
    if plan.rest:
        piece = width // plan.cuts
        tail = rows[plan.full * block :].astype(BF16)
        total = None
        for q in range(plan.cuts):
            term = dot_tn(picker(plan, q), tail[:, q * piece : (q + 1) * piece])
            total = term if total is None else total + term
        parts.append(total)
    return jnp.concatenate(parts, axis=1)


def is_hot(plan, placement_ref):
    me = lax.axis_index("expert")
    partner = lax.rem(me + plan.half, plan.slots)
    return placement_ref[me] == placement_ref[partner]


def token_places(plan, slot):
    me = lax.axis_index("expert")
    my_half = me // plan.half
    my_place = lax.rem(me, plan.half)
    upper = (slot >= plan.half).astype(jnp.int32)
    place = slot - plan.half * upper
    far = jnp.where(upper == my_half, 0, 1)
    step = steps_between(place, jnp.zeros_like(place) + my_place, plan.half)
    block = 2 * step + far
    count = plan.tokens
    onehot = (iota((2 * plan.half, count), 0) == block).astype(F32)
    upto = (iota((count, count), 0) <= iota((count, count), 1)).astype(BF16)
    seen = dot(onehot.astype(BF16), upto)
    rank = jnp.sum(onehot * (seen - 1.0), axis=0, keepdims=True).astype(jnp.int32)
    return block, rank


def row_targets(plan, block, rank):
    targets = []
    for i in range(plan.full):
        inside = (rank >= i * SUB) & (rank < (i + 1) * SUB)
        targets.append(jnp.where(inside, block * SUB + rank - i * SUB, -1))
    for q in range(plan.cuts if plan.rest else 0):
        inside = rank >= plan.full * SUB
        targets.append(
            jnp.where(inside, block * SUB + q * plan.rest + rank - plan.full * SUB, -1)
        )
    return targets


def to_column(row):
    n = row.shape[1]
    eye = (iota((n, n), 0) == iota((n, n), 1)).astype(F32)
    return jnp.sum(eye * row.astype(F32), axis=1, keepdims=True)


def pack_kernel(far, plan, slot_hbm, gate_hbm, tok_hbm, cot_hbm, *refs):
    half = plan.half
    outs, refs = refs[-half - 5 : -5], refs[-5:]
    slot_ref, gate_ref, tok_ref, cot_ref, sems = refs
    copies = [
        pltpu.make_async_copy(source, held, sems.at[i])
        for i, (source, held) in enumerate(
            ((slot_hbm, slot_ref), (tok_hbm, tok_ref), (gate_hbm, gate_ref), (cot_hbm, cot_ref))
        )
    ]
    for copy in copies:
        copy.start()
    copies[0].wait()
    block, rank = token_places(plan, slot_ref[...])
    wanted = lax.rem(block, 2) == far
    block = jnp.where(wanted, block // 2, -2)
    targets = row_targets(plan, block, rank)
    height = half * SUB
    onehots = [(iota((height, plan.tokens), 0) == t).astype(BF16) for t in targets]

    def store(values, start):
        stop = start + values.shape[1]
        for m in range(half):
            outs[m][:, start:stop] = values[m * SUB : (m + 1) * SUB].astype(BF16)

    def place(data, base):
        width = data.shape[1]
        for i in range(plan.full):
            store(dot(onehots[i], data), base + i * width)
        if plan.rest:
            piece = width // plan.cuts
            total = None
            for q in range(plan.cuts):
                term = dot(onehots[plan.full + q], data[:, q * piece : (q + 1) * piece])
                total = term if total is None else total + term
            store(total, base + plan.full * width)

    copies[1].wait()
    place(tok_ref[...], 0)
    copies[2].wait()
    copies[3].wait()
    scaled = (to_column(gate_ref[...]) * cot_ref[...].astype(F32)).astype(BF16)
    place(scaled, plan.DX)


def blocks_of(refs, start, stop):
    return [r[:, start:stop].astype(F32) for r in refs]


def columns_kernel(plan, *refs):
    half = plan.half
    near, far = refs[:half], refs[half : 2 * half]
    outs, held = refs[-plan.groups - 1 : -1], refs[-1]
    for i, blocks in enumerate((near, far)):
        held[i] = unfold(plan, blocks_of(blocks, 0, plan.DX), plan.D)
    for m in range(plan.groups):
        start = pl.multiple_of(plan.group_at(lax.axis_index("dp"), m) * plan.share, LANES)
        for i in range(2):
            outs[m][i] = held[i, :, pl.ds(start, plan.share)]


def activate(preact, scaled):
    sigma = jax.nn.sigmoid(preact)
    act = (preact * sigma).astype(BF16)
    grad_pre = (scaled.astype(F32) * sigma * (1.0 + preact * (1.0 - sigma))).astype(BF16)
    return act, grad_pre


def chip_columns(plan, rows, outs):
    width = INNER * plan.share
    chip = lax.axis_index("dp") // INNER
    for o in range(plan.outer):
        start = pl.multiple_of(away_traced(chip, o, plan.outer) * width, LANES)
        outs[o][:, :width] = rows[:, pl.ds(start, width)]


def near_kernel(plan, placement_ref, weight_ref, *refs):
    half = plan.half
    near, refs = refs[:half], refs[half:]
    far, refs = refs[:half], refs[half:]
    back_near, local_back, local_act, folded_grad, grads = refs[-5:]
    x_near = unfold(plan, blocks_of(near, 0, plan.DX), plan.D)
    x_far = unfold(plan, blocks_of(far, 0, plan.DX), plan.D)
    g_near = unfold(plan, blocks_of(near, plan.DX, plan.C), plan.F)
    g_far = unfold(plan, blocks_of(far, plan.DX, plan.C), plan.F)
    x = jnp.concatenate([x_near.astype(F32), x_far.astype(F32)], axis=0).astype(BF16)
    g = jnp.concatenate([g_near.astype(F32), g_far.astype(F32)], axis=0).astype(BF16)
    act, grad_pre = activate(dot(x, weight_ref[0]), g)
    back = dot_nt(grad_pre, weight_ref[0])
    act, grad32 = act.astype(F32), grad_pre.astype(F32)
    back_near[:, : plan.DX] = fold(plan, back[: plan.rows]).astype(BF16)
    back_near[:, plan.DX :] = fold(plan, act[: plan.rows]).astype(BF16)
    local_back[...] = fold(plan, back[plan.rows :]).astype(BF16)
    local_act[...] = fold(plan, act[plan.rows :]).astype(BF16)
    grad_near = grad32[: plan.rows]
    grad_far = jnp.where(is_hot(plan, placement_ref), grad32[plan.rows :], 0.0)
    folded_grad[...] = fold(plan, grad_near).astype(BF16)
    grads[:, : plan.F] = grad_near.astype(BF16)
    grads[:, plan.F :] = grad_far.astype(BF16)


def payload_kernel(
    plan, placement_ref, weight_ref, folded_grad, near_grads, *refs
):
    half, groups = plan.half, plan.groups
    far, refs = refs[:half], refs[half:]
    columns, refs = refs[:groups], refs[groups:]
    small, large, refs = refs[0], refs[1], refs[2:]
    share, refs = refs[:groups], refs[groups:]
    (rows,) = refs
    hot = is_hot(plan, placement_ref)
    width = plan.share
    x = unfold(plan, blocks_of(far, 0, plan.DX), plan.D)
    g = unfold(plan, blocks_of(far, plan.DX, plan.C), plan.F)
    rows[...] = x
    act, grad_pre = activate(dot(x, weight_ref[0]), g)

    @pl.when(jnp.logical_not(hot))
    def _():
        back = dot_nt(grad_pre, weight_ref[0])
        large[...] = fold(plan, back).astype(BF16)
        small[...] = fold(plan, act.astype(F32)).astype(BF16)

    @pl.when(hot)
    def _():
        together = jnp.concatenate([c[0].astype(F32) for c in columns], axis=0)
        block = half * SUB
        for i in range(plan.pieces):
            large[:, i * plan.share : (i + 1) * plan.share] = together[
                i * block : (i + 1) * block
            ].astype(BF16)
        small[...] = folded_grad[...]

    group = lax.axis_index("dp")
    for o in range(groups):
        start = pl.multiple_of(plan.group_at(group, o) * width, LANES)
        share[o][:, :width] = rows[:, pl.ds(start, width)]
        share[o][:, width : width + 2 * plan.F] = near_grads[...]
        share[o][:, width + 2 * plan.F :] = grad_pre


def after_small_kernel(plan, placement_ref, small, local_act, near_back, *outs):
    hot = is_hot(plan, placement_ref)
    payload = small[...].astype(F32)
    chosen = jnp.where(hot, local_act[...].astype(F32), payload)
    back = near_back[...].astype(F32)
    for m in range(plan.half):
        span = slice(m * SUB, (m + 1) * SUB)
        outs[m][:, : plan.C] = back[span].astype(BF16)
        outs[m][:, plan.C :] = chosen[span].astype(BF16)
    blocks = [payload[m * SUB : (m + 1) * SUB] for m in range(plan.half)]
    outs[plan.half][...] = jnp.where(hot, unfold(plan, blocks, plan.F).astype(F32), 0.0).astype(BF16)


def after_large_kernel(plan, placement_ref, large, local_back, *refs):
    outs = refs[-plan.half :]
    hot = is_hot(plan, placement_ref)
    chosen = jnp.where(hot, local_back[...].astype(F32), large[...].astype(F32))
    for m in range(plan.half):
        outs[m][...] = chosen[m * SUB : (m + 1) * SUB].astype(BF16)


def unpack_kernel(plan, slot_ref, gate_ref, *refs):
    early, refs = refs[: plan.half], refs[plan.half :]
    late, refs = refs[: plan.half], refs[plan.half :]
    out_ref, grad_ref = refs
    block, rank = token_places(plan, slot_ref[...])
    width = 2 * plan.half * SUB
    picks = []
    for target in row_targets(plan, block, rank):
        column = to_column(target).astype(jnp.int32)
        picks.append((iota((plan.tokens, width), 1) == column).astype(BF16))

    def gather(near, far, size):
        stacked = []
        for m in range(plan.half):
            stacked += [near[m], far[m]]
        stacked = jnp.concatenate(stacked, axis=0).astype(BF16)
        total = None
        for i in range(plan.full):
            term = dot(picks[i], stacked[:, i * size : (i + 1) * size])
            total = term if total is None else total + term
        if plan.rest:
            tail = stacked[:, plan.full * size :]
            term = jnp.concatenate(
                [dot(picks[plan.full + q], tail) for q in range(plan.cuts)], axis=1
            )
            total = term if total is None else total + term
        return total

    near = blocks_of(early, 0, plan.DX)
    grad_ref[...] = gather(near, blocks_of(late, 0, plan.DX), plan.D).astype(BF16)
    near = blocks_of(early, plan.DX, plan.C)
    far = blocks_of(early, plan.C, plan.C + plan.FG)
    out_ref[...] = (to_column(gate_ref[...]) * gather(near, far, plan.F)).astype(BF16)


def rows_of(parts):
    return jnp.concatenate([p.astype(F32) for p in parts], axis=0).astype(BF16)


def gather_kernel(plan, *refs):
    groups, share, width = plan.groups, plan.share, plan.F
    columns, refs = refs[:groups], refs[groups:]
    shared, refs = refs[:groups], refs[groups:]
    total, x_all = refs
    base = share
    x_parts, g_parts = [], []
    for m in range(groups):
        x_parts += [columns[m][0], columns[m][1], shared[m][:, :share]]
        g_parts += [shared[m][:, base + i * width : base + (i + 1) * width] for i in range(3)]
    x_all[...] = rows_of(x_parts)
    g_all = rows_of(g_parts)
    for i in range(share // LANES):
        span = slice(i * LANES, (i + 1) * LANES)
        total[span, :] = dot_tn(x_all[:, span], g_all)


def update_kernel(plan, placement_ref, large, *refs):
    other_g, refs = refs[: plan.groups], refs[plan.groups :]
    total_ref, weight_ref, momentum_ref, new_weight, new_momentum, x_all, g_all = refs
    step = pl.program_id(0)
    share = plan.share
    tile = new_weight.shape[1]

    @pl.when(step == 0)
    def _():
        hot = is_hot(plan, placement_ref)
        pieces = [
            large[:, i * share : (i + 1) * share].astype(F32) for i in range(plan.pieces)
        ]
        x_all[...] = jnp.where(hot, jnp.concatenate(pieces, axis=0), 0.0).astype(BF16)
        g_all[...] = rows_of([g[...] for g in other_g])

    start = pl.multiple_of(step * tile, LANES)
    total = total_ref[...] + dot_tn(x_all[:, pl.ds(start, tile)], g_all[...])
    momentum = (decay_rate * momentum_ref[0].astype(F32) + total).astype(BF16)
    new_momentum[0] = momentum
    new_weight[0] = (
        weight_ref[0].astype(F32) - learning_rate * momentum.astype(F32)
    ).astype(BF16)


MIB = 1024 * 1024
SMEM_SPEC = pl.BlockSpec(memory_space=pltpu.SMEM)
ANY_SPEC = pl.BlockSpec(memory_space=pl.ANY)
VMEM_SPEC = pl.BlockSpec(memory_space=pltpu.VMEM)


def call(kernel, plan, ins, specs, outs, scratch, flops, name, limit=16, dtype=BF16):
    moved = sum(a.size * a.dtype.itemsize for a in ins) + sum(2 * math.prod(o) for o in outs)
    return pl.pallas_call(
        functools.partial(kernel, plan),
        out_shape=[jax.ShapeDtypeStruct(s, dtype) for s in outs],
        in_specs=specs,
        out_specs=[VMEM_SPEC] * len(outs),
        scratch_shapes=scratch,
        compiler_params=pltpu.CompilerParams(vmem_limit_bytes=limit * MIB),
        cost_estimate=pl.CostEstimate(
            flops=flops, bytes_accessed=moved if flops else 0, transcendentals=0
        ),
        name=name,
    )(*ins)


def routed(plan, tokens, route_weight, cotangent, slot_ids, placement, weight, momentum):
    half, groups, outer = plan.half, plan.groups, plan.outer
    D, F, C, rows, share = plan.D, plan.F, plan.C, plan.rows, plan.share
    slot = slot_ids.reshape(1, -1)
    gate = route_weight.reshape(1, -1)

    def to_slot(data, m):
        pairs = []
        for e in range(plan.slots):
            h, k = divmod(e, half)
            pairs.append((e, h * half + away(k, m, half)))
        return lax.ppermute(data, "expert", pairs)

    def to_source(data, m):
        pairs = []
        for e in range(plan.slots):
            h, k = divmod(e, half)
            pairs.append((h * half + away(k, m, half), e))
        return lax.ppermute(data, "expert", pairs)

    def to_partner(data):
        pairs = [(e, (e + half) % plan.slots) for e in range(plan.slots)]
        return lax.ppermute(data, "expert", pairs)

    def from_group(data, m):
        pairs = []
        for d in range(groups):
            pairs.append((plan.group_at(d, m), d))
        return lax.ppermute(data, "dp", pairs)

    def from_chips(per_chip):
        got = [per_chip[0]]
        for o in range(1, outer):
            sent = o if outer & (outer - 1) == 0 else outer - o
            got.append(from_group(per_chip[sent], INNER * o))
        return got

    def with_sisters(got):
        return [data for own in got for data in (own, from_group(own, 1))]

    def pack(far, name, after, limit):
        return call(
            functools.partial(pack_kernel, far),
            plan,
            [slot, gate, tokens, cotangent] + after,
            [ANY_SPEC] * (4 + len(after)),
            [(SUB, C)] * half,
            [
                pltpu.VMEM(slot.shape, slot.dtype),
                pltpu.VMEM(gate.shape, gate.dtype),
                pltpu.VMEM(tokens.shape, tokens.dtype),
                pltpu.VMEM(cotangent.shape, cotangent.dtype),
                pltpu.SemaphoreType.DMA((4,)),
            ],
            2 * 4 * half * SUB * plan.tokens * (D + F),
            name,
            limit=limit,
        )

    packed = pack(1, "pack_far", [], 60)
    relay = [packed[0]] + [to_slot(packed[m], m) for m in range(1, half)]
    far = [to_partner(block) for block in relay]
    packed = pack(0, "pack_near", relay[1:] + far[:1], 8)
    near = [packed[0]] + [to_slot(packed[m], m) for m in range(1, half)]

    columns = call(
        columns_kernel,
        plan,
        near + relay + far[1:2],
        [VMEM_SPEC] * (2 * half) + [ANY_SPEC],
        [(2, rows, share)] * groups,
        [pltpu.VMEM((2, rows, D), BF16)],
        0,
        "near_columns",
    )
    columns_here = [columns[0]] + [
        from_group(columns[plan.group_from(m)], m) for m in range(1, groups)
    ]
    back_near, local_back, local_act, folded_grad, grads = call(
        near_kernel,
        plan,
        [placement, weight] + near + relay + [columns[0], far[2]],
        [SMEM_SPEC, VMEM_SPEC] + [VMEM_SPEC] * (2 * half) + [ANY_SPEC] * 2,
        [
            (half * SUB, C),
            (half * SUB, plan.DX),
            (half * SUB, plan.FG),
            (half * SUB, plan.FG),
            (rows, 2 * F),
        ],
        [],
        8 * rows * D * F,
        "near_rows",
    )
    outs = call(
        payload_kernel,
        plan,
        [placement, weight, folded_grad, grads] + far + columns_here,
        [SMEM_SPEC] + [VMEM_SPEC] * (3 + half + groups),
        [(half * SUB, plan.FG), (half * SUB, plan.DX)]
        + [(rows, share + 3 * F)] * groups,
        [pltpu.VMEM((rows, D), BF16)],
        4 * rows * D * F,
        "payload",
    )
    small = to_partner(outs[0])
    large = to_partner(outs[1])
    shared = outs[2 : 2 + groups]
    shared = [shared[0]] + [from_group(shared[plan.group_from(m)], m) for m in range(1, groups)]
    outs = call(
        after_small_kernel,
        plan,
        [placement, small, local_act, back_near],
        [SMEM_SPEC] + [VMEM_SPEC] * 3,
        [(SUB, C + plan.FG)] * half + [(rows, F)],
        [],
        0,
        "after_small",
    )
    early = [outs[0]] + [to_source(outs[m], m) for m in range(1, half)]
    other_g = with_sisters(from_chips([outs[half]] * outer))
    (total,) = call(
        gather_kernel,
        plan,
        columns_here + shared,
        [VMEM_SPEC] * (2 * groups),
        [(share, F)],
        [pltpu.VMEM((3 * groups * rows, share), BF16)],
        0,
        "own_terms",
        dtype=F32,
    )
    first = [total] + other_g[1:]
    outs = call(
        after_large_kernel,
        plan,
        [placement, large, local_back] + first,
        [SMEM_SPEC] + [VMEM_SPEC] * 2 + [ANY_SPEC] * len(first),
        [(SUB, plan.DX)] * half,
        [],
        1000000,
        "after_large",
    )
    far_back = [outs[0]] + [to_source(outs[m], m) for m in range(1, half)]

    tile = LANES
    steps = share // tile
    group = lax.axis_index("dp").reshape(1)

    def whole(*shape):
        return pl.BlockSpec(shape, lambda i, g: (0,) * len(shape))

    new_weight, new_momentum = pl.pallas_call(
        lambda g_ref, *refs: update_kernel(plan, *refs),
        grid_spec=pltpu.PrefetchScalarGridSpec(
            num_scalar_prefetch=1,
            grid=(steps,),
            in_specs=[SMEM_SPEC, whole(half * SUB, plan.DX)]
            + [whole(rows, F)] * groups
            + [
                pl.BlockSpec((tile, F), lambda i, g: (i, 0)),
                pl.BlockSpec((1, tile, F), lambda i, g: (0, g[0] * steps + i, 0)),
                pl.BlockSpec((1, tile, F), lambda i, g: (0, i, 0)),
            ],
            out_specs=[pl.BlockSpec((1, tile, F), lambda i, g: (0, i, 0))] * 2,
            scratch_shapes=[
                pltpu.VMEM((groups * rows, share), BF16),
                pltpu.VMEM((groups * rows, F), BF16),
            ],
        ),
        out_shape=[jax.ShapeDtypeStruct((1, share, F), BF16)] * 2,
        compiler_params=pltpu.CompilerParams(vmem_limit_bytes=16 * MIB),
        cost_estimate=pl.CostEstimate(
            flops=2 * groups * rows * share * F, bytes_accessed=12 * share * F, transcendentals=0
        ),
        name="update",
    )(group, placement, large, *other_g, total, weight, momentum)

    expert_out, token_grad = call(
        unpack_kernel,
        plan,
        [slot, gate] + early + far_back,
        [VMEM_SPEC] * (2 + 2 * half),
        [(plan.tokens, F), (plan.tokens, D)],
        [],
        2 * 4 * half * SUB * plan.tokens * (D + F),
        "unpack",
    )
    return expert_out, token_grad, new_weight, new_momentum


def general(tokens, route_weight, cotangent, slot_ids, placement, weight, momentum):
    n_slots = lax.axis_size("expert")
    n_groups = lax.axis_size("dp")
    tok_count, D = tokens.shape
    F = cotangent.shape[1]
    capacity = tok_count * 9 // 8 // n_slots
    onehot = (slot_ids[:, None] == jnp.arange(n_slots, dtype=jnp.int32)[None, :]).astype(jnp.int32)
    ranks = jnp.sum((jnp.cumsum(onehot, axis=0) - 1) * onehot, axis=1)
    position = slot_ids * capacity + ranks
    send_rows = jnp.zeros((n_slots * capacity, D), BF16).at[position].set(tokens)
    scaled = (route_weight[:, None] * cotangent.astype(F32)).astype(BF16)
    send_grads = jnp.zeros((n_slots * capacity, F), BF16).at[position].set(scaled)
    matrix = weight[0]

    def exchange(rows):
        width = rows.shape[-1]
        return lax.all_to_all(
            rows.reshape(n_slots, capacity, width), "expert", split_axis=0, concat_axis=0, tiled=True
        ).reshape(-1, width)

    flat_x = exchange(send_rows)
    act, flat_grad = activate(dot(flat_x, matrix), exchange(send_grads))
    back = dot_nt(flat_grad, matrix).astype(BF16)
    act_rows = exchange(act)[position]
    expert_out = (route_weight[:, None] * act_rows.astype(F32)).astype(BF16)
    token_grad = exchange(back)[position]
    row_count = flat_x.shape[0]
    share = D // n_groups
    columns = lax.all_to_all(
        flat_x.reshape(1, row_count, n_groups, share), "dp", split_axis=2, concat_axis=0, tiled=True
    )
    columns = columns.reshape(n_groups, row_count, share)
    terms = jnp.einsum(
        "krd,krf->kdf",
        columns,
        lax.all_gather(flat_grad[None], "dp", axis=0, tiled=True),
        preferred_element_type=F32,
    )
    terms = lax.optimization_barrier(terms.astype(BF16)).astype(F32)
    reduced = jnp.sum(terms, axis=0).astype(BF16)
    half = n_slots // 2
    partner_grad = lax.ppermute(
        reduced, "expert", [(i, (i + half) % n_slots) for i in range(n_slots)]
    ).astype(F32)
    my_slot = lax.axis_index("expert")
    partner_slot = (my_slot + half) % n_slots
    same = placement[my_slot] == placement[partner_slot]
    total = reduced.astype(F32) + jnp.where(same, partner_grad, 0.0)
    new_momentum = (decay_rate * momentum[0].astype(F32) + total).astype(BF16)
    old = lax.dynamic_slice_in_dim(matrix, lax.axis_index("dp") * share, share, 0).astype(F32)
    new_weight = (old - learning_rate * new_momentum.astype(F32)).astype(BF16)
    return expert_out, token_grad, new_weight[None], new_momentum[None]


def solution(mesh):
    def shards(tokens, route_weight, cotangent, slot_ids, placement, weight, momentum):
        plan = Plan(
            mesh.shape["expert"],
            mesh.shape["dp"],
            tokens.shape[0],
            tokens.shape[1],
            cotangent.shape[1],
        )
        body = functools.partial(routed, plan) if plan.fits() else general
        return body(tokens, route_weight, cotangent, slot_ids, placement, weight, momentum)

    return jax.shard_map(
        shards,
        mesh=mesh,
        in_specs=(
            P(("dp", "expert"), None),
            P(("dp", "expert")),
            P(("dp", "expert"), None),
            P(("dp", "expert")),
            P(),
            P("expert", None, None),
            P("expert", "dp", None),
        ),
        out_specs=(
            P(("dp", "expert"), None),
            P(("dp", "expert"), None),
            P("expert", "dp", None),
            P("expert", "dp", None),
        ),
        check_vma=False,
    )
```

```python
import functools
import math

import jax
import jax.numpy as jnp
from jax import lax
from jax.experimental import pallas as pl
from jax.experimental.pallas import tpu as pltpu
from jax.sharding import PartitionSpec as P

learning_rate = 0.004
decay_rate = 0.9

BF16 = jnp.bfloat16
F32 = jnp.float32
SUB = 8
LANES = 128
INNER = 2


class Plan:
    def __init__(self, slots, groups, tokens, features, hidden):
        self.slots, self.groups, self.tokens = slots, groups, tokens
        self.D, self.F = features, hidden
        self.half = slots // 2
        self.cap = tokens * 9 // 8 // slots
        self.full, self.rest = divmod(self.cap, SUB)
        self.cuts = SUB // self.rest if self.rest else 1
        self.rows = self.half * self.cap
        self.share = features // groups
        self.DX = features * self.cap // SUB
        self.FG = hidden * self.cap // SUB
        self.C = self.DX + self.FG
        self.pieces = self.cap * groups // SUB
        self.outer = groups // INNER

    def group_at(self, group, step):
        chip, core = group // INNER, group % INNER
        if isinstance(group, int):
            return away(chip, step // INNER, self.outer) * INNER + (core ^ (step % INNER))
        return away_traced(chip, step // INNER, self.outer) * INNER + jnp.bitwise_xor(
            core, step % INNER
        )

    def group_from(self, step):
        chips = step // INNER
        if self.outer & (self.outer - 1):
            chips = (self.outer - chips) % self.outer
        return chips * INNER + step % INNER

    def fits(self):
        return (
            self.slots % 2 == 0
            and (self.rest == 0 or SUB % self.rest == 0)
            and self.D % (self.cuts * LANES) == 0
            and self.F % (self.cuts * LANES) == 0
            and self.D % (self.groups * LANES) == 0
            and self.groups % INNER == 0
            and (self.cap * self.groups) % SUB == 0
            and self.rows % SUB == 0
            and (self.half * self.rest) % SUB == 0
            and self.tokens % LANES == 0
        )


def away(place, step, count):
    if count & (count - 1) == 0:
        return place ^ step
    return (place + step) % count


def away_traced(place, step, count):
    if count & (count - 1) == 0:
        return jnp.bitwise_xor(place, step)
    return lax.rem(place + step, count)


def steps_between(first, second, count):
    if count & (count - 1) == 0:
        return jnp.bitwise_xor(first, second)
    return lax.rem(first - second + count, count)


def iota(shape, dim):
    return lax.broadcasted_iota(jnp.int32, shape, dim)


def dot(a, b):
    return jnp.dot(a, b, preferred_element_type=F32)


def dot_nt(a, b):
    return lax.dot_general(a, b, (((1,), (1,)), ((), ())), preferred_element_type=F32)


def dot_tn(a, b):
    return lax.dot_general(a, b, (((0,), (0,)), ((), ())), preferred_element_type=F32)


def picker(plan, cut):
    shape = (plan.half * plan.rest, plan.half * SUB)
    row, col = iota(shape, 0), iota(shape, 1)
    wanted = (row // plan.rest) * SUB + cut * plan.rest + row % plan.rest
    return (wanted == col).astype(BF16)


def unfold(plan, blocks, width):
    parts = [
        jnp.concatenate([b[:, i * width : (i + 1) * width] for b in blocks], axis=0)
        for i in range(plan.full)
    ]
    if plan.rest:
        piece = width // plan.cuts
        tail = jnp.concatenate([b[:, plan.full * width :] for b in blocks], axis=0).astype(BF16)
        parts.append(
            jnp.concatenate([dot(picker(plan, q), tail) for q in range(plan.cuts)], axis=1)
        )
    return jnp.concatenate(parts, axis=0).astype(BF16)


def fold(plan, rows):
    width = rows.shape[1]
    block = plan.half * SUB
    parts = [rows[i * block : (i + 1) * block] for i in range(plan.full)]
    if plan.rest:
        piece = width // plan.cuts
        tail = rows[plan.full * block :].astype(BF16)
        total = None
        for q in range(plan.cuts):
            term = dot_tn(picker(plan, q), tail[:, q * piece : (q + 1) * piece])
            total = term if total is None else total + term
        parts.append(total)
    return jnp.concatenate(parts, axis=1)


def is_hot(plan, placement_ref):
    me = lax.axis_index("expert")
    partner = lax.rem(me + plan.half, plan.slots)
    return placement_ref[me] == placement_ref[partner]


def token_places(plan, slot):
    me = lax.axis_index("expert")
    my_half = me // plan.half
    my_place = lax.rem(me, plan.half)
    upper = (slot >= plan.half).astype(jnp.int32)
    place = slot - plan.half * upper
    far = jnp.where(upper == my_half, 0, 1)
    step = steps_between(place, jnp.zeros_like(place) + my_place, plan.half)
    block = 2 * step + far
    count = plan.tokens
    onehot = (iota((2 * plan.half, count), 0) == block).astype(F32)
    upto = (iota((count, count), 0) <= iota((count, count), 1)).astype(BF16)
    seen = dot(onehot.astype(BF16), upto)
    rank = jnp.sum(onehot * (seen - 1.0), axis=0, keepdims=True).astype(jnp.int32)
    return block, rank


def row_targets(plan, block, rank):
    targets = []
    for i in range(plan.full):
        inside = (rank >= i * SUB) & (rank < (i + 1) * SUB)
        targets.append(jnp.where(inside, block * SUB + rank - i * SUB, -1))
    for q in range(plan.cuts if plan.rest else 0):
        inside = rank >= plan.full * SUB
        targets.append(
            jnp.where(inside, block * SUB + q * plan.rest + rank - plan.full * SUB, -1)
        )
    return targets


def to_column(row):
    n = row.shape[1]
    eye = (iota((n, n), 0) == iota((n, n), 1)).astype(F32)
    return jnp.sum(eye * row.astype(F32), axis=1, keepdims=True)


def pack_kernel(plan, slot_hbm, gate_hbm, tok_hbm, cot_hbm, *refs):
    half = plan.half
    near, far = refs[:half], refs[half : 2 * half]
    slot_ref, gate_ref, tok_ref, cot_ref, sems = refs[2 * half :]
    copies = [
        pltpu.make_async_copy(source, held, sems.at[i])
        for i, (source, held) in enumerate(
            ((slot_hbm, slot_ref), (tok_hbm, tok_ref), (gate_hbm, gate_ref), (cot_hbm, cot_ref))
        )
    ]
    for copy in copies:
        copy.start()
    copies[0].wait()
    block, rank = token_places(plan, slot_ref[...])
    targets = row_targets(plan, block, rank)
    height = 2 * half * SUB
    onehots = [(iota((height, plan.tokens), 0) == t).astype(BF16) for t in targets]

    def store(values, start):
        stop = start + values.shape[1]
        for m in range(half):
            low = 2 * m * SUB
            near[m][:, start:stop] = values[low : low + 2 * SUB].astype(BF16)
            far[m][:, start:stop] = values[low + SUB : low + 2 * SUB].astype(BF16)

    def place(data, base):
        width = data.shape[1]
        for i in range(plan.full):
            store(dot(onehots[i], data), base + i * width)
        if plan.rest:
            piece = width // plan.cuts
            total = None
            for q in range(plan.cuts):
                term = dot(onehots[plan.full + q], data[:, q * piece : (q + 1) * piece])
                total = term if total is None else total + term
            store(total, base + plan.full * width)

    copies[1].wait()
    place(tok_ref[...], 0)
    copies[2].wait()
    copies[3].wait()
    scaled = (to_column(gate_ref[...]) * cot_ref[...].astype(F32)).astype(BF16)
    place(scaled, plan.DX)


def pass_kernel(plan, *refs):
    count = plan.half - 2
    for source, target in zip(refs[:count], refs[-count:]):
        target[...] = source[...]


def hold_kernel(plan, weight_hbm, held, sem):
    copy = pltpu.make_async_copy(weight_hbm.at[0], held, sem)
    copy.start()
    copy.wait()


def blocks_of(refs, start, stop, low=0):
    return [r[:, start:stop].astype(F32)[low : low + SUB] for r in refs]


def columns_kernel(plan, *refs):
    near, outs, held = refs[: plan.half], refs[-plan.groups - 1 : -1], refs[-1]
    for i in range(2):
        held[i] = unfold(plan, blocks_of(near, 0, plan.DX, i * SUB), plan.D)
    for m in range(plan.groups):
        start = pl.multiple_of(plan.group_at(lax.axis_index("dp"), m) * plan.share, LANES)
        for i in range(2):
            outs[m][i] = held[i, :, pl.ds(start, plan.share)]


def activate(preact, scaled):
    sigma = jax.nn.sigmoid(preact)
    act = (preact * sigma).astype(BF16)
    grad_pre = (scaled.astype(F32) * sigma * (1.0 + preact * (1.0 - sigma))).astype(BF16)
    return act, grad_pre


def chip_columns(plan, rows, outs):
    width = INNER * plan.share
    chip = lax.axis_index("dp") // INNER
    for o in range(plan.outer):
        start = pl.multiple_of(away_traced(chip, o, plan.outer) * width, LANES)
        outs[o][:, :width] = rows[:, pl.ds(start, width)]


def near_kernel(plan, placement_ref, weight_ref, *refs):
    near = refs[: plan.half]
    back_near, local_back, local_act, folded_grad, grads = refs[-5:]
    x_near = unfold(plan, blocks_of(near, 0, plan.DX), plan.D)
    x_far = unfold(plan, blocks_of(near, 0, plan.DX, SUB), plan.D)
    g_near = unfold(plan, blocks_of(near, plan.DX, plan.C), plan.F)
    g_far = unfold(plan, blocks_of(near, plan.DX, plan.C, SUB), plan.F)
    x = jnp.concatenate([x_near.astype(F32), x_far.astype(F32)], axis=0).astype(BF16)
    g = jnp.concatenate([g_near.astype(F32), g_far.astype(F32)], axis=0).astype(BF16)
    act, grad_pre = activate(dot(x, weight_ref[...]), g)
    back = dot_nt(grad_pre, weight_ref[...])
    act, grad32 = act.astype(F32), grad_pre.astype(F32)
    back_near[:, : plan.DX] = fold(plan, back[: plan.rows]).astype(BF16)
    back_near[:, plan.DX :] = fold(plan, act[: plan.rows]).astype(BF16)
    local_back[...] = fold(plan, back[plan.rows :]).astype(BF16)
    local_act[...] = fold(plan, act[plan.rows :]).astype(BF16)
    grad_near = grad32[: plan.rows]
    grad_far = jnp.where(is_hot(plan, placement_ref), grad32[plan.rows :], 0.0)
    folded_grad[...] = fold(plan, grad_near).astype(BF16)
    grads[:, : plan.F] = grad_near.astype(BF16)
    grads[:, plan.F :] = grad_far.astype(BF16)


def payload_kernel(
    plan, placement_ref, weight_ref, folded_grad, near_grads, *refs
):
    half, groups = plan.half, plan.groups
    far, refs = refs[:half], refs[half:]
    columns, refs = refs[:groups], refs[groups:]
    small, large, refs = refs[0], refs[1], refs[2:]
    share, refs = refs[:groups], refs[groups:]
    (rows,) = refs
    hot = is_hot(plan, placement_ref)
    width = plan.share
    x = unfold(plan, blocks_of(far, 0, plan.DX), plan.D)
    g = unfold(plan, blocks_of(far, plan.DX, plan.C), plan.F)
    rows[...] = x
    act, grad_pre = activate(dot(x, weight_ref[...]), g)

    @pl.when(jnp.logical_not(hot))
    def _():
        back = dot_nt(grad_pre, weight_ref[...])
        large[...] = fold(plan, back).astype(BF16)
        small[...] = fold(plan, act.astype(F32)).astype(BF16)

    @pl.when(hot)
    def _():
        together = jnp.concatenate([c[0].astype(F32) for c in columns], axis=0)
        block = half * SUB
        for i in range(plan.pieces):
            large[:, i * plan.share : (i + 1) * plan.share] = together[
                i * block : (i + 1) * block
            ].astype(BF16)
        small[...] = folded_grad[...]

    group = lax.axis_index("dp")
    for o in range(groups):
        start = pl.multiple_of(plan.group_at(group, o) * width, LANES)
        share[o][:, :width] = rows[:, pl.ds(start, width)]
        share[o][:, width : width + 2 * plan.F] = near_grads[...]
        share[o][:, width + 2 * plan.F :] = grad_pre


def after_small_kernel(plan, placement_ref, small, local_act, near_back, *outs):
    hot = is_hot(plan, placement_ref)
    payload = small[...].astype(F32)
    chosen = jnp.where(hot, local_act[...].astype(F32), payload)
    back = near_back[...].astype(F32)
    for m in range(plan.half):
        span = slice(m * SUB, (m + 1) * SUB)
        outs[m][:, : plan.C] = back[span].astype(BF16)
        outs[m][:, plan.C :] = chosen[span].astype(BF16)
    blocks = [payload[m * SUB : (m + 1) * SUB] for m in range(plan.half)]
    outs[plan.half][...] = jnp.where(hot, unfold(plan, blocks, plan.F).astype(F32), 0.0).astype(BF16)


def after_large_kernel(plan, placement_ref, large, local_back, *refs):
    outs = refs[-plan.half :]
    hot = is_hot(plan, placement_ref)
    chosen = jnp.where(hot, local_back[...].astype(F32), large[...].astype(F32))
    for m in range(plan.half):
        outs[m][...] = chosen[m * SUB : (m + 1) * SUB].astype(BF16)


def unpack_kernel(plan, slot_ref, gate_ref, *refs):
    early, refs = refs[: plan.half], refs[plan.half :]
    late, refs = refs[: plan.half], refs[plan.half :]
    out_ref, grad_ref = refs
    block, rank = token_places(plan, slot_ref[...])
    width = 2 * plan.half * SUB
    picks = []
    for target in row_targets(plan, block, rank):
        column = to_column(target).astype(jnp.int32)
        picks.append((iota((plan.tokens, width), 1) == column).astype(BF16))

    def gather(near, far, size):
        stacked = []
        for m in range(plan.half):
            stacked += [near[m], far[m]]
        stacked = jnp.concatenate(stacked, axis=0).astype(BF16)
        total = None
        for i in range(plan.full):
            term = dot(picks[i], stacked[:, i * size : (i + 1) * size])
            total = term if total is None else total + term
        if plan.rest:
            tail = stacked[:, plan.full * size :]
            term = jnp.concatenate(
                [dot(picks[plan.full + q], tail) for q in range(plan.cuts)], axis=1
            )
            total = term if total is None else total + term
        return total

    near = blocks_of(early, 0, plan.DX)
    grad_ref[...] = gather(near, blocks_of(late, 0, plan.DX), plan.D).astype(BF16)
    near = blocks_of(early, plan.DX, plan.C)
    far = blocks_of(early, plan.C, plan.C + plan.FG)
    out_ref[...] = (to_column(gate_ref[...]) * gather(near, far, plan.F)).astype(BF16)


def rows_of(parts):
    return jnp.concatenate([p.astype(F32) for p in parts], axis=0).astype(BF16)


def gather_kernel(plan, weight_hbm, momentum_hbm, waiting, *refs):
    groups, share, width = plan.groups, plan.share, plan.F
    columns, refs = refs[:groups], refs[groups:]
    shared, refs = refs[:groups], refs[groups:]
    total, old_weight, passed, x_all, momentum, sems = refs
    mine = pl.multiple_of(lax.axis_index("dp") * share, LANES)
    copies = [
        pltpu.make_async_copy(momentum_hbm.at[0], momentum, sems.at[0]),
        pltpu.make_async_copy(weight_hbm.at[0, pl.ds(mine, share), :], old_weight, sems.at[1]),
    ]
    for copy in copies:
        copy.start()
    passed[...] = waiting[...]
    x_parts, g_parts = [], []
    for m in range(groups):
        x_parts += [columns[m][0], columns[m][1], shared[m][:, :share]]
        g_parts += [shared[m][:, share + i * width : share + (i + 1) * width] for i in range(3)]
    x_all[...] = rows_of(x_parts)
    g_all = rows_of(g_parts)
    for copy in copies:
        copy.wait()
    for i in range(share // LANES):
        span = slice(i * LANES, (i + 1) * LANES)
        before = decay_rate * momentum[span, :].astype(F32)
        total[span, :] = before + dot_tn(x_all[:, span], g_all)


def update_kernel(plan, placement_ref, large, *refs):
    other_g, refs = refs[: plan.groups], refs[plan.groups :]
    total_ref, weight_ref, new_weight, new_momentum, x_all, g_all = refs
    step = pl.program_id(0)
    share = plan.share
    tile = new_weight.shape[1]

    @pl.when(step == 0)
    def _():
        hot = is_hot(plan, placement_ref)
        pieces = [
            large[:, i * share : (i + 1) * share].astype(F32) for i in range(plan.pieces)
        ]
        x_all[...] = jnp.where(hot, jnp.concatenate(pieces, axis=0), 0.0).astype(BF16)
        g_all[...] = rows_of([g[...] for g in other_g])

    start = pl.multiple_of(step * tile, LANES)
    total = total_ref[...] + dot_tn(x_all[:, pl.ds(start, tile)], g_all[...])
    momentum = total.astype(BF16)
    new_momentum[0] = momentum
    new_weight[0] = (
        weight_ref[...].astype(F32) - learning_rate * momentum.astype(F32)
    ).astype(BF16)


MIB = 1024 * 1024
SMEM_SPEC = pl.BlockSpec(memory_space=pltpu.SMEM)
ANY_SPEC = pl.BlockSpec(memory_space=pl.ANY)
VMEM_SPEC = pl.BlockSpec(memory_space=pltpu.VMEM)


def call(kernel, plan, ins, specs, outs, scratch, flops, name, limit=16, dtypes=None):
    moved = sum(a.size * a.dtype.itemsize for a in ins) + sum(2 * math.prod(o) for o in outs)
    return pl.pallas_call(
        functools.partial(kernel, plan),
        out_shape=[
            jax.ShapeDtypeStruct(s, dtypes[i] if dtypes else BF16) for i, s in enumerate(outs)
        ],
        in_specs=specs,
        out_specs=[VMEM_SPEC] * len(outs),
        scratch_shapes=scratch,
        compiler_params=pltpu.CompilerParams(vmem_limit_bytes=limit * MIB),
        cost_estimate=pl.CostEstimate(
            flops=flops, bytes_accessed=moved if flops else 0, transcendentals=0
        ),
        name=name,
    )(*ins)


def routed(plan, tokens, route_weight, cotangent, slot_ids, placement, weight, momentum):
    half, groups, outer = plan.half, plan.groups, plan.outer
    D, F, C, rows, share = plan.D, plan.F, plan.C, plan.rows, plan.share
    slot = slot_ids.reshape(1, -1)
    gate = route_weight.reshape(1, -1)

    def to_slot(data, m, flip=0):
        pairs = []
        for e in range(plan.slots):
            h, k = divmod(e, half)
            pairs.append((e, (h ^ flip) * half + away(k, m, half)))
        return lax.ppermute(data, "expert", pairs)

    def to_source(data, m):
        pairs = []
        for e in range(plan.slots):
            h, k = divmod(e, half)
            pairs.append((h * half + away(k, m, half), e))
        return lax.ppermute(data, "expert", pairs)

    def to_partner(data):
        pairs = [(e, (e + half) % plan.slots) for e in range(plan.slots)]
        return lax.ppermute(data, "expert", pairs)

    def from_group(data, m):
        pairs = []
        for d in range(groups):
            pairs.append((plan.group_at(d, m), d))
        return lax.ppermute(data, "dp", pairs)

    def from_chips(per_chip):
        got = [per_chip[0]]
        for o in range(1, outer):
            sent = o if outer & (outer - 1) == 0 else outer - o
            got.append(from_group(per_chip[sent], INNER * o))
        return got

    def with_sisters(got):
        return [data for own in got for data in (own, from_group(own, 1))]

    packed = call(
        pack_kernel,
        plan,
        [slot, gate, tokens, cotangent],
        [ANY_SPEC] * 4,
        [(2 * SUB, C)] * half + [(SUB, C)] * half,
        [
            pltpu.VMEM(slot.shape, slot.dtype),
            pltpu.VMEM(gate.shape, gate.dtype),
            pltpu.VMEM(tokens.shape, tokens.dtype),
            pltpu.VMEM(cotangent.shape, cotangent.dtype),
            pltpu.SemaphoreType.DMA((4,)),
        ],
        2 * 4 * half * SUB * plan.tokens * (D + F),
        "pack",
        limit=60,
    )
    near = [packed[0]] + [to_slot(packed[m], m) for m in range(1, half)]
    far = [to_slot(packed[half + m], m, 1) for m in range(2)]
    later = call(
        pass_kernel,
        plan,
        list(packed[half + 2 :]) + far[:1],
        [VMEM_SPEC] * (half - 2) + [ANY_SPEC],
        [(SUB, C)] * (half - 2),
        [],
        0,
        "pass_on",
    )
    far += [to_slot(later[m - 2], m, 1) for m in range(2, half)]
    (held,) = call(
        hold_kernel,
        plan,
        [weight],
        [ANY_SPEC],
        [(D, F)],
        [pltpu.SemaphoreType.DMA],
        0,
        "hold",
        limit=40,
    )
    columns = call(
        columns_kernel,
        plan,
        near + [held] + [later[0], far[1]],
        [VMEM_SPEC] * half + [ANY_SPEC] * 3,
        [(2, rows, share)] * groups,
        [pltpu.VMEM((2, rows, D), BF16)],
        0,
        "near_columns",
    )
    columns_here = [columns[0]] + [
        from_group(columns[plan.group_from(m)], m) for m in range(1, groups)
    ]
    back_near, local_back, local_act, folded_grad, grads = call(
        near_kernel,
        plan,
        [placement, held] + near + [columns[0], far[2]],
        [SMEM_SPEC] + [VMEM_SPEC] * (1 + half) + [ANY_SPEC] * 2,
        [
            (half * SUB, C),
            (half * SUB, plan.DX),
            (half * SUB, plan.FG),
            (half * SUB, plan.FG),
            (rows, 2 * F),
        ],
        [],
        8 * rows * D * F,
        "near_rows",
    )
    outs = call(
        payload_kernel,
        plan,
        [placement, held, folded_grad, grads] + far + columns_here,
        [SMEM_SPEC] + [VMEM_SPEC] * (3 + half + groups),
        [(half * SUB, plan.FG), (half * SUB, plan.DX)]
        + [(rows, share + 3 * F)] * groups,
        [pltpu.VMEM((rows, D), BF16)],
        4 * rows * D * F,
        "payload",
    )
    small = to_partner(outs[0])
    large = to_partner(outs[1])
    shared = outs[2 : 2 + groups]
    shared = [shared[0]] + [from_group(shared[plan.group_from(m)], m) for m in range(1, groups)]
    outs = call(
        after_small_kernel,
        plan,
        [placement, small, local_act, back_near],
        [SMEM_SPEC] + [VMEM_SPEC] * 3,
        [(SUB, C + plan.FG)] * half + [(rows, F)],
        [],
        0,
        "after_small",
    )
    early = [outs[0]] + [to_source(outs[m], m) for m in range(1, half)]
    total, old_weight, passed = call(
        gather_kernel,
        plan,
        [weight, momentum, outs[half]] + columns_here + shared,
        [ANY_SPEC] * 2 + [VMEM_SPEC] * (1 + 2 * groups),
        [(share, F), (share, F), (rows, F)],
        [
            pltpu.VMEM((3 * groups * rows, share), BF16),
            pltpu.VMEM((share, F), BF16),
            pltpu.SemaphoreType.DMA((2,)),
        ],
        0,
        "own_terms",
        limit=24,
        dtypes=[F32, BF16, BF16],
    )
    other_g = with_sisters(from_chips([passed] * outer))
    first = [total] + early[1:]
    outs = call(
        after_large_kernel,
        plan,
        [placement, large, local_back] + first,
        [SMEM_SPEC] + [VMEM_SPEC] * 2 + [ANY_SPEC] * len(first),
        [(SUB, plan.DX)] * half,
        [],
        1000000,
        "after_large",
    )
    far_back = [outs[0]] + [to_source(outs[m], m) for m in range(1, half)]

    tile = LANES
    steps = share // tile
    group = lax.axis_index("dp").reshape(1)

    def whole(*shape):
        return pl.BlockSpec(shape, lambda i, g: (0,) * len(shape))

    new_weight, new_momentum = pl.pallas_call(
        lambda g_ref, *refs: update_kernel(plan, *refs),
        grid_spec=pltpu.PrefetchScalarGridSpec(
            num_scalar_prefetch=1,
            grid=(steps,),
            in_specs=[SMEM_SPEC, whole(half * SUB, plan.DX)]
            + [whole(rows, F)] * groups
            + [
                pl.BlockSpec((tile, F), lambda i, g: (i, 0)),
                pl.BlockSpec((tile, F), lambda i, g: (i, 0)),
            ],
            out_specs=[pl.BlockSpec((1, tile, F), lambda i, g: (0, i, 0))] * 2,
            scratch_shapes=[
                pltpu.VMEM((groups * rows, share), BF16),
                pltpu.VMEM((groups * rows, F), BF16),
            ],
        ),
        out_shape=[jax.ShapeDtypeStruct((1, share, F), BF16)] * 2,
        compiler_params=pltpu.CompilerParams(vmem_limit_bytes=16 * MIB),
        cost_estimate=pl.CostEstimate(
            flops=2 * groups * rows * share * F, bytes_accessed=12 * share * F, transcendentals=0
        ),
        name="update",
    )(group, placement, large, *other_g, total, old_weight)

    expert_out, token_grad = call(
        unpack_kernel,
        plan,
        [slot, gate] + early + far_back,
        [VMEM_SPEC] * (2 + 2 * half),
        [(plan.tokens, F), (plan.tokens, D)],
        [],
        2 * 4 * half * SUB * plan.tokens * (D + F),
        "unpack",
    )
    return expert_out, token_grad, new_weight, new_momentum


def general(tokens, route_weight, cotangent, slot_ids, placement, weight, momentum):
    n_slots = lax.axis_size("expert")
    n_groups = lax.axis_size("dp")
    tok_count, D = tokens.shape
    F = cotangent.shape[1]
    capacity = tok_count * 9 // 8 // n_slots
    onehot = (slot_ids[:, None] == jnp.arange(n_slots, dtype=jnp.int32)[None, :]).astype(jnp.int32)
    ranks = jnp.sum((jnp.cumsum(onehot, axis=0) - 1) * onehot, axis=1)
    position = slot_ids * capacity + ranks
    send_rows = jnp.zeros((n_slots * capacity, D), BF16).at[position].set(tokens)
    scaled = (route_weight[:, None] * cotangent.astype(F32)).astype(BF16)
    send_grads = jnp.zeros((n_slots * capacity, F), BF16).at[position].set(scaled)
    matrix = weight[0]

    def exchange(rows):
        width = rows.shape[-1]
        return lax.all_to_all(
            rows.reshape(n_slots, capacity, width), "expert", split_axis=0, concat_axis=0, tiled=True
        ).reshape(-1, width)

    flat_x = exchange(send_rows)
    act, flat_grad = activate(dot(flat_x, matrix), exchange(send_grads))
    back = dot_nt(flat_grad, matrix).astype(BF16)
    act_rows = exchange(act)[position]
    expert_out = (route_weight[:, None] * act_rows.astype(F32)).astype(BF16)
    token_grad = exchange(back)[position]
    row_count = flat_x.shape[0]
    share = D // n_groups
    columns = lax.all_to_all(
        flat_x.reshape(1, row_count, n_groups, share), "dp", split_axis=2, concat_axis=0, tiled=True
    )
    columns = columns.reshape(n_groups, row_count, share)
    terms = jnp.einsum(
        "krd,krf->kdf",
        columns,
        lax.all_gather(flat_grad[None], "dp", axis=0, tiled=True),
        preferred_element_type=F32,
    )
    terms = lax.optimization_barrier(terms.astype(BF16)).astype(F32)
    reduced = jnp.sum(terms, axis=0).astype(BF16)
    half = n_slots // 2
    partner_grad = lax.ppermute(
        reduced, "expert", [(i, (i + half) % n_slots) for i in range(n_slots)]
    ).astype(F32)
    my_slot = lax.axis_index("expert")
    partner_slot = (my_slot + half) % n_slots
    same = placement[my_slot] == placement[partner_slot]
    total = reduced.astype(F32) + jnp.where(same, partner_grad, 0.0)
    new_momentum = (decay_rate * momentum[0].astype(F32) + total).astype(BF16)
    old = lax.dynamic_slice_in_dim(matrix, lax.axis_index("dp") * share, share, 0).astype(F32)
    new_weight = (old - learning_rate * new_momentum.astype(F32)).astype(BF16)
    return expert_out, token_grad, new_weight[None], new_momentum[None]


def solution(mesh):
    def shards(tokens, route_weight, cotangent, slot_ids, placement, weight, momentum):
        plan = Plan(
            mesh.shape["expert"],
            mesh.shape["dp"],
            tokens.shape[0],
            tokens.shape[1],
            cotangent.shape[1],
        )
        body = functools.partial(routed, plan) if plan.fits() else general
        return body(tokens, route_weight, cotangent, slot_ids, placement, weight, momentum)

    return jax.shard_map(
        shards,
        mesh=mesh,
        in_specs=(
            P(("dp", "expert"), None),
            P(("dp", "expert")),
            P(("dp", "expert"), None),
            P(("dp", "expert")),
            P(),
            P("expert", None, None),
            P("expert", "dp", None),
        ),
        out_specs=(
            P(("dp", "expert"), None),
            P(("dp", "expert"), None),
            P("expert", "dp", None),
            P("expert", "dp", None),
        ),
        check_vma=False,
    )
```

```python
import functools
import math

import jax
import jax.numpy as jnp
from jax import lax
from jax.experimental import pallas as pl
from jax.experimental.pallas import tpu as pltpu
from jax.sharding import PartitionSpec as P

learning_rate = 0.004
decay_rate = 0.9

BF16 = jnp.bfloat16
F32 = jnp.float32
SUB = 8
LANES = 128
INNER = 2


class Plan:
    def __init__(self, slots, groups, tokens, features, hidden):
        self.slots, self.groups, self.tokens = slots, groups, tokens
        self.D, self.F = features, hidden
        self.half = slots // 2
        self.cap = tokens * 9 // 8 // slots
        self.full, self.rest = divmod(self.cap, SUB)
        self.cuts = SUB // self.rest if self.rest else 1
        self.rows = self.half * self.cap
        self.share = features // groups
        self.DX = features * self.cap // SUB
        self.FG = hidden * self.cap // SUB
        self.C = self.DX + self.FG
        self.pieces = self.cap * groups // SUB
        self.outer = groups // INNER

    def group_at(self, group, step):
        chip, core = group // INNER, group % INNER
        if isinstance(group, int):
            return away(chip, step // INNER, self.outer) * INNER + (core ^ (step % INNER))
        return away_traced(chip, step // INNER, self.outer) * INNER + jnp.bitwise_xor(
            core, step % INNER
        )

    def group_from(self, step):
        chips = step // INNER
        if self.outer & (self.outer - 1):
            chips = (self.outer - chips) % self.outer
        return chips * INNER + step % INNER

    def fits(self):
        return (
            self.slots % 2 == 0
            and (self.rest == 0 or SUB % self.rest == 0)
            and self.D % (self.cuts * LANES) == 0
            and self.F % (self.cuts * LANES) == 0
            and self.D % (self.groups * LANES) == 0
            and self.groups % INNER == 0
            and (self.cap * self.groups) % SUB == 0
            and self.rows % SUB == 0
            and (self.half * self.rest) % SUB == 0
            and self.tokens % LANES == 0
        )


def away(place, step, count):
    if count & (count - 1) == 0:
        return place ^ step
    return (place + step) % count


def away_traced(place, step, count):
    if count & (count - 1) == 0:
        return jnp.bitwise_xor(place, step)
    return lax.rem(place + step, count)


def steps_between(first, second, count):
    if count & (count - 1) == 0:
        return jnp.bitwise_xor(first, second)
    return lax.rem(first - second + count, count)


def iota(shape, dim):
    return lax.broadcasted_iota(jnp.int32, shape, dim)


def dot(a, b):
    return jnp.dot(a, b, preferred_element_type=F32)


def dot_nt(a, b):
    return lax.dot_general(a, b, (((1,), (1,)), ((), ())), preferred_element_type=F32)


def dot_tn(a, b):
    return lax.dot_general(a, b, (((0,), (0,)), ((), ())), preferred_element_type=F32)


def picker(plan, cut):
    shape = (plan.half * plan.rest, plan.half * SUB)
    row, col = iota(shape, 0), iota(shape, 1)
    wanted = (row // plan.rest) * SUB + cut * plan.rest + row % plan.rest
    return (wanted == col).astype(BF16)


def unfold(plan, blocks, width):
    parts = [
        jnp.concatenate([b[:, i * width : (i + 1) * width] for b in blocks], axis=0)
        for i in range(plan.full)
    ]
    if plan.rest:
        piece = width // plan.cuts
        tail = jnp.concatenate([b[:, plan.full * width :] for b in blocks], axis=0).astype(BF16)
        parts.append(
            jnp.concatenate([dot(picker(plan, q), tail) for q in range(plan.cuts)], axis=1)
        )
    return jnp.concatenate(parts, axis=0).astype(BF16)


def fold(plan, rows):
    width = rows.shape[1]
    block = plan.half * SUB
    parts = [rows[i * block : (i + 1) * block] for i in range(plan.full)]
    if plan.rest:
        piece = width // plan.cuts
        tail = rows[plan.full * block :].astype(BF16)
        total = None
        for q in range(plan.cuts):
            term = dot_tn(picker(plan, q), tail[:, q * piece : (q + 1) * piece])
            total = term if total is None else total + term
        parts.append(total)
    return jnp.concatenate(parts, axis=1)


def is_hot(plan, placement_ref):
    me = lax.axis_index("expert")
    partner = lax.rem(me + plan.half, plan.slots)
    return placement_ref[me] == placement_ref[partner]


def token_places(plan, slot):
    me = lax.axis_index("expert")
    my_half = me // plan.half
    my_place = lax.rem(me, plan.half)
    upper = (slot >= plan.half).astype(jnp.int32)
    place = slot - plan.half * upper
    far = jnp.where(upper == my_half, 0, 1)
    step = steps_between(place, jnp.zeros_like(place) + my_place, plan.half)
    block = 2 * step + far
    count = plan.tokens
    onehot = (iota((2 * plan.half, count), 0) == block).astype(F32)
    upto = (iota((count, count), 0) <= iota((count, count), 1)).astype(BF16)
    seen = dot(onehot.astype(BF16), upto)
    rank = jnp.sum(onehot * (seen - 1.0), axis=0, keepdims=True).astype(jnp.int32)
    return block, rank


def row_targets(plan, block, rank):
    targets = []
    for i in range(plan.full):
        inside = (rank >= i * SUB) & (rank < (i + 1) * SUB)
        targets.append(jnp.where(inside, block * SUB + rank - i * SUB, -1))
    for q in range(plan.cuts if plan.rest else 0):
        inside = rank >= plan.full * SUB
        targets.append(
            jnp.where(inside, block * SUB + q * plan.rest + rank - plan.full * SUB, -1)
        )
    return targets


def to_column(row):
    n = row.shape[1]
    eye = (iota((n, n), 0) == iota((n, n), 1)).astype(F32)
    return jnp.sum(eye * row.astype(F32), axis=1, keepdims=True)


def pack_kernel(plan, slot_hbm, gate_hbm, tok_hbm, cot_hbm, *refs):
    half = plan.half
    near, far = refs[:half], refs[half : 2 * half]
    slot_ref, gate_ref, tok_ref, cot_ref, sems = refs[2 * half :]
    copies = [
        pltpu.make_async_copy(source, held, sems.at[i])
        for i, (source, held) in enumerate(
            ((slot_hbm, slot_ref), (tok_hbm, tok_ref), (gate_hbm, gate_ref), (cot_hbm, cot_ref))
        )
    ]
    for copy in copies:
        copy.start()
    copies[0].wait()
    block, rank = token_places(plan, slot_ref[...])
    targets = row_targets(plan, block, rank)
    height = 2 * half * SUB
    onehots = [(iota((height, plan.tokens), 0) == t).astype(BF16) for t in targets]

    def store(values, start):
        stop = start + values.shape[1]
        for m in range(half):
            low = 2 * m * SUB
            near[m][:, start:stop] = values[low : low + 2 * SUB].astype(BF16)
            far[m][:, start:stop] = values[low + SUB : low + 2 * SUB].astype(BF16)

    def place(data, base):
        width = data.shape[1]
        for i in range(plan.full):
            store(dot(onehots[i], data), base + i * width)
        if plan.rest:
            piece = width // plan.cuts
            total = None
            for q in range(plan.cuts):
                term = dot(onehots[plan.full + q], data[:, q * piece : (q + 1) * piece])
                total = term if total is None else total + term
            store(total, base + plan.full * width)

    copies[1].wait()
    place(tok_ref[...], 0)
    copies[2].wait()
    copies[3].wait()
    scaled = (to_column(gate_ref[...]) * cot_ref[...].astype(F32)).astype(BF16)
    place(scaled, plan.DX)


def hold_kernel(plan, weight_hbm, held, sem):
    copy = pltpu.make_async_copy(weight_hbm.at[0], held, sem)
    copy.start()
    copy.wait()


def blocks_of(refs, start, stop, low=0):
    return [r[:, start:stop].astype(F32)[low : low + SUB] for r in refs]


def columns_kernel(plan, *refs):
    near, outs, held = refs[: plan.half], refs[-plan.groups - 1 : -1], refs[-1]
    held[...] = unfold(plan, blocks_of(near, 0, plan.DX), plan.D)
    for m in range(plan.groups):
        start = pl.multiple_of(plan.group_at(lax.axis_index("dp"), m) * plan.share, LANES)
        outs[m][...] = held[:, pl.ds(start, plan.share)]


def activate(preact, scaled):
    sigma = jax.nn.sigmoid(preact)
    act = (preact * sigma).astype(BF16)
    grad_pre = (scaled.astype(F32) * sigma * (1.0 + preact * (1.0 - sigma))).astype(BF16)
    return act, grad_pre


def chip_columns(plan, rows, outs):
    width = INNER * plan.share
    chip = lax.axis_index("dp") // INNER
    for o in range(plan.outer):
        start = pl.multiple_of(away_traced(chip, o, plan.outer) * width, LANES)
        outs[o][:, :width] = rows[:, pl.ds(start, width)]


def near_kernel(plan, placement_ref, weight_ref, *refs):
    near = refs[: plan.half]
    back_near, local_back, local_act, folded_grad, grads, far_rows = refs[-6:]
    x_near = unfold(plan, blocks_of(near, 0, plan.DX), plan.D)
    x_far = unfold(plan, blocks_of(near, 0, plan.DX, SUB), plan.D)
    g_near = unfold(plan, blocks_of(near, plan.DX, plan.C), plan.F)
    g_far = unfold(plan, blocks_of(near, plan.DX, plan.C, SUB), plan.F)
    far_rows[...] = x_far
    x = jnp.concatenate([x_near.astype(F32), x_far.astype(F32)], axis=0).astype(BF16)
    g = jnp.concatenate([g_near.astype(F32), g_far.astype(F32)], axis=0).astype(BF16)
    act, grad_pre = activate(dot(x, weight_ref[...]), g)
    back = dot_nt(grad_pre, weight_ref[...])
    act, grad32 = act.astype(F32), grad_pre.astype(F32)
    back_near[:, : plan.DX] = fold(plan, back[: plan.rows]).astype(BF16)
    back_near[:, plan.DX :] = fold(plan, act[: plan.rows]).astype(BF16)
    local_back[...] = fold(plan, back[plan.rows :]).astype(BF16)
    local_act[...] = fold(plan, act[plan.rows :]).astype(BF16)
    grad_near = grad32[: plan.rows]
    grad_far = jnp.where(is_hot(plan, placement_ref), grad32[plan.rows :], 0.0)
    folded_grad[...] = fold(plan, grad_near).astype(BF16)
    grads[:, : plan.F] = grad_near.astype(BF16)
    grads[:, plan.F :] = grad_far.astype(BF16)


def payload_kernel(
    sizes, plan, placement_ref, weight_ref, folded_grad, near_grads, far_rows, *refs
):
    half, groups = plan.half, plan.groups
    far, refs = refs[:half], refs[half:]
    columns, refs = refs[:groups], refs[groups:]
    small, large, refs = refs[0], refs[1 : 1 + len(sizes)], refs[1 + len(sizes) :]
    shared, rows = refs[:groups], refs[groups]
    hot = is_hot(plan, placement_ref)
    x = unfold(plan, blocks_of(far, 0, plan.DX), plan.D)
    g = unfold(plan, blocks_of(far, plan.DX, plan.C), plan.F)
    rows[...] = x
    act, grad_pre = activate(dot(x, weight_ref[...]), g)

    def store(data, start, stop):
        low = 0
        for out, size in zip(large, sizes):
            out[:, start:stop] = data[low : low + size].astype(BF16)
            low += size

    @pl.when(jnp.logical_not(hot))
    def _():
        folded = fold(plan, dot_nt(grad_pre, weight_ref[...]))
        store(jnp.concatenate([folded[SUB:], folded[:SUB]], axis=0), 0, plan.DX)
        small[...] = fold(plan, act.astype(F32)).astype(BF16)

    @pl.when(hot)
    def _():
        together = jnp.concatenate([c[...].astype(F32) for c in columns], axis=0)
        block = half * SUB
        for i in range(plan.pieces):
            store(
                together[i * block : (i + 1) * block], i * plan.share, (i + 1) * plan.share
            )
        small[...] = folded_grad[...]

    group = lax.axis_index("dp")
    width = plan.share
    for m in range(groups):
        start = pl.multiple_of(plan.group_at(group, m) * width, LANES)
        shared[m][:, :width] = far_rows[:, pl.ds(start, width)]
        shared[m][:, width : 2 * width] = rows[:, pl.ds(start, width)]
        shared[m][:, 2 * width : 2 * width + 2 * plan.F] = near_grads[...]
        shared[m][:, 2 * width + 2 * plan.F :] = grad_pre


def after_small_kernel(plan, placement_ref, small, local_act, near_back, waiting, *outs):
    outs[plan.half + 1][...] = waiting[...]
    hot = is_hot(plan, placement_ref)
    payload = small[...].astype(F32)
    chosen = jnp.where(hot, local_act[...].astype(F32), payload)
    back = near_back[...].astype(F32)
    for m in range(plan.half):
        span = slice(m * SUB, (m + 1) * SUB)
        outs[m][:, : plan.C] = back[span].astype(BF16)
        outs[m][:, plan.C :] = chosen[span].astype(BF16)
    blocks = [payload[m * SUB : (m + 1) * SUB] for m in range(plan.half)]
    outs[plan.half][...] = jnp.where(hot, unfold(plan, blocks, plan.F).astype(F32), 0.0).astype(BF16)


def after_large_kernel(first, passing, plan, placement_ref, large, local_back, *refs):
    count = large.shape[0] // SUB
    outs = refs[-count - passing :]
    for source, target in zip(refs[:passing], outs[count:]):
        target[...] = source[...]
    hot = is_hot(plan, placement_ref)
    local = local_back[...].astype(F32)[first * SUB : (first + count) * SUB]
    chosen = jnp.where(hot, local, large[...].astype(F32))
    for m in range(count):
        outs[m][...] = chosen[m * SUB : (m + 1) * SUB].astype(BF16)


def unpack_kernel(plan, slot_ref, gate_ref, *refs):
    early, refs = refs[: plan.half], refs[plan.half :]
    late, refs = refs[: plan.half], refs[plan.half :]
    out_ref, grad_ref = refs
    block, rank = token_places(plan, slot_ref[...])
    width = 2 * plan.half * SUB
    picks = []
    for target in row_targets(plan, block, rank):
        column = to_column(target).astype(jnp.int32)
        picks.append((iota((plan.tokens, width), 1) == column).astype(BF16))

    def gather(near, far, size):
        stacked = []
        for m in range(plan.half):
            stacked += [near[m], far[m]]
        stacked = jnp.concatenate(stacked, axis=0).astype(BF16)
        total = None
        for i in range(plan.full):
            term = dot(picks[i], stacked[:, i * size : (i + 1) * size])
            total = term if total is None else total + term
        if plan.rest:
            tail = stacked[:, plan.full * size :]
            term = jnp.concatenate(
                [dot(picks[plan.full + q], tail) for q in range(plan.cuts)], axis=1
            )
            total = term if total is None else total + term
        return total

    near = blocks_of(early, 0, plan.DX)
    grad_ref[...] = gather(near, blocks_of(late, 0, plan.DX), plan.D).astype(BF16)
    near = blocks_of(early, plan.DX, plan.C)
    far = blocks_of(early, plan.C, plan.C + plan.FG)
    out_ref[...] = (to_column(gate_ref[...]) * gather(near, far, plan.F)).astype(BF16)


def rows_of(parts):
    return jnp.concatenate([p.astype(F32) for p in parts], axis=0).astype(BF16)


def gather_kernel(plan, weight_hbm, momentum_hbm, *refs):
    groups, share, width = plan.groups, plan.share, plan.F
    columns, refs = refs[:groups], refs[groups:]
    shared, refs = refs[:groups], refs[groups:]
    total, old_weight, x_all, momentum, sems = refs
    mine = pl.multiple_of(lax.axis_index("dp") * share, LANES)
    copies = [
        pltpu.make_async_copy(momentum_hbm.at[0], momentum, sems.at[0]),
        pltpu.make_async_copy(weight_hbm.at[0, pl.ds(mine, share), :], old_weight, sems.at[1]),
    ]
    for copy in copies:
        copy.start()
    base = 2 * share
    x_parts, g_parts = [], []
    for m in range(groups):
        x_parts.append(columns[m][...])
        x_parts += [shared[m][:, i * share : (i + 1) * share] for i in range(2)]
        g_parts += [shared[m][:, base + i * width : base + (i + 1) * width] for i in range(3)]
    x_all[...] = rows_of(x_parts)
    g_all = rows_of(g_parts)
    for copy in copies:
        copy.wait()
    for i in range(share // LANES):
        span = slice(i * LANES, (i + 1) * LANES)
        before = decay_rate * momentum[span, :].astype(F32)
        total[span, :] = before + dot_tn(x_all[:, span], g_all)


def update_kernel(plan, count, placement_ref, *refs):
    large, refs = refs[:count], refs[count:]
    other_g, refs = refs[: plan.groups], refs[plan.groups :]
    total_ref, weight_ref, new_weight, new_momentum, x_all, g_all = refs
    step = pl.program_id(0)
    share = plan.share
    tile = new_weight.shape[1]

    @pl.when(step == 0)
    def _():
        hot = is_hot(plan, placement_ref)
        pieces = [
            block[:, i * share : (i + 1) * share].astype(F32)
            for i in range(plan.pieces)
            for block in large
        ]
        x_all[...] = jnp.where(hot, jnp.concatenate(pieces, axis=0), 0.0).astype(BF16)
        g_all[...] = rows_of([g[...] for g in other_g])

    start = pl.multiple_of(step * tile, LANES)
    total = total_ref[...] + dot_tn(x_all[:, pl.ds(start, tile)], g_all[...])
    momentum = total.astype(BF16)
    new_momentum[0] = momentum
    new_weight[0] = (
        weight_ref[...].astype(F32) - learning_rate * momentum.astype(F32)
    ).astype(BF16)


MIB = 1024 * 1024
SMEM_SPEC = pl.BlockSpec(memory_space=pltpu.SMEM)
ANY_SPEC = pl.BlockSpec(memory_space=pl.ANY)
VMEM_SPEC = pl.BlockSpec(memory_space=pltpu.VMEM)


def call(kernel, plan, ins, specs, outs, scratch, flops, name, limit=16, dtypes=None):
    moved = sum(a.size * a.dtype.itemsize for a in ins) + sum(2 * math.prod(o) for o in outs)
    return pl.pallas_call(
        functools.partial(kernel, plan),
        out_shape=[
            jax.ShapeDtypeStruct(s, dtypes[i] if dtypes else BF16) for i, s in enumerate(outs)
        ],
        in_specs=specs,
        out_specs=[VMEM_SPEC] * len(outs),
        scratch_shapes=scratch,
        compiler_params=pltpu.CompilerParams(vmem_limit_bytes=limit * MIB),
        cost_estimate=pl.CostEstimate(
            flops=flops, bytes_accessed=moved if flops else 0, transcendentals=0
        ),
        name=name,
    )(*ins)


def routed(plan, tokens, route_weight, cotangent, slot_ids, placement, weight, momentum):
    half, groups = plan.half, plan.groups
    D, F, C, rows, share = plan.D, plan.F, plan.C, plan.rows, plan.share
    slot = slot_ids.reshape(1, -1)
    gate = route_weight.reshape(1, -1)

    def to_slot(data, m, flip=0):
        pairs = []
        for e in range(plan.slots):
            h, k = divmod(e, half)
            pairs.append((e, (h ^ flip) * half + away(k, m, half)))
        return lax.ppermute(data, "expert", pairs)

    def to_source(data, m):
        pairs = []
        for e in range(plan.slots):
            h, k = divmod(e, half)
            pairs.append((h * half + away(k, m, half), e))
        return lax.ppermute(data, "expert", pairs)

    def to_partner(data):
        pairs = [(e, (e + half) % plan.slots) for e in range(plan.slots)]
        return lax.ppermute(data, "expert", pairs)

    def from_group(data, m):
        pairs = []
        for d in range(groups):
            pairs.append((plan.group_at(d, m), d))
        return lax.ppermute(data, "dp", pairs)

    def from_groups(per_group):
        return [per_group[0]] + [
            from_group(per_group[plan.group_from(m)], m) for m in range(1, groups)
        ]

    packed = call(
        pack_kernel,
        plan,
        [slot, gate, tokens, cotangent],
        [ANY_SPEC] * 4,
        [(2 * SUB, C)] * half + [(SUB, C)] * half,
        [
            pltpu.VMEM(slot.shape, slot.dtype),
            pltpu.VMEM(gate.shape, gate.dtype),
            pltpu.VMEM(tokens.shape, tokens.dtype),
            pltpu.VMEM(cotangent.shape, cotangent.dtype),
            pltpu.SemaphoreType.DMA((4,)),
        ],
        2 * 4 * half * SUB * plan.tokens * (D + F),
        "pack",
        limit=60,
    )
    near = [packed[0]] + [to_slot(packed[m], m) for m in range(1, half)]
    far = [to_slot(packed[half + m], m, 1) for m in range(half)]
    (held,) = call(
        hold_kernel,
        plan,
        [weight],
        [ANY_SPEC],
        [(D, F)],
        [pltpu.SemaphoreType.DMA],
        0,
        "hold",
        limit=40,
    )
    columns = call(
        columns_kernel,
        plan,
        near,
        [VMEM_SPEC] * half,
        [(rows, share)] * groups,
        [pltpu.VMEM((rows, D), BF16)],
        0,
        "near_columns",
    )
    columns_here = from_groups(columns)
    back_near, local_back, local_act, folded_grad, grads, far_rows = call(
        near_kernel,
        plan,
        [placement, held] + near + [columns[0]],
        [SMEM_SPEC] + [VMEM_SPEC] * (1 + half) + [ANY_SPEC],
        [
            (half * SUB, C),
            (half * SUB, plan.DX),
            (half * SUB, plan.FG),
            (half * SUB, plan.FG),
            (rows, 2 * F),
            (rows, D),
        ],
        [],
        8 * rows * D * F,
        "near_rows",
    )
    sizes = [SUB] * half
    outs = call(
        functools.partial(payload_kernel, sizes),
        plan,
        [placement, held, folded_grad, grads, far_rows] + far + columns_here,
        [SMEM_SPEC] + [VMEM_SPEC] * (4 + half + groups),
        [(half * SUB, plan.FG)]
        + [(size, plan.DX) for size in sizes]
        + [(rows, 2 * share + 3 * F)] * groups,
        [pltpu.VMEM((rows, D), BF16)],
        4 * rows * D * F,
        "payload",
    )
    small = to_partner(outs[0])
    large = [to_partner(outs[1])]
    waiting = outs[2 : 1 + half]
    shared = from_groups(outs[1 + half :])
    outs = call(
        after_small_kernel,
        plan,
        [placement, small, local_act, back_near, waiting[0]],
        [SMEM_SPEC] + [VMEM_SPEC] * 4,
        [(SUB, C + plan.FG)] * half + [(rows, F), (sizes[1], plan.DX)],
        [],
        0,
        "after_small",
    )
    early = [outs[0]] + [to_source(outs[m], m) for m in range(1, half)]
    large.append(to_partner(outs[half + 1]))
    other_g = from_groups([outs[half]] * groups)

    def after_large(first, data, passing, before):
        count = data.shape[0] // SUB
        return call(
            functools.partial(after_large_kernel, first, len(passing)),
            plan,
            [placement, data, local_back] + passing + before,
            [SMEM_SPEC] + [VMEM_SPEC] * (2 + len(passing)) + [ANY_SPEC] * len(before),
            [(SUB, plan.DX)] * count + [p.shape for p in passing],
            [],
            0,
            "after_large",
        )

    far_back = []
    for i in range(half - 2):
        outs = after_large(i + 1, large[i], [waiting[i + 1]], [])
        large.append(to_partner(outs[1]))
        far_back.append(to_source(outs[0], i + 1))
    total, old_weight = call(
        gather_kernel,
        plan,
        [weight, momentum] + columns_here + shared,
        [ANY_SPEC] * 2 + [VMEM_SPEC] * (2 * groups),
        [(share, F)] * 2,
        [
            pltpu.VMEM((3 * groups * rows, share), BF16),
            pltpu.VMEM((share, F), BF16),
            pltpu.SemaphoreType.DMA((2,)),
        ],
        0,
        "own_terms",
        limit=24,
        dtypes=[F32, BF16],
    )
    outs = after_large(half - 1, large[-2], [], [])
    far_back.append(to_source(outs[0], half - 1))
    outs = after_large(0, large[-1], [], [total] + early[1:])
    far_back = [outs[0]] + far_back

    tile = LANES
    steps = share // tile
    group = lax.axis_index("dp").reshape(1)

    def whole(*shape):
        return pl.BlockSpec(shape, lambda i, g: (0,) * len(shape))

    new_weight, new_momentum = pl.pallas_call(
        lambda g_ref, *refs: update_kernel(plan, len(sizes), *refs),
        grid_spec=pltpu.PrefetchScalarGridSpec(
            num_scalar_prefetch=1,
            grid=(steps,),
            in_specs=[SMEM_SPEC]
            + [whole(size, plan.DX) for size in sizes]
            + [whole(*g.shape) for g in other_g]
            + [
                pl.BlockSpec((tile, F), lambda i, g: (i, 0)),
                pl.BlockSpec((tile, F), lambda i, g: (i, 0)),
            ],
            out_specs=[pl.BlockSpec((1, tile, F), lambda i, g: (0, i, 0))] * 2,
            scratch_shapes=[
                pltpu.VMEM((groups * rows, share), BF16),
                pltpu.VMEM((groups * rows, F), BF16),
            ],
        ),
        out_shape=[jax.ShapeDtypeStruct((1, share, F), BF16)] * 2,
        compiler_params=pltpu.CompilerParams(vmem_limit_bytes=16 * MIB),
        cost_estimate=pl.CostEstimate(
            flops=2 * groups * rows * share * F, bytes_accessed=12 * share * F, transcendentals=0
        ),
        name="update",
    )(group, placement, *large, *other_g, total, old_weight)

    expert_out, token_grad = call(
        unpack_kernel,
        plan,
        [slot, gate] + early + far_back,
        [VMEM_SPEC] * (2 + 2 * half),
        [(plan.tokens, F), (plan.tokens, D)],
        [],
        2 * 4 * half * SUB * plan.tokens * (D + F),
        "unpack",
    )
    return expert_out, token_grad, new_weight, new_momentum


def general(tokens, route_weight, cotangent, slot_ids, placement, weight, momentum):
    n_slots = lax.axis_size("expert")
    n_groups = lax.axis_size("dp")
    tok_count, D = tokens.shape
    F = cotangent.shape[1]
    capacity = tok_count * 9 // 8 // n_slots
    onehot = (slot_ids[:, None] == jnp.arange(n_slots, dtype=jnp.int32)[None, :]).astype(jnp.int32)
    ranks = jnp.sum((jnp.cumsum(onehot, axis=0) - 1) * onehot, axis=1)
    position = slot_ids * capacity + ranks
    send_rows = jnp.zeros((n_slots * capacity, D), BF16).at[position].set(tokens)
    scaled = (route_weight[:, None] * cotangent.astype(F32)).astype(BF16)
    send_grads = jnp.zeros((n_slots * capacity, F), BF16).at[position].set(scaled)
    matrix = weight[0]

    def exchange(rows):
        width = rows.shape[-1]
        return lax.all_to_all(
            rows.reshape(n_slots, capacity, width), "expert", split_axis=0, concat_axis=0, tiled=True
        ).reshape(-1, width)

    flat_x = exchange(send_rows)
    act, flat_grad = activate(dot(flat_x, matrix), exchange(send_grads))
    back = dot_nt(flat_grad, matrix).astype(BF16)
    act_rows = exchange(act)[position]
    expert_out = (route_weight[:, None] * act_rows.astype(F32)).astype(BF16)
    token_grad = exchange(back)[position]
    row_count = flat_x.shape[0]
    share = D // n_groups
    columns = lax.all_to_all(
        flat_x.reshape(1, row_count, n_groups, share), "dp", split_axis=2, concat_axis=0, tiled=True
    )
    columns = columns.reshape(n_groups, row_count, share)
    terms = jnp.einsum(
        "krd,krf->kdf",
        columns,
        lax.all_gather(flat_grad[None], "dp", axis=0, tiled=True),
        preferred_element_type=F32,
    )
    terms = lax.optimization_barrier(terms.astype(BF16)).astype(F32)
    reduced = jnp.sum(terms, axis=0).astype(BF16)
    half = n_slots // 2
    partner_grad = lax.ppermute(
        reduced, "expert", [(i, (i + half) % n_slots) for i in range(n_slots)]
    ).astype(F32)
    my_slot = lax.axis_index("expert")
    partner_slot = (my_slot + half) % n_slots
    same = placement[my_slot] == placement[partner_slot]
    total = reduced.astype(F32) + jnp.where(same, partner_grad, 0.0)
    new_momentum = (decay_rate * momentum[0].astype(F32) + total).astype(BF16)
    old = lax.dynamic_slice_in_dim(matrix, lax.axis_index("dp") * share, share, 0).astype(F32)
    new_weight = (old - learning_rate * new_momentum.astype(F32)).astype(BF16)
    return expert_out, token_grad, new_weight[None], new_momentum[None]


def solution(mesh):
    def shards(tokens, route_weight, cotangent, slot_ids, placement, weight, momentum):
        plan = Plan(
            mesh.shape["expert"],
            mesh.shape["dp"],
            tokens.shape[0],
            tokens.shape[1],
            cotangent.shape[1],
        )
        body = functools.partial(routed, plan) if plan.fits() else general
        return body(tokens, route_weight, cotangent, slot_ids, placement, weight, momentum)

    return jax.shard_map(
        shards,
        mesh=mesh,
        in_specs=(
            P(("dp", "expert"), None),
            P(("dp", "expert")),
            P(("dp", "expert"), None),
            P(("dp", "expert")),
            P(),
            P("expert", None, None),
            P("expert", "dp", None),
        ),
        out_specs=(
            P(("dp", "expert"), None),
            P(("dp", "expert"), None),
            P("expert", "dp", None),
            P("expert", "dp", None),
        ),
        check_vma=False,
    )
```

```python
import functools
import math

import jax
import jax.numpy as jnp
from jax import lax
from jax.experimental import pallas as pl
from jax.experimental.pallas import tpu as pltpu
from jax.sharding import PartitionSpec as P

learning_rate = 0.004
decay_rate = 0.9

BF16 = jnp.bfloat16
F32 = jnp.float32
SUB = 8
LANES = 128
INNER = 2


class Plan:
    def __init__(self, slots, groups, tokens, features, hidden):
        self.slots, self.groups, self.tokens = slots, groups, tokens
        self.D, self.F = features, hidden
        self.half = slots // 2
        self.cap = tokens * 9 // 8 // slots
        self.full, self.rest = divmod(self.cap, SUB)
        self.cuts = SUB // self.rest if self.rest else 1
        self.rows = self.half * self.cap
        self.share = features // groups
        self.DX = features * self.cap // SUB
        self.FG = hidden * self.cap // SUB
        self.C = self.DX + self.FG
        self.pieces = self.cap * groups // SUB
        self.outer = groups // INNER

    def group_at(self, group, step):
        chip, core = group // INNER, group % INNER
        if isinstance(group, int):
            return away(chip, step // INNER, self.outer) * INNER + (core ^ (step % INNER))
        return away_traced(chip, step // INNER, self.outer) * INNER + jnp.bitwise_xor(
            core, step % INNER
        )

    def group_from(self, step):
        chips = step // INNER
        if self.outer & (self.outer - 1):
            chips = (self.outer - chips) % self.outer
        return chips * INNER + step % INNER

    def fits(self):
        return (
            self.slots % 2 == 0
            and (self.rest == 0 or SUB % self.rest == 0)
            and self.D % (self.cuts * LANES) == 0
            and self.F % (self.cuts * LANES) == 0
            and self.D % (self.groups * LANES) == 0
            and self.groups % INNER == 0
            and (self.cap * self.groups) % SUB == 0
            and self.rows % SUB == 0
            and (self.half * self.rest) % SUB == 0
            and self.tokens % LANES == 0
        )


def away(place, step, count):
    if count & (count - 1) == 0:
        return place ^ step
    return (place + step) % count


def away_traced(place, step, count):
    if count & (count - 1) == 0:
        return jnp.bitwise_xor(place, step)
    return lax.rem(place + step, count)


def steps_between(first, second, count):
    if count & (count - 1) == 0:
        return jnp.bitwise_xor(first, second)
    return lax.rem(first - second + count, count)


def iota(shape, dim):
    return lax.broadcasted_iota(jnp.int32, shape, dim)


def dot(a, b):
    return jnp.dot(a, b, preferred_element_type=F32)


def dot_nt(a, b):
    return lax.dot_general(a, b, (((1,), (1,)), ((), ())), preferred_element_type=F32)


def dot_tn(a, b):
    return lax.dot_general(a, b, (((0,), (0,)), ((), ())), preferred_element_type=F32)


def picker(plan, cut):
    shape = (plan.half * plan.rest, plan.half * SUB)
    row, col = iota(shape, 0), iota(shape, 1)
    wanted = (row // plan.rest) * SUB + cut * plan.rest + row % plan.rest
    return (wanted == col).astype(BF16)


def unfold(plan, blocks, width):
    parts = [
        jnp.concatenate([b[:, i * width : (i + 1) * width] for b in blocks], axis=0)
        for i in range(plan.full)
    ]
    if plan.rest:
        piece = width // plan.cuts
        tail = jnp.concatenate([b[:, plan.full * width :] for b in blocks], axis=0).astype(BF16)
        parts.append(
            jnp.concatenate([dot(picker(plan, q), tail) for q in range(plan.cuts)], axis=1)
        )
    return jnp.concatenate(parts, axis=0).astype(BF16)


def fold(plan, rows):
    width = rows.shape[1]
    block = plan.half * SUB
    parts = [rows[i * block : (i + 1) * block] for i in range(plan.full)]
    if plan.rest:
        piece = width // plan.cuts
        tail = rows[plan.full * block :].astype(BF16)
        total = None
        for q in range(plan.cuts):
            term = dot_tn(picker(plan, q), tail[:, q * piece : (q + 1) * piece])
            total = term if total is None else total + term
        parts.append(total)
    return jnp.concatenate(parts, axis=1)


def is_hot(plan, placement_ref):
    me = lax.axis_index("expert")
    partner = lax.rem(me + plan.half, plan.slots)
    return placement_ref[me] == placement_ref[partner]


def token_places(plan, slot):
    me = lax.axis_index("expert")
    my_half = me // plan.half
    my_place = lax.rem(me, plan.half)
    upper = (slot >= plan.half).astype(jnp.int32)
    place = slot - plan.half * upper
    far = jnp.where(upper == my_half, 0, 1)
    step = steps_between(place, jnp.zeros_like(place) + my_place, plan.half)
    block = 2 * step + far
    count = plan.tokens
    onehot = (iota((2 * plan.half, count), 0) == block).astype(F32)
    upto = (iota((count, count), 0) <= iota((count, count), 1)).astype(BF16)
    seen = dot(onehot.astype(BF16), upto)
    rank = jnp.sum(onehot * (seen - 1.0), axis=0, keepdims=True).astype(jnp.int32)
    return block, rank


def row_targets(plan, block, rank):
    targets = []
    for i in range(plan.full):
        inside = (rank >= i * SUB) & (rank < (i + 1) * SUB)
        targets.append(jnp.where(inside, block * SUB + rank - i * SUB, -1))
    for q in range(plan.cuts if plan.rest else 0):
        inside = rank >= plan.full * SUB
        targets.append(
            jnp.where(inside, block * SUB + q * plan.rest + rank - plan.full * SUB, -1)
        )
    return targets


def to_column(row):
    n = row.shape[1]
    eye = (iota((n, n), 0) == iota((n, n), 1)).astype(F32)
    return jnp.sum(eye * row.astype(F32), axis=1, keepdims=True)


def pack_kernel(plan, slot_hbm, gate_hbm, tok_hbm, cot_hbm, *refs):
    half = plan.half
    near, far = refs[:half], refs[half : 2 * half]
    slot_ref, gate_ref, tok_ref, cot_ref, sems = refs[2 * half :]
    copies = [
        pltpu.make_async_copy(source, held, sems.at[i])
        for i, (source, held) in enumerate(
            ((slot_hbm, slot_ref), (tok_hbm, tok_ref), (gate_hbm, gate_ref), (cot_hbm, cot_ref))
        )
    ]
    for copy in copies:
        copy.start()
    copies[0].wait()
    block, rank = token_places(plan, slot_ref[...])
    targets = row_targets(plan, block, rank)
    height = 2 * half * SUB
    onehots = [(iota((height, plan.tokens), 0) == t).astype(BF16) for t in targets]

    def store(values, start):
        stop = start + values.shape[1]
        for m in range(half):
            low = 2 * m * SUB
            near[m][:, start:stop] = values[low : low + 2 * SUB].astype(BF16)
            far[m][:, start:stop] = values[low + SUB : low + 2 * SUB].astype(BF16)

    def place(data, base):
        width = data.shape[1]
        for i in range(plan.full):
            store(dot(onehots[i], data), base + i * width)
        if plan.rest:
            piece = width // plan.cuts
            total = None
            for q in range(plan.cuts):
                term = dot(onehots[plan.full + q], data[:, q * piece : (q + 1) * piece])
                total = term if total is None else total + term
            store(total, base + plan.full * width)

    copies[1].wait()
    place(tok_ref[...], 0)
    copies[2].wait()
    copies[3].wait()
    scaled = (to_column(gate_ref[...]) * cot_ref[...].astype(F32)).astype(BF16)
    place(scaled, plan.DX)


def hold_kernel(plan, weight_hbm, held, mine, sems):
    start = pl.multiple_of(lax.axis_index("dp") * plan.share, LANES)
    copies = [
        pltpu.make_async_copy(weight_hbm.at[0], held, sems.at[0]),
        pltpu.make_async_copy(weight_hbm.at[0, pl.ds(start, plan.share), :], mine, sems.at[1]),
    ]
    for copy in copies:
        copy.start()
    for copy in copies:
        copy.wait()


def blocks_of(refs, start, stop, low=0):
    return [r[:, start:stop].astype(F32)[low : low + SUB] for r in refs]


def columns_kernel(plan, *refs):
    near, outs, held = refs[: plan.half], refs[-plan.groups - 1 : -1], refs[-1]
    held[...] = unfold(plan, blocks_of(near, 0, plan.DX), plan.D)
    for m in range(plan.groups):
        start = pl.multiple_of(plan.group_at(lax.axis_index("dp"), m) * plan.share, LANES)
        outs[m][...] = held[:, pl.ds(start, plan.share)]


def activate(preact, scaled):
    sigma = jax.nn.sigmoid(preact)
    act = (preact * sigma).astype(BF16)
    grad_pre = (scaled.astype(F32) * sigma * (1.0 + preact * (1.0 - sigma))).astype(BF16)
    return act, grad_pre


def chip_columns(plan, rows, outs):
    width = INNER * plan.share
    chip = lax.axis_index("dp") // INNER
    for o in range(plan.outer):
        start = pl.multiple_of(away_traced(chip, o, plan.outer) * width, LANES)
        outs[o][:, :width] = rows[:, pl.ds(start, width)]


def near_kernel(plan, placement_ref, weight_ref, *refs):
    near = refs[: plan.half]
    back_near, local, folded_grad, grads, far_rows = refs[-5:]
    x_near = unfold(plan, blocks_of(near, 0, plan.DX), plan.D)
    x_far = unfold(plan, blocks_of(near, 0, plan.DX, SUB), plan.D)
    g_near = unfold(plan, blocks_of(near, plan.DX, plan.C), plan.F)
    g_far = unfold(plan, blocks_of(near, plan.DX, plan.C, SUB), plan.F)
    far_rows[...] = x_far
    x = jnp.concatenate([x_near.astype(F32), x_far.astype(F32)], axis=0).astype(BF16)
    g = jnp.concatenate([g_near.astype(F32), g_far.astype(F32)], axis=0).astype(BF16)
    act, grad_pre = activate(dot(x, weight_ref[...]), g)
    back = dot_nt(grad_pre, weight_ref[...])
    act, grad32 = act.astype(F32), grad_pre.astype(F32)
    back_near[:, : plan.DX] = fold(plan, back[: plan.rows]).astype(BF16)
    back_near[:, plan.DX :] = fold(plan, act[: plan.rows]).astype(BF16)
    local[:, : plan.DX] = fold(plan, back[plan.rows :]).astype(BF16)
    local[:, plan.DX :] = fold(plan, act[plan.rows :]).astype(BF16)
    grad_near = grad32[: plan.rows]
    grad_far = jnp.where(is_hot(plan, placement_ref), grad32[plan.rows :], 0.0)
    folded_grad[...] = fold(plan, grad_near).astype(BF16)
    grads[:, : plan.F] = grad_near.astype(BF16)
    grads[:, plan.F :] = grad_far.astype(BF16)


def payload_kernel(
    plan, placement_ref, weight_ref, folded_grad, near_grads, far_rows, near_back, *refs
):
    half, groups = plan.half, plan.groups
    far, refs = refs[:half], refs[half:]
    columns, refs = refs[:groups], refs[groups:]
    first, last, refs = refs[0], refs[1], refs[2:]
    shared, early, rows = refs[:groups], refs[groups : groups + half], refs[groups + half]
    hot = is_hot(plan, placement_ref)
    x = unfold(plan, blocks_of(far, 0, plan.DX), plan.D)
    g = unfold(plan, blocks_of(far, plan.DX, plan.C), plan.F)
    rows[...] = x
    act, grad_pre = activate(dot(x, weight_ref[...]), g)

    def store(data, start):
        stop = start + data.shape[1]
        first[:, start:stop] = data[SUB:].astype(BF16)
        last[:, start:stop] = data[:SUB].astype(BF16)

    @pl.when(jnp.logical_not(hot))
    def _():
        store(fold(plan, dot_nt(grad_pre, weight_ref[...])), 0)
        store(fold(plan, act.astype(F32)), plan.DX)

    @pl.when(hot)
    def _():
        together = jnp.concatenate([c[...].astype(F32) for c in columns], axis=0)
        block = half * SUB
        for i in range(plan.pieces):
            store(together[i * block : (i + 1) * block], i * plan.share)
        store(folded_grad[...].astype(F32), plan.DX)

    group = lax.axis_index("dp")
    width = plan.share
    for m in range(groups):
        start = pl.multiple_of(plan.group_at(group, m) * width, LANES)
        shared[m][:, :width] = far_rows[:, pl.ds(start, width)]
        shared[m][:, width : 2 * width] = rows[:, pl.ds(start, width)]
        shared[m][:, 2 * width : 2 * width + 2 * plan.F] = near_grads[...]
        shared[m][:, 2 * width + 2 * plan.F :] = grad_pre
    back = near_back[...].astype(F32)
    for m in range(half):
        early[m][...] = back[m * SUB : (m + 1) * SUB].astype(BF16)


def choose(plan, placement_ref, local, got):
    hot = is_hot(plan, placement_ref)
    return jnp.where(hot, local, got[...].astype(F32))


def after_first_kernel(plan, placement_ref, first, local, *refs):
    outs = refs[1 - plan.half :]
    chosen = choose(plan, placement_ref, local[...].astype(F32)[SUB:], first)
    for m in range(plan.half - 1):
        outs[m][...] = chosen[m * SUB : (m + 1) * SUB].astype(BF16)


def after_last_kernel(plan, placement_ref, last, local, first, total, back, grad):
    chosen = choose(plan, placement_ref, local[...].astype(F32)[:SUB], last)
    back[...] = chosen.astype(BF16)
    got = first[:, plan.DX :].astype(F32)
    blocks = [last[:, plan.DX :].astype(F32)]
    blocks += [got[m * SUB : (m + 1) * SUB] for m in range(plan.half - 1)]
    hot = is_hot(plan, placement_ref)
    grad[...] = jnp.where(hot, unfold(plan, blocks, plan.F).astype(F32), 0.0).astype(BF16)


def unpack_kernel(plan, slot_ref, gate_ref, *refs):
    early, refs = refs[: plan.half], refs[plan.half :]
    late, refs = refs[: plan.half], refs[plan.half :]
    out_ref, grad_ref = refs
    block, rank = token_places(plan, slot_ref[...])
    width = 2 * plan.half * SUB
    picks = []
    for target in row_targets(plan, block, rank):
        column = to_column(target).astype(jnp.int32)
        picks.append((iota((plan.tokens, width), 1) == column).astype(BF16))

    def gather(near, far, size):
        stacked = []
        for m in range(plan.half):
            stacked += [near[m], far[m]]
        stacked = jnp.concatenate(stacked, axis=0).astype(BF16)
        total = None
        for i in range(plan.full):
            term = dot(picks[i], stacked[:, i * size : (i + 1) * size])
            total = term if total is None else total + term
        if plan.rest:
            tail = stacked[:, plan.full * size :]
            term = jnp.concatenate(
                [dot(picks[plan.full + q], tail) for q in range(plan.cuts)], axis=1
            )
            total = term if total is None else total + term
        return total

    def both(start, stop):
        return blocks_of(early, start, stop), blocks_of(late, start, stop)

    grad_ref[...] = gather(*both(0, plan.DX), plan.D).astype(BF16)
    gate = to_column(gate_ref[...])
    out_ref[...] = (gate * gather(*both(plan.DX, plan.C), plan.F)).astype(BF16)


def rows_of(parts):
    return jnp.concatenate([p.astype(F32) for p in parts], axis=0).astype(BF16)


def gather_kernel(plan, momentum_hbm, *refs):
    groups, share, width = plan.groups, plan.share, plan.F
    columns, refs = refs[:groups], refs[groups:]
    shared, refs = refs[:groups], refs[groups:]
    total, x_all, momentum, sem = refs
    copy = pltpu.make_async_copy(momentum_hbm.at[0], momentum, sem)
    copy.start()
    base = 2 * share
    x_parts, g_parts = [], []
    for m in range(groups):
        x_parts.append(columns[m][...])
        x_parts += [shared[m][:, i * share : (i + 1) * share] for i in range(2)]
        g_parts += [shared[m][:, base + i * width : base + (i + 1) * width] for i in range(3)]
    x_all[...] = rows_of(x_parts)
    g_all = rows_of(g_parts)
    copy.wait()
    for i in range(share // LANES):
        span = slice(i * LANES, (i + 1) * LANES)
        before = decay_rate * momentum[span, :].astype(F32)
        total[span, :] = before + dot_tn(x_all[:, span], g_all)


def update_kernel(plan, placement_ref, last, first, *refs):
    other_g, refs = refs[: plan.groups], refs[plan.groups :]
    total_ref, weight_ref, new_weight, new_momentum, x_all, g_all = refs
    step = pl.program_id(0)
    share = plan.share
    tile = new_weight.shape[1]

    @pl.when(step == 0)
    def _():
        hot = is_hot(plan, placement_ref)
        pieces = [
            block[:, i * share : (i + 1) * share].astype(F32)
            for i in range(plan.pieces)
            for block in (last, first)
        ]
        x_all[...] = jnp.where(hot, jnp.concatenate(pieces, axis=0), 0.0).astype(BF16)
        g_all[...] = rows_of([g[...] for g in other_g])

    start = pl.multiple_of(step * tile, LANES)
    total = total_ref[...] + dot_tn(x_all[:, pl.ds(start, tile)], g_all[...])
    momentum = total.astype(BF16)
    new_momentum[0] = momentum
    new_weight[0] = (
        weight_ref[...].astype(F32) - learning_rate * momentum.astype(F32)
    ).astype(BF16)


MIB = 1024 * 1024
SMEM_SPEC = pl.BlockSpec(memory_space=pltpu.SMEM)
ANY_SPEC = pl.BlockSpec(memory_space=pl.ANY)
VMEM_SPEC = pl.BlockSpec(memory_space=pltpu.VMEM)


def call(kernel, plan, ins, specs, outs, scratch, flops, name, limit=16, dtypes=None):
    moved = sum(a.size * a.dtype.itemsize for a in ins) + sum(2 * math.prod(o) for o in outs)
    return pl.pallas_call(
        functools.partial(kernel, plan),
        out_shape=[
            jax.ShapeDtypeStruct(s, dtypes[i] if dtypes else BF16) for i, s in enumerate(outs)
        ],
        in_specs=specs,
        out_specs=[VMEM_SPEC] * len(outs),
        scratch_shapes=scratch,
        compiler_params=pltpu.CompilerParams(vmem_limit_bytes=limit * MIB),
        cost_estimate=pl.CostEstimate(
            flops=flops, bytes_accessed=moved if flops else 0, transcendentals=0
        ),
        name=name,
    )(*ins)


def routed(plan, tokens, route_weight, cotangent, slot_ids, placement, weight, momentum):
    half, groups = plan.half, plan.groups
    D, F, C, rows, share = plan.D, plan.F, plan.C, plan.rows, plan.share
    slot = slot_ids.reshape(1, -1)
    gate = route_weight.reshape(1, -1)

    def to_slot(data, m, flip=0):
        pairs = []
        for e in range(plan.slots):
            h, k = divmod(e, half)
            pairs.append((e, (h ^ flip) * half + away(k, m, half)))
        return lax.ppermute(data, "expert", pairs)

    def to_source(data, m):
        pairs = []
        for e in range(plan.slots):
            h, k = divmod(e, half)
            pairs.append((h * half + away(k, m, half), e))
        return lax.ppermute(data, "expert", pairs)

    def to_partner(data):
        pairs = [(e, (e + half) % plan.slots) for e in range(plan.slots)]
        return lax.ppermute(data, "expert", pairs)

    def from_group(data, m):
        pairs = []
        for d in range(groups):
            pairs.append((plan.group_at(d, m), d))
        return lax.ppermute(data, "dp", pairs)

    def from_groups(per_group):
        return [per_group[0]] + [
            from_group(per_group[plan.group_from(m)], m) for m in range(1, groups)
        ]

    packed = call(
        pack_kernel,
        plan,
        [slot, gate, tokens, cotangent],
        [ANY_SPEC] * 4,
        [(2 * SUB, C)] * half + [(SUB, C)] * half,
        [
            pltpu.VMEM(slot.shape, slot.dtype),
            pltpu.VMEM(gate.shape, gate.dtype),
            pltpu.VMEM(tokens.shape, tokens.dtype),
            pltpu.VMEM(cotangent.shape, cotangent.dtype),
            pltpu.SemaphoreType.DMA((4,)),
        ],
        2 * 4 * half * SUB * plan.tokens * (D + F),
        "pack",
        limit=60,
    )
    near = [packed[0]] + [to_slot(packed[m], m) for m in range(1, half)]
    far = [to_slot(packed[half + m], m, 1) for m in range(half)]
    held, old_weight = call(
        hold_kernel,
        plan,
        [weight],
        [ANY_SPEC],
        [(D, F), (share, F)],
        [pltpu.SemaphoreType.DMA((2,))],
        0,
        "hold",
        limit=40,
    )
    columns = call(
        columns_kernel,
        plan,
        near,
        [VMEM_SPEC] * half,
        [(rows, share)] * groups,
        [pltpu.VMEM((rows, D), BF16)],
        0,
        "near_columns",
    )
    columns_here = from_groups(columns)
    back_near, local, folded_grad, grads, far_rows = call(
        near_kernel,
        plan,
        [placement, held] + near + [columns[0]],
        [SMEM_SPEC] + [VMEM_SPEC] * (1 + half) + [ANY_SPEC],
        [
            (half * SUB, C),
            (half * SUB, C),
            (half * SUB, plan.FG),
            (rows, 2 * F),
            (rows, D),
        ],
        [],
        8 * rows * D * F,
        "near_rows",
    )
    outs = call(
        payload_kernel,
        plan,
        [placement, held, folded_grad, grads, far_rows, back_near] + far + columns_here,
        [SMEM_SPEC] + [VMEM_SPEC] * (5 + half + groups),
        [((half - 1) * SUB, C), (SUB, C)]
        + [(rows, 2 * share + 3 * F)] * groups
        + [(SUB, C)] * half,
        [pltpu.VMEM((rows, D), BF16)],
        4 * rows * D * F,
        "payload",
    )
    first, last = to_partner(outs[0]), to_partner(outs[1])
    shared, outs = from_groups(outs[2 : 2 + groups]), outs[2 + groups :]
    early = [outs[0]] + [to_source(outs[m], m) for m in range(1, half)]
    outs = call(
        after_first_kernel,
        plan,
        [placement, first, local] + early[1:],
        [SMEM_SPEC] + [VMEM_SPEC] * 2 + [ANY_SPEC] * (half - 1),
        [(SUB, C)] * (half - 1),
        [],
        0,
        "after_first",
    )
    late = [to_source(out, m + 1) for m, out in enumerate(outs)]
    (total,) = call(
        gather_kernel,
        plan,
        [momentum] + columns_here + shared,
        [ANY_SPEC] + [VMEM_SPEC] * (2 * groups),
        [(share, F)],
        [
            pltpu.VMEM((3 * groups * rows, share), BF16),
            pltpu.VMEM((share, F), BF16),
            pltpu.SemaphoreType.DMA,
        ],
        0,
        "own_terms",
        dtypes=[F32],
    )
    back, grad = call(
        after_last_kernel,
        plan,
        [placement, last, local, first, total],
        [SMEM_SPEC] + [VMEM_SPEC] * 3 + [ANY_SPEC],
        [(SUB, C), (rows, F)],
        [],
        0,
        "after_last",
    )
    late = [back] + late
    other_g = from_groups([grad] * groups)

    tile = LANES
    steps = share // tile
    group = lax.axis_index("dp").reshape(1)

    def whole(*shape):
        return pl.BlockSpec(shape, lambda i, g: (0,) * len(shape))

    new_weight, new_momentum = pl.pallas_call(
        lambda g_ref, *refs: update_kernel(plan, *refs),
        grid_spec=pltpu.PrefetchScalarGridSpec(
            num_scalar_prefetch=1,
            grid=(steps,),
            in_specs=[SMEM_SPEC]
            + [whole(*p.shape) for p in (last, first)]
            + [whole(*g.shape) for g in other_g]
            + [
                pl.BlockSpec((tile, F), lambda i, g: (i, 0)),
                pl.BlockSpec((tile, F), lambda i, g: (i, 0)),
            ],
            out_specs=[pl.BlockSpec((1, tile, F), lambda i, g: (0, i, 0))] * 2,
            scratch_shapes=[
                pltpu.VMEM((groups * rows, share), BF16),
                pltpu.VMEM((groups * rows, F), BF16),
            ],
        ),
        out_shape=[jax.ShapeDtypeStruct((1, share, F), BF16)] * 2,
        compiler_params=pltpu.CompilerParams(vmem_limit_bytes=16 * MIB),
        cost_estimate=pl.CostEstimate(
            flops=2 * groups * rows * share * F, bytes_accessed=12 * share * F, transcendentals=0
        ),
        name="update",
    )(group, placement, last, first, *other_g, total, old_weight)

    expert_out, token_grad = call(
        unpack_kernel,
        plan,
        [slot, gate] + early + late,
        [VMEM_SPEC] * (2 + 2 * half),
        [(plan.tokens, F), (plan.tokens, D)],
        [],
        2 * 4 * half * SUB * plan.tokens * (D + F),
        "unpack",
    )
    return expert_out, token_grad, new_weight, new_momentum


def general(tokens, route_weight, cotangent, slot_ids, placement, weight, momentum):
    n_slots = lax.axis_size("expert")
    n_groups = lax.axis_size("dp")
    tok_count, D = tokens.shape
    F = cotangent.shape[1]
    capacity = tok_count * 9 // 8 // n_slots
    onehot = (slot_ids[:, None] == jnp.arange(n_slots, dtype=jnp.int32)[None, :]).astype(jnp.int32)
    ranks = jnp.sum((jnp.cumsum(onehot, axis=0) - 1) * onehot, axis=1)
    position = slot_ids * capacity + ranks
    send_rows = jnp.zeros((n_slots * capacity, D), BF16).at[position].set(tokens)
    scaled = (route_weight[:, None] * cotangent.astype(F32)).astype(BF16)
    send_grads = jnp.zeros((n_slots * capacity, F), BF16).at[position].set(scaled)
    matrix = weight[0]

    def exchange(rows):
        width = rows.shape[-1]
        return lax.all_to_all(
            rows.reshape(n_slots, capacity, width), "expert", split_axis=0, concat_axis=0, tiled=True
        ).reshape(-1, width)

    flat_x = exchange(send_rows)
    act, flat_grad = activate(dot(flat_x, matrix), exchange(send_grads))
    back = dot_nt(flat_grad, matrix).astype(BF16)
    act_rows = exchange(act)[position]
    expert_out = (route_weight[:, None] * act_rows.astype(F32)).astype(BF16)
    token_grad = exchange(back)[position]
    row_count = flat_x.shape[0]
    share = D // n_groups
    columns = lax.all_to_all(
        flat_x.reshape(1, row_count, n_groups, share), "dp", split_axis=2, concat_axis=0, tiled=True
    )
    columns = columns.reshape(n_groups, row_count, share)
    terms = jnp.einsum(
        "krd,krf->kdf",
        columns,
        lax.all_gather(flat_grad[None], "dp", axis=0, tiled=True),
        preferred_element_type=F32,
    )
    terms = lax.optimization_barrier(terms.astype(BF16)).astype(F32)
    reduced = jnp.sum(terms, axis=0).astype(BF16)
    half = n_slots // 2
    partner_grad = lax.ppermute(
        reduced, "expert", [(i, (i + half) % n_slots) for i in range(n_slots)]
    ).astype(F32)
    my_slot = lax.axis_index("expert")
    partner_slot = (my_slot + half) % n_slots
    same = placement[my_slot] == placement[partner_slot]
    total = reduced.astype(F32) + jnp.where(same, partner_grad, 0.0)
    new_momentum = (decay_rate * momentum[0].astype(F32) + total).astype(BF16)
    old = lax.dynamic_slice_in_dim(matrix, lax.axis_index("dp") * share, share, 0).astype(F32)
    new_weight = (old - learning_rate * new_momentum.astype(F32)).astype(BF16)
    return expert_out, token_grad, new_weight[None], new_momentum[None]


def solution(mesh):
    def shards(tokens, route_weight, cotangent, slot_ids, placement, weight, momentum):
        plan = Plan(
            mesh.shape["expert"],
            mesh.shape["dp"],
            tokens.shape[0],
            tokens.shape[1],
            cotangent.shape[1],
        )
        body = functools.partial(routed, plan) if plan.fits() else general
        return body(tokens, route_weight, cotangent, slot_ids, placement, weight, momentum)

    return jax.shard_map(
        shards,
        mesh=mesh,
        in_specs=(
            P(("dp", "expert"), None),
            P(("dp", "expert")),
            P(("dp", "expert"), None),
            P(("dp", "expert")),
            P(),
            P("expert", None, None),
            P("expert", "dp", None),
        ),
        out_specs=(
            P(("dp", "expert"), None),
            P(("dp", "expert"), None),
            P("expert", "dp", None),
            P("expert", "dp", None),
        ),
        check_vma=False,
    )
```

```python
import functools
import math

import jax
import jax.numpy as jnp
from jax import lax
from jax.experimental import pallas as pl
from jax.experimental.pallas import tpu as pltpu
from jax.sharding import PartitionSpec as P

learning_rate = 0.004
decay_rate = 0.9

BF16 = jnp.bfloat16
F32 = jnp.float32
SUB = 8
LANES = 128
INNER = 2


class Plan:
    def __init__(self, slots, groups, tokens, features, hidden):
        self.slots, self.groups, self.tokens = slots, groups, tokens
        self.D, self.F = features, hidden
        self.half = slots // 2
        self.cap = tokens * 9 // 8 // slots
        self.full, self.rest = divmod(self.cap, SUB)
        self.cuts = SUB // self.rest if self.rest else 1
        self.rows = self.half * self.cap
        self.share = features // groups
        self.DX = features * self.cap // SUB
        self.FG = hidden * self.cap // SUB
        self.C = self.DX + self.FG
        self.pieces = self.cap * groups // SUB
        self.outer = groups // INNER

    def group_at(self, group, step):
        chip, core = group // INNER, group % INNER
        if isinstance(group, int):
            return away(chip, step // INNER, self.outer) * INNER + (core ^ (step % INNER))
        return away_traced(chip, step // INNER, self.outer) * INNER + jnp.bitwise_xor(
            core, step % INNER
        )

    def group_from(self, step):
        chips = step // INNER
        if self.outer & (self.outer - 1):
            chips = (self.outer - chips) % self.outer
        return chips * INNER + step % INNER

    def fits(self):
        return (
            self.slots % 2 == 0
            and (self.rest == 0 or SUB % self.rest == 0)
            and self.D % (self.cuts * LANES) == 0
            and self.F % (self.cuts * LANES) == 0
            and self.D % (self.groups * LANES) == 0
            and self.groups % INNER == 0
            and (self.cap * self.groups) % SUB == 0
            and self.rows % SUB == 0
            and (self.half * self.rest) % SUB == 0
            and self.tokens % LANES == 0
        )


def away(place, step, count):
    if count & (count - 1) == 0:
        return place ^ step
    return (place + step) % count


def away_traced(place, step, count):
    if count & (count - 1) == 0:
        return jnp.bitwise_xor(place, step)
    return lax.rem(place + step, count)


def steps_between(first, second, count):
    if count & (count - 1) == 0:
        return jnp.bitwise_xor(first, second)
    return lax.rem(first - second + count, count)


def iota(shape, dim):
    return lax.broadcasted_iota(jnp.int32, shape, dim)


def dot(a, b):
    return jnp.dot(a, b, preferred_element_type=F32)


def dot_nt(a, b):
    return lax.dot_general(a, b, (((1,), (1,)), ((), ())), preferred_element_type=F32)


def dot_tn(a, b):
    return lax.dot_general(a, b, (((0,), (0,)), ((), ())), preferred_element_type=F32)


def picker(plan, cut):
    shape = (plan.half * plan.rest, plan.half * SUB)
    row, col = iota(shape, 0), iota(shape, 1)
    wanted = (row // plan.rest) * SUB + cut * plan.rest + row % plan.rest
    return (wanted == col).astype(BF16)


def unfold(plan, blocks, width):
    parts = [
        jnp.concatenate([b[:, i * width : (i + 1) * width] for b in blocks], axis=0)
        for i in range(plan.full)
    ]
    if plan.rest:
        piece = width // plan.cuts
        tail = jnp.concatenate([b[:, plan.full * width :] for b in blocks], axis=0).astype(BF16)
        parts.append(
            jnp.concatenate([dot(picker(plan, q), tail) for q in range(plan.cuts)], axis=1)
        )
    return jnp.concatenate(parts, axis=0).astype(BF16)


def fold(plan, rows):
    width = rows.shape[1]
    block = plan.half * SUB
    parts = [rows[i * block : (i + 1) * block] for i in range(plan.full)]
    if plan.rest:
        piece = width // plan.cuts
        tail = rows[plan.full * block :].astype(BF16)
        total = None
        for q in range(plan.cuts):
            term = dot_tn(picker(plan, q), tail[:, q * piece : (q + 1) * piece])
            total = term if total is None else total + term
        parts.append(total)
    return jnp.concatenate(parts, axis=1)


def is_hot(plan, placement_ref):
    me = lax.axis_index("expert")
    partner = lax.rem(me + plan.half, plan.slots)
    return placement_ref[me] == placement_ref[partner]


def token_places(plan, slot):
    me = lax.axis_index("expert")
    my_half = me // plan.half
    my_place = lax.rem(me, plan.half)
    upper = (slot >= plan.half).astype(jnp.int32)
    place = slot - plan.half * upper
    far = jnp.where(upper == my_half, 0, 1)
    step = steps_between(place, jnp.zeros_like(place) + my_place, plan.half)
    block = 2 * step + far
    count = plan.tokens
    onehot = (iota((2 * plan.half, count), 0) == block).astype(F32)
    upto = (iota((count, count), 0) <= iota((count, count), 1)).astype(BF16)
    seen = dot(onehot.astype(BF16), upto)
    rank = jnp.sum(onehot * (seen - 1.0), axis=0, keepdims=True).astype(jnp.int32)
    return block, rank


def row_targets(plan, block, rank):
    targets = []
    for i in range(plan.full):
        inside = (rank >= i * SUB) & (rank < (i + 1) * SUB)
        targets.append(jnp.where(inside, block * SUB + rank - i * SUB, -1))
    for q in range(plan.cuts if plan.rest else 0):
        inside = rank >= plan.full * SUB
        targets.append(
            jnp.where(inside, block * SUB + q * plan.rest + rank - plan.full * SUB, -1)
        )
    return targets


def to_column(row):
    n = row.shape[1]
    eye = (iota((n, n), 0) == iota((n, n), 1)).astype(F32)
    return jnp.sum(eye * row.astype(F32), axis=1, keepdims=True)


def pack_kernel(plan, slot_hbm, gate_hbm, tok_hbm, cot_hbm, *refs):
    half = plan.half
    near, far = refs[:half], refs[half : 2 * half]
    slot_ref, gate_ref, tok_ref, cot_ref, sems = refs[2 * half :]
    copies = [
        pltpu.make_async_copy(source, held, sems.at[i])
        for i, (source, held) in enumerate(
            ((slot_hbm, slot_ref), (tok_hbm, tok_ref), (gate_hbm, gate_ref), (cot_hbm, cot_ref))
        )
    ]
    for copy in copies:
        copy.start()
    copies[0].wait()
    block, rank = token_places(plan, slot_ref[...])
    targets = row_targets(plan, block, rank)
    height = 2 * half * SUB
    onehots = [(iota((height, plan.tokens), 0) == t).astype(BF16) for t in targets]

    def store(values, start):
        stop = start + values.shape[1]
        for m in range(half):
            low = 2 * m * SUB
            near[m][:, start:stop] = values[low : low + 2 * SUB].astype(BF16)
            far[m][:, start:stop] = values[low + SUB : low + 2 * SUB].astype(BF16)

    def place(data, base):
        width = data.shape[1]
        for i in range(plan.full):
            store(dot(onehots[i], data), base + i * width)
        if plan.rest:
            piece = width // plan.cuts
            total = None
            for q in range(plan.cuts):
                term = dot(onehots[plan.full + q], data[:, q * piece : (q + 1) * piece])
                total = term if total is None else total + term
            store(total, base + plan.full * width)

    copies[1].wait()
    place(tok_ref[...], 0)
    copies[2].wait()
    copies[3].wait()
    scaled = (to_column(gate_ref[...]) * cot_ref[...].astype(F32)).astype(BF16)
    place(scaled, plan.DX)


def hold_kernel(plan, weight_hbm, held, mine, sems):
    start = pl.multiple_of(lax.axis_index("dp") * plan.share, LANES)
    copies = [
        pltpu.make_async_copy(weight_hbm.at[0], held, sems.at[0]),
        pltpu.make_async_copy(weight_hbm.at[0, pl.ds(start, plan.share), :], mine, sems.at[1]),
    ]
    for copy in copies:
        copy.start()
    for copy in copies:
        copy.wait()


def blocks_of(refs, start, stop, low=0):
    return [r[:, start:stop].astype(F32)[low : low + SUB] for r in refs]


def columns_kernel(plan, *refs):
    near, outs, held = refs[: plan.half], refs[-plan.groups - 1 : -1], refs[-1]
    held[...] = unfold(plan, blocks_of(near, 0, plan.DX), plan.D)
    for m in range(plan.groups):
        start = pl.multiple_of(plan.group_at(lax.axis_index("dp"), m) * plan.share, LANES)
        outs[m][...] = held[:, pl.ds(start, plan.share)]


def activate(preact, scaled):
    sigma = jax.nn.sigmoid(preact)
    act = (preact * sigma).astype(BF16)
    grad_pre = (scaled.astype(F32) * sigma * (1.0 + preact * (1.0 - sigma))).astype(BF16)
    return act, grad_pre


def chip_columns(plan, rows, outs):
    width = INNER * plan.share
    chip = lax.axis_index("dp") // INNER
    for o in range(plan.outer):
        start = pl.multiple_of(away_traced(chip, o, plan.outer) * width, LANES)
        outs[o][:, :width] = rows[:, pl.ds(start, width)]


def near_kernel(plan, placement_ref, weight_ref, *refs):
    near = refs[: plan.half]
    back_near, local, folded_grad, grads, far_rows = refs[-5:]
    x_near = unfold(plan, blocks_of(near, 0, plan.DX), plan.D)
    x_far = unfold(plan, blocks_of(near, 0, plan.DX, SUB), plan.D)
    g_near = unfold(plan, blocks_of(near, plan.DX, plan.C), plan.F)
    g_far = unfold(plan, blocks_of(near, plan.DX, plan.C, SUB), plan.F)
    far_rows[...] = x_far
    x = jnp.concatenate([x_near.astype(F32), x_far.astype(F32)], axis=0).astype(BF16)
    g = jnp.concatenate([g_near.astype(F32), g_far.astype(F32)], axis=0).astype(BF16)
    act, grad_pre = activate(dot(x, weight_ref[...]), g)
    back = dot_nt(grad_pre, weight_ref[...])
    act, grad32 = act.astype(F32), grad_pre.astype(F32)
    back_near[:, : plan.DX] = fold(plan, back[: plan.rows]).astype(BF16)
    back_near[:, plan.DX :] = fold(plan, act[: plan.rows]).astype(BF16)
    local[:, : plan.DX] = fold(plan, back[plan.rows :]).astype(BF16)
    local[:, plan.DX :] = fold(plan, act[plan.rows :]).astype(BF16)
    grad_near = grad32[: plan.rows]
    grad_far = jnp.where(is_hot(plan, placement_ref), grad32[plan.rows :], 0.0)
    folded_grad[...] = fold(plan, grad_near).astype(BF16)
    grads[:, : plan.F] = grad_near.astype(BF16)
    grads[:, plan.F :] = grad_far.astype(BF16)


def payload_kernel(
    plan, placement_ref, weight_ref, folded_grad, near_grads, far_rows, *refs
):
    half, groups = plan.half, plan.groups
    far, refs = refs[:half], refs[half:]
    columns, refs = refs[:groups], refs[groups:]
    payload, refs = refs[0], refs[1:]
    shared, rows = refs[:groups], refs[groups]
    hot = is_hot(plan, placement_ref)
    x = unfold(plan, blocks_of(far, 0, plan.DX), plan.D)
    g = unfold(plan, blocks_of(far, plan.DX, plan.C), plan.F)
    rows[...] = x
    act, grad_pre = activate(dot(x, weight_ref[...]), g)

    @pl.when(jnp.logical_not(hot))
    def _():
        payload[:, : plan.DX] = fold(plan, dot_nt(grad_pre, weight_ref[...])).astype(BF16)
        payload[:, plan.DX :] = fold(plan, act.astype(F32)).astype(BF16)

    @pl.when(hot)
    def _():
        together = jnp.concatenate([c[...].astype(F32) for c in columns], axis=0)
        block = half * SUB
        for i in range(plan.pieces):
            payload[:, i * plan.share : (i + 1) * plan.share] = together[
                i * block : (i + 1) * block
            ].astype(BF16)
        payload[:, plan.DX :] = folded_grad[...]

    group = lax.axis_index("dp")
    width = plan.share
    for m in range(groups):
        start = pl.multiple_of(plan.group_at(group, m) * width, LANES)
        shared[m][:, :width] = far_rows[:, pl.ds(start, width)]
        shared[m][:, width : 2 * width] = rows[:, pl.ds(start, width)]
        shared[m][:, 2 * width : 2 * width + 2 * plan.F] = near_grads[...]
        shared[m][:, 2 * width + 2 * plan.F :] = grad_pre


def early_kernel(plan, near_back, *refs):
    back = near_back[...].astype(F32)
    for m, out in enumerate(refs[-plan.half :]):
        out[...] = back[m * SUB : (m + 1) * SUB].astype(BF16)


def after_kernel(plan, placement_ref, payload, local, *refs):
    outs = refs[-plan.half - 1 :]
    hot = is_hot(plan, placement_ref)
    got = payload[...].astype(F32)
    chosen = jnp.where(hot, local[...].astype(F32), got)
    for m in range(plan.half):
        outs[m][...] = chosen[m * SUB : (m + 1) * SUB].astype(BF16)
    blocks = [got[m * SUB : (m + 1) * SUB, plan.DX :] for m in range(plan.half)]
    outs[plan.half][...] = jnp.where(hot, unfold(plan, blocks, plan.F).astype(F32), 0.0).astype(BF16)


def unpack_kernel(plan, slot_ref, gate_ref, *refs):
    count = 2 * plan.half
    got, refs = refs[:count], refs[count:]
    out_ref, grad_ref, held, sems = refs
    copies = [
        pltpu.make_async_copy(source, held.at[i], sems.at[i]) for i, source in enumerate(got)
    ]
    for copy in copies:
        copy.start()
    block, rank = token_places(plan, slot_ref[...])
    width = count * SUB
    picks = []
    for target in row_targets(plan, block, rank):
        column = to_column(target).astype(jnp.int32)
        picks.append((iota((plan.tokens, width), 1) == column).astype(BF16))
    gate = to_column(gate_ref[...])
    for copy in copies:
        copy.wait()

    def gather(base, size):
        rows = [held[i, :, base : base + size * plan.cap // SUB].astype(F32) for i in range(count)]
        rows = jnp.concatenate(rows, axis=0).astype(BF16)
        piece = size // plan.cuts
        parts = []
        for q in range(plan.cuts):
            lhs, rhs = list(picks[: plan.full]), []
            for i in range(plan.full):
                start = i * size + q * piece
                rhs.append(rows[:, start : start + piece])
            if plan.rest:
                lhs.append(picks[plan.full + q])
                rhs.append(rows[:, plan.full * size :])
            parts.append(dot(jnp.concatenate(lhs, axis=1), jnp.concatenate(rhs, axis=0)))
        return jnp.concatenate(parts, axis=1)

    grad_ref[...] = gather(0, plan.D).astype(BF16)
    out_ref[...] = (gate * gather(plan.DX, plan.F)).astype(BF16)


def rows_of(parts):
    return jnp.concatenate([p.astype(F32) for p in parts], axis=0).astype(BF16)


def gather_kernel(plan, momentum_hbm, *refs):
    groups, share, width = plan.groups, plan.share, plan.F
    columns, refs = refs[:groups], refs[groups:]
    shared, refs = refs[:groups], refs[groups:]
    total, x_all, momentum, sem = refs
    copy = pltpu.make_async_copy(momentum_hbm.at[0], momentum, sem)
    copy.start()
    base = 2 * share
    x_parts, g_parts = [], []
    for m in range(groups):
        x_parts.append(columns[m][...])
        x_parts += [shared[m][:, i * share : (i + 1) * share] for i in range(2)]
        g_parts += [shared[m][:, base + i * width : base + (i + 1) * width] for i in range(3)]
    x_all[...] = rows_of(x_parts)
    g_all = rows_of(g_parts)
    copy.wait()
    for i in range(share // LANES):
        span = slice(i * LANES, (i + 1) * LANES)
        before = decay_rate * momentum[span, :].astype(F32)
        total[span, :] = before + dot_tn(x_all[:, span], g_all)


def update_kernel(plan, placement_ref, *refs):
    groups, share = plan.groups, plan.share
    sources, refs = refs[: groups + 3], refs[groups + 3 :]
    new_weight, new_momentum, payload, other_g, total, weight, momentum, sems, out_sems = refs
    targets = [payload] + [other_g.at[m] for m in range(groups)] + [total, weight]
    copies = [
        pltpu.make_async_copy(source, target, sems.at[i])
        for i, (source, target) in enumerate(zip(sources, targets))
    ]
    for copy in copies:
        copy.start()
    hot = is_hot(plan, placement_ref)
    for copy in copies[: groups + 1]:
        copy.wait()
    pieces = [payload[:, i * share : (i + 1) * share] for i in range(plan.pieces)]
    x = jnp.concatenate(pieces, axis=0)
    x = jnp.where(hot, x.astype(F32), 0.0).astype(BF16)
    g = rows_of([other_g[m] for m in range(groups)])
    for copy in copies[groups + 1 :]:
        copy.wait()
    done = []
    for i in range(share // LANES):
        span = pl.ds(i * LANES, LANES)
        value = total[span, :] + dot_tn(x[:, i * LANES : (i + 1) * LANES], g)
        value = value.astype(BF16)
        momentum[span, :] = value
        weight[span, :] = (
            weight[span, :].astype(F32) - learning_rate * value.astype(F32)
        ).astype(BF16)
        for j, (source, target) in enumerate(((momentum, new_momentum), (weight, new_weight))):
            copy = pltpu.make_async_copy(
                source.at[span, :], target.at[0, span, :], out_sems.at[i, j]
            )
            copy.start()
            done.append(copy)
    for copy in done:
        copy.wait()


MIB = 1024 * 1024
SMEM_SPEC = pl.BlockSpec(memory_space=pltpu.SMEM)
ANY_SPEC = pl.BlockSpec(memory_space=pl.ANY)
VMEM_SPEC = pl.BlockSpec(memory_space=pltpu.VMEM)


def call(kernel, plan, ins, specs, outs, scratch, flops, name, limit=16, dtypes=None):
    moved = sum(a.size * a.dtype.itemsize for a in ins) + sum(2 * math.prod(o) for o in outs)
    return pl.pallas_call(
        functools.partial(kernel, plan),
        out_shape=[
            jax.ShapeDtypeStruct(s, dtypes[i] if dtypes else BF16) for i, s in enumerate(outs)
        ],
        in_specs=specs,
        out_specs=[VMEM_SPEC] * len(outs),
        scratch_shapes=scratch,
        compiler_params=pltpu.CompilerParams(vmem_limit_bytes=limit * MIB),
        cost_estimate=pl.CostEstimate(
            flops=flops, bytes_accessed=moved if flops else 0, transcendentals=0
        ),
        name=name,
    )(*ins)


def routed(plan, tokens, route_weight, cotangent, slot_ids, placement, weight, momentum):
    half, groups = plan.half, plan.groups
    D, F, C, rows, share = plan.D, plan.F, plan.C, plan.rows, plan.share
    slot = slot_ids.reshape(1, -1)
    gate = route_weight.reshape(1, -1)

    def to_slot(data, m, flip=0):
        pairs = []
        for e in range(plan.slots):
            h, k = divmod(e, half)
            pairs.append((e, (h ^ flip) * half + away(k, m, half)))
        return lax.ppermute(data, "expert", pairs)

    def to_source(data, m):
        pairs = []
        for e in range(plan.slots):
            h, k = divmod(e, half)
            pairs.append((h * half + away(k, m, half), e))
        return lax.ppermute(data, "expert", pairs)

    def to_partner(data):
        pairs = [(e, (e + half) % plan.slots) for e in range(plan.slots)]
        return lax.ppermute(data, "expert", pairs)

    def from_group(data, m):
        pairs = []
        for d in range(groups):
            pairs.append((plan.group_at(d, m), d))
        return lax.ppermute(data, "dp", pairs)

    def from_groups(per_group):
        return [per_group[0]] + [
            from_group(per_group[plan.group_from(m)], m) for m in range(1, groups)
        ]

    packed = call(
        pack_kernel,
        plan,
        [slot, gate, tokens, cotangent],
        [ANY_SPEC] * 4,
        [(2 * SUB, C)] * half + [(SUB, C)] * half,
        [
            pltpu.VMEM(slot.shape, slot.dtype),
            pltpu.VMEM(gate.shape, gate.dtype),
            pltpu.VMEM(tokens.shape, tokens.dtype),
            pltpu.VMEM(cotangent.shape, cotangent.dtype),
            pltpu.SemaphoreType.DMA((4,)),
        ],
        2 * 4 * half * SUB * plan.tokens * (D + F),
        "pack",
        limit=60,
    )
    near = [packed[0]] + [to_slot(packed[m], m) for m in range(1, half)]
    far = [to_slot(packed[half + m], m, 1) for m in range(half)]
    held, old_weight = call(
        hold_kernel,
        plan,
        [weight],
        [ANY_SPEC],
        [(D, F), (share, F)],
        [pltpu.SemaphoreType.DMA((2,))],
        0,
        "hold",
        limit=40,
    )
    columns = call(
        columns_kernel,
        plan,
        near,
        [VMEM_SPEC] * half,
        [(rows, share)] * groups,
        [pltpu.VMEM((rows, D), BF16)],
        0,
        "near_columns",
    )
    columns_here = from_groups(columns)
    back_near, local, folded_grad, grads, far_rows = call(
        near_kernel,
        plan,
        [placement, held] + near + [columns[0]],
        [SMEM_SPEC] + [VMEM_SPEC] * (1 + half) + [ANY_SPEC],
        [
            (half * SUB, C),
            (half * SUB, C),
            (half * SUB, plan.FG),
            (rows, 2 * F),
            (rows, D),
        ],
        [],
        8 * rows * D * F,
        "near_rows",
    )
    outs = call(
        payload_kernel,
        plan,
        [placement, held, folded_grad, grads, far_rows] + far + columns_here,
        [SMEM_SPEC] + [VMEM_SPEC] * (4 + half + groups),
        [(half * SUB, C)] + [(rows, 2 * share + 3 * F)] * groups,
        [pltpu.VMEM((rows, D), BF16)],
        4 * rows * D * F,
        "payload",
    )
    payload = to_partner(outs[0])
    shared = from_groups(outs[1:])
    outs = call(
        early_kernel,
        plan,
        [back_near, shared[1]],
        [VMEM_SPEC, ANY_SPEC],
        [(SUB, C)] * half,
        [],
        0,
        "early",
        limit=4,
    )
    early = [outs[0]] + [to_source(outs[m], m) for m in range(1, half)]
    (total,) = call(
        gather_kernel,
        plan,
        [momentum] + columns_here + shared,
        [ANY_SPEC] + [VMEM_SPEC] * (2 * groups),
        [(share, F)],
        [
            pltpu.VMEM((3 * groups * rows, share), BF16),
            pltpu.VMEM((share, F), BF16),
            pltpu.SemaphoreType.DMA,
        ],
        0,
        "own_terms",
        dtypes=[F32],
    )
    outs = call(
        after_kernel,
        plan,
        [placement, payload, local, total] + early[1:-1],
        [SMEM_SPEC] + [VMEM_SPEC] * 2 + [ANY_SPEC] * (half - 1),
        [(SUB, C)] * half + [(rows, F)],
        [],
        0,
        "after_swap",
        limit=8,
    )
    late = [outs[0]] + [to_source(outs[m], m) for m in range(1, half)]
    other_g = from_groups([outs[half]] * groups)

    new_weight, new_momentum = pl.pallas_call(
        functools.partial(update_kernel, plan),
        out_shape=[jax.ShapeDtypeStruct((1, share, F), BF16)] * 2,
        in_specs=[SMEM_SPEC] + [ANY_SPEC] * (groups + 3),
        out_specs=[ANY_SPEC] * 2,
        scratch_shapes=[
            pltpu.VMEM((half * SUB, C), BF16),
            pltpu.VMEM((groups, rows, F), BF16),
            pltpu.VMEM((share, F), F32),
            pltpu.VMEM((share, F), BF16),
            pltpu.VMEM((share, F), BF16),
            pltpu.SemaphoreType.DMA((groups + 3,)),
            pltpu.SemaphoreType.DMA((share // LANES, 2)),
        ],
        compiler_params=pltpu.CompilerParams(vmem_limit_bytes=20 * MIB),
        cost_estimate=pl.CostEstimate(
            flops=2 * groups * rows * share * F, bytes_accessed=12 * share * F, transcendentals=0
        ),
        name="update",
    )(placement, payload, *other_g, total, old_weight)

    expert_out, token_grad = call(
        unpack_kernel,
        plan,
        [slot, gate] + [data for pair in zip(early, late) for data in pair],
        [VMEM_SPEC] * 2 + [ANY_SPEC] * (2 * half),
        [(plan.tokens, F), (plan.tokens, D)],
        [
            pltpu.VMEM((2 * half, SUB, C), BF16),
            pltpu.SemaphoreType.DMA((2 * half,)),
        ],
        2 * 4 * half * SUB * plan.tokens * (D + F),
        "unpack",
        limit=12,
    )
    return expert_out, token_grad, new_weight, new_momentum


def general(tokens, route_weight, cotangent, slot_ids, placement, weight, momentum):
    n_slots = lax.axis_size("expert")
    n_groups = lax.axis_size("dp")
    tok_count, D = tokens.shape
    F = cotangent.shape[1]
    capacity = tok_count * 9 // 8 // n_slots
    onehot = (slot_ids[:, None] == jnp.arange(n_slots, dtype=jnp.int32)[None, :]).astype(jnp.int32)
    ranks = jnp.sum((jnp.cumsum(onehot, axis=0) - 1) * onehot, axis=1)
    position = slot_ids * capacity + ranks
    send_rows = jnp.zeros((n_slots * capacity, D), BF16).at[position].set(tokens)
    scaled = (route_weight[:, None] * cotangent.astype(F32)).astype(BF16)
    send_grads = jnp.zeros((n_slots * capacity, F), BF16).at[position].set(scaled)
    matrix = weight[0]

    def exchange(rows):
        width = rows.shape[-1]
        return lax.all_to_all(
            rows.reshape(n_slots, capacity, width), "expert", split_axis=0, concat_axis=0, tiled=True
        ).reshape(-1, width)

    flat_x = exchange(send_rows)
    act, flat_grad = activate(dot(flat_x, matrix), exchange(send_grads))
    back = dot_nt(flat_grad, matrix).astype(BF16)
    act_rows = exchange(act)[position]
    expert_out = (route_weight[:, None] * act_rows.astype(F32)).astype(BF16)
    token_grad = exchange(back)[position]
    row_count = flat_x.shape[0]
    share = D // n_groups
    columns = lax.all_to_all(
        flat_x.reshape(1, row_count, n_groups, share), "dp", split_axis=2, concat_axis=0, tiled=True
    )
    columns = columns.reshape(n_groups, row_count, share)
    terms = jnp.einsum(
        "krd,krf->kdf",
        columns,
        lax.all_gather(flat_grad[None], "dp", axis=0, tiled=True),
        preferred_element_type=F32,
    )
    terms = lax.optimization_barrier(terms.astype(BF16)).astype(F32)
    reduced = jnp.sum(terms, axis=0).astype(BF16)
    half = n_slots // 2
    partner_grad = lax.ppermute(
        reduced, "expert", [(i, (i + half) % n_slots) for i in range(n_slots)]
    ).astype(F32)
    my_slot = lax.axis_index("expert")
    partner_slot = (my_slot + half) % n_slots
    same = placement[my_slot] == placement[partner_slot]
    total = reduced.astype(F32) + jnp.where(same, partner_grad, 0.0)
    new_momentum = (decay_rate * momentum[0].astype(F32) + total).astype(BF16)
    old = lax.dynamic_slice_in_dim(matrix, lax.axis_index("dp") * share, share, 0).astype(F32)
    new_weight = (old - learning_rate * new_momentum.astype(F32)).astype(BF16)
    return expert_out, token_grad, new_weight[None], new_momentum[None]


def solution(mesh):
    def shards(tokens, route_weight, cotangent, slot_ids, placement, weight, momentum):
        plan = Plan(
            mesh.shape["expert"],
            mesh.shape["dp"],
            tokens.shape[0],
            tokens.shape[1],
            cotangent.shape[1],
        )
        body = functools.partial(routed, plan) if plan.fits() else general
        return body(tokens, route_weight, cotangent, slot_ids, placement, weight, momentum)

    return jax.shard_map(
        shards,
        mesh=mesh,
        in_specs=(
            P(("dp", "expert"), None),
            P(("dp", "expert")),
            P(("dp", "expert"), None),
            P(("dp", "expert")),
            P(),
            P("expert", None, None),
            P("expert", "dp", None),
        ),
        out_specs=(
            P(("dp", "expert"), None),
            P(("dp", "expert"), None),
            P("expert", "dp", None),
            P("expert", "dp", None),
        ),
        check_vma=False,
    )
```

```python
import functools
import math

import jax
import jax.numpy as jnp
from jax import lax
from jax.experimental import pallas as pl
from jax.experimental.pallas import tpu as pltpu
from jax.sharding import PartitionSpec as P

learning_rate = 0.004
decay_rate = 0.9

BF16 = jnp.bfloat16
F32 = jnp.float32
SUB = 8
LANES = 128
INNER = 2


class Plan:
    def __init__(self, slots, groups, tokens, features, hidden):
        self.slots, self.groups, self.tokens = slots, groups, tokens
        self.D, self.F = features, hidden
        self.half = slots // 2
        self.cap = tokens * 9 // 8 // slots
        self.full, self.rest = divmod(self.cap, SUB)
        self.cuts = SUB // self.rest if self.rest else 1
        self.rows = self.half * self.cap
        self.share = features // groups
        self.DX = features * self.cap // SUB
        self.FG = hidden * self.cap // SUB
        self.C = self.DX + self.FG
        self.pieces = self.cap * groups // SUB
        self.outer = groups // INNER
        self.ahead = self.pieces // 2
        self.cut = self.ahead * self.share

    def group_at(self, group, step):
        chip, core = group // INNER, group % INNER
        if isinstance(group, int):
            return away(chip, step // INNER, self.outer) * INNER + (core ^ (step % INNER))
        return away_traced(chip, step // INNER, self.outer) * INNER + jnp.bitwise_xor(
            core, step % INNER
        )

    def place_of_piece(self, piece, first, second):
        if piece < self.ahead:
            return first, self.FG + piece * self.share
        return second, (piece - self.ahead) * self.share

    def group_from(self, step):
        chips = step // INNER
        if self.outer & (self.outer - 1):
            chips = (self.outer - chips) % self.outer
        return chips * INNER + step % INNER

    def fits(self):
        return (
            self.slots % 2 == 0
            and (self.rest == 0 or SUB % self.rest == 0)
            and self.D % (self.cuts * LANES) == 0
            and self.F % (self.cuts * LANES) == 0
            and self.D % (self.groups * LANES) == 0
            and self.groups % INNER == 0
            and (self.cap * self.groups) % SUB == 0
            and self.rows % SUB == 0
            and (self.half * self.rest) % SUB == 0
            and self.tokens % LANES == 0
        )


def away(place, step, count):
    if count & (count - 1) == 0:
        return place ^ step
    return (place + step) % count


def away_traced(place, step, count):
    if count & (count - 1) == 0:
        return jnp.bitwise_xor(place, step)
    return lax.rem(place + step, count)


def steps_between(first, second, count):
    if count & (count - 1) == 0:
        return jnp.bitwise_xor(first, second)
    return lax.rem(first - second + count, count)


def iota(shape, dim):
    return lax.broadcasted_iota(jnp.int32, shape, dim)


def dot(a, b):
    return jnp.dot(a, b, preferred_element_type=F32)


def dot_nt(a, b):
    return lax.dot_general(a, b, (((1,), (1,)), ((), ())), preferred_element_type=F32)


def dot_tn(a, b):
    return lax.dot_general(a, b, (((0,), (0,)), ((), ())), preferred_element_type=F32)


def picker(plan, cut):
    shape = (plan.half * plan.rest, plan.half * SUB)
    row, col = iota(shape, 0), iota(shape, 1)
    wanted = (row // plan.rest) * SUB + cut * plan.rest + row % plan.rest
    return (wanted == col).astype(BF16)


def unfold(plan, blocks, width):
    parts = [
        jnp.concatenate([b[:, i * width : (i + 1) * width] for b in blocks], axis=0)
        for i in range(plan.full)
    ]
    if plan.rest:
        piece = width // plan.cuts
        tail = jnp.concatenate([b[:, plan.full * width :] for b in blocks], axis=0).astype(BF16)
        parts.append(
            jnp.concatenate([dot(picker(plan, q), tail) for q in range(plan.cuts)], axis=1)
        )
    return jnp.concatenate(parts, axis=0).astype(BF16)


def fold(plan, rows):
    width = rows.shape[1]
    block = plan.half * SUB
    parts = [rows[i * block : (i + 1) * block] for i in range(plan.full)]
    if plan.rest:
        piece = width // plan.cuts
        tail = rows[plan.full * block :].astype(BF16)
        total = None
        for q in range(plan.cuts):
            term = dot_tn(picker(plan, q), tail[:, q * piece : (q + 1) * piece])
            total = term if total is None else total + term
        parts.append(total)
    return jnp.concatenate(parts, axis=1)


def is_hot(plan, placement_ref):
    me = lax.axis_index("expert")
    partner = lax.rem(me + plan.half, plan.slots)
    return placement_ref[me] == placement_ref[partner]


def token_places(plan, slot):
    me = lax.axis_index("expert")
    my_half = me // plan.half
    my_place = lax.rem(me, plan.half)
    upper = (slot >= plan.half).astype(jnp.int32)
    place = slot - plan.half * upper
    far = jnp.where(upper == my_half, 0, 1)
    step = steps_between(place, jnp.zeros_like(place) + my_place, plan.half)
    block = 2 * step + far
    count = plan.tokens
    onehot = (iota((2 * plan.half, count), 0) == block).astype(F32)
    upto = (iota((count, count), 0) <= iota((count, count), 1)).astype(BF16)
    seen = dot(onehot.astype(BF16), upto)
    rank = jnp.sum(onehot * (seen - 1.0), axis=0, keepdims=True).astype(jnp.int32)
    return block, rank


def row_targets(plan, block, rank):
    targets = []
    for i in range(plan.full):
        inside = (rank >= i * SUB) & (rank < (i + 1) * SUB)
        targets.append(jnp.where(inside, block * SUB + rank - i * SUB, -1))
    for q in range(plan.cuts if plan.rest else 0):
        inside = rank >= plan.full * SUB
        targets.append(
            jnp.where(inside, block * SUB + q * plan.rest + rank - plan.full * SUB, -1)
        )
    return targets


def to_column(row):
    n = row.shape[1]
    eye = (iota((n, n), 0) == iota((n, n), 1)).astype(F32)
    return jnp.sum(eye * row.astype(F32), axis=1, keepdims=True)


def pack_kernel(plan, slot_hbm, gate_hbm, tok_hbm, cot_hbm, *refs):
    half = plan.half
    near, far = refs[:half], refs[half : 2 * half]
    slot_ref, gate_ref, tok_ref, cot_ref, sems = refs[2 * half :]
    copies = [
        pltpu.make_async_copy(source, held, sems.at[i])
        for i, (source, held) in enumerate(
            ((slot_hbm, slot_ref), (tok_hbm, tok_ref), (gate_hbm, gate_ref), (cot_hbm, cot_ref))
        )
    ]
    for copy in copies:
        copy.start()
    copies[0].wait()
    block, rank = token_places(plan, slot_ref[...])
    targets = row_targets(plan, block, rank)
    height = 2 * half * SUB
    onehots = [(iota((height, plan.tokens), 0) == t).astype(BF16) for t in targets]

    def store(values, start):
        stop = start + values.shape[1]
        for m in range(half):
            low = 2 * m * SUB
            near[m][:, start:stop] = values[low : low + 2 * SUB].astype(BF16)
            far[m][:, start:stop] = values[low + SUB : low + 2 * SUB].astype(BF16)

    def place(data, base):
        width = data.shape[1]
        for i in range(plan.full):
            store(dot(onehots[i], data), base + i * width)
        if plan.rest:
            piece = width // plan.cuts
            total = None
            for q in range(plan.cuts):
                term = dot(onehots[plan.full + q], data[:, q * piece : (q + 1) * piece])
                total = term if total is None else total + term
            store(total, base + plan.full * width)

    copies[1].wait()
    place(tok_ref[...], 0)
    copies[2].wait()
    copies[3].wait()
    scaled = (to_column(gate_ref[...]) * cot_ref[...].astype(F32)).astype(BF16)
    place(scaled, plan.DX)


def hold_kernel(plan, weight_hbm, held, mine, sems):
    start = pl.multiple_of(lax.axis_index("dp") * plan.share, LANES)
    copies = [
        pltpu.make_async_copy(weight_hbm.at[0], held, sems.at[0]),
        pltpu.make_async_copy(weight_hbm.at[0, pl.ds(start, plan.share), :], mine, sems.at[1]),
    ]
    for copy in copies:
        copy.start()
    for copy in copies:
        copy.wait()


def blocks_of(refs, start, stop, low=0):
    return [r[:, start:stop].astype(F32)[low : low + SUB] for r in refs]


def columns_kernel(plan, *refs):
    near, outs, held = refs[: plan.half], refs[-plan.groups - 1 : -1], refs[-1]
    held[...] = unfold(plan, blocks_of(near, 0, plan.DX), plan.D)
    for m in range(plan.groups):
        start = pl.multiple_of(plan.group_at(lax.axis_index("dp"), m) * plan.share, LANES)
        outs[m][...] = held[:, pl.ds(start, plan.share)]


def activate(preact, scaled):
    sigma = jax.nn.sigmoid(preact)
    act = (preact * sigma).astype(BF16)
    grad_pre = (scaled.astype(F32) * sigma * (1.0 + preact * (1.0 - sigma))).astype(BF16)
    return act, grad_pre


def chip_columns(plan, rows, outs):
    width = INNER * plan.share
    chip = lax.axis_index("dp") // INNER
    for o in range(plan.outer):
        start = pl.multiple_of(away_traced(chip, o, plan.outer) * width, LANES)
        outs[o][:, :width] = rows[:, pl.ds(start, width)]


def near_kernel(plan, placement_ref, weight_ref, *refs):
    near = refs[: plan.half]
    back_near, local, folded_grad, grads, far_rows = refs[-5:]
    x_near = unfold(plan, blocks_of(near, 0, plan.DX), plan.D)
    x_far = unfold(plan, blocks_of(near, 0, plan.DX, SUB), plan.D)
    g_near = unfold(plan, blocks_of(near, plan.DX, plan.C), plan.F)
    g_far = unfold(plan, blocks_of(near, plan.DX, plan.C, SUB), plan.F)
    far_rows[...] = x_far
    x = jnp.concatenate([x_near.astype(F32), x_far.astype(F32)], axis=0).astype(BF16)
    g = jnp.concatenate([g_near.astype(F32), g_far.astype(F32)], axis=0).astype(BF16)
    act, grad_pre = activate(dot(x, weight_ref[...]), g)
    back = dot_nt(grad_pre, weight_ref[...])
    act, grad32 = act.astype(F32), grad_pre.astype(F32)
    back_near[:, : plan.DX] = fold(plan, back[: plan.rows]).astype(BF16)
    back_near[:, plan.DX :] = fold(plan, act[: plan.rows]).astype(BF16)
    local[:, : plan.DX] = fold(plan, back[plan.rows :]).astype(BF16)
    local[:, plan.DX :] = fold(plan, act[plan.rows :]).astype(BF16)
    grad_near = grad32[: plan.rows]
    grad_far = jnp.where(is_hot(plan, placement_ref), grad32[plan.rows :], 0.0)
    folded_grad[...] = fold(plan, grad_near).astype(BF16)
    grads[:, : plan.F] = grad_near.astype(BF16)
    grads[:, plan.F :] = grad_far.astype(BF16)


def payload_kernel(
    plan, placement_ref, weight_ref, folded_grad, near_grads, far_rows, *refs
):
    half, groups = plan.half, plan.groups
    far, refs = refs[:half], refs[half:]
    columns, refs = refs[:groups], refs[groups:]
    first, second, refs = refs[0], refs[1], refs[2:]
    shared, rows = refs[:groups], refs[groups]
    hot = is_hot(plan, placement_ref)
    x = unfold(plan, blocks_of(far, 0, plan.DX), plan.D)
    g = unfold(plan, blocks_of(far, plan.DX, plan.C), plan.F)
    rows[...] = x
    act, grad_pre = activate(dot(x, weight_ref[...]), g)

    @pl.when(jnp.logical_not(hot))
    def _():
        back = fold(plan, dot_nt(grad_pre, weight_ref[...])).astype(BF16)
        first[:, : plan.FG] = fold(plan, act.astype(F32)).astype(BF16)
        first[:, plan.FG :] = back[:, : plan.cut]
        second[...] = back[:, plan.cut :]

    @pl.when(hot)
    def _():
        together = jnp.concatenate([c[...].astype(F32) for c in columns], axis=0)
        block = half * SUB
        for i in range(plan.pieces):
            target, start = plan.place_of_piece(i, first, second)
            target[:, start : start + plan.share] = together[
                i * block : (i + 1) * block
            ].astype(BF16)
        first[:, : plan.FG] = folded_grad[...]

    group = lax.axis_index("dp")
    width = plan.share
    for o in range(groups):
        start = pl.multiple_of(plan.group_at(group, o) * width, LANES)
        shared[o][:, :width] = far_rows[:, pl.ds(start, width)]
        shared[o][:, width : 2 * width] = rows[:, pl.ds(start, width)]
        shared[o][:, 2 * width : 2 * width + 2 * plan.F] = near_grads[...]
        shared[o][:, 2 * width + 2 * plan.F :] = grad_pre


def early_kernel(plan, near_back, *refs):
    back = near_back[...].astype(F32)
    for m, out in enumerate(refs[-plan.half :]):
        out[...] = back[m * SUB : (m + 1) * SUB].astype(BF16)


def after_first_kernel(plan, placement_ref, first, *refs):
    grad = refs[-1]
    got = first[:, : plan.FG].astype(F32)
    blocks = [got[m * SUB : (m + 1) * SUB] for m in range(plan.half)]
    rows = unfold(plan, blocks, plan.F).astype(F32)
    grad[...] = jnp.where(is_hot(plan, placement_ref), rows, 0.0).astype(BF16)


def after_second_kernel(plan, placement_ref, first, second, local, *refs):
    outs = refs[-plan.half :]
    hot = is_hot(plan, placement_ref)
    for source, low, high, start in (
        (first, plan.FG, plan.FG + plan.cut, 0),
        (second, 0, plan.DX - plan.cut, plan.cut),
        (first, 0, plan.FG, plan.DX),
    ):
        stop = start + high - low
        chosen = jnp.where(
            hot, local[:, start:stop].astype(F32), source[:, low:high].astype(F32)
        )
        for m in range(plan.half):
            outs[m][:, start:stop] = chosen[m * SUB : (m + 1) * SUB].astype(BF16)


def unpack_kernel(plan, slot_ref, gate_ref, *refs):
    count = 2 * plan.half
    got, refs = refs[:count], refs[count:]
    out_ref, grad_ref, held, sems = refs
    copies = [
        pltpu.make_async_copy(source, held.at[i], sems.at[i]) for i, source in enumerate(got)
    ]
    for copy in copies:
        copy.start()
    block, rank = token_places(plan, slot_ref[...])
    width = count * SUB
    picks = []
    for target in row_targets(plan, block, rank):
        column = to_column(target).astype(jnp.int32)
        picks.append((iota((plan.tokens, width), 1) == column).astype(BF16))
    gate = to_column(gate_ref[...])
    for copy in copies:
        copy.wait()

    def gather(base, size):
        rows = [held[i, :, base : base + size * plan.cap // SUB].astype(F32) for i in range(count)]
        rows = jnp.concatenate(rows, axis=0).astype(BF16)
        piece = size // plan.cuts
        parts = []
        for q in range(plan.cuts):
            lhs, rhs = list(picks[: plan.full]), []
            for i in range(plan.full):
                start = i * size + q * piece
                rhs.append(rows[:, start : start + piece])
            if plan.rest:
                lhs.append(picks[plan.full + q])
                rhs.append(rows[:, plan.full * size :])
            parts.append(dot(jnp.concatenate(lhs, axis=1), jnp.concatenate(rhs, axis=0)))
        return jnp.concatenate(parts, axis=1)

    grad_ref[...] = gather(0, plan.D).astype(BF16)
    out_ref[...] = (gate * gather(plan.DX, plan.F)).astype(BF16)


def rows_of(parts):
    return jnp.concatenate([p.astype(F32) for p in parts], axis=0).astype(BF16)


def gather_kernel(plan, momentum_hbm, *refs):
    groups, share, width = plan.groups, plan.share, plan.F
    columns, refs = refs[:groups], refs[groups:]
    shared, refs = refs[:groups], refs[groups:]
    total, x_all, momentum, sem = refs
    copy = pltpu.make_async_copy(momentum_hbm.at[0], momentum, sem)
    copy.start()
    base = 2 * share
    x_parts, g_parts = [], []
    for m in range(groups):
        x_parts.append(columns[m][...])
        x_parts += [shared[m][:, i * share : (i + 1) * share] for i in range(2)]
        g_parts += [shared[m][:, base + i * width : base + (i + 1) * width] for i in range(3)]
    x_all[...] = rows_of(x_parts)
    g_all = rows_of(g_parts)
    copy.wait()
    for i in range(share // LANES):
        span = slice(i * LANES, (i + 1) * LANES)
        before = decay_rate * momentum[span, :].astype(F32)
        total[span, :] = before + dot_tn(x_all[:, span], g_all)


def update_kernel(plan, placement_ref, *refs):
    groups, share = plan.groups, plan.share
    sources, refs = refs[: groups + 4], refs[groups + 4 :]
    new_weight, new_momentum, first, second, other_g = refs[:5]
    total, weight, momentum, sems, out_sems = refs[5:]
    targets = [first, second] + [other_g.at[m] for m in range(groups)] + [total, weight]
    copies = [
        pltpu.make_async_copy(source, target, sems.at[i])
        for i, (source, target) in enumerate(zip(sources, targets))
    ]
    for copy in copies:
        copy.start()
    hot = is_hot(plan, placement_ref)
    for copy in copies[: groups + 2]:
        copy.wait()
    pieces = []
    for i in range(plan.pieces):
        source, start = plan.place_of_piece(i, first, second)
        pieces.append(source[:, start : start + share])
    x = jnp.concatenate(pieces, axis=0)
    x = jnp.where(hot, x.astype(F32), 0.0).astype(BF16)
    g = rows_of([other_g[m] for m in range(groups)])
    for copy in copies[groups + 2 :]:
        copy.wait()
    done = []
    for i in range(share // LANES):
        span = pl.ds(i * LANES, LANES)
        value = total[span, :] + dot_tn(x[:, i * LANES : (i + 1) * LANES], g)
        value = value.astype(BF16)
        momentum[span, :] = value
        weight[span, :] = (
            weight[span, :].astype(F32) - learning_rate * value.astype(F32)
        ).astype(BF16)
        for j, (source, target) in enumerate(((momentum, new_momentum), (weight, new_weight))):
            copy = pltpu.make_async_copy(
                source.at[span, :], target.at[0, span, :], out_sems.at[i, j]
            )
            copy.start()
            done.append(copy)
    for copy in done:
        copy.wait()


MIB = 1024 * 1024
SMEM_SPEC = pl.BlockSpec(memory_space=pltpu.SMEM)
ANY_SPEC = pl.BlockSpec(memory_space=pl.ANY)
VMEM_SPEC = pl.BlockSpec(memory_space=pltpu.VMEM)


def call(kernel, plan, ins, specs, outs, scratch, flops, name, limit=16, dtypes=None):
    moved = sum(a.size * a.dtype.itemsize for a in ins) + sum(2 * math.prod(o) for o in outs)
    return pl.pallas_call(
        functools.partial(kernel, plan),
        out_shape=[
            jax.ShapeDtypeStruct(s, dtypes[i] if dtypes else BF16) for i, s in enumerate(outs)
        ],
        in_specs=specs,
        out_specs=[VMEM_SPEC] * len(outs),
        scratch_shapes=scratch,
        compiler_params=pltpu.CompilerParams(vmem_limit_bytes=limit * MIB),
        cost_estimate=pl.CostEstimate(
            flops=flops, bytes_accessed=moved if flops else 0, transcendentals=0
        ),
        name=name,
    )(*ins)


def routed(plan, tokens, route_weight, cotangent, slot_ids, placement, weight, momentum):
    half, groups, outer = plan.half, plan.groups, plan.outer
    D, F, C, rows, share = plan.D, plan.F, plan.C, plan.rows, plan.share
    slot = slot_ids.reshape(1, -1)
    gate = route_weight.reshape(1, -1)

    def to_slot(data, m, flip=0):
        pairs = []
        for e in range(plan.slots):
            h, k = divmod(e, half)
            pairs.append((e, (h ^ flip) * half + away(k, m, half)))
        return lax.ppermute(data, "expert", pairs)

    def to_source(data, m):
        pairs = []
        for e in range(plan.slots):
            h, k = divmod(e, half)
            pairs.append((h * half + away(k, m, half), e))
        return lax.ppermute(data, "expert", pairs)

    def to_partner(data):
        pairs = [(e, (e + half) % plan.slots) for e in range(plan.slots)]
        return lax.ppermute(data, "expert", pairs)

    def from_group(data, m):
        pairs = []
        for d in range(groups):
            pairs.append((plan.group_at(d, m), d))
        return lax.ppermute(data, "dp", pairs)

    def from_chips(per_chip):
        return [per_chip[0]] + [
            from_group(per_chip[plan.group_from(INNER * o) // INNER], INNER * o)
            for o in range(1, outer)
        ]

    def with_sisters(got):
        return [data for own in got for data in (own, from_group(own, 1))]

    def from_groups(per_group):
        return [per_group[0]] + [
            from_group(per_group[plan.group_from(m)], m) for m in range(1, groups)
        ]

    packed = call(
        pack_kernel,
        plan,
        [slot, gate, tokens, cotangent],
        [ANY_SPEC] * 4,
        [(2 * SUB, C)] * half + [(SUB, C)] * half,
        [
            pltpu.VMEM(slot.shape, slot.dtype),
            pltpu.VMEM(gate.shape, gate.dtype),
            pltpu.VMEM(tokens.shape, tokens.dtype),
            pltpu.VMEM(cotangent.shape, cotangent.dtype),
            pltpu.SemaphoreType.DMA((4,)),
        ],
        2 * 4 * half * SUB * plan.tokens * (D + F),
        "pack",
        limit=60,
    )
    near = [packed[0]] + [to_slot(packed[m], m) for m in range(1, half)]
    far = [to_slot(packed[half + m], m, 1) for m in range(half)]
    held, old_weight = call(
        hold_kernel,
        plan,
        [weight],
        [ANY_SPEC],
        [(D, F), (share, F)],
        [pltpu.SemaphoreType.DMA((2,))],
        0,
        "hold",
        limit=40,
    )
    columns = call(
        columns_kernel,
        plan,
        near,
        [VMEM_SPEC] * half,
        [(rows, share)] * groups,
        [pltpu.VMEM((rows, D), BF16)],
        0,
        "near_columns",
    )
    columns_here = from_groups(columns)
    back_near, local, folded_grad, grads, far_rows = call(
        near_kernel,
        plan,
        [placement, held] + near + [columns[0]],
        [SMEM_SPEC] + [VMEM_SPEC] * (1 + half) + [ANY_SPEC],
        [
            (half * SUB, C),
            (half * SUB, C),
            (half * SUB, plan.FG),
            (rows, 2 * F),
            (rows, D),
        ],
        [],
        8 * rows * D * F,
        "near_rows",
    )
    outs = call(
        payload_kernel,
        plan,
        [placement, held, folded_grad, grads, far_rows] + far + columns_here,
        [SMEM_SPEC] + [VMEM_SPEC] * (4 + half + groups),
        [(half * SUB, plan.FG + plan.cut), (half * SUB, plan.DX - plan.cut)]
        + [(rows, 2 * share + 3 * F)] * groups,
        [pltpu.VMEM((rows, D), BF16)],
        4 * rows * D * F,
        "payload",
    )
    first, second = to_partner(outs[0]), to_partner(outs[1])
    shared = from_groups(outs[2:])
    outs = call(
        early_kernel,
        plan,
        [back_near, shared[1]],
        [VMEM_SPEC, ANY_SPEC],
        [(SUB, C)] * half,
        [],
        0,
        "early",
        limit=4,
    )
    early = [outs[0]] + [to_source(outs[m], m) for m in range(1, half)]
    (grad,) = call(
        after_first_kernel,
        plan,
        [placement, first] + early[1:2],
        [SMEM_SPEC, VMEM_SPEC] + [ANY_SPEC],
        [(rows, F)],
        [],
        0,
        "after_first",
        limit=4,
    )
    other_g = from_chips([grad] * outer)
    (total,) = call(
        gather_kernel,
        plan,
        [momentum] + columns_here + shared,
        [ANY_SPEC] + [VMEM_SPEC] * (2 * groups),
        [(share, F)],
        [
            pltpu.VMEM((3 * groups * rows, share), BF16),
            pltpu.VMEM((share, F), BF16),
            pltpu.SemaphoreType.DMA,
        ],
        0,
        "own_terms",
        dtypes=[F32],
    )
    before = other_g[1:] + early[2:3]
    other_g = with_sisters(other_g)
    outs = call(
        after_second_kernel,
        plan,
        [placement, first, second, local] + before,
        [SMEM_SPEC] + [VMEM_SPEC] * 3 + [ANY_SPEC] * len(before),
        [(SUB, C)] * half,
        [],
        0,
        "after_second",
        limit=8,
    )
    late = [outs[0]] + [to_source(outs[m], m) for m in range(1, half)]

    new_weight, new_momentum = pl.pallas_call(
        functools.partial(update_kernel, plan),
        out_shape=[jax.ShapeDtypeStruct((1, share, F), BF16)] * 2,
        in_specs=[SMEM_SPEC] + [ANY_SPEC] * (groups + 4),
        out_specs=[ANY_SPEC] * 2,
        scratch_shapes=[
            pltpu.VMEM(first.shape, BF16),
            pltpu.VMEM(second.shape, BF16),
            pltpu.VMEM((groups, rows, F), BF16),
            pltpu.VMEM((share, F), F32),
            pltpu.VMEM((share, F), BF16),
            pltpu.VMEM((share, F), BF16),
            pltpu.SemaphoreType.DMA((groups + 4,)),
            pltpu.SemaphoreType.DMA((share // LANES, 2)),
        ],
        compiler_params=pltpu.CompilerParams(vmem_limit_bytes=20 * MIB),
        cost_estimate=pl.CostEstimate(
            flops=2 * groups * rows * share * F, bytes_accessed=12 * share * F, transcendentals=0
        ),
        name="update",
    )(placement, first, second, *other_g, total, old_weight)

    expert_out, token_grad = call(
        unpack_kernel,
        plan,
        [slot, gate] + [data for pair in zip(early, late) for data in pair],
        [VMEM_SPEC] * 2 + [ANY_SPEC] * (2 * half),
        [(plan.tokens, F), (plan.tokens, D)],
        [
            pltpu.VMEM((2 * half, SUB, C), BF16),
            pltpu.SemaphoreType.DMA((2 * half,)),
        ],
        2 * 4 * half * SUB * plan.tokens * (D + F),
        "unpack",
        limit=12,
    )
    return expert_out, token_grad, new_weight, new_momentum


def general(tokens, route_weight, cotangent, slot_ids, placement, weight, momentum):
    n_slots = lax.axis_size("expert")
    n_groups = lax.axis_size("dp")
    tok_count, D = tokens.shape
    F = cotangent.shape[1]
    capacity = tok_count * 9 // 8 // n_slots
    onehot = (slot_ids[:, None] == jnp.arange(n_slots, dtype=jnp.int32)[None, :]).astype(jnp.int32)
    ranks = jnp.sum((jnp.cumsum(onehot, axis=0) - 1) * onehot, axis=1)
    position = slot_ids * capacity + ranks
    send_rows = jnp.zeros((n_slots * capacity, D), BF16).at[position].set(tokens)
    scaled = (route_weight[:, None] * cotangent.astype(F32)).astype(BF16)
    send_grads = jnp.zeros((n_slots * capacity, F), BF16).at[position].set(scaled)
    matrix = weight[0]

    def exchange(rows):
        width = rows.shape[-1]
        return lax.all_to_all(
            rows.reshape(n_slots, capacity, width), "expert", split_axis=0, concat_axis=0, tiled=True
        ).reshape(-1, width)

    flat_x = exchange(send_rows)
    act, flat_grad = activate(dot(flat_x, matrix), exchange(send_grads))
    back = dot_nt(flat_grad, matrix).astype(BF16)
    act_rows = exchange(act)[position]
    expert_out = (route_weight[:, None] * act_rows.astype(F32)).astype(BF16)
    token_grad = exchange(back)[position]
    row_count = flat_x.shape[0]
    share = D // n_groups
    columns = lax.all_to_all(
        flat_x.reshape(1, row_count, n_groups, share), "dp", split_axis=2, concat_axis=0, tiled=True
    )
    columns = columns.reshape(n_groups, row_count, share)
    terms = jnp.einsum(
        "krd,krf->kdf",
        columns,
        lax.all_gather(flat_grad[None], "dp", axis=0, tiled=True),
        preferred_element_type=F32,
    )
    terms = lax.optimization_barrier(terms.astype(BF16)).astype(F32)
    reduced = jnp.sum(terms, axis=0).astype(BF16)
    half = n_slots // 2
    partner_grad = lax.ppermute(
        reduced, "expert", [(i, (i + half) % n_slots) for i in range(n_slots)]
    ).astype(F32)
    my_slot = lax.axis_index("expert")
    partner_slot = (my_slot + half) % n_slots
    same = placement[my_slot] == placement[partner_slot]
    total = reduced.astype(F32) + jnp.where(same, partner_grad, 0.0)
    new_momentum = (decay_rate * momentum[0].astype(F32) + total).astype(BF16)
    old = lax.dynamic_slice_in_dim(matrix, lax.axis_index("dp") * share, share, 0).astype(F32)
    new_weight = (old - learning_rate * new_momentum.astype(F32)).astype(BF16)
    return expert_out, token_grad, new_weight[None], new_momentum[None]


def solution(mesh):
    def shards(tokens, route_weight, cotangent, slot_ids, placement, weight, momentum):
        plan = Plan(
            mesh.shape["expert"],
            mesh.shape["dp"],
            tokens.shape[0],
            tokens.shape[1],
            cotangent.shape[1],
        )
        body = functools.partial(routed, plan) if plan.fits() else general
        return body(tokens, route_weight, cotangent, slot_ids, placement, weight, momentum)

    return jax.shard_map(
        shards,
        mesh=mesh,
        in_specs=(
            P(("dp", "expert"), None),
            P(("dp", "expert")),
            P(("dp", "expert"), None),
            P(("dp", "expert")),
            P(),
            P("expert", None, None),
            P("expert", "dp", None),
        ),
        out_specs=(
            P(("dp", "expert"), None),
            P(("dp", "expert"), None),
            P("expert", "dp", None),
            P("expert", "dp", None),
        ),
        check_vma=False,
    )
```

```python
import functools
import math

import jax
import jax.numpy as jnp
from jax import lax
from jax.experimental import pallas as pl
from jax.experimental.pallas import tpu as pltpu
from jax.sharding import PartitionSpec as P

learning_rate = 0.004
decay_rate = 0.9

BF16 = jnp.bfloat16
F32 = jnp.float32
SUB = 8
LANES = 128
INNER = 2


class Plan:
    def __init__(self, slots, groups, tokens, features, hidden):
        self.slots, self.groups, self.tokens = slots, groups, tokens
        self.D, self.F = features, hidden
        self.half = slots // 2
        self.cap = tokens * 9 // 8 // slots
        self.full, self.rest = divmod(self.cap, SUB)
        self.cuts = SUB // self.rest if self.rest else 1
        self.rows = self.half * self.cap
        self.share = features // groups
        self.DX = features * self.cap // SUB
        self.FG = hidden * self.cap // SUB
        self.C = self.DX + self.FG
        self.pieces = self.cap * groups // SUB
        self.outer = groups // INNER
        self.ahead = self.pieces // 2
        self.cut = self.ahead * self.share

    def group_at(self, group, step):
        chip, core = group // INNER, group % INNER
        if isinstance(group, int):
            return away(chip, step // INNER, self.outer) * INNER + (core ^ (step % INNER))
        return away_traced(chip, step // INNER, self.outer) * INNER + jnp.bitwise_xor(
            core, step % INNER
        )

    def place_of_piece(self, piece, first, second):
        if piece < self.ahead:
            return first, self.FG + piece * self.share
        return second, (piece - self.ahead) * self.share

    def group_from(self, step):
        chips = step // INNER
        if self.outer & (self.outer - 1):
            chips = (self.outer - chips) % self.outer
        return chips * INNER + step % INNER

    def fits(self):
        return (
            self.slots % 2 == 0
            and (self.rest == 0 or SUB % self.rest == 0)
            and self.D % (self.cuts * LANES) == 0
            and self.F % (self.cuts * LANES) == 0
            and self.D % (self.groups * LANES) == 0
            and self.groups % INNER == 0
            and (self.cap * self.groups) % SUB == 0
            and self.rows % SUB == 0
            and (self.half * self.rest) % SUB == 0
            and self.tokens % LANES == 0
        )


def away(place, step, count):
    if count & (count - 1) == 0:
        return place ^ step
    return (place + step) % count


def away_traced(place, step, count):
    if count & (count - 1) == 0:
        return jnp.bitwise_xor(place, step)
    return lax.rem(place + step, count)


def steps_between(first, second, count):
    if count & (count - 1) == 0:
        return jnp.bitwise_xor(first, second)
    return lax.rem(first - second + count, count)


def iota(shape, dim):
    return lax.broadcasted_iota(jnp.int32, shape, dim)


def dot(a, b):
    return jnp.dot(a, b, preferred_element_type=F32)


def dot_nt(a, b):
    return lax.dot_general(a, b, (((1,), (1,)), ((), ())), preferred_element_type=F32)


def dot_tn(a, b):
    return lax.dot_general(a, b, (((0,), (0,)), ((), ())), preferred_element_type=F32)


def picker(plan, cut):
    shape = (plan.half * plan.rest, plan.half * SUB)
    row, col = iota(shape, 0), iota(shape, 1)
    wanted = (row // plan.rest) * SUB + cut * plan.rest + row % plan.rest
    return (wanted == col).astype(BF16)


def unfold(plan, blocks, width):
    parts = [
        jnp.concatenate([b[:, i * width : (i + 1) * width] for b in blocks], axis=0)
        for i in range(plan.full)
    ]
    if plan.rest:
        piece = width // plan.cuts
        tail = jnp.concatenate([b[:, plan.full * width :] for b in blocks], axis=0).astype(BF16)
        parts.append(
            jnp.concatenate([dot(picker(plan, q), tail) for q in range(plan.cuts)], axis=1)
        )
    return jnp.concatenate(parts, axis=0).astype(BF16)


def fold(plan, rows):
    width = rows.shape[1]
    block = plan.half * SUB
    parts = [rows[i * block : (i + 1) * block] for i in range(plan.full)]
    if plan.rest:
        piece = width // plan.cuts
        tail = rows[plan.full * block :].astype(BF16)
        total = None
        for q in range(plan.cuts):
            term = dot_tn(picker(plan, q), tail[:, q * piece : (q + 1) * piece])
            total = term if total is None else total + term
        parts.append(total)
    return jnp.concatenate(parts, axis=1)


def is_hot(plan, placement_ref):
    me = lax.axis_index("expert")
    partner = lax.rem(me + plan.half, plan.slots)
    return placement_ref[me] == placement_ref[partner]


def token_places(plan, slot):
    me = lax.axis_index("expert")
    my_half = me // plan.half
    my_place = lax.rem(me, plan.half)
    upper = (slot >= plan.half).astype(jnp.int32)
    place = slot - plan.half * upper
    far = jnp.where(upper == my_half, 0, 1)
    step = steps_between(place, jnp.zeros_like(place) + my_place, plan.half)
    block = 2 * step + far
    count = plan.tokens
    onehot = (iota((2 * plan.half, count), 0) == block).astype(F32)
    upto = (iota((count, count), 0) <= iota((count, count), 1)).astype(BF16)
    seen = dot(onehot.astype(BF16), upto)
    rank = jnp.sum(onehot * (seen - 1.0), axis=0, keepdims=True).astype(jnp.int32)
    return block, rank


def row_targets(plan, block, rank):
    targets = []
    for i in range(plan.full):
        inside = (rank >= i * SUB) & (rank < (i + 1) * SUB)
        targets.append(jnp.where(inside, block * SUB + rank - i * SUB, -1))
    for q in range(plan.cuts if plan.rest else 0):
        inside = rank >= plan.full * SUB
        targets.append(
            jnp.where(inside, block * SUB + q * plan.rest + rank - plan.full * SUB, -1)
        )
    return targets


def to_column(row):
    n = row.shape[1]
    eye = (iota((n, n), 0) == iota((n, n), 1)).astype(F32)
    return jnp.sum(eye * row.astype(F32), axis=1, keepdims=True)


def pack_kernel(plan, slot_hbm, gate_hbm, tok_hbm, cot_hbm, *refs):
    half = plan.half
    near, far = refs[:half], refs[half : 2 * half]
    slot_ref, gate_ref, tok_ref, cot_ref, sems = refs[2 * half :]
    copies = [
        pltpu.make_async_copy(source, held, sems.at[i])
        for i, (source, held) in enumerate(
            ((slot_hbm, slot_ref), (tok_hbm, tok_ref), (gate_hbm, gate_ref), (cot_hbm, cot_ref))
        )
    ]
    for copy in copies:
        copy.start()
    copies[0].wait()
    block, rank = token_places(plan, slot_ref[...])
    targets = row_targets(plan, block, rank)
    height = 2 * half * SUB
    onehots = [(iota((height, plan.tokens), 0) == t).astype(BF16) for t in targets]

    def store(values, start):
        stop = start + values.shape[1]
        for m in range(half):
            low = 2 * m * SUB
            near[m][:, start:stop] = values[low : low + 2 * SUB].astype(BF16)
            far[m][:, start:stop] = values[low + SUB : low + 2 * SUB].astype(BF16)

    def place(data, base):
        width = data.shape[1]
        for i in range(plan.full):
            store(dot(onehots[i], data), base + i * width)
        if plan.rest:
            piece = width // plan.cuts
            total = None
            for q in range(plan.cuts):
                term = dot(onehots[plan.full + q], data[:, q * piece : (q + 1) * piece])
                total = term if total is None else total + term
            store(total, base + plan.full * width)

    copies[1].wait()
    place(tok_ref[...], 0)
    copies[2].wait()
    copies[3].wait()
    scaled = (to_column(gate_ref[...]) * cot_ref[...].astype(F32)).astype(BF16)
    place(scaled, plan.DX)


def hold_kernel(plan, weight_hbm, held, mine, sems):
    start = pl.multiple_of(lax.axis_index("dp") * plan.share, LANES)
    copies = [
        pltpu.make_async_copy(weight_hbm.at[0], held, sems.at[0]),
        pltpu.make_async_copy(weight_hbm.at[0, pl.ds(start, plan.share), :], mine, sems.at[1]),
    ]
    for copy in copies:
        copy.start()
    for copy in copies:
        copy.wait()


def blocks_of(refs, start, stop, low=0):
    return [r[:, start:stop].astype(F32)[low : low + SUB] for r in refs]


def columns_kernel(plan, *refs):
    near, outs, held = refs[: plan.half], refs[-plan.groups - 1 : -1], refs[-1]
    held[...] = unfold(plan, blocks_of(near, 0, plan.DX), plan.D)
    for m in range(plan.groups):
        start = pl.multiple_of(plan.group_at(lax.axis_index("dp"), m) * plan.share, LANES)
        outs[m][...] = held[:, pl.ds(start, plan.share)]


def activate(preact, scaled):
    sigma = jax.nn.sigmoid(preact)
    act = (preact * sigma).astype(BF16)
    grad_pre = (scaled.astype(F32) * sigma * (1.0 + preact * (1.0 - sigma))).astype(BF16)
    return act, grad_pre


def chip_columns(plan, rows, outs):
    width = INNER * plan.share
    chip = lax.axis_index("dp") // INNER
    for o in range(plan.outer):
        start = pl.multiple_of(away_traced(chip, o, plan.outer) * width, LANES)
        outs[o][:, :width] = rows[:, pl.ds(start, width)]


def near_kernel(plan, placement_ref, weight_ref, *refs):
    near = refs[: plan.half]
    back_near, local, folded_grad, grads, far_rows = refs[-5:]
    x_near = unfold(plan, blocks_of(near, 0, plan.DX), plan.D)
    x_far = unfold(plan, blocks_of(near, 0, plan.DX, SUB), plan.D)
    g_near = unfold(plan, blocks_of(near, plan.DX, plan.C), plan.F)
    g_far = unfold(plan, blocks_of(near, plan.DX, plan.C, SUB), plan.F)
    far_rows[...] = x_far
    x = jnp.concatenate([x_near.astype(F32), x_far.astype(F32)], axis=0).astype(BF16)
    g = jnp.concatenate([g_near.astype(F32), g_far.astype(F32)], axis=0).astype(BF16)
    act, grad_pre = activate(dot(x, weight_ref[...]), g)
    back = dot_nt(grad_pre, weight_ref[...])
    act, grad32 = act.astype(F32), grad_pre.astype(F32)
    back_near[:, : plan.DX] = fold(plan, back[: plan.rows]).astype(BF16)
    back_near[:, plan.DX :] = fold(plan, act[: plan.rows]).astype(BF16)
    local[:, : plan.DX] = fold(plan, back[plan.rows :]).astype(BF16)
    local[:, plan.DX :] = fold(plan, act[plan.rows :]).astype(BF16)
    grad_near = grad32[: plan.rows]
    grad_far = jnp.where(is_hot(plan, placement_ref), grad32[plan.rows :], 0.0)
    folded_grad[...] = fold(plan, grad_near).astype(BF16)
    grads[:, : plan.F] = grad_near.astype(BF16)
    grads[:, plan.F :] = grad_far.astype(BF16)


def payload_kernel(
    plan, placement_ref, weight_ref, folded_grad, near_grads, far_rows, *refs
):
    half, groups = plan.half, plan.groups
    far, refs = refs[:half], refs[half:]
    columns, refs = refs[:groups], refs[groups:]
    first, second, refs = refs[0], refs[1], refs[2:]
    shared, rows = refs[:groups], refs[groups]
    hot = is_hot(plan, placement_ref)
    x = unfold(plan, blocks_of(far, 0, plan.DX), plan.D)
    g = unfold(plan, blocks_of(far, plan.DX, plan.C), plan.F)
    rows[...] = x
    act, grad_pre = activate(dot(x, weight_ref[...]), g)

    @pl.when(jnp.logical_not(hot))
    def _():
        back = fold(plan, dot_nt(grad_pre, weight_ref[...])).astype(BF16)
        first[:, : plan.FG] = fold(plan, act.astype(F32)).astype(BF16)
        first[:, plan.FG :] = back[:, : plan.cut]
        second[...] = back[:, plan.cut :]

    @pl.when(hot)
    def _():
        together = jnp.concatenate([c[...].astype(F32) for c in columns], axis=0)
        block = half * SUB
        for i in range(plan.pieces):
            target, start = plan.place_of_piece(i, first, second)
            target[:, start : start + plan.share] = together[
                i * block : (i + 1) * block
            ].astype(BF16)
        first[:, : plan.FG] = folded_grad[...]

    group = lax.axis_index("dp")
    width = plan.share
    for o in range(groups):
        start = pl.multiple_of(plan.group_at(group, o) * width, LANES)
        shared[o][:, :width] = far_rows[:, pl.ds(start, width)]
        shared[o][:, width : 2 * width] = rows[:, pl.ds(start, width)]
        shared[o][:, 2 * width : 2 * width + 2 * plan.F] = near_grads[...]
        shared[o][:, 2 * width + 2 * plan.F :] = grad_pre


def early_kernel(plan, near_back, *refs):
    back = near_back[...].astype(F32)
    for m, out in enumerate(refs[-plan.half :]):
        out[...] = back[m * SUB : (m + 1) * SUB].astype(BF16)


def after_first_kernel(plan, placement_ref, first, *refs):
    grad = refs[-1]
    got = first[:, : plan.FG].astype(F32)
    blocks = [got[m * SUB : (m + 1) * SUB] for m in range(plan.half)]
    rows = unfold(plan, blocks, plan.F).astype(F32)
    grad[...] = jnp.where(is_hot(plan, placement_ref), rows, 0.0).astype(BF16)


def after_second_kernel(plan, placement_ref, first, second, local, *refs):
    outs = refs[-plan.half :]
    hot = is_hot(plan, placement_ref)
    for source, low, high, start in (
        (first, plan.FG, plan.FG + plan.cut, 0),
        (second, 0, plan.DX - plan.cut, plan.cut),
        (first, 0, plan.FG, plan.DX),
    ):
        stop = start + high - low
        chosen = jnp.where(
            hot, local[:, start:stop].astype(F32), source[:, low:high].astype(F32)
        )
        for m in range(plan.half):
            outs[m][:, start:stop] = chosen[m * SUB : (m + 1) * SUB].astype(BF16)


def unpack_kernel(plan, slot_ref, gate_ref, *refs):
    count = 2 * plan.half
    got, refs = refs[:count], refs[count:]
    out_ref, grad_ref, held, sems = refs
    copies = [
        pltpu.make_async_copy(source, held.at[i], sems.at[i]) for i, source in enumerate(got)
    ]
    for copy in copies:
        copy.start()
    block, rank = token_places(plan, slot_ref[...])
    width = count * SUB
    picks = []
    for target in row_targets(plan, block, rank):
        column = to_column(target).astype(jnp.int32)
        picks.append((iota((plan.tokens, width), 1) == column).astype(BF16))
    gate = to_column(gate_ref[...])
    for copy in copies:
        copy.wait()

    def gather(base, size):
        rows = [held[i, :, base : base + size * plan.cap // SUB].astype(F32) for i in range(count)]
        rows = jnp.concatenate(rows, axis=0).astype(BF16)
        piece = size // plan.cuts
        parts = []
        for q in range(plan.cuts):
            lhs, rhs = list(picks[: plan.full]), []
            for i in range(plan.full):
                start = i * size + q * piece
                rhs.append(rows[:, start : start + piece])
            if plan.rest:
                lhs.append(picks[plan.full + q])
                rhs.append(rows[:, plan.full * size :])
            parts.append(dot(jnp.concatenate(lhs, axis=1), jnp.concatenate(rhs, axis=0)))
        return jnp.concatenate(parts, axis=1)

    grad_ref[...] = gather(0, plan.D).astype(BF16)
    out_ref[...] = (gate * gather(plan.DX, plan.F)).astype(BF16)


def rows_of(parts):
    return jnp.concatenate([p.astype(F32) for p in parts], axis=0).astype(BF16)


def gather_kernel(plan, momentum_hbm, *refs):
    groups, share, width = plan.groups, plan.share, plan.F
    columns, refs = refs[:groups], refs[groups:]
    shared, refs = refs[:groups], refs[groups:]
    total, x_all, momentum, sem = refs
    copy = pltpu.make_async_copy(momentum_hbm.at[0], momentum, sem)
    copy.start()
    base = 2 * share
    x_parts, g_parts = [], []
    for m in range(groups):
        x_parts.append(columns[m][...])
        x_parts += [shared[m][:, i * share : (i + 1) * share] for i in range(2)]
        g_parts += [shared[m][:, base + i * width : base + (i + 1) * width] for i in range(3)]
    x_all[...] = rows_of(x_parts)
    g_all = rows_of(g_parts)
    copy.wait()
    for i in range(share // LANES):
        span = slice(i * LANES, (i + 1) * LANES)
        before = decay_rate * momentum[span, :].astype(F32)
        total[span, :] = before + dot_tn(x_all[:, span], g_all)


def update_kernel(plan, placement_ref, *refs):
    groups, share = plan.groups, plan.share
    sources, refs = refs[: groups + 4], refs[groups + 4 :]
    new_weight, new_momentum, first, second, other_g = refs[:5]
    total, weight, momentum, sems, out_sems = refs[5:]
    targets = [first, second] + [other_g.at[m] for m in range(groups)] + [total, weight]
    copies = [
        pltpu.make_async_copy(source, target, sems.at[i])
        for i, (source, target) in enumerate(zip(sources, targets))
    ]
    for copy in copies:
        copy.start()
    hot = is_hot(plan, placement_ref)
    for copy in copies[: groups + 2]:
        copy.wait()
    pieces = []
    for i in range(plan.pieces):
        source, start = plan.place_of_piece(i, first, second)
        pieces.append(source[:, start : start + share])
    x = jnp.concatenate(pieces, axis=0)
    x = jnp.where(hot, x.astype(F32), 0.0).astype(BF16)
    g = rows_of([other_g[m] for m in range(groups)])
    for copy in copies[groups + 2 :]:
        copy.wait()
    done = []
    for i in range(share // LANES):
        span = pl.ds(i * LANES, LANES)
        value = total[span, :] + dot_tn(x[:, i * LANES : (i + 1) * LANES], g)
        value = value.astype(BF16)
        momentum[span, :] = value
        weight[span, :] = (
            weight[span, :].astype(F32) - learning_rate * value.astype(F32)
        ).astype(BF16)
        for j, (source, target) in enumerate(((momentum, new_momentum), (weight, new_weight))):
            copy = pltpu.make_async_copy(
                source.at[span, :], target.at[0, span, :], out_sems.at[i, j]
            )
            copy.start()
            done.append(copy)
    for copy in done:
        copy.wait()


MIB = 1024 * 1024
SMEM_SPEC = pl.BlockSpec(memory_space=pltpu.SMEM)
ANY_SPEC = pl.BlockSpec(memory_space=pl.ANY)
VMEM_SPEC = pl.BlockSpec(memory_space=pltpu.VMEM)


def call(kernel, plan, ins, specs, outs, scratch, flops, name, limit=16, dtypes=None):
    moved = sum(a.size * a.dtype.itemsize for a in ins) + sum(2 * math.prod(o) for o in outs)
    return pl.pallas_call(
        functools.partial(kernel, plan),
        out_shape=[
            jax.ShapeDtypeStruct(s, dtypes[i] if dtypes else BF16) for i, s in enumerate(outs)
        ],
        in_specs=specs,
        out_specs=[VMEM_SPEC] * len(outs),
        scratch_shapes=scratch,
        compiler_params=pltpu.CompilerParams(vmem_limit_bytes=limit * MIB),
        cost_estimate=pl.CostEstimate(
            flops=flops, bytes_accessed=moved if flops else 0, transcendentals=0
        ),
        name=name,
    )(*ins)


def routed(plan, tokens, route_weight, cotangent, slot_ids, placement, weight, momentum):
    half, groups, outer = plan.half, plan.groups, plan.outer
    D, F, C, rows, share = plan.D, plan.F, plan.C, plan.rows, plan.share
    slot = slot_ids.reshape(1, -1)
    gate = route_weight.reshape(1, -1)

    def to_slot(data, m, flip=0):
        pairs = []
        for e in range(plan.slots):
            h, k = divmod(e, half)
            pairs.append((e, (h ^ flip) * half + away(k, m, half)))
        return lax.ppermute(data, "expert", pairs)

    def to_source(data, m):
        pairs = []
        for e in range(plan.slots):
            h, k = divmod(e, half)
            pairs.append((h * half + away(k, m, half), e))
        return lax.ppermute(data, "expert", pairs)

    def to_partner(data):
        pairs = [(e, (e + half) % plan.slots) for e in range(plan.slots)]
        return lax.ppermute(data, "expert", pairs)

    def from_group(data, m):
        pairs = []
        for d in range(groups):
            pairs.append((plan.group_at(d, m), d))
        return lax.ppermute(data, "dp", pairs)

    def from_chips(per_chip):
        return [per_chip[0]] + [
            from_group(per_chip[plan.group_from(INNER * o) // INNER], INNER * o)
            for o in range(1, outer)
        ]

    def with_sisters(got):
        return [data for own in got for data in (own, from_group(own, 1))]

    def from_groups(per_group):
        return [per_group[0]] + [
            from_group(per_group[plan.group_from(m)], m) for m in range(1, groups)
        ]

    packed = call(
        pack_kernel,
        plan,
        [slot, gate, tokens, cotangent],
        [ANY_SPEC] * 4,
        [(2 * SUB, C)] * half + [(SUB, C)] * half,
        [
            pltpu.VMEM(slot.shape, slot.dtype),
            pltpu.VMEM(gate.shape, gate.dtype),
            pltpu.VMEM(tokens.shape, tokens.dtype),
            pltpu.VMEM(cotangent.shape, cotangent.dtype),
            pltpu.SemaphoreType.DMA((4,)),
        ],
        2 * 4 * half * SUB * plan.tokens * (D + F),
        "pack",
        limit=60,
    )
    near = [packed[0]] + [to_slot(packed[m], m) for m in range(1, half)]
    far = [to_slot(packed[half + m], m, 1) for m in range(half)]
    held, old_weight = call(
        hold_kernel,
        plan,
        [weight],
        [ANY_SPEC],
        [(D, F), (share, F)],
        [pltpu.SemaphoreType.DMA((2,))],
        0,
        "hold",
        limit=40,
    )
    columns = call(
        columns_kernel,
        plan,
        near,
        [VMEM_SPEC] * half,
        [(rows, share)] * groups,
        [pltpu.VMEM((rows, D), BF16)],
        0,
        "near_columns",
    )
    columns_here = from_groups(columns)
    back_near, local, folded_grad, grads, far_rows = call(
        near_kernel,
        plan,
        [placement, held] + near + [columns[0]],
        [SMEM_SPEC] + [VMEM_SPEC] * (1 + half) + [ANY_SPEC],
        [
            (half * SUB, C),
            (half * SUB, C),
            (half * SUB, plan.FG),
            (rows, 2 * F),
            (rows, D),
        ],
        [],
        8 * rows * D * F,
        "near_rows",
    )
    outs = call(
        payload_kernel,
        plan,
        [placement, held, folded_grad, grads, far_rows] + far + columns_here,
        [SMEM_SPEC] + [VMEM_SPEC] * (4 + half + groups),
        [(half * SUB, plan.FG + plan.cut), (half * SUB, plan.DX - plan.cut)]
        + [(rows, 2 * share + 3 * F)] * groups,
        [pltpu.VMEM((rows, D), BF16)],
        4 * rows * D * F,
        "payload",
    )
    first, second = to_partner(outs[0]), to_partner(outs[1])
    shared = from_groups(outs[2:])
    outs = call(
        early_kernel,
        plan,
        [back_near, shared[1]],
        [VMEM_SPEC, ANY_SPEC],
        [(SUB, C)] * half,
        [],
        0,
        "early",
        limit=4,
    )
    early = [outs[0]] + [to_source(outs[m], m) for m in range(1, half)]
    (grad,) = call(
        after_first_kernel,
        plan,
        [placement, first] + early[1:2],
        [SMEM_SPEC, VMEM_SPEC] + [ANY_SPEC],
        [(rows, F)],
        [],
        0,
        "after_first",
        limit=4,
    )
    other_g = from_chips([grad] * outer)
    (total,) = call(
        gather_kernel,
        plan,
        [momentum] + columns_here + shared,
        [ANY_SPEC] + [VMEM_SPEC] * (2 * groups),
        [(share, F)],
        [
            pltpu.VMEM((3 * groups * rows, share), BF16),
            pltpu.VMEM((share, F), BF16),
            pltpu.SemaphoreType.DMA,
        ],
        0,
        "own_terms",
        dtypes=[F32],
    )
    before = early[2:3]
    other_g = with_sisters(other_g)
    outs = call(
        after_second_kernel,
        plan,
        [placement, first, second, local] + before,
        [SMEM_SPEC] + [VMEM_SPEC] * 3 + [ANY_SPEC] * len(before),
        [(SUB, C)] * half,
        [],
        0,
        "after_second",
        limit=8,
    )
    late = [outs[0]] + [to_source(outs[m], m) for m in range(1, half)]

    new_weight, new_momentum = pl.pallas_call(
        functools.partial(update_kernel, plan),
        out_shape=[jax.ShapeDtypeStruct((1, share, F), BF16)] * 2,
        in_specs=[SMEM_SPEC] + [ANY_SPEC] * (groups + 4),
        out_specs=[ANY_SPEC] * 2,
        scratch_shapes=[
            pltpu.VMEM(first.shape, BF16),
            pltpu.VMEM(second.shape, BF16),
            pltpu.VMEM((groups, rows, F), BF16),
            pltpu.VMEM((share, F), F32),
            pltpu.VMEM((share, F), BF16),
            pltpu.VMEM((share, F), BF16),
            pltpu.SemaphoreType.DMA((groups + 4,)),
            pltpu.SemaphoreType.DMA((share // LANES, 2)),
        ],
        compiler_params=pltpu.CompilerParams(vmem_limit_bytes=20 * MIB),
        cost_estimate=pl.CostEstimate(
            flops=2 * groups * rows * share * F, bytes_accessed=12 * share * F, transcendentals=0
        ),
        name="update",
    )(placement, first, second, *other_g, total, old_weight)

    expert_out, token_grad = call(
        unpack_kernel,
        plan,
        [slot, gate] + [data for pair in zip(early, late) for data in pair],
        [VMEM_SPEC] * 2 + [ANY_SPEC] * (2 * half),
        [(plan.tokens, F), (plan.tokens, D)],
        [
            pltpu.VMEM((2 * half, SUB, C), BF16),
            pltpu.SemaphoreType.DMA((2 * half,)),
        ],
        2 * 4 * half * SUB * plan.tokens * (D + F),
        "unpack",
        limit=12,
    )
    return expert_out, token_grad, new_weight, new_momentum


def general(tokens, route_weight, cotangent, slot_ids, placement, weight, momentum):
    n_slots = lax.axis_size("expert")
    n_groups = lax.axis_size("dp")
    tok_count, D = tokens.shape
    F = cotangent.shape[1]
    capacity = tok_count * 9 // 8 // n_slots
    onehot = (slot_ids[:, None] == jnp.arange(n_slots, dtype=jnp.int32)[None, :]).astype(jnp.int32)
    ranks = jnp.sum((jnp.cumsum(onehot, axis=0) - 1) * onehot, axis=1)
    position = slot_ids * capacity + ranks
    send_rows = jnp.zeros((n_slots * capacity, D), BF16).at[position].set(tokens)
    scaled = (route_weight[:, None] * cotangent.astype(F32)).astype(BF16)
    send_grads = jnp.zeros((n_slots * capacity, F), BF16).at[position].set(scaled)
    matrix = weight[0]

    def exchange(rows):
        width = rows.shape[-1]
        return lax.all_to_all(
            rows.reshape(n_slots, capacity, width), "expert", split_axis=0, concat_axis=0, tiled=True
        ).reshape(-1, width)

    flat_x = exchange(send_rows)
    act, flat_grad = activate(dot(flat_x, matrix), exchange(send_grads))
    back = dot_nt(flat_grad, matrix).astype(BF16)
    act_rows = exchange(act)[position]
    expert_out = (route_weight[:, None] * act_rows.astype(F32)).astype(BF16)
    token_grad = exchange(back)[position]
    row_count = flat_x.shape[0]
    share = D // n_groups
    columns = lax.all_to_all(
        flat_x.reshape(1, row_count, n_groups, share), "dp", split_axis=2, concat_axis=0, tiled=True
    )
    columns = columns.reshape(n_groups, row_count, share)
    terms = jnp.einsum(
        "krd,krf->kdf",
        columns,
        lax.all_gather(flat_grad[None], "dp", axis=0, tiled=True),
        preferred_element_type=F32,
    )
    terms = lax.optimization_barrier(terms.astype(BF16)).astype(F32)
    reduced = jnp.sum(terms, axis=0).astype(BF16)
    half = n_slots // 2
    partner_grad = lax.ppermute(
        reduced, "expert", [(i, (i + half) % n_slots) for i in range(n_slots)]
    ).astype(F32)
    my_slot = lax.axis_index("expert")
    partner_slot = (my_slot + half) % n_slots
    same = placement[my_slot] == placement[partner_slot]
    total = reduced.astype(F32) + jnp.where(same, partner_grad, 0.0)
    new_momentum = (decay_rate * momentum[0].astype(F32) + total).astype(BF16)
    old = lax.dynamic_slice_in_dim(matrix, lax.axis_index("dp") * share, share, 0).astype(F32)
    new_weight = (old - learning_rate * new_momentum.astype(F32)).astype(BF16)
    return expert_out, token_grad, new_weight[None], new_momentum[None]


def solution(mesh):
    def shards(tokens, route_weight, cotangent, slot_ids, placement, weight, momentum):
        plan = Plan(
            mesh.shape["expert"],
            mesh.shape["dp"],
            tokens.shape[0],
            tokens.shape[1],
            cotangent.shape[1],
        )
        body = functools.partial(routed, plan) if plan.fits() else general
        return body(tokens, route_weight, cotangent, slot_ids, placement, weight, momentum)

    return jax.shard_map(
        shards,
        mesh=mesh,
        in_specs=(
            P(("dp", "expert"), None),
            P(("dp", "expert")),
            P(("dp", "expert"), None),
            P(("dp", "expert")),
            P(),
            P("expert", None, None),
            P("expert", "dp", None),
        ),
        out_specs=(
            P(("dp", "expert"), None),
            P(("dp", "expert"), None),
            P("expert", "dp", None),
            P("expert", "dp", None),
        ),
        check_vma=False,
    )
```

```python
import functools
import math

import jax
import jax.numpy as jnp
from jax import lax
from jax.experimental import pallas as pl
from jax.experimental.pallas import tpu as pltpu
from jax.sharding import PartitionSpec as P

learning_rate = 0.004
decay_rate = 0.9

BF16 = jnp.bfloat16
F32 = jnp.float32
SUB = 8
LANES = 128
INNER = 2


class Plan:
    def __init__(self, slots, groups, tokens, features, hidden):
        self.slots, self.groups, self.tokens = slots, groups, tokens
        self.D, self.F = features, hidden
        self.half = slots // 2
        self.cap = tokens * 9 // 8 // slots
        self.full, self.rest = divmod(self.cap, SUB)
        self.cuts = SUB // self.rest if self.rest else 1
        self.rows = self.half * self.cap
        self.share = features // groups
        self.DX = features * self.cap // SUB
        self.FG = hidden * self.cap // SUB
        self.C = self.DX + self.FG
        self.pieces = self.cap * groups // SUB
        self.outer = groups // INNER

    def group_at(self, group, step):
        chip, core = group // INNER, group % INNER
        if isinstance(group, int):
            return away(chip, step // INNER, self.outer) * INNER + (core ^ (step % INNER))
        return away_traced(chip, step // INNER, self.outer) * INNER + jnp.bitwise_xor(
            core, step % INNER
        )

    def group_from(self, step):
        chips = step // INNER
        if self.outer & (self.outer - 1):
            chips = (self.outer - chips) % self.outer
        return chips * INNER + step % INNER

    def fits(self):
        return (
            self.slots % 2 == 0
            and (self.rest == 0 or SUB % self.rest == 0)
            and self.D % (self.cuts * LANES) == 0
            and self.F % (self.cuts * LANES) == 0
            and self.D % (self.groups * LANES) == 0
            and self.groups % INNER == 0
            and (self.cap * self.groups) % SUB == 0
            and self.rows % SUB == 0
            and (self.half * self.rest) % SUB == 0
            and self.tokens % LANES == 0
        )


def away(place, step, count):
    if count & (count - 1) == 0:
        return place ^ step
    return (place + step) % count


def away_traced(place, step, count):
    if count & (count - 1) == 0:
        return jnp.bitwise_xor(place, step)
    return lax.rem(place + step, count)


def steps_between(first, second, count):
    if count & (count - 1) == 0:
        return jnp.bitwise_xor(first, second)
    return lax.rem(first - second + count, count)


def iota(shape, dim):
    return lax.broadcasted_iota(jnp.int32, shape, dim)


def dot(a, b):
    return jnp.dot(a, b, preferred_element_type=F32)


def dot_nt(a, b):
    return lax.dot_general(a, b, (((1,), (1,)), ((), ())), preferred_element_type=F32)


def dot_tn(a, b):
    return lax.dot_general(a, b, (((0,), (0,)), ((), ())), preferred_element_type=F32)


def picker(plan, cut):
    shape = (plan.half * plan.rest, plan.half * SUB)
    row, col = iota(shape, 0), iota(shape, 1)
    wanted = (row // plan.rest) * SUB + cut * plan.rest + row % plan.rest
    return (wanted == col).astype(BF16)


def unfold(plan, blocks, width):
    parts = [
        jnp.concatenate([b[:, i * width : (i + 1) * width] for b in blocks], axis=0)
        for i in range(plan.full)
    ]
    if plan.rest:
        piece = width // plan.cuts
        tail = jnp.concatenate([b[:, plan.full * width :] for b in blocks], axis=0).astype(BF16)
        parts.append(
            jnp.concatenate([dot(picker(plan, q), tail) for q in range(plan.cuts)], axis=1)
        )
    return jnp.concatenate(parts, axis=0).astype(BF16)


def fold(plan, rows):
    width = rows.shape[1]
    block = plan.half * SUB
    parts = [rows[i * block : (i + 1) * block] for i in range(plan.full)]
    if plan.rest:
        piece = width // plan.cuts
        tail = rows[plan.full * block :].astype(BF16)
        total = None
        for q in range(plan.cuts):
            term = dot_tn(picker(plan, q), tail[:, q * piece : (q + 1) * piece])
            total = term if total is None else total + term
        parts.append(total)
    return jnp.concatenate(parts, axis=1)


def is_hot(plan, placement_ref):
    me = lax.axis_index("expert")
    partner = lax.rem(me + plan.half, plan.slots)
    return placement_ref[me] == placement_ref[partner]


def token_places(plan, slot):
    me = lax.axis_index("expert")
    my_half = me // plan.half
    my_place = lax.rem(me, plan.half)
    upper = (slot >= plan.half).astype(jnp.int32)
    place = slot - plan.half * upper
    far = jnp.where(upper == my_half, 0, 1)
    step = steps_between(place, jnp.zeros_like(place) + my_place, plan.half)
    block = 2 * step + far
    count = plan.tokens
    onehot = (iota((2 * plan.half, count), 0) == block).astype(F32)
    upto = (iota((count, count), 0) <= iota((count, count), 1)).astype(BF16)
    seen = dot(onehot.astype(BF16), upto)
    rank = jnp.sum(onehot * (seen - 1.0), axis=0, keepdims=True).astype(jnp.int32)
    return block, rank


def row_targets(plan, block, rank):
    targets = []
    for i in range(plan.full):
        inside = (rank >= i * SUB) & (rank < (i + 1) * SUB)
        targets.append(jnp.where(inside, block * SUB + rank - i * SUB, -1))
    for q in range(plan.cuts if plan.rest else 0):
        inside = rank >= plan.full * SUB
        targets.append(
            jnp.where(inside, block * SUB + q * plan.rest + rank - plan.full * SUB, -1)
        )
    return targets


def to_column(row):
    n = row.shape[1]
    eye = (iota((n, n), 0) == iota((n, n), 1)).astype(F32)
    return jnp.sum(eye * row.astype(F32), axis=1, keepdims=True)


def pack_kernel(plan, slot_hbm, gate_hbm, tok_hbm, cot_hbm, *refs):
    half = plan.half
    near, far = refs[:half], refs[half : 2 * half]
    slot_ref, gate_ref, tok_ref, cot_ref, sems = refs[2 * half :]
    copies = [
        pltpu.make_async_copy(source, held, sems.at[i])
        for i, (source, held) in enumerate(
            ((slot_hbm, slot_ref), (tok_hbm, tok_ref), (gate_hbm, gate_ref), (cot_hbm, cot_ref))
        )
    ]
    for copy in copies:
        copy.start()
    copies[0].wait()
    block, rank = token_places(plan, slot_ref[...])
    targets = row_targets(plan, block, rank)
    height = 2 * half * SUB
    onehots = [(iota((height, plan.tokens), 0) == t).astype(BF16) for t in targets]

    def store(values, start):
        stop = start + values.shape[1]
        for m in range(half):
            low = 2 * m * SUB
            near[m][:, start:stop] = values[low : low + 2 * SUB].astype(BF16)
            far[m][:, start:stop] = values[low + SUB : low + 2 * SUB].astype(BF16)

    def place(data, base):
        width = data.shape[1]
        for i in range(plan.full):
            store(dot(onehots[i], data), base + i * width)
        if plan.rest:
            piece = width // plan.cuts
            total = None
            for q in range(plan.cuts):
                term = dot(onehots[plan.full + q], data[:, q * piece : (q + 1) * piece])
                total = term if total is None else total + term
            store(total, base + plan.full * width)

    copies[1].wait()
    place(tok_ref[...], 0)
    copies[2].wait()
    copies[3].wait()
    scaled = (to_column(gate_ref[...]) * cot_ref[...].astype(F32)).astype(BF16)
    place(scaled, plan.DX)


def hold_kernel(plan, weight_hbm, held, mine, sems):
    start = pl.multiple_of(lax.axis_index("dp") * plan.share, LANES)
    copies = [
        pltpu.make_async_copy(weight_hbm.at[0], held, sems.at[0]),
        pltpu.make_async_copy(weight_hbm.at[0, pl.ds(start, plan.share), :], mine, sems.at[1]),
    ]
    for copy in copies:
        copy.start()
    for copy in copies:
        copy.wait()


def blocks_of(refs, start, stop, low=0):
    return [r[:, start:stop].astype(F32)[low : low + SUB] for r in refs]


def columns_kernel(plan, *refs):
    near, outs, held = refs[: plan.half], refs[-plan.groups - 1 : -1], refs[-1]
    held[...] = unfold(plan, blocks_of(near, 0, plan.DX), plan.D)
    for m in range(plan.groups):
        start = pl.multiple_of(plan.group_at(lax.axis_index("dp"), m) * plan.share, LANES)
        outs[m][...] = held[:, pl.ds(start, plan.share)]


def activate(preact, scaled):
    sigma = jax.nn.sigmoid(preact)
    act = (preact * sigma).astype(BF16)
    grad_pre = (scaled.astype(F32) * sigma * (1.0 + preact * (1.0 - sigma))).astype(BF16)
    return act, grad_pre


def chip_columns(plan, rows, outs):
    width = INNER * plan.share
    chip = lax.axis_index("dp") // INNER
    for o in range(plan.outer):
        start = pl.multiple_of(away_traced(chip, o, plan.outer) * width, LANES)
        outs[o][:, :width] = rows[:, pl.ds(start, width)]


def near_kernel(plan, placement_ref, weight_ref, *refs):
    near = refs[: plan.half]
    back_near, local, folded_grad, grads, far_rows = refs[-5:]
    x_near = unfold(plan, blocks_of(near, 0, plan.DX), plan.D)
    x_far = unfold(plan, blocks_of(near, 0, plan.DX, SUB), plan.D)
    g_near = unfold(plan, blocks_of(near, plan.DX, plan.C), plan.F)
    g_far = unfold(plan, blocks_of(near, plan.DX, plan.C, SUB), plan.F)
    far_rows[...] = x_far
    x = jnp.concatenate([x_near.astype(F32), x_far.astype(F32)], axis=0).astype(BF16)
    g = jnp.concatenate([g_near.astype(F32), g_far.astype(F32)], axis=0).astype(BF16)
    act, grad_pre = activate(dot(x, weight_ref[...]), g)
    back = dot_nt(grad_pre, weight_ref[...])
    act, grad32 = act.astype(F32), grad_pre.astype(F32)
    back_near[:, : plan.DX] = fold(plan, back[: plan.rows]).astype(BF16)
    back_near[:, plan.DX :] = fold(plan, act[: plan.rows]).astype(BF16)
    local[:, : plan.DX] = fold(plan, back[plan.rows :]).astype(BF16)
    local[:, plan.DX :] = fold(plan, act[plan.rows :]).astype(BF16)
    grad_near = grad32[: plan.rows]
    grad_far = jnp.where(is_hot(plan, placement_ref), grad32[plan.rows :], 0.0)
    folded_grad[...] = fold(plan, grad_near).astype(BF16)
    grads[:, : plan.F] = grad_near.astype(BF16)
    grads[:, plan.F :] = grad_far.astype(BF16)


def payload_kernel(
    plan, placement_ref, weight_ref, folded_grad, near_grads, far_rows, *refs
):
    half, groups = plan.half, plan.groups
    far, refs = refs[:half], refs[half:]
    columns, refs = refs[:groups], refs[groups:]
    payload, refs = refs[0], refs[1:]
    shared, rows = refs[:groups], refs[groups]
    hot = is_hot(plan, placement_ref)
    x = unfold(plan, blocks_of(far, 0, plan.DX), plan.D)
    g = unfold(plan, blocks_of(far, plan.DX, plan.C), plan.F)
    rows[...] = x
    act, grad_pre = activate(dot(x, weight_ref[...]), g)

    @pl.when(jnp.logical_not(hot))
    def _():
        payload[:, : plan.DX] = fold(plan, dot_nt(grad_pre, weight_ref[...])).astype(BF16)
        payload[:, plan.DX :] = fold(plan, act.astype(F32)).astype(BF16)

    @pl.when(hot)
    def _():
        together = jnp.concatenate([c[...].astype(F32) for c in columns], axis=0)
        block = half * SUB
        for i in range(plan.pieces):
            payload[:, i * plan.share : (i + 1) * plan.share] = together[
                i * block : (i + 1) * block
            ].astype(BF16)
        payload[:, plan.DX :] = folded_grad[...]

    group = lax.axis_index("dp")
    width = plan.share
    for m in range(groups):
        start = pl.multiple_of(plan.group_at(group, m) * width, LANES)
        shared[m][:, :width] = far_rows[:, pl.ds(start, width)]
        shared[m][:, width : 2 * width] = rows[:, pl.ds(start, width)]
        shared[m][:, 2 * width : 2 * width + 2 * plan.F] = near_grads[...]
        shared[m][:, 2 * width + 2 * plan.F :] = grad_pre


def early_kernel(plan, near_back, *refs):
    back = near_back[...].astype(F32)
    for m, out in enumerate(refs[-plan.half :]):
        out[...] = back[m * SUB : (m + 1) * SUB].astype(BF16)


def after_kernel(plan, placement_ref, payload, local, *refs):
    outs = refs[-plan.half - 1 :]
    hot = is_hot(plan, placement_ref)
    got = payload[...].astype(F32)
    chosen = jnp.where(hot, local[...].astype(F32), got)
    for m in range(plan.half):
        outs[m][...] = chosen[m * SUB : (m + 1) * SUB].astype(BF16)
    blocks = [got[m * SUB : (m + 1) * SUB, plan.DX :] for m in range(plan.half)]
    outs[plan.half][...] = jnp.where(hot, unfold(plan, blocks, plan.F).astype(F32), 0.0).astype(BF16)


def unpack_kernel(far, plan, slot_ref, gate_ref, *refs):
    half = plan.half
    got, refs = refs[:half], refs[half:]
    before, refs = (refs[:2], refs[2:]) if far else ((None, None), refs)
    out_ref, grad_ref, held, sems = refs
    copies = [
        pltpu.make_async_copy(source, held.at[i], sems.at[i]) for i, source in enumerate(got)
    ]
    for copy in copies:
        copy.start()
    block, rank = token_places(plan, slot_ref[...])
    block = jnp.where(lax.rem(block, 2) == far, block // 2, -2)
    width = half * SUB
    picks = []
    for target in row_targets(plan, block, rank):
        column = to_column(target).astype(jnp.int32)
        picks.append((iota((plan.tokens, width), 1) == column).astype(BF16))
    gate = to_column(gate_ref[...])
    for copy in copies:
        copy.wait()

    def gather(base, size, scale, placed, out):
        rows = [held[i, :, base : base + size * plan.cap // SUB].astype(F32) for i in range(half)]
        rows = jnp.concatenate(rows, axis=0).astype(BF16)
        piece = size // plan.cuts
        for q in range(plan.cuts):
            span = slice(q * piece, (q + 1) * piece)
            lhs, rhs = list(picks[: plan.full]), []
            for i in range(plan.full):
                rhs.append(rows[:, i * size + q * piece : i * size + (q + 1) * piece])
            if plan.rest:
                lhs.append(picks[plan.full + q])
                rhs.append(rows[:, plan.full * size :])
            value = dot(jnp.concatenate(lhs, axis=1), jnp.concatenate(rhs, axis=0))
            if scale is not None:
                value = scale * value
            if placed is not None:
                value = value + placed[:, span].astype(F32)
            out[:, span] = value.astype(BF16)

    gather(0, plan.D, None, before[1], grad_ref)
    gather(plan.DX, plan.F, gate, before[0], out_ref)


def rows_of(parts):
    return jnp.concatenate([p.astype(F32) for p in parts], axis=0).astype(BF16)


def gather_kernel(plan, momentum_hbm, *refs):
    groups, share, width = plan.groups, plan.share, plan.F
    columns, refs = refs[:groups], refs[groups:]
    shared, refs = refs[:groups], refs[groups:]
    total, x_all, momentum, sem = refs
    copy = pltpu.make_async_copy(momentum_hbm.at[0], momentum, sem)
    copy.start()
    base = 2 * share
    x_parts, g_parts = [], []
    for m in range(groups):
        x_parts.append(columns[m][...])
        x_parts += [shared[m][:, i * share : (i + 1) * share] for i in range(2)]
        g_parts += [shared[m][:, base + i * width : base + (i + 1) * width] for i in range(3)]
    x_all[...] = rows_of(x_parts)
    g_all = rows_of(g_parts)
    copy.wait()
    for i in range(share // LANES):
        span = slice(i * LANES, (i + 1) * LANES)
        before = decay_rate * momentum[span, :].astype(F32)
        total[span, :] = before + dot_tn(x_all[:, span], g_all)


def update_kernel(plan, placement_ref, payload_hbm, *refs):
    groups, share = plan.groups, plan.share
    other_hbm, refs = refs[:groups], refs[groups:]
    total_hbm, weight_hbm, new_weight, new_momentum, payload, other_g = refs[:6]
    total, weight, momentum, sems, tile_sems, out_sems = refs[6:]
    first = [pltpu.make_async_copy(payload_hbm, payload, sems.at[groups])]
    for m in range(groups):
        first.append(pltpu.make_async_copy(other_hbm[m], other_g.at[m], sems.at[m]))
    spans = [pl.ds(i * LANES, LANES) for i in range(share // LANES)]
    tiles = [
        [
            pltpu.make_async_copy(source.at[span, :], target.at[span, :], tile_sems.at[i, j])
            for j, (source, target) in enumerate(((total_hbm, total), (weight_hbm, weight)))
        ]
        for i, span in enumerate(spans)
    ]
    for copy in first + [copy for pair in tiles for copy in pair]:
        copy.start()
    hot = is_hot(plan, placement_ref)
    for copy in first:
        copy.wait()
    pieces = [payload[:, i * share : (i + 1) * share] for i in range(plan.pieces)]
    x = jnp.concatenate(pieces, axis=0)
    x = jnp.where(hot, x.astype(F32), 0.0).astype(BF16)
    g = rows_of([other_g[m] for m in range(groups)])
    done = []
    for i, span in enumerate(spans):
        for copy in tiles[i]:
            copy.wait()
        value = total[span, :] + dot_tn(x[:, i * LANES : (i + 1) * LANES], g)
        value = value.astype(BF16)
        momentum[span, :] = value
        weight[span, :] = (
            weight[span, :].astype(F32) - learning_rate * value.astype(F32)
        ).astype(BF16)
        for j, (source, target) in enumerate(((momentum, new_momentum), (weight, new_weight))):
            copy = pltpu.make_async_copy(
                source.at[span, :], target.at[0, span, :], out_sems.at[i, j]
            )
            copy.start()
            done.append(copy)
    for copy in done:
        copy.wait()


MIB = 1024 * 1024
SMEM_SPEC = pl.BlockSpec(memory_space=pltpu.SMEM)
ANY_SPEC = pl.BlockSpec(memory_space=pl.ANY)
VMEM_SPEC = pl.BlockSpec(memory_space=pltpu.VMEM)


def call(kernel, plan, ins, specs, outs, scratch, flops, name, limit=16, dtypes=None):
    moved = sum(a.size * a.dtype.itemsize for a in ins) + sum(2 * math.prod(o) for o in outs)
    return pl.pallas_call(
        functools.partial(kernel, plan),
        out_shape=[
            jax.ShapeDtypeStruct(s, dtypes[i] if dtypes else BF16) for i, s in enumerate(outs)
        ],
        in_specs=specs,
        out_specs=[VMEM_SPEC] * len(outs),
        scratch_shapes=scratch,
        compiler_params=pltpu.CompilerParams(vmem_limit_bytes=limit * MIB),
        cost_estimate=pl.CostEstimate(
            flops=flops, bytes_accessed=moved if flops else 0, transcendentals=0
        ),
        name=name,
    )(*ins)


def routed(plan, tokens, route_weight, cotangent, slot_ids, placement, weight, momentum):
    half, groups, outer = plan.half, plan.groups, plan.outer
    D, F, C, rows, share = plan.D, plan.F, plan.C, plan.rows, plan.share
    slot = slot_ids.reshape(1, -1)
    gate = route_weight.reshape(1, -1)

    def to_slot(data, m, flip=0):
        pairs = []
        for e in range(plan.slots):
            h, k = divmod(e, half)
            pairs.append((e, (h ^ flip) * half + away(k, m, half)))
        return lax.ppermute(data, "expert", pairs)

    def to_source(data, m):
        pairs = []
        for e in range(plan.slots):
            h, k = divmod(e, half)
            pairs.append((h * half + away(k, m, half), e))
        return lax.ppermute(data, "expert", pairs)

    def to_partner(data):
        pairs = [(e, (e + half) % plan.slots) for e in range(plan.slots)]
        return lax.ppermute(data, "expert", pairs)

    def from_group(data, m):
        pairs = []
        for d in range(groups):
            pairs.append((plan.group_at(d, m), d))
        return lax.ppermute(data, "dp", pairs)

    def from_chips(per_chip):
        return [per_chip[0]] + [
            from_group(per_chip[plan.group_from(INNER * o) // INNER], INNER * o)
            for o in range(1, outer)
        ]

    def with_sisters(got):
        return [data for own in got for data in (own, from_group(own, 1))]

    def from_groups(per_group):
        return [per_group[0]] + [
            from_group(per_group[plan.group_from(m)], m) for m in range(1, groups)
        ]

    packed = call(
        pack_kernel,
        plan,
        [slot, gate, tokens, cotangent],
        [ANY_SPEC] * 4,
        [(2 * SUB, C)] * half + [(SUB, C)] * half,
        [
            pltpu.VMEM(slot.shape, slot.dtype),
            pltpu.VMEM(gate.shape, gate.dtype),
            pltpu.VMEM(tokens.shape, tokens.dtype),
            pltpu.VMEM(cotangent.shape, cotangent.dtype),
            pltpu.SemaphoreType.DMA((4,)),
        ],
        2 * 4 * half * SUB * plan.tokens * (D + F),
        "pack",
        limit=60,
    )
    near = [packed[0]] + [to_slot(packed[m], m) for m in range(1, half)]
    far = [to_slot(packed[half + m], m, 1) for m in range(half)]
    held, old_weight = call(
        hold_kernel,
        plan,
        [weight],
        [ANY_SPEC],
        [(D, F), (share, F)],
        [pltpu.SemaphoreType.DMA((2,))],
        0,
        "hold",
        limit=40,
    )
    columns = call(
        columns_kernel,
        plan,
        near,
        [VMEM_SPEC] * half,
        [(rows, share)] * groups,
        [pltpu.VMEM((rows, D), BF16)],
        0,
        "near_columns",
    )
    columns_here = from_groups(columns)
    back_near, local, folded_grad, grads, far_rows = call(
        near_kernel,
        plan,
        [placement, held] + near + [columns[0]],
        [SMEM_SPEC] + [VMEM_SPEC] * (1 + half) + [ANY_SPEC],
        [
            (half * SUB, C),
            (half * SUB, C),
            (half * SUB, plan.FG),
            (rows, 2 * F),
            (rows, D),
        ],
        [],
        8 * rows * D * F,
        "near_rows",
    )
    outs = call(
        payload_kernel,
        plan,
        [placement, held, folded_grad, grads, far_rows] + far + columns_here,
        [SMEM_SPEC] + [VMEM_SPEC] * (4 + half + groups),
        [(half * SUB, C)] + [(rows, 2 * share + 3 * F)] * groups,
        [pltpu.VMEM((rows, D), BF16)],
        4 * rows * D * F,
        "payload",
    )
    payload = to_partner(outs[0])
    shared = from_groups(outs[1:])
    outs = call(
        early_kernel,
        plan,
        [back_near, shared[1]],
        [VMEM_SPEC, ANY_SPEC],
        [(SUB, C)] * half,
        [],
        0,
        "early",
        limit=4,
    )
    early = [outs[0]] + [to_source(outs[m], m) for m in range(1, half)]
    (total,) = call(
        gather_kernel,
        plan,
        [momentum] + columns_here + shared,
        [ANY_SPEC] + [VMEM_SPEC] * (2 * groups),
        [(share, F)],
        [
            pltpu.VMEM((3 * groups * rows, share), BF16),
            pltpu.VMEM((share, F), BF16),
            pltpu.SemaphoreType.DMA,
        ],
        0,
        "own_terms",
        dtypes=[F32],
    )
    def place(far, got, placed, name):
        return call(
            functools.partial(unpack_kernel, far),
            plan,
            [slot, gate] + got + placed,
            [VMEM_SPEC] * 2 + [ANY_SPEC] * half + [VMEM_SPEC] * len(placed),
            [(plan.tokens, F), (plan.tokens, D)],
            [pltpu.VMEM((half, SUB, C), BF16), pltpu.SemaphoreType.DMA((half,))],
            0,
            name,
            limit=12,
        )

    placed = list(place(0, early, [], "near_results"))
    outs = call(
        after_kernel,
        plan,
        [placement, payload, local] + early[1:3],
        [SMEM_SPEC] + [VMEM_SPEC] * 2 + [ANY_SPEC] * 2,
        [(SUB, C)] * half + [(rows, F)],
        [],
        0,
        "after_swap",
        limit=8,
    )
    late = [outs[0]] + [to_source(outs[m], m) for m in range(1, half)]
    other_g = with_sisters(from_chips([outs[half]] * outer))

    new_weight, new_momentum = pl.pallas_call(
        functools.partial(update_kernel, plan),
        out_shape=[jax.ShapeDtypeStruct((1, share, F), BF16)] * 2,
        in_specs=[SMEM_SPEC] + [ANY_SPEC] * (groups + 3),
        out_specs=[ANY_SPEC] * 2,
        scratch_shapes=[
            pltpu.VMEM((half * SUB, C), BF16),
            pltpu.VMEM((groups, rows, F), BF16),
            pltpu.VMEM((share, F), F32),
            pltpu.VMEM((share, F), BF16),
            pltpu.VMEM((share, F), BF16),
            pltpu.SemaphoreType.DMA((groups + 1,)),
            pltpu.SemaphoreType.DMA((share // LANES, 2)),
            pltpu.SemaphoreType.DMA((share // LANES, 2)),
        ],
        compiler_params=pltpu.CompilerParams(vmem_limit_bytes=20 * MIB),
        cost_estimate=pl.CostEstimate(
            flops=2 * groups * rows * share * F, bytes_accessed=12 * share * F, transcendentals=0
        ),
        name="update",
    )(placement, payload, *other_g, total, old_weight)

    expert_out, token_grad = place(1, late, placed, "far_results")
    return expert_out, token_grad, new_weight, new_momentum


def general(tokens, route_weight, cotangent, slot_ids, placement, weight, momentum):
    n_slots = lax.axis_size("expert")
    n_groups = lax.axis_size("dp")
    tok_count, D = tokens.shape
    F = cotangent.shape[1]
    capacity = tok_count * 9 // 8 // n_slots
    onehot = (slot_ids[:, None] == jnp.arange(n_slots, dtype=jnp.int32)[None, :]).astype(jnp.int32)
    ranks = jnp.sum((jnp.cumsum(onehot, axis=0) - 1) * onehot, axis=1)
    position = slot_ids * capacity + ranks
    send_rows = jnp.zeros((n_slots * capacity, D), BF16).at[position].set(tokens)
    scaled = (route_weight[:, None] * cotangent.astype(F32)).astype(BF16)
    send_grads = jnp.zeros((n_slots * capacity, F), BF16).at[position].set(scaled)
    matrix = weight[0]

    def exchange(rows):
        width = rows.shape[-1]
        return lax.all_to_all(
            rows.reshape(n_slots, capacity, width), "expert", split_axis=0, concat_axis=0, tiled=True
        ).reshape(-1, width)

    flat_x = exchange(send_rows)
    act, flat_grad = activate(dot(flat_x, matrix), exchange(send_grads))
    back = dot_nt(flat_grad, matrix).astype(BF16)
    act_rows = exchange(act)[position]
    expert_out = (route_weight[:, None] * act_rows.astype(F32)).astype(BF16)
    token_grad = exchange(back)[position]
    row_count = flat_x.shape[0]
    share = D // n_groups
    columns = lax.all_to_all(
        flat_x.reshape(1, row_count, n_groups, share), "dp", split_axis=2, concat_axis=0, tiled=True
    )
    columns = columns.reshape(n_groups, row_count, share)
    terms = jnp.einsum(
        "krd,krf->kdf",
        columns,
        lax.all_gather(flat_grad[None], "dp", axis=0, tiled=True),
        preferred_element_type=F32,
    )
    terms = lax.optimization_barrier(terms.astype(BF16)).astype(F32)
    reduced = jnp.sum(terms, axis=0).astype(BF16)
    half = n_slots // 2
    partner_grad = lax.ppermute(
        reduced, "expert", [(i, (i + half) % n_slots) for i in range(n_slots)]
    ).astype(F32)
    my_slot = lax.axis_index("expert")
    partner_slot = (my_slot + half) % n_slots
    same = placement[my_slot] == placement[partner_slot]
    total = reduced.astype(F32) + jnp.where(same, partner_grad, 0.0)
    new_momentum = (decay_rate * momentum[0].astype(F32) + total).astype(BF16)
    old = lax.dynamic_slice_in_dim(matrix, lax.axis_index("dp") * share, share, 0).astype(F32)
    new_weight = (old - learning_rate * new_momentum.astype(F32)).astype(BF16)
    return expert_out, token_grad, new_weight[None], new_momentum[None]


def solution(mesh):
    def shards(tokens, route_weight, cotangent, slot_ids, placement, weight, momentum):
        plan = Plan(
            mesh.shape["expert"],
            mesh.shape["dp"],
            tokens.shape[0],
            tokens.shape[1],
            cotangent.shape[1],
        )
        body = functools.partial(routed, plan) if plan.fits() else general
        return body(tokens, route_weight, cotangent, slot_ids, placement, weight, momentum)

    return jax.shard_map(
        shards,
        mesh=mesh,
        in_specs=(
            P(("dp", "expert"), None),
            P(("dp", "expert")),
            P(("dp", "expert"), None),
            P(("dp", "expert")),
            P(),
            P("expert", None, None),
            P("expert", "dp", None),
        ),
        out_specs=(
            P(("dp", "expert"), None),
            P(("dp", "expert"), None),
            P("expert", "dp", None),
            P("expert", "dp", None),
        ),
        check_vma=False,
    )
```

```python
import functools
import math

import jax
import jax.numpy as jnp
from jax import lax
from jax.experimental import pallas as pl
from jax.experimental.pallas import tpu as pltpu
from jax.sharding import PartitionSpec as P

learning_rate = 0.004
decay_rate = 0.9

BF16 = jnp.bfloat16
F32 = jnp.float32
SUB = 8
LANES = 128
INNER = 2


class Plan:
    def __init__(self, slots, groups, tokens, features, hidden):
        self.slots, self.groups, self.tokens = slots, groups, tokens
        self.D, self.F = features, hidden
        self.half = slots // 2
        self.cap = tokens * 9 // 8 // slots
        self.full, self.rest = divmod(self.cap, SUB)
        self.cuts = SUB // self.rest if self.rest else 1
        self.rows = self.half * self.cap
        self.share = features // groups
        self.DX = features * self.cap // SUB
        self.FG = hidden * self.cap // SUB
        self.C = self.DX + self.FG
        self.pieces = self.cap * groups // SUB
        self.outer = groups // INNER

    def group_at(self, group, step):
        chip, core = group // INNER, group % INNER
        if isinstance(group, int):
            return away(chip, step // INNER, self.outer) * INNER + (core ^ (step % INNER))
        return away_traced(chip, step // INNER, self.outer) * INNER + jnp.bitwise_xor(
            core, step % INNER
        )

    def group_from(self, step):
        chips = step // INNER
        if self.outer & (self.outer - 1):
            chips = (self.outer - chips) % self.outer
        return chips * INNER + step % INNER

    def fits(self):
        return (
            self.slots % 2 == 0
            and (self.rest == 0 or SUB % self.rest == 0)
            and self.D % (self.cuts * LANES) == 0
            and self.F % (self.cuts * LANES) == 0
            and self.D % (self.groups * LANES) == 0
            and self.groups % INNER == 0
            and (self.cap * self.groups) % SUB == 0
            and self.rows % SUB == 0
            and (self.half * self.rest) % SUB == 0
            and self.tokens % LANES == 0
        )


def away(place, step, count):
    if count & (count - 1) == 0:
        return place ^ step
    return (place + step) % count


def away_traced(place, step, count):
    if count & (count - 1) == 0:
        return jnp.bitwise_xor(place, step)
    return lax.rem(place + step, count)


def steps_between(first, second, count):
    if count & (count - 1) == 0:
        return jnp.bitwise_xor(first, second)
    return lax.rem(first - second + count, count)


def iota(shape, dim):
    return lax.broadcasted_iota(jnp.int32, shape, dim)


def dot(a, b):
    return jnp.dot(a, b, preferred_element_type=F32)


def dot_nt(a, b):
    return lax.dot_general(a, b, (((1,), (1,)), ((), ())), preferred_element_type=F32)


def dot_tn(a, b):
    return lax.dot_general(a, b, (((0,), (0,)), ((), ())), preferred_element_type=F32)


def picker(plan, cut):
    shape = (plan.half * plan.rest, plan.half * SUB)
    row, col = iota(shape, 0), iota(shape, 1)
    wanted = (row // plan.rest) * SUB + cut * plan.rest + row % plan.rest
    return (wanted == col).astype(BF16)


def unfold(plan, blocks, width):
    parts = [
        jnp.concatenate([b[:, i * width : (i + 1) * width] for b in blocks], axis=0)
        for i in range(plan.full)
    ]
    if plan.rest:
        piece = width // plan.cuts
        tail = jnp.concatenate([b[:, plan.full * width :] for b in blocks], axis=0).astype(BF16)
        parts.append(
            jnp.concatenate([dot(picker(plan, q), tail) for q in range(plan.cuts)], axis=1)
        )
    return jnp.concatenate(parts, axis=0).astype(BF16)


def fold(plan, rows):
    width = rows.shape[1]
    block = plan.half * SUB
    parts = [rows[i * block : (i + 1) * block] for i in range(plan.full)]
    if plan.rest:
        piece = width // plan.cuts
        tail = rows[plan.full * block :].astype(BF16)
        total = None
        for q in range(plan.cuts):
            term = dot_tn(picker(plan, q), tail[:, q * piece : (q + 1) * piece])
            total = term if total is None else total + term
        parts.append(total)
    return jnp.concatenate(parts, axis=1)


def is_hot(plan, placement_ref):
    me = lax.axis_index("expert")
    partner = lax.rem(me + plan.half, plan.slots)
    return placement_ref[me] == placement_ref[partner]


def token_places(plan, slot):
    me = lax.axis_index("expert")
    my_half = me // plan.half
    my_place = lax.rem(me, plan.half)
    upper = (slot >= plan.half).astype(jnp.int32)
    place = slot - plan.half * upper
    far = jnp.where(upper == my_half, 0, 1)
    step = steps_between(place, jnp.zeros_like(place) + my_place, plan.half)
    block = 2 * step + far
    count = plan.tokens
    onehot = (iota((2 * plan.half, count), 0) == block).astype(F32)
    upto = (iota((count, count), 0) <= iota((count, count), 1)).astype(BF16)
    seen = dot(onehot.astype(BF16), upto)
    rank = jnp.sum(onehot * (seen - 1.0), axis=0, keepdims=True).astype(jnp.int32)
    return block, rank


def row_targets(plan, block, rank):
    targets = []
    for i in range(plan.full):
        inside = (rank >= i * SUB) & (rank < (i + 1) * SUB)
        targets.append(jnp.where(inside, block * SUB + rank - i * SUB, -1))
    for q in range(plan.cuts if plan.rest else 0):
        inside = rank >= plan.full * SUB
        targets.append(
            jnp.where(inside, block * SUB + q * plan.rest + rank - plan.full * SUB, -1)
        )
    return targets


def to_column(row):
    n = row.shape[1]
    eye = (iota((n, n), 0) == iota((n, n), 1)).astype(F32)
    return jnp.sum(eye * row.astype(F32), axis=1, keepdims=True)


def pack_kernel(plan, slot_hbm, gate_hbm, tok_hbm, cot_hbm, *refs):
    half = plan.half
    near, far = refs[:half], refs[half : 2 * half]
    slot_ref, gate_ref, tok_ref, cot_ref, sems = refs[2 * half :]
    copies = [
        pltpu.make_async_copy(source, held, sems.at[i])
        for i, (source, held) in enumerate(
            ((slot_hbm, slot_ref), (tok_hbm, tok_ref), (gate_hbm, gate_ref), (cot_hbm, cot_ref))
        )
    ]
    for copy in copies:
        copy.start()
    copies[0].wait()
    block, rank = token_places(plan, slot_ref[...])
    targets = row_targets(plan, block, rank)
    height = 2 * half * SUB
    onehots = [(iota((height, plan.tokens), 0) == t).astype(BF16) for t in targets]

    def store(values, start):
        stop = start + values.shape[1]
        for m in range(half):
            low = 2 * m * SUB
            near[m][:, start:stop] = values[low : low + 2 * SUB].astype(BF16)
            far[m][:, start:stop] = values[low + SUB : low + 2 * SUB].astype(BF16)

    def place(data, base):
        width = data.shape[1]
        for i in range(plan.full):
            store(dot(onehots[i], data), base + i * width)
        if plan.rest:
            piece = width // plan.cuts
            total = None
            for q in range(plan.cuts):
                term = dot(onehots[plan.full + q], data[:, q * piece : (q + 1) * piece])
                total = term if total is None else total + term
            store(total, base + plan.full * width)

    copies[1].wait()
    place(tok_ref[...], 0)
    copies[2].wait()
    copies[3].wait()
    scaled = (to_column(gate_ref[...]) * cot_ref[...].astype(F32)).astype(BF16)
    place(scaled, plan.DX)


def hold_kernel(plan, weight_hbm, held, mine, sems):
    start = pl.multiple_of(lax.axis_index("dp") * plan.share, LANES)
    copies = [
        pltpu.make_async_copy(weight_hbm.at[0], held, sems.at[0]),
        pltpu.make_async_copy(weight_hbm.at[0, pl.ds(start, plan.share), :], mine, sems.at[1]),
    ]
    for copy in copies:
        copy.start()
    for copy in copies:
        copy.wait()


def blocks_of(refs, start, stop, low=0):
    return [r[:, start:stop].astype(F32)[low : low + SUB] for r in refs]


def columns_kernel(plan, *refs):
    near, outs, held = refs[: plan.half], refs[-plan.groups - 1 : -1], refs[-1]
    held[...] = unfold(plan, blocks_of(near, 0, plan.DX), plan.D)
    for m in range(plan.groups):
        start = pl.multiple_of(plan.group_at(lax.axis_index("dp"), m) * plan.share, LANES)
        outs[m][...] = held[:, pl.ds(start, plan.share)]


def activate(preact, scaled):
    sigma = jax.nn.sigmoid(preact)
    act = (preact * sigma).astype(BF16)
    grad_pre = (scaled.astype(F32) * sigma * (1.0 + preact * (1.0 - sigma))).astype(BF16)
    return act, grad_pre


def chip_columns(plan, rows, outs):
    width = INNER * plan.share
    chip = lax.axis_index("dp") // INNER
    for o in range(plan.outer):
        start = pl.multiple_of(away_traced(chip, o, plan.outer) * width, LANES)
        outs[o][:, :width] = rows[:, pl.ds(start, width)]


def near_kernel(plan, placement_ref, weight_ref, *refs):
    near = refs[: plan.half]
    back_near, local, folded_grad, grads, far_rows = refs[-5:]
    x_near = unfold(plan, blocks_of(near, 0, plan.DX), plan.D)
    x_far = unfold(plan, blocks_of(near, 0, plan.DX, SUB), plan.D)
    g_near = unfold(plan, blocks_of(near, plan.DX, plan.C), plan.F)
    g_far = unfold(plan, blocks_of(near, plan.DX, plan.C, SUB), plan.F)
    far_rows[...] = x_far
    x = jnp.concatenate([x_near.astype(F32), x_far.astype(F32)], axis=0).astype(BF16)
    g = jnp.concatenate([g_near.astype(F32), g_far.astype(F32)], axis=0).astype(BF16)
    act, grad_pre = activate(dot(x, weight_ref[...]), g)
    back = dot_nt(grad_pre, weight_ref[...])
    act, grad32 = act.astype(F32), grad_pre.astype(F32)
    back_near[:, : plan.DX] = fold(plan, back[: plan.rows]).astype(BF16)
    back_near[:, plan.DX :] = fold(plan, act[: plan.rows]).astype(BF16)
    local[:, : plan.DX] = fold(plan, back[plan.rows :]).astype(BF16)
    local[:, plan.DX :] = fold(plan, act[plan.rows :]).astype(BF16)
    grad_near = grad32[: plan.rows]
    grad_far = jnp.where(is_hot(plan, placement_ref), grad32[plan.rows :], 0.0)
    folded_grad[...] = fold(plan, grad_near).astype(BF16)
    grads[:, : plan.F] = grad_near.astype(BF16)
    grads[:, plan.F :] = grad_far.astype(BF16)


def payload_kernel(
    plan, placement_ref, weight_ref, folded_grad, near_grads, far_rows, *refs
):
    half, groups, outer = plan.half, plan.groups, plan.outer
    far, refs = refs[:half], refs[half:]
    columns, refs = refs[:groups], refs[groups:]
    payload, refs = refs[0], refs[1:]
    shared, rows = refs[:outer], refs[outer]
    hot = is_hot(plan, placement_ref)
    x = unfold(plan, blocks_of(far, 0, plan.DX), plan.D)
    g = unfold(plan, blocks_of(far, plan.DX, plan.C), plan.F)
    rows[...] = x
    act, grad_pre = activate(dot(x, weight_ref[...]), g)

    @pl.when(jnp.logical_not(hot))
    def _():
        payload[:, : plan.DX] = fold(plan, dot_nt(grad_pre, weight_ref[...])).astype(BF16)
        payload[:, plan.DX :] = fold(plan, act.astype(F32)).astype(BF16)

    @pl.when(hot)
    def _():
        together = jnp.concatenate([c[...].astype(F32) for c in columns], axis=0)
        block = half * SUB
        for i in range(plan.pieces):
            payload[:, i * plan.share : (i + 1) * plan.share] = together[
                i * block : (i + 1) * block
            ].astype(BF16)
        payload[:, plan.DX :] = folded_grad[...]

    chip = lax.axis_index("dp") // INNER
    width = INNER * plan.share
    for o in range(outer):
        start = pl.multiple_of(away_traced(chip, o, outer) * width, LANES)
        shared[o][:, :width] = far_rows[:, pl.ds(start, width)]
        shared[o][:, width : 2 * width] = rows[:, pl.ds(start, width)]
        shared[o][:, 2 * width : 2 * width + 2 * plan.F] = near_grads[...]
        shared[o][:, 2 * width + 2 * plan.F :] = grad_pre


def relay_kernel(plan, *refs):
    count = plan.outer - 1
    for source, target in zip(refs[:count], refs[-count:]):
        target[...] = source[...]


def early_kernel(plan, near_back, *refs):
    back = near_back[...].astype(F32)
    for m, out in enumerate(refs[-plan.half :]):
        out[...] = back[m * SUB : (m + 1) * SUB].astype(BF16)


def after_kernel(plan, placement_ref, payload, local, *refs):
    outs = refs[-plan.half - 1 :]
    hot = is_hot(plan, placement_ref)
    got = payload[...].astype(F32)
    chosen = jnp.where(hot, local[...].astype(F32), got)
    for m in range(plan.half):
        outs[m][...] = chosen[m * SUB : (m + 1) * SUB].astype(BF16)
    blocks = [got[m * SUB : (m + 1) * SUB, plan.DX :] for m in range(plan.half)]
    outs[plan.half][...] = jnp.where(hot, unfold(plan, blocks, plan.F).astype(F32), 0.0).astype(BF16)


def unpack_kernel(far, plan, slot_ref, gate_ref, *refs):
    half = plan.half
    got, refs = refs[:half], refs[half:]
    before, refs = (refs[:2], refs[2:]) if far else ((None, None), refs)
    out_ref, grad_ref, held, sems = refs
    copies = [
        pltpu.make_async_copy(source, held.at[i], sems.at[i]) for i, source in enumerate(got)
    ]
    for copy in copies:
        copy.start()
    block, rank = token_places(plan, slot_ref[...])
    block = jnp.where(lax.rem(block, 2) == far, block // 2, -2)
    width = half * SUB
    picks = []
    for target in row_targets(plan, block, rank):
        column = to_column(target).astype(jnp.int32)
        picks.append((iota((plan.tokens, width), 1) == column).astype(BF16))
    gate = to_column(gate_ref[...])
    for copy in copies:
        copy.wait()

    def gather(base, size, scale, placed, out):
        rows = [held[i, :, base : base + size * plan.cap // SUB].astype(F32) for i in range(half)]
        rows = jnp.concatenate(rows, axis=0).astype(BF16)
        piece = size // plan.cuts
        for q in range(plan.cuts):
            span = slice(q * piece, (q + 1) * piece)
            lhs, rhs = list(picks[: plan.full]), []
            for i in range(plan.full):
                rhs.append(rows[:, i * size + q * piece : i * size + (q + 1) * piece])
            if plan.rest:
                lhs.append(picks[plan.full + q])
                rhs.append(rows[:, plan.full * size :])
            value = dot(jnp.concatenate(lhs, axis=1), jnp.concatenate(rhs, axis=0))
            if scale is not None:
                value = scale * value
            if placed is not None:
                value = value + placed[:, span].astype(F32)
            out[:, span] = value.astype(BF16)

    gather(0, plan.D, None, before[1], grad_ref)
    gather(plan.DX, plan.F, gate, before[0], out_ref)


def rows_of(parts):
    return jnp.concatenate([p.astype(F32) for p in parts], axis=0).astype(BF16)


def gather_kernel(plan, momentum_hbm, *refs):
    groups, share, width = plan.groups, plan.share, plan.F
    columns, refs = refs[:groups], refs[groups:]
    shared, refs = refs[:groups], refs[groups:]
    total, x_all, momentum, sem = refs
    copy = pltpu.make_async_copy(momentum_hbm.at[0], momentum, sem)
    copy.start()
    core = lax.rem(lax.axis_index("dp"), INNER)
    base = 2 * INNER * share
    x_parts, g_parts = [], []
    for m in range(groups):
        x_parts.append(columns[m][...])
        for i in range(2):
            start = pl.multiple_of((i * INNER + core) * share, LANES)
            x_parts.append(shared[m][:, pl.ds(start, share)])
        g_parts += [shared[m][:, base + i * width : base + (i + 1) * width] for i in range(3)]
    x_all[...] = rows_of(x_parts)
    g_all = rows_of(g_parts)
    copy.wait()
    for i in range(share // LANES):
        span = slice(i * LANES, (i + 1) * LANES)
        before = decay_rate * momentum[span, :].astype(F32)
        total[span, :] = before + dot_tn(x_all[:, span], g_all)


def update_kernel(plan, placement_ref, total, old_weight, payload_hbm, *refs):
    groups, share = plan.groups, plan.share
    other_hbm, refs = refs[:groups], refs[groups:]
    new_weight, new_momentum, payload, other_g, weight, momentum, sems, out_sems = refs
    copies = [pltpu.make_async_copy(payload_hbm, payload, sems.at[groups])]
    for m in range(groups):
        copies.append(pltpu.make_async_copy(other_hbm[m], other_g.at[m], sems.at[m]))
    for copy in copies:
        copy.start()
    hot = is_hot(plan, placement_ref)
    for copy in copies:
        copy.wait()
    pieces = [payload[:, i * share : (i + 1) * share] for i in range(plan.pieces)]
    x = jnp.concatenate(pieces, axis=0)
    x = jnp.where(hot, x.astype(F32), 0.0).astype(BF16)
    g = rows_of([other_g[m] for m in range(groups)])
    done = []
    for i in range(share // LANES):
        span = pl.ds(i * LANES, LANES)
        value = total[span, :] + dot_tn(x[:, i * LANES : (i + 1) * LANES], g)
        value = value.astype(BF16)
        momentum[span, :] = value
        weight[span, :] = (
            old_weight[span, :].astype(F32) - learning_rate * value.astype(F32)
        ).astype(BF16)
        for j, (source, target) in enumerate(((momentum, new_momentum), (weight, new_weight))):
            copy = pltpu.make_async_copy(
                source.at[span, :], target.at[0, span, :], out_sems.at[i, j]
            )
            copy.start()
            done.append(copy)
    for copy in done:
        copy.wait()


MIB = 1024 * 1024
SMEM_SPEC = pl.BlockSpec(memory_space=pltpu.SMEM)
ANY_SPEC = pl.BlockSpec(memory_space=pl.ANY)
VMEM_SPEC = pl.BlockSpec(memory_space=pltpu.VMEM)


def call(kernel, plan, ins, specs, outs, scratch, flops, name, limit=16, dtypes=None):
    moved = sum(a.size * a.dtype.itemsize for a in ins) + sum(2 * math.prod(o) for o in outs)
    return pl.pallas_call(
        functools.partial(kernel, plan),
        out_shape=[
            jax.ShapeDtypeStruct(s, dtypes[i] if dtypes else BF16) for i, s in enumerate(outs)
        ],
        in_specs=specs,
        out_specs=[VMEM_SPEC] * len(outs),
        scratch_shapes=scratch,
        compiler_params=pltpu.CompilerParams(vmem_limit_bytes=limit * MIB),
        cost_estimate=pl.CostEstimate(
            flops=flops, bytes_accessed=moved if flops else 0, transcendentals=0
        ),
        name=name,
    )(*ins)


def routed(plan, tokens, route_weight, cotangent, slot_ids, placement, weight, momentum):
    half, groups, outer = plan.half, plan.groups, plan.outer
    D, F, C, rows, share = plan.D, plan.F, plan.C, plan.rows, plan.share
    slot = slot_ids.reshape(1, -1)
    gate = route_weight.reshape(1, -1)

    def to_slot(data, m, flip=0):
        pairs = []
        for e in range(plan.slots):
            h, k = divmod(e, half)
            pairs.append((e, (h ^ flip) * half + away(k, m, half)))
        return lax.ppermute(data, "expert", pairs)

    def to_source(data, m):
        pairs = []
        for e in range(plan.slots):
            h, k = divmod(e, half)
            pairs.append((h * half + away(k, m, half), e))
        return lax.ppermute(data, "expert", pairs)

    def to_partner(data):
        pairs = [(e, (e + half) % plan.slots) for e in range(plan.slots)]
        return lax.ppermute(data, "expert", pairs)

    def from_group(data, m):
        pairs = []
        for d in range(groups):
            pairs.append((plan.group_at(d, m), d))
        return lax.ppermute(data, "dp", pairs)

    def from_chips(per_chip):
        return [per_chip[0]] + [
            from_group(per_chip[plan.group_from(INNER * o) // INNER], INNER * o)
            for o in range(1, outer)
        ]

    def with_sisters(got):
        return [data for own in got for data in (own, from_group(own, 1))]

    def from_groups(per_group):
        return [per_group[0]] + [
            from_group(per_group[plan.group_from(m)], m) for m in range(1, groups)
        ]

    packed = call(
        pack_kernel,
        plan,
        [slot, gate, tokens, cotangent],
        [ANY_SPEC] * 4,
        [(2 * SUB, C)] * half + [(SUB, C)] * half,
        [
            pltpu.VMEM(slot.shape, slot.dtype),
            pltpu.VMEM(gate.shape, gate.dtype),
            pltpu.VMEM(tokens.shape, tokens.dtype),
            pltpu.VMEM(cotangent.shape, cotangent.dtype),
            pltpu.SemaphoreType.DMA((4,)),
        ],
        2 * 4 * half * SUB * plan.tokens * (D + F),
        "pack",
        limit=60,
    )
    near = [packed[0]] + [to_slot(packed[m], m) for m in range(1, half)]
    far = [to_slot(packed[half + m], m, 1) for m in range(half)]
    held, old_weight = call(
        hold_kernel,
        plan,
        [weight],
        [ANY_SPEC],
        [(D, F), (share, F)],
        [pltpu.SemaphoreType.DMA((2,))],
        0,
        "hold",
        limit=40,
    )
    columns = call(
        columns_kernel,
        plan,
        near,
        [VMEM_SPEC] * half,
        [(rows, share)] * groups,
        [pltpu.VMEM((rows, D), BF16)],
        0,
        "near_columns",
    )
    columns_here = from_groups(columns)
    back_near, local, folded_grad, grads, far_rows = call(
        near_kernel,
        plan,
        [placement, held] + near + [columns[0]],
        [SMEM_SPEC] + [VMEM_SPEC] * (1 + half) + [ANY_SPEC],
        [
            (half * SUB, C),
            (half * SUB, C),
            (half * SUB, plan.FG),
            (rows, 2 * F),
            (rows, D),
        ],
        [],
        8 * rows * D * F,
        "near_rows",
    )
    outs = call(
        payload_kernel,
        plan,
        [placement, held, folded_grad, grads, far_rows] + far + columns_here,
        [SMEM_SPEC] + [VMEM_SPEC] * (4 + half + groups),
        [(half * SUB, C)] + [(rows, 2 * INNER * share + 3 * F)] * outer,
        [pltpu.VMEM((rows, D), BF16)],
        4 * rows * D * F,
        "payload",
    )
    payload = to_partner(outs[0])
    shared = from_chips(outs[1:])
    sister = from_group(shared[0], 1)
    outs = call(
        early_kernel,
        plan,
        [back_near, sister],
        [VMEM_SPEC, ANY_SPEC],
        [(SUB, C)] * half,
        [],
        0,
        "early",
        limit=4,
    )
    early = [outs[0]] + [to_source(outs[m], m) for m in range(1, half)]
    gate_by = early[1:]
    relayed = call(
        relay_kernel,
        plan,
        shared[1:] + gate_by,
        [VMEM_SPEC] * (outer - 1) + [ANY_SPEC] * len(gate_by),
        [data.shape for data in shared[1:]],
        [],
        0,
        "relay",
        limit=8,
    )
    sisters = [sister] + [from_group(data, 1) for data in relayed]
    shared = [data for pair in zip(shared, sisters) for data in pair]
    (total,) = call(
        gather_kernel,
        plan,
        [momentum] + columns_here + shared,
        [ANY_SPEC] + [VMEM_SPEC] * (2 * groups),
        [(share, F)],
        [
            pltpu.VMEM((3 * groups * rows, share), BF16),
            pltpu.VMEM((share, F), BF16),
            pltpu.SemaphoreType.DMA,
        ],
        0,
        "own_terms",
        dtypes=[F32],
    )
    def place(far, got, placed, name):
        return call(
            functools.partial(unpack_kernel, far),
            plan,
            [slot, gate] + got + placed,
            [VMEM_SPEC] * 2 + [ANY_SPEC] * half + [VMEM_SPEC] * len(placed),
            [(plan.tokens, F), (plan.tokens, D)],
            [pltpu.VMEM((half, SUB, C), BF16), pltpu.SemaphoreType.DMA((half,))],
            0,
            name,
            limit=12,
        )

    placed = list(place(0, early, [], "near_results"))
    outs = call(
        after_kernel,
        plan,
        [placement, payload, local] + placed[:1],
        [SMEM_SPEC] + [VMEM_SPEC] * 2 + [ANY_SPEC] * 1,
        [(SUB, C)] * half + [(rows, F)],
        [],
        0,
        "after_swap",
        limit=8,
    )
    late = [outs[0]] + [to_source(outs[m], m) for m in range(1, half)]
    other_g = with_sisters(from_chips([outs[half]] * outer))

    new_weight, new_momentum = pl.pallas_call(
        functools.partial(update_kernel, plan),
        out_shape=[jax.ShapeDtypeStruct((1, share, F), BF16)] * 2,
        in_specs=[SMEM_SPEC] + [VMEM_SPEC] * 2 + [ANY_SPEC] * (groups + 1),
        out_specs=[ANY_SPEC] * 2,
        scratch_shapes=[
            pltpu.VMEM((half * SUB, C), BF16),
            pltpu.VMEM((groups, rows, F), BF16),
            pltpu.VMEM((share, F), BF16),
            pltpu.VMEM((share, F), BF16),
            pltpu.SemaphoreType.DMA((groups + 1,)),
            pltpu.SemaphoreType.DMA((share // LANES, 2)),
        ],
        compiler_params=pltpu.CompilerParams(vmem_limit_bytes=20 * MIB),
        cost_estimate=pl.CostEstimate(
            flops=2 * groups * rows * share * F, bytes_accessed=12 * share * F, transcendentals=0
        ),
        name="update",
    )(placement, total, old_weight, payload, *other_g)

    expert_out, token_grad = place(1, late, placed, "far_results")
    return expert_out, token_grad, new_weight, new_momentum


def general(tokens, route_weight, cotangent, slot_ids, placement, weight, momentum):
    n_slots = lax.axis_size("expert")
    n_groups = lax.axis_size("dp")
    tok_count, D = tokens.shape
    F = cotangent.shape[1]
    capacity = tok_count * 9 // 8 // n_slots
    onehot = (slot_ids[:, None] == jnp.arange(n_slots, dtype=jnp.int32)[None, :]).astype(jnp.int32)
    ranks = jnp.sum((jnp.cumsum(onehot, axis=0) - 1) * onehot, axis=1)
    position = slot_ids * capacity + ranks
    send_rows = jnp.zeros((n_slots * capacity, D), BF16).at[position].set(tokens)
    scaled = (route_weight[:, None] * cotangent.astype(F32)).astype(BF16)
    send_grads = jnp.zeros((n_slots * capacity, F), BF16).at[position].set(scaled)
    matrix = weight[0]

    def exchange(rows):
        width = rows.shape[-1]
        return lax.all_to_all(
            rows.reshape(n_slots, capacity, width), "expert", split_axis=0, concat_axis=0, tiled=True
        ).reshape(-1, width)

    flat_x = exchange(send_rows)
    act, flat_grad = activate(dot(flat_x, matrix), exchange(send_grads))
    back = dot_nt(flat_grad, matrix).astype(BF16)
    act_rows = exchange(act)[position]
    expert_out = (route_weight[:, None] * act_rows.astype(F32)).astype(BF16)
    token_grad = exchange(back)[position]
    row_count = flat_x.shape[0]
    share = D // n_groups
    columns = lax.all_to_all(
        flat_x.reshape(1, row_count, n_groups, share), "dp", split_axis=2, concat_axis=0, tiled=True
    )
    columns = columns.reshape(n_groups, row_count, share)
    terms = jnp.einsum(
        "krd,krf->kdf",
        columns,
        lax.all_gather(flat_grad[None], "dp", axis=0, tiled=True),
        preferred_element_type=F32,
    )
    terms = lax.optimization_barrier(terms.astype(BF16)).astype(F32)
    reduced = jnp.sum(terms, axis=0).astype(BF16)
    half = n_slots // 2
    partner_grad = lax.ppermute(
        reduced, "expert", [(i, (i + half) % n_slots) for i in range(n_slots)]
    ).astype(F32)
    my_slot = lax.axis_index("expert")
    partner_slot = (my_slot + half) % n_slots
    same = placement[my_slot] == placement[partner_slot]
    total = reduced.astype(F32) + jnp.where(same, partner_grad, 0.0)
    new_momentum = (decay_rate * momentum[0].astype(F32) + total).astype(BF16)
    old = lax.dynamic_slice_in_dim(matrix, lax.axis_index("dp") * share, share, 0).astype(F32)
    new_weight = (old - learning_rate * new_momentum.astype(F32)).astype(BF16)
    return expert_out, token_grad, new_weight[None], new_momentum[None]


def solution(mesh):
    def shards(tokens, route_weight, cotangent, slot_ids, placement, weight, momentum):
        plan = Plan(
            mesh.shape["expert"],
            mesh.shape["dp"],
            tokens.shape[0],
            tokens.shape[1],
            cotangent.shape[1],
        )
        body = functools.partial(routed, plan) if plan.fits() else general
        return body(tokens, route_weight, cotangent, slot_ids, placement, weight, momentum)

    return jax.shard_map(
        shards,
        mesh=mesh,
        in_specs=(
            P(("dp", "expert"), None),
            P(("dp", "expert")),
            P(("dp", "expert"), None),
            P(("dp", "expert")),
            P(),
            P("expert", None, None),
            P("expert", "dp", None),
        ),
        out_specs=(
            P(("dp", "expert"), None),
            P(("dp", "expert"), None),
            P("expert", "dp", None),
            P("expert", "dp", None),
        ),
        check_vma=False,
    )
```

```python
import functools
import math

import jax
import jax.numpy as jnp
from jax import lax
from jax.experimental import pallas as pl
from jax.experimental.pallas import tpu as pltpu
from jax.sharding import PartitionSpec as P

learning_rate = 0.004
decay_rate = 0.9

BF16 = jnp.bfloat16
F32 = jnp.float32
SUB = 8
LANES = 128
INNER = 2


class Plan:
    def __init__(self, slots, groups, tokens, features, hidden):
        self.slots, self.groups, self.tokens = slots, groups, tokens
        self.D, self.F = features, hidden
        self.half = slots // 2
        self.cap = tokens * 9 // 8 // slots
        self.full, self.rest = divmod(self.cap, SUB)
        self.cuts = SUB // self.rest if self.rest else 1
        self.rows = self.half * self.cap
        self.far_order = [*range(0, self.half, 2), *range(1, self.half, 2)]
        self.share = features // groups
        self.DX = features * self.cap // SUB
        self.FG = hidden * self.cap // SUB
        self.C = self.DX + self.FG
        self.pieces = self.cap * groups // SUB
        self.outer = groups // INNER

    def group_at(self, group, step):
        chip, core = group // INNER, group % INNER
        if isinstance(group, int):
            return away(chip, step // INNER, self.outer) * INNER + (core ^ (step % INNER))
        return away_traced(chip, step // INNER, self.outer) * INNER + jnp.bitwise_xor(
            core, step % INNER
        )

    def group_from(self, step):
        chips = step // INNER
        if self.outer & (self.outer - 1):
            chips = (self.outer - chips) % self.outer
        return chips * INNER + step % INNER

    def fits(self):
        return (
            self.slots % 2 == 0
            and (self.rest == 0 or SUB % self.rest == 0)
            and self.D % (self.cuts * LANES) == 0
            and self.F % (self.cuts * LANES) == 0
            and self.D % (self.groups * LANES) == 0
            and self.groups % INNER == 0
            and (self.cap * self.groups) % SUB == 0
            and self.rows % SUB == 0
            and (self.half * self.rest) % SUB == 0
            and self.tokens % LANES == 0
        )


def away(place, step, count):
    if count & (count - 1) == 0:
        return place ^ step
    return (place + step) % count


def away_traced(place, step, count):
    if count & (count - 1) == 0:
        return jnp.bitwise_xor(place, step)
    return lax.rem(place + step, count)


def steps_between(first, second, count):
    if count & (count - 1) == 0:
        return jnp.bitwise_xor(first, second)
    return lax.rem(first - second + count, count)


def iota(shape, dim):
    return lax.broadcasted_iota(jnp.int32, shape, dim)


def dot(a, b):
    return jnp.dot(a, b, preferred_element_type=F32)


def dot_nt(a, b):
    return lax.dot_general(a, b, (((1,), (1,)), ((), ())), preferred_element_type=F32)


def dot_tn(a, b):
    return lax.dot_general(a, b, (((0,), (0,)), ((), ())), preferred_element_type=F32)


def picker(plan, cut):
    shape = (plan.half * plan.rest, plan.half * SUB)
    row, col = iota(shape, 0), iota(shape, 1)
    wanted = (row // plan.rest) * SUB + cut * plan.rest + row % plan.rest
    return (wanted == col).astype(BF16)


def unfold(plan, blocks, width):
    parts = [
        jnp.concatenate([b[:, i * width : (i + 1) * width] for b in blocks], axis=0)
        for i in range(plan.full)
    ]
    if plan.rest:
        piece = width // plan.cuts
        tail = jnp.concatenate([b[:, plan.full * width :] for b in blocks], axis=0).astype(BF16)
        parts.append(
            jnp.concatenate([dot(picker(plan, q), tail) for q in range(plan.cuts)], axis=1)
        )
    return jnp.concatenate(parts, axis=0).astype(BF16)


def fold(plan, rows):
    width = rows.shape[1]
    block = plan.half * SUB
    parts = [rows[i * block : (i + 1) * block] for i in range(plan.full)]
    if plan.rest:
        piece = width // plan.cuts
        tail = rows[plan.full * block :].astype(BF16)
        total = None
        for q in range(plan.cuts):
            term = dot_tn(picker(plan, q), tail[:, q * piece : (q + 1) * piece])
            total = term if total is None else total + term
        parts.append(total)
    return jnp.concatenate(parts, axis=1)


def is_hot(plan, placement_ref):
    me = lax.axis_index("expert")
    partner = lax.rem(me + plan.half, plan.slots)
    return placement_ref[me] == placement_ref[partner]


def token_places(plan, slot):
    me = lax.axis_index("expert")
    my_half = me // plan.half
    my_place = lax.rem(me, plan.half)
    upper = (slot >= plan.half).astype(jnp.int32)
    place = slot - plan.half * upper
    far = jnp.where(upper == my_half, 0, 1)
    step = steps_between(place, jnp.zeros_like(place) + my_place, plan.half)
    block = 2 * step + far
    count = plan.tokens
    onehot = (iota((2 * plan.half, count), 0) == block).astype(F32)
    upto = (iota((count, count), 0) <= iota((count, count), 1)).astype(BF16)
    seen = dot(onehot.astype(BF16), upto)
    rank = jnp.sum(onehot * (seen - 1.0), axis=0, keepdims=True).astype(jnp.int32)
    return block, rank


def row_targets(plan, block, rank):
    targets = []
    for i in range(plan.full):
        inside = (rank >= i * SUB) & (rank < (i + 1) * SUB)
        targets.append(jnp.where(inside, block * SUB + rank - i * SUB, -1))
    for q in range(plan.cuts if plan.rest else 0):
        inside = rank >= plan.full * SUB
        targets.append(
            jnp.where(inside, block * SUB + q * plan.rest + rank - plan.full * SUB, -1)
        )
    return targets


def to_column(row):
    n = row.shape[1]
    eye = (iota((n, n), 0) == iota((n, n), 1)).astype(F32)
    return jnp.sum(eye * row.astype(F32), axis=1, keepdims=True)


def pack_kernel(plan, slot_hbm, gate_hbm, tok_hbm, cot_hbm, *refs):
    half = plan.half
    near, far = refs[:half], refs[half : 2 * half]
    slot_ref, gate_ref, tok_ref, cot_ref, sems = refs[2 * half :]
    copies = [
        pltpu.make_async_copy(source, held, sems.at[i])
        for i, (source, held) in enumerate(
            ((slot_hbm, slot_ref), (tok_hbm, tok_ref), (gate_hbm, gate_ref), (cot_hbm, cot_ref))
        )
    ]
    for copy in copies:
        copy.start()
    copies[0].wait()
    block, rank = token_places(plan, slot_ref[...])
    targets = row_targets(plan, block, rank)
    height = 2 * half * SUB
    onehots = [(iota((height, plan.tokens), 0) == t).astype(BF16) for t in targets]

    def store(values, start):
        stop = start + values.shape[1]
        for m in range(half):
            low = 2 * m * SUB
            near[m][:, start:stop] = values[low : low + 2 * SUB].astype(BF16)
            far[m][:, start:stop] = values[low + SUB : low + 2 * SUB].astype(BF16)

    def place(data, base):
        width = data.shape[1]
        for i in range(plan.full):
            store(dot(onehots[i], data), base + i * width)
        if plan.rest:
            piece = width // plan.cuts
            total = None
            for q in range(plan.cuts):
                term = dot(onehots[plan.full + q], data[:, q * piece : (q + 1) * piece])
                total = term if total is None else total + term
            store(total, base + plan.full * width)

    copies[1].wait()
    place(tok_ref[...], 0)
    copies[2].wait()
    copies[3].wait()
    scaled = (to_column(gate_ref[...]) * cot_ref[...].astype(F32)).astype(BF16)
    place(scaled, plan.DX)


def hold_kernel(plan, weight_hbm, held, mine, sems):
    start = pl.multiple_of(lax.axis_index("dp") * plan.share, LANES)
    copies = [
        pltpu.make_async_copy(weight_hbm.at[0], held, sems.at[0]),
        pltpu.make_async_copy(weight_hbm.at[0, pl.ds(start, plan.share), :], mine, sems.at[1]),
    ]
    for copy in copies:
        copy.start()
    for copy in copies:
        copy.wait()


def blocks_of(refs, start, stop, low=0):
    return [r[:, start:stop].astype(F32)[low : low + SUB] for r in refs]


def columns_kernel(plan, *refs):
    near, outs, held = refs[: plan.half], refs[-plan.groups - 1 : -1], refs[-1]
    held[...] = unfold(plan, blocks_of(near, 0, plan.DX), plan.D)
    for m in range(plan.groups):
        start = pl.multiple_of(plan.group_at(lax.axis_index("dp"), m) * plan.share, LANES)
        outs[m][...] = held[:, pl.ds(start, plan.share)]


def activate(preact, scaled):
    sigma = jax.nn.sigmoid(preact)
    act = (preact * sigma).astype(BF16)
    grad_pre = (scaled.astype(F32) * sigma * (1.0 + preact * (1.0 - sigma))).astype(BF16)
    return act, grad_pre


def chip_columns(plan, rows, outs):
    width = INNER * plan.share
    chip = lax.axis_index("dp") // INNER
    for o in range(plan.outer):
        start = pl.multiple_of(away_traced(chip, o, plan.outer) * width, LANES)
        outs[o][:, :width] = rows[:, pl.ds(start, width)]


def near_kernel(plan, placement_ref, weight_ref, *refs):
    near = refs[: plan.half]
    back_near, local, folded_grad, grads, far_rows = refs[-5:]
    x_near = unfold(plan, blocks_of(near, 0, plan.DX), plan.D)
    x_far = unfold(plan, blocks_of(near, 0, plan.DX, SUB), plan.D)
    g_near = unfold(plan, blocks_of(near, plan.DX, plan.C), plan.F)
    g_far = unfold(plan, blocks_of(near, plan.DX, plan.C, SUB), plan.F)
    far_rows[...] = x_far
    x = jnp.concatenate([x_near.astype(F32), x_far.astype(F32)], axis=0).astype(BF16)
    g = jnp.concatenate([g_near.astype(F32), g_far.astype(F32)], axis=0).astype(BF16)
    act, grad_pre = activate(dot(x, weight_ref[...]), g)
    back = dot_nt(grad_pre, weight_ref[...])
    act, grad32 = act.astype(F32), grad_pre.astype(F32)
    back_near[:, : plan.DX] = fold(plan, back[: plan.rows]).astype(BF16)
    back_near[:, plan.DX :] = fold(plan, act[: plan.rows]).astype(BF16)
    local[:, : plan.DX] = fold(plan, back[plan.rows :]).astype(BF16)
    local[:, plan.DX :] = fold(plan, act[plan.rows :]).astype(BF16)
    grad_near = grad32[: plan.rows]
    grad_far = jnp.where(is_hot(plan, placement_ref), grad32[plan.rows :], 0.0)
    folded_grad[...] = fold(plan, grad_near).astype(BF16)
    grads[:, : plan.F] = grad_near.astype(BF16)
    grads[:, plan.F :] = grad_far.astype(BF16)


def payload_kernel(
    plan, placement_ref, weight_ref, folded_grad, near_grads, far_rows, *refs
):
    half, groups = plan.half, plan.groups
    far, refs = [refs[plan.far_order.index(m)] for m in range(half)], refs[half:]
    columns, refs = refs[:groups], refs[groups:]
    payload, refs = refs[0], refs[1:]
    shared, rows = refs[:groups], refs[groups]
    hot = is_hot(plan, placement_ref)
    x = unfold(plan, blocks_of(far, 0, plan.DX), plan.D)
    g = unfold(plan, blocks_of(far, plan.DX, plan.C), plan.F)
    rows[...] = x
    act, grad_pre = activate(dot(x, weight_ref[...]), g)

    @pl.when(jnp.logical_not(hot))
    def _():
        payload[:, : plan.DX] = fold(plan, dot_nt(grad_pre, weight_ref[...])).astype(BF16)
        payload[:, plan.DX :] = fold(plan, act.astype(F32)).astype(BF16)

    @pl.when(hot)
    def _():
        together = jnp.concatenate([c[...].astype(F32) for c in columns], axis=0)
        block = half * SUB
        for i in range(plan.pieces):
            payload[:, i * plan.share : (i + 1) * plan.share] = together[
                i * block : (i + 1) * block
            ].astype(BF16)
        payload[:, plan.DX :] = folded_grad[...]

    group = lax.axis_index("dp")
    width = plan.share
    for m in range(groups):
        start = pl.multiple_of(plan.group_at(group, m) * width, LANES)
        shared[m][:, :width] = far_rows[:, pl.ds(start, width)]
        shared[m][:, width : 2 * width] = rows[:, pl.ds(start, width)]
        shared[m][:, 2 * width : 2 * width + 2 * plan.F] = near_grads[...]
        shared[m][:, 2 * width + 2 * plan.F :] = grad_pre


def early_kernel(plan, near_back, *refs):
    back = near_back[...].astype(F32)
    for m, out in enumerate(refs[-plan.half :]):
        out[...] = back[m * SUB : (m + 1) * SUB].astype(BF16)


def after_kernel(plan, placement_ref, payload, local, *refs):
    outs = refs[-plan.half - 1 :]
    hot = is_hot(plan, placement_ref)
    got = payload[...].astype(F32)
    chosen = jnp.where(hot, local[...].astype(F32), got)
    for m in range(plan.half):
        outs[m][...] = chosen[m * SUB : (m + 1) * SUB].astype(BF16)
    blocks = [got[m * SUB : (m + 1) * SUB, plan.DX :] for m in range(plan.half)]
    outs[plan.half][...] = jnp.where(hot, unfold(plan, blocks, plan.F).astype(F32), 0.0).astype(BF16)


def unpack_kernel(far, plan, slot_ref, gate_ref, *refs):
    half = plan.half
    got, refs = refs[:half], refs[half:]
    before, refs = (refs[:2], refs[2:]) if far else ((None, None), refs)
    out_ref, grad_ref, held, sems = refs
    copies = [
        pltpu.make_async_copy(source, held.at[i], sems.at[i]) for i, source in enumerate(got)
    ]
    for copy in copies:
        copy.start()
    block, rank = token_places(plan, slot_ref[...])
    block = jnp.where(lax.rem(block, 2) == far, block // 2, -2)
    width = half * SUB
    picks = []
    for target in row_targets(plan, block, rank):
        column = to_column(target).astype(jnp.int32)
        picks.append((iota((plan.tokens, width), 1) == column).astype(BF16))
    gate = to_column(gate_ref[...])
    for copy in copies:
        copy.wait()

    def gather(base, size, scale, placed, out):
        rows = [held[i, :, base : base + size * plan.cap // SUB].astype(F32) for i in range(half)]
        rows = jnp.concatenate(rows, axis=0).astype(BF16)
        piece = size // plan.cuts
        for q in range(plan.cuts):
            span = slice(q * piece, (q + 1) * piece)
            lhs, rhs = list(picks[: plan.full]), []
            for i in range(plan.full):
                rhs.append(rows[:, i * size + q * piece : i * size + (q + 1) * piece])
            if plan.rest:
                lhs.append(picks[plan.full + q])
                rhs.append(rows[:, plan.full * size :])
            value = dot(jnp.concatenate(lhs, axis=1), jnp.concatenate(rhs, axis=0))
            if scale is not None:
                value = scale * value
            if placed is not None:
                value = value + placed[:, span].astype(F32)
            out[:, span] = value.astype(BF16)

    gather(0, plan.D, None, before[1], grad_ref)
    gather(plan.DX, plan.F, gate, before[0], out_ref)


def rows_of(parts):
    return jnp.concatenate([p.astype(F32) for p in parts], axis=0).astype(BF16)


def gather_kernel(plan, momentum_hbm, *refs):
    groups, share, width = plan.groups, plan.share, plan.F
    columns, refs = refs[:groups], refs[groups:]
    shared, refs = refs[:groups], refs[groups:]
    total, x_all, momentum, sem = refs
    copy = pltpu.make_async_copy(momentum_hbm.at[0], momentum, sem)
    copy.start()
    base = 2 * share
    x_parts, g_parts = [], []
    for m in range(groups):
        x_parts.append(columns[m][...])
        x_parts += [shared[m][:, i * share : (i + 1) * share] for i in range(2)]
        g_parts += [shared[m][:, base + i * width : base + (i + 1) * width] for i in range(3)]
    x_all[...] = rows_of(x_parts)
    g_all = rows_of(g_parts)
    copy.wait()
    for i in range(share // LANES):
        span = slice(i * LANES, (i + 1) * LANES)
        before = decay_rate * momentum[span, :].astype(F32)
        total[span, :] = before + dot_tn(x_all[:, span], g_all)


def update_kernel(plan, placement_ref, total, old_weight, payload_hbm, *refs):
    groups, share = plan.groups, plan.share
    other_hbm, refs = refs[:groups], refs[groups:]
    new_weight, new_momentum, payload, other_g, weight, momentum, sems, out_sems = refs
    copies = [pltpu.make_async_copy(payload_hbm, payload, sems.at[groups])]
    for m in range(groups):
        copies.append(pltpu.make_async_copy(other_hbm[m], other_g.at[m], sems.at[m]))
    for copy in copies:
        copy.start()
    hot = is_hot(plan, placement_ref)
    for copy in copies:
        copy.wait()
    pieces = [payload[:, i * share : (i + 1) * share] for i in range(plan.pieces)]
    x = jnp.concatenate(pieces, axis=0)
    x = jnp.where(hot, x.astype(F32), 0.0).astype(BF16)
    g = rows_of([other_g[m] for m in range(groups)])
    done = []
    for i in range(share // LANES):
        span = pl.ds(i * LANES, LANES)
        value = total[span, :] + dot_tn(x[:, i * LANES : (i + 1) * LANES], g)
        value = value.astype(BF16)
        momentum[span, :] = value
        weight[span, :] = (
            old_weight[span, :].astype(F32) - learning_rate * value.astype(F32)
        ).astype(BF16)
        for j, (source, target) in enumerate(((momentum, new_momentum), (weight, new_weight))):
            copy = pltpu.make_async_copy(
                source.at[span, :], target.at[0, span, :], out_sems.at[i, j]
            )
            copy.start()
            done.append(copy)
    for copy in done:
        copy.wait()


MIB = 1024 * 1024
SMEM_SPEC = pl.BlockSpec(memory_space=pltpu.SMEM)
ANY_SPEC = pl.BlockSpec(memory_space=pl.ANY)
VMEM_SPEC = pl.BlockSpec(memory_space=pltpu.VMEM)


def call(kernel, plan, ins, specs, outs, scratch, flops, name, limit=16, dtypes=None):
    moved = sum(a.size * a.dtype.itemsize for a in ins) + sum(2 * math.prod(o) for o in outs)
    return pl.pallas_call(
        functools.partial(kernel, plan),
        out_shape=[
            jax.ShapeDtypeStruct(s, dtypes[i] if dtypes else BF16) for i, s in enumerate(outs)
        ],
        in_specs=specs,
        out_specs=[VMEM_SPEC] * len(outs),
        scratch_shapes=scratch,
        compiler_params=pltpu.CompilerParams(vmem_limit_bytes=limit * MIB),
        cost_estimate=pl.CostEstimate(
            flops=flops, bytes_accessed=moved if flops else 0, transcendentals=0
        ),
        name=name,
    )(*ins)


def routed(plan, tokens, route_weight, cotangent, slot_ids, placement, weight, momentum):
    half, groups, outer = plan.half, plan.groups, plan.outer
    D, F, C, rows, share = plan.D, plan.F, plan.C, plan.rows, plan.share
    slot = slot_ids.reshape(1, -1)
    gate = route_weight.reshape(1, -1)

    def to_slot(data, m, flip=0):
        pairs = []
        for e in range(plan.slots):
            h, k = divmod(e, half)
            pairs.append((e, (h ^ flip) * half + away(k, m, half)))
        return lax.ppermute(data, "expert", pairs)

    def to_source(data, m):
        pairs = []
        for e in range(plan.slots):
            h, k = divmod(e, half)
            pairs.append((h * half + away(k, m, half), e))
        return lax.ppermute(data, "expert", pairs)

    def to_partner(data):
        pairs = [(e, (e + half) % plan.slots) for e in range(plan.slots)]
        return lax.ppermute(data, "expert", pairs)

    def from_group(data, m):
        pairs = []
        for d in range(groups):
            pairs.append((plan.group_at(d, m), d))
        return lax.ppermute(data, "dp", pairs)

    def from_chips(per_chip):
        return [per_chip[0]] + [
            from_group(per_chip[plan.group_from(INNER * o) // INNER], INNER * o)
            for o in range(1, outer)
        ]

    def with_sisters(got):
        return [data for own in got for data in (own, from_group(own, 1))]

    def from_groups(per_group):
        return [per_group[0]] + [
            from_group(per_group[plan.group_from(m)], m) for m in range(1, groups)
        ]

    packed = call(
        pack_kernel,
        plan,
        [slot, gate, tokens, cotangent],
        [ANY_SPEC] * 4,
        [(2 * SUB, C)] * half + [(SUB, C)] * half,
        [
            pltpu.VMEM(slot.shape, slot.dtype),
            pltpu.VMEM(gate.shape, gate.dtype),
            pltpu.VMEM(tokens.shape, tokens.dtype),
            pltpu.VMEM(cotangent.shape, cotangent.dtype),
            pltpu.SemaphoreType.DMA((4,)),
        ],
        2 * 4 * half * SUB * plan.tokens * (D + F),
        "pack",
        limit=60,
    )
    near = [packed[0]] + [to_slot(packed[m], m) for m in range(1, half)]
    far = [to_slot(packed[half + m], m, 1) for m in range(half)]
    held, old_weight = call(
        hold_kernel,
        plan,
        [weight],
        [ANY_SPEC],
        [(D, F), (share, F)],
        [pltpu.SemaphoreType.DMA((2,))],
        0,
        "hold",
        limit=40,
    )
    columns = call(
        columns_kernel,
        plan,
        near,
        [VMEM_SPEC] * half,
        [(rows, share)] * groups,
        [pltpu.VMEM((rows, D), BF16)],
        0,
        "near_columns",
    )
    columns_here = from_groups(columns)
    back_near, local, folded_grad, grads, far_rows = call(
        near_kernel,
        plan,
        [placement, held] + near + [columns[0]],
        [SMEM_SPEC] + [VMEM_SPEC] * (1 + half) + [ANY_SPEC],
        [
            (half * SUB, C),
            (half * SUB, C),
            (half * SUB, plan.FG),
            (rows, 2 * F),
            (rows, D),
        ],
        [],
        8 * rows * D * F,
        "near_rows",
    )
    outs = call(
        payload_kernel,
        plan,
        [placement, held, folded_grad, grads, far_rows]
        + [far[m] for m in plan.far_order]
        + columns_here,
        [SMEM_SPEC] + [VMEM_SPEC] * (4 + half + groups),
        [(half * SUB, C)] + [(rows, 2 * share + 3 * F)] * groups,
        [pltpu.VMEM((rows, D), BF16)],
        4 * rows * D * F,
        "payload",
    )
    payload = to_partner(outs[0])
    shared = from_groups(outs[1:])
    outs = call(
        early_kernel,
        plan,
        [back_near, shared[1]],
        [VMEM_SPEC, ANY_SPEC],
        [(SUB, C)] * half,
        [],
        0,
        "early",
        limit=4,
    )
    early = [outs[0]] + [to_source(outs[m], m) for m in range(1, half)]
    (total,) = call(
        gather_kernel,
        plan,
        [momentum] + columns_here + shared,
        [ANY_SPEC] + [VMEM_SPEC] * (2 * groups),
        [(share, F)],
        [
            pltpu.VMEM((3 * groups * rows, share), BF16),
            pltpu.VMEM((share, F), BF16),
            pltpu.SemaphoreType.DMA,
        ],
        0,
        "own_terms",
        dtypes=[F32],
    )
    def place(far, got, placed, name):
        return call(
            functools.partial(unpack_kernel, far),
            plan,
            [slot, gate] + got + placed,
            [VMEM_SPEC] * 2 + [ANY_SPEC] * half + [VMEM_SPEC] * len(placed),
            [(plan.tokens, F), (plan.tokens, D)],
            [pltpu.VMEM((half, SUB, C), BF16), pltpu.SemaphoreType.DMA((half,))],
            0,
            name,
            limit=12,
        )

    placed = list(place(0, early, [], "near_results"))
    outs = call(
        after_kernel,
        plan,
        [placement, payload, local] + early[1:3],
        [SMEM_SPEC] + [VMEM_SPEC] * 2 + [ANY_SPEC] * 2,
        [(SUB, C)] * half + [(rows, F)],
        [],
        0,
        "after_swap",
        limit=8,
    )
    late = [outs[0]] + [to_source(outs[m], m) for m in range(1, half)]
    other_g = with_sisters(from_chips([outs[half]] * outer))

    new_weight, new_momentum = pl.pallas_call(
        functools.partial(update_kernel, plan),
        out_shape=[jax.ShapeDtypeStruct((1, share, F), BF16)] * 2,
        in_specs=[SMEM_SPEC] + [VMEM_SPEC] * 2 + [ANY_SPEC] * (groups + 1),
        out_specs=[ANY_SPEC] * 2,
        scratch_shapes=[
            pltpu.VMEM((half * SUB, C), BF16),
            pltpu.VMEM((groups, rows, F), BF16),
            pltpu.VMEM((share, F), BF16),
            pltpu.VMEM((share, F), BF16),
            pltpu.SemaphoreType.DMA((groups + 1,)),
            pltpu.SemaphoreType.DMA((share // LANES, 2)),
        ],
        compiler_params=pltpu.CompilerParams(vmem_limit_bytes=20 * MIB),
        cost_estimate=pl.CostEstimate(
            flops=2 * groups * rows * share * F, bytes_accessed=12 * share * F, transcendentals=0
        ),
        name="update",
    )(placement, total, old_weight, payload, *other_g)

    expert_out, token_grad = place(1, late, placed, "far_results")
    return expert_out, token_grad, new_weight, new_momentum


def general(tokens, route_weight, cotangent, slot_ids, placement, weight, momentum):
    n_slots = lax.axis_size("expert")
    n_groups = lax.axis_size("dp")
    tok_count, D = tokens.shape
    F = cotangent.shape[1]
    capacity = tok_count * 9 // 8 // n_slots
    onehot = (slot_ids[:, None] == jnp.arange(n_slots, dtype=jnp.int32)[None, :]).astype(jnp.int32)
    ranks = jnp.sum((jnp.cumsum(onehot, axis=0) - 1) * onehot, axis=1)
    position = slot_ids * capacity + ranks
    send_rows = jnp.zeros((n_slots * capacity, D), BF16).at[position].set(tokens)
    scaled = (route_weight[:, None] * cotangent.astype(F32)).astype(BF16)
    send_grads = jnp.zeros((n_slots * capacity, F), BF16).at[position].set(scaled)
    matrix = weight[0]

    def exchange(rows):
        width = rows.shape[-1]
        return lax.all_to_all(
            rows.reshape(n_slots, capacity, width), "expert", split_axis=0, concat_axis=0, tiled=True
        ).reshape(-1, width)

    flat_x = exchange(send_rows)
    act, flat_grad = activate(dot(flat_x, matrix), exchange(send_grads))
    back = dot_nt(flat_grad, matrix).astype(BF16)
    act_rows = exchange(act)[position]
    expert_out = (route_weight[:, None] * act_rows.astype(F32)).astype(BF16)
    token_grad = exchange(back)[position]
    row_count = flat_x.shape[0]
    share = D // n_groups
    columns = lax.all_to_all(
        flat_x.reshape(1, row_count, n_groups, share), "dp", split_axis=2, concat_axis=0, tiled=True
    )
    columns = columns.reshape(n_groups, row_count, share)
    terms = jnp.einsum(
        "krd,krf->kdf",
        columns,
        lax.all_gather(flat_grad[None], "dp", axis=0, tiled=True),
        preferred_element_type=F32,
    )
    terms = lax.optimization_barrier(terms.astype(BF16)).astype(F32)
    reduced = jnp.sum(terms, axis=0).astype(BF16)
    half = n_slots // 2
    partner_grad = lax.ppermute(
        reduced, "expert", [(i, (i + half) % n_slots) for i in range(n_slots)]
    ).astype(F32)
    my_slot = lax.axis_index("expert")
    partner_slot = (my_slot + half) % n_slots
    same = placement[my_slot] == placement[partner_slot]
    total = reduced.astype(F32) + jnp.where(same, partner_grad, 0.0)
    new_momentum = (decay_rate * momentum[0].astype(F32) + total).astype(BF16)
    old = lax.dynamic_slice_in_dim(matrix, lax.axis_index("dp") * share, share, 0).astype(F32)
    new_weight = (old - learning_rate * new_momentum.astype(F32)).astype(BF16)
    return expert_out, token_grad, new_weight[None], new_momentum[None]


def solution(mesh):
    def shards(tokens, route_weight, cotangent, slot_ids, placement, weight, momentum):
        plan = Plan(
            mesh.shape["expert"],
            mesh.shape["dp"],
            tokens.shape[0],
            tokens.shape[1],
            cotangent.shape[1],
        )
        body = functools.partial(routed, plan) if plan.fits() else general
        return body(tokens, route_weight, cotangent, slot_ids, placement, weight, momentum)

    return jax.shard_map(
        shards,
        mesh=mesh,
        in_specs=(
            P(("dp", "expert"), None),
            P(("dp", "expert")),
            P(("dp", "expert"), None),
            P(("dp", "expert")),
            P(),
            P("expert", None, None),
            P("expert", "dp", None),
        ),
        out_specs=(
            P(("dp", "expert"), None),
            P(("dp", "expert"), None),
            P("expert", "dp", None),
            P("expert", "dp", None),
        ),
        check_vma=False,
    )
```

```python
import functools
import math

import jax
import jax.numpy as jnp
from jax import lax
from jax.experimental import pallas as pl
from jax.experimental.pallas import tpu as pltpu
from jax.sharding import PartitionSpec as P

learning_rate = 0.004
decay_rate = 0.9

BF16 = jnp.bfloat16
F32 = jnp.float32
SUB = 8
LANES = 128
INNER = 2


class Plan:
    def __init__(self, slots, groups, tokens, features, hidden):
        self.slots, self.groups, self.tokens = slots, groups, tokens
        self.D, self.F = features, hidden
        self.half = slots // 2
        self.cap = tokens * 9 // 8 // slots
        self.full, self.rest = divmod(self.cap, SUB)
        self.cuts = SUB // self.rest if self.rest else 1
        self.rows = self.half * self.cap
        self.far_order = [*range(0, self.half, 2), *range(1, self.half, 2)]
        self.share = features // groups
        self.DX = features * self.cap // SUB
        self.FG = hidden * self.cap // SUB
        self.C = self.DX + self.FG
        self.pieces = self.cap * groups // SUB
        self.outer = groups // INNER

    def group_at(self, group, step):
        chip, core = group // INNER, group % INNER
        if isinstance(group, int):
            return away(chip, step // INNER, self.outer) * INNER + (core ^ (step % INNER))
        return away_traced(chip, step // INNER, self.outer) * INNER + jnp.bitwise_xor(
            core, step % INNER
        )

    def group_from(self, step):
        chips = step // INNER
        if self.outer & (self.outer - 1):
            chips = (self.outer - chips) % self.outer
        return chips * INNER + step % INNER

    def fits(self):
        return (
            self.slots % 2 == 0
            and (self.rest == 0 or SUB % self.rest == 0)
            and self.D % (self.cuts * LANES) == 0
            and self.F % (self.cuts * LANES) == 0
            and self.D % (self.groups * LANES) == 0
            and self.groups % INNER == 0
            and (self.cap * self.groups) % SUB == 0
            and self.rows % SUB == 0
            and (self.half * self.rest) % SUB == 0
            and self.tokens % LANES == 0
        )


def away(place, step, count):
    if count & (count - 1) == 0:
        return place ^ step
    return (place + step) % count


def away_traced(place, step, count):
    if count & (count - 1) == 0:
        return jnp.bitwise_xor(place, step)
    return lax.rem(place + step, count)


def steps_between(first, second, count):
    if count & (count - 1) == 0:
        return jnp.bitwise_xor(first, second)
    return lax.rem(first - second + count, count)


def iota(shape, dim):
    return lax.broadcasted_iota(jnp.int32, shape, dim)


def dot(a, b):
    return jnp.dot(a, b, preferred_element_type=F32)


def dot_nt(a, b):
    return lax.dot_general(a, b, (((1,), (1,)), ((), ())), preferred_element_type=F32)


def dot_tn(a, b):
    return lax.dot_general(a, b, (((0,), (0,)), ((), ())), preferred_element_type=F32)


def picker(plan, cut):
    shape = (plan.half * plan.rest, plan.half * SUB)
    row, col = iota(shape, 0), iota(shape, 1)
    wanted = (row // plan.rest) * SUB + cut * plan.rest + row % plan.rest
    return (wanted == col).astype(BF16)


def unfold(plan, blocks, width):
    parts = [
        jnp.concatenate([b[:, i * width : (i + 1) * width] for b in blocks], axis=0)
        for i in range(plan.full)
    ]
    if plan.rest:
        piece = width // plan.cuts
        tail = jnp.concatenate([b[:, plan.full * width :] for b in blocks], axis=0).astype(BF16)
        parts.append(
            jnp.concatenate([dot(picker(plan, q), tail) for q in range(plan.cuts)], axis=1)
        )
    return jnp.concatenate(parts, axis=0).astype(BF16)


def fold(plan, rows):
    width = rows.shape[1]
    block = plan.half * SUB
    parts = [rows[i * block : (i + 1) * block] for i in range(plan.full)]
    if plan.rest:
        piece = width // plan.cuts
        tail = rows[plan.full * block :].astype(BF16)
        total = None
        for q in range(plan.cuts):
            term = dot_tn(picker(plan, q), tail[:, q * piece : (q + 1) * piece])
            total = term if total is None else total + term
        parts.append(total)
    return jnp.concatenate(parts, axis=1)


def is_hot(plan, placement_ref):
    me = lax.axis_index("expert")
    partner = lax.rem(me + plan.half, plan.slots)
    return placement_ref[me] == placement_ref[partner]


def token_places(plan, slot):
    me = lax.axis_index("expert")
    my_half = me // plan.half
    my_place = lax.rem(me, plan.half)
    upper = (slot >= plan.half).astype(jnp.int32)
    place = slot - plan.half * upper
    far = jnp.where(upper == my_half, 0, 1)
    step = steps_between(place, jnp.zeros_like(place) + my_place, plan.half)
    block = 2 * step + far
    count = plan.tokens
    onehot = (iota((2 * plan.half, count), 0) == block).astype(F32)
    upto = (iota((count, count), 0) <= iota((count, count), 1)).astype(BF16)
    seen = dot(onehot.astype(BF16), upto)
    rank = jnp.sum(onehot * (seen - 1.0), axis=0, keepdims=True).astype(jnp.int32)
    return block, rank


def row_targets(plan, block, rank):
    targets = []
    for i in range(plan.full):
        inside = (rank >= i * SUB) & (rank < (i + 1) * SUB)
        targets.append(jnp.where(inside, block * SUB + rank - i * SUB, -1))
    for q in range(plan.cuts if plan.rest else 0):
        inside = rank >= plan.full * SUB
        targets.append(
            jnp.where(inside, block * SUB + q * plan.rest + rank - plan.full * SUB, -1)
        )
    return targets


def to_column(row):
    n = row.shape[1]
    eye = (iota((n, n), 0) == iota((n, n), 1)).astype(F32)
    return jnp.sum(eye * row.astype(F32), axis=1, keepdims=True)


def pack_kernel(plan, slot_hbm, gate_hbm, tok_hbm, cot_hbm, *refs):
    half = plan.half
    near, far = refs[:half], refs[half : 2 * half]
    slot_ref, gate_ref, tok_ref, cot_ref, sems = refs[2 * half :]
    copies = [
        pltpu.make_async_copy(source, held, sems.at[i])
        for i, (source, held) in enumerate(
            ((slot_hbm, slot_ref), (tok_hbm, tok_ref), (gate_hbm, gate_ref), (cot_hbm, cot_ref))
        )
    ]
    for copy in copies:
        copy.start()
    copies[0].wait()
    block, rank = token_places(plan, slot_ref[...])
    targets = row_targets(plan, block, rank)
    height = 2 * half * SUB
    onehots = [(iota((height, plan.tokens), 0) == t).astype(BF16) for t in targets]

    def store(values, start):
        stop = start + values.shape[1]
        for m in range(half):
            low = 2 * m * SUB
            near[m][:, start:stop] = values[low : low + 2 * SUB].astype(BF16)
            far[m][:, start:stop] = values[low + SUB : low + 2 * SUB].astype(BF16)

    def place(data, base):
        width = data.shape[1]
        for i in range(plan.full):
            store(dot(onehots[i], data), base + i * width)
        if plan.rest:
            piece = width // plan.cuts
            total = None
            for q in range(plan.cuts):
                term = dot(onehots[plan.full + q], data[:, q * piece : (q + 1) * piece])
                total = term if total is None else total + term
            store(total, base + plan.full * width)

    copies[1].wait()
    place(tok_ref[...], 0)
    copies[2].wait()
    copies[3].wait()
    scaled = (to_column(gate_ref[...]) * cot_ref[...].astype(F32)).astype(BF16)
    place(scaled, plan.DX)


def hold_kernel(plan, weight_hbm, held, mine, sems):
    start = pl.multiple_of(lax.axis_index("dp") * plan.share, LANES)
    copies = [
        pltpu.make_async_copy(weight_hbm.at[0], held, sems.at[0]),
        pltpu.make_async_copy(weight_hbm.at[0, pl.ds(start, plan.share), :], mine, sems.at[1]),
    ]
    for copy in copies:
        copy.start()
    for copy in copies:
        copy.wait()


def blocks_of(refs, start, stop, low=0):
    return [r[:, start:stop].astype(F32)[low : low + SUB] for r in refs]


def columns_kernel(plan, *refs):
    near, outs, held = refs[: plan.half], refs[-plan.groups - 1 : -1], refs[-1]
    held[...] = unfold(plan, blocks_of(near, 0, plan.DX), plan.D)
    for m in range(plan.groups):
        start = pl.multiple_of(plan.group_at(lax.axis_index("dp"), m) * plan.share, LANES)
        outs[m][...] = held[:, pl.ds(start, plan.share)]


def activate(preact, scaled):
    sigma = jax.nn.sigmoid(preact)
    act = (preact * sigma).astype(BF16)
    grad_pre = (scaled.astype(F32) * sigma * (1.0 + preact * (1.0 - sigma))).astype(BF16)
    return act, grad_pre


def chip_columns(plan, rows, outs):
    width = INNER * plan.share
    chip = lax.axis_index("dp") // INNER
    for o in range(plan.outer):
        start = pl.multiple_of(away_traced(chip, o, plan.outer) * width, LANES)
        outs[o][:, :width] = rows[:, pl.ds(start, width)]


def near_kernel(plan, placement_ref, weight_ref, *refs):
    near = refs[: plan.half]
    back_near, local, folded_grad, grads, far_rows = refs[-5:]
    x_near = unfold(plan, blocks_of(near, 0, plan.DX), plan.D)
    x_far = unfold(plan, blocks_of(near, 0, plan.DX, SUB), plan.D)
    g_near = unfold(plan, blocks_of(near, plan.DX, plan.C), plan.F)
    g_far = unfold(plan, blocks_of(near, plan.DX, plan.C, SUB), plan.F)
    far_rows[...] = x_far
    x = jnp.concatenate([x_near.astype(F32), x_far.astype(F32)], axis=0).astype(BF16)
    g = jnp.concatenate([g_near.astype(F32), g_far.astype(F32)], axis=0).astype(BF16)
    act, grad_pre = activate(dot(x, weight_ref[...]), g)
    back = dot_nt(grad_pre, weight_ref[...])
    act, grad32 = act.astype(F32), grad_pre.astype(F32)
    back_near[:, : plan.DX] = fold(plan, back[: plan.rows]).astype(BF16)
    back_near[:, plan.DX :] = fold(plan, act[: plan.rows]).astype(BF16)
    local[:, : plan.DX] = fold(plan, back[plan.rows :]).astype(BF16)
    local[:, plan.DX :] = fold(plan, act[plan.rows :]).astype(BF16)
    grad_near = grad32[: plan.rows]
    grad_far = jnp.where(is_hot(plan, placement_ref), grad32[plan.rows :], 0.0)
    folded_grad[...] = fold(plan, grad_near).astype(BF16)
    grads[:, : plan.F] = grad_near.astype(BF16)
    grads[:, plan.F :] = grad_far.astype(BF16)


def payload_kernel(
    plan, placement_ref, weight_ref, folded_grad, near_grads, far_rows, *refs
):
    half, groups = plan.half, plan.groups
    far, refs = [refs[plan.far_order.index(m)] for m in range(half)], refs[half:]
    columns, refs = refs[:groups], refs[groups:]
    payload, refs = refs[0], refs[1:]
    shared, rows = refs[:groups], refs[groups]
    hot = is_hot(plan, placement_ref)
    x = unfold(plan, blocks_of(far, 0, plan.DX), plan.D)
    g = unfold(plan, blocks_of(far, plan.DX, plan.C), plan.F)
    rows[...] = x
    act, grad_pre = activate(dot(x, weight_ref[...]), g)

    @pl.when(jnp.logical_not(hot))
    def _():
        payload[:, : plan.DX] = fold(plan, dot_nt(grad_pre, weight_ref[...])).astype(BF16)
        payload[:, plan.DX :] = fold(plan, act.astype(F32)).astype(BF16)

    @pl.when(hot)
    def _():
        together = jnp.concatenate([c[...].astype(F32) for c in columns], axis=0)
        block = half * SUB
        for i in range(plan.pieces):
            payload[:, i * plan.share : (i + 1) * plan.share] = together[
                i * block : (i + 1) * block
            ].astype(BF16)
        payload[:, plan.DX :] = folded_grad[...]

    group = lax.axis_index("dp")
    width = plan.share
    for m in range(groups):
        start = pl.multiple_of(plan.group_at(group, m) * width, LANES)
        shared[m][:, :width] = far_rows[:, pl.ds(start, width)]
        shared[m][:, width : 2 * width] = rows[:, pl.ds(start, width)]
        shared[m][:, 2 * width : 2 * width + 2 * plan.F] = near_grads[...]
        shared[m][:, 2 * width + 2 * plan.F :] = grad_pre


def pass_kernel(plan, source, before, target):
    target[...] = source[...]


def early_kernel(plan, near_back, *refs):
    back = near_back[...].astype(F32)
    for m, out in enumerate(refs[-plan.half :]):
        out[...] = back[m * SUB : (m + 1) * SUB].astype(BF16)


def after_kernel(plan, placement_ref, payload, local, *refs):
    outs = refs[-plan.half - 1 :]
    hot = is_hot(plan, placement_ref)
    got = payload[...].astype(F32)
    chosen = jnp.where(hot, local[...].astype(F32), got)
    for m in range(plan.half):
        outs[m][...] = chosen[m * SUB : (m + 1) * SUB].astype(BF16)
    blocks = [got[m * SUB : (m + 1) * SUB, plan.DX :] for m in range(plan.half)]
    outs[plan.half][...] = jnp.where(hot, unfold(plan, blocks, plan.F).astype(F32), 0.0).astype(BF16)


def picks_kernel(plan, slot_ref, gate_ref, before, near, far, gate):
    block, rank = token_places(plan, slot_ref[...])
    width = plan.half * SUB
    for side, out in enumerate((near, far)):
        place = jnp.where(lax.rem(block, 2) == side, block // 2, -2)
        picks = []
        for target in row_targets(plan, place, rank):
            column = to_column(target).astype(jnp.int32)
            picks.append((iota((plan.tokens, width), 1) == column).astype(BF16))
        for q in range(plan.cuts):
            out[q] = jnp.concatenate(picks[: plan.full] + picks[plan.full + q :][:1], axis=1)
    gate[...] = to_column(gate_ref[...])


def unpack_kernel(plan, picks_ref, gate_ref, *refs):
    half = plan.half
    got, refs = refs[:half], refs[half:]
    before, refs = (refs[:-4], refs[-4:])
    out_ref, grad_ref, held, sems = refs
    copies = [
        pltpu.make_async_copy(source, held.at[i], sems.at[i]) for i, source in enumerate(got)
    ]
    for copy in copies:
        copy.start()
    for copy in copies:
        copy.wait()

    def gather(base, size, scale, placed, out):
        rows = [held[i, :, base : base + size * plan.cap // SUB].astype(F32) for i in range(half)]
        rows = jnp.concatenate(rows, axis=0).astype(BF16)
        piece = size // plan.cuts
        for q in range(plan.cuts):
            span = slice(q * piece, (q + 1) * piece)
            parts = []
            for i in range(plan.full):
                parts.append(rows[:, i * size + q * piece : i * size + (q + 1) * piece])
            if plan.rest:
                parts.append(rows[:, plan.full * size :])
            value = dot(picks_ref[q], jnp.concatenate(parts, axis=0))
            if scale is not None:
                value = scale * value
            if placed:
                value = value + placed[0][:, span].astype(F32)
            out[:, span] = value.astype(BF16)

    gather(0, plan.D, None, before[1:], grad_ref)
    gather(plan.DX, plan.F, gate_ref[...], before[:1], out_ref)


def rows_of(parts):
    return jnp.concatenate([p.astype(F32) for p in parts], axis=0).astype(BF16)


def gather_kernel(plan, momentum_hbm, *refs):
    groups, share, width = plan.groups, plan.share, plan.F
    columns, refs = refs[:groups], refs[groups:]
    shared, refs = refs[:groups], refs[groups:]
    total, x_all, momentum, sem = refs
    copy = pltpu.make_async_copy(momentum_hbm.at[0], momentum, sem)
    copy.start()
    base = 2 * share
    x_parts, g_parts = [], []
    for m in range(groups):
        x_parts.append(columns[m][...])
        x_parts += [shared[m][:, i * share : (i + 1) * share] for i in range(2)]
        g_parts += [shared[m][:, base + i * width : base + (i + 1) * width] for i in range(3)]
    x_all[...] = rows_of(x_parts)
    g_all = rows_of(g_parts)
    copy.wait()
    for i in range(share // LANES):
        span = slice(i * LANES, (i + 1) * LANES)
        before = decay_rate * momentum[span, :].astype(F32)
        total[span, :] = before + dot_tn(x_all[:, span], g_all)


def update_kernel(plan, placement_ref, total, old_weight, payload_hbm, *refs):
    groups, share = plan.groups, plan.share
    other_hbm, refs = refs[:groups], refs[groups:]
    new_weight, new_momentum, payload, other_g, weight, momentum, sems, out_sems = refs
    copies = [pltpu.make_async_copy(payload_hbm, payload, sems.at[groups])]
    for m in range(groups):
        copies.append(pltpu.make_async_copy(other_hbm[m], other_g.at[m], sems.at[m]))
    for copy in copies:
        copy.start()
    hot = is_hot(plan, placement_ref)
    for copy in copies:
        copy.wait()
    pieces = [payload[:, i * share : (i + 1) * share] for i in range(plan.pieces)]
    x = jnp.concatenate(pieces, axis=0)
    x = jnp.where(hot, x.astype(F32), 0.0).astype(BF16)
    g = rows_of([other_g[m] for m in range(groups)])
    done = []
    for i in range(share // LANES):
        span = pl.ds(i * LANES, LANES)
        value = total[span, :] + dot_tn(x[:, i * LANES : (i + 1) * LANES], g)
        value = value.astype(BF16)
        momentum[span, :] = value
        weight[span, :] = (
            old_weight[span, :].astype(F32) - learning_rate * value.astype(F32)
        ).astype(BF16)
        for j, (source, target) in enumerate(((momentum, new_momentum), (weight, new_weight))):
            copy = pltpu.make_async_copy(
                source.at[span, :], target.at[0, span, :], out_sems.at[i, j]
            )
            copy.start()
            done.append(copy)
    for copy in done:
        copy.wait()


MIB = 1024 * 1024
SMEM_SPEC = pl.BlockSpec(memory_space=pltpu.SMEM)
ANY_SPEC = pl.BlockSpec(memory_space=pl.ANY)
VMEM_SPEC = pl.BlockSpec(memory_space=pltpu.VMEM)


def call(kernel, plan, ins, specs, outs, scratch, flops, name, limit=16, dtypes=None):
    moved = sum(a.size * a.dtype.itemsize for a in ins) + sum(2 * math.prod(o) for o in outs)
    return pl.pallas_call(
        functools.partial(kernel, plan),
        out_shape=[
            jax.ShapeDtypeStruct(s, dtypes[i] if dtypes else BF16) for i, s in enumerate(outs)
        ],
        in_specs=specs,
        out_specs=[VMEM_SPEC] * len(outs),
        scratch_shapes=scratch,
        compiler_params=pltpu.CompilerParams(vmem_limit_bytes=limit * MIB),
        cost_estimate=pl.CostEstimate(
            flops=flops, bytes_accessed=moved if flops else 0, transcendentals=0
        ),
        name=name,
    )(*ins)


def routed(plan, tokens, route_weight, cotangent, slot_ids, placement, weight, momentum):
    half, groups, outer = plan.half, plan.groups, plan.outer
    D, F, C, rows, share = plan.D, plan.F, plan.C, plan.rows, plan.share
    slot = slot_ids.reshape(1, -1)
    gate = route_weight.reshape(1, -1)

    def to_slot(data, m, flip=0):
        pairs = []
        for e in range(plan.slots):
            h, k = divmod(e, half)
            pairs.append((e, (h ^ flip) * half + away(k, m, half)))
        return lax.ppermute(data, "expert", pairs)

    def to_source(data, m):
        pairs = []
        for e in range(plan.slots):
            h, k = divmod(e, half)
            pairs.append((h * half + away(k, m, half), e))
        return lax.ppermute(data, "expert", pairs)

    def to_partner(data):
        pairs = [(e, (e + half) % plan.slots) for e in range(plan.slots)]
        return lax.ppermute(data, "expert", pairs)

    def from_group(data, m):
        pairs = []
        for d in range(groups):
            pairs.append((plan.group_at(d, m), d))
        return lax.ppermute(data, "dp", pairs)

    def from_chips(per_chip):
        return [per_chip[0]] + [
            from_group(per_chip[plan.group_from(INNER * o) // INNER], INNER * o)
            for o in range(1, outer)
        ]

    def with_sisters(got):
        return [data for own in got for data in (own, from_group(own, 1))]

    def from_groups(per_group):
        return [per_group[0]] + [
            from_group(per_group[plan.group_from(m)], m) for m in range(1, groups)
        ]

    packed = call(
        pack_kernel,
        plan,
        [slot, gate, tokens, cotangent],
        [ANY_SPEC] * 4,
        [(2 * SUB, C)] * half + [(SUB, C)] * half,
        [
            pltpu.VMEM(slot.shape, slot.dtype),
            pltpu.VMEM(gate.shape, gate.dtype),
            pltpu.VMEM(tokens.shape, tokens.dtype),
            pltpu.VMEM(cotangent.shape, cotangent.dtype),
            pltpu.SemaphoreType.DMA((4,)),
        ],
        2 * 4 * half * SUB * plan.tokens * (D + F),
        "pack",
        limit=60,
    )
    near = [packed[0]] + [to_slot(packed[m], m) for m in range(1, half)]
    far = [to_slot(packed[half + m], m, 1) for m in range(half)]
    held, old_weight = call(
        hold_kernel,
        plan,
        [weight],
        [ANY_SPEC],
        [(D, F), (share, F)],
        [pltpu.SemaphoreType.DMA((2,))],
        0,
        "hold",
        limit=40,
    )
    columns = call(
        columns_kernel,
        plan,
        near,
        [VMEM_SPEC] * half,
        [(rows, share)] * groups,
        [pltpu.VMEM((rows, D), BF16)],
        0,
        "near_columns",
    )
    columns_here = from_groups(columns)
    back_near, local, folded_grad, grads, far_rows = call(
        near_kernel,
        plan,
        [placement, held] + near + [columns[0]],
        [SMEM_SPEC] + [VMEM_SPEC] * (1 + half) + [ANY_SPEC],
        [
            (half * SUB, C),
            (half * SUB, C),
            (half * SUB, plan.FG),
            (rows, 2 * F),
            (rows, D),
        ],
        [],
        8 * rows * D * F,
        "near_rows",
    )
    outs = call(
        payload_kernel,
        plan,
        [placement, held, folded_grad, grads, far_rows]
        + [far[m] for m in plan.far_order]
        + columns_here,
        [SMEM_SPEC] + [VMEM_SPEC] * (4 + half + groups),
        [(half * SUB, C)] + [(rows, 2 * share + 3 * F)] * groups,
        [pltpu.VMEM((rows, D), BF16)],
        4 * rows * D * F,
        "payload",
    )
    payload = to_partner(outs[0])
    shared = from_groups(outs[1:])
    depth = half * SUB * (plan.full + (1 if plan.rest else 0))
    near_picks, far_picks, gates = call(
        picks_kernel,
        plan,
        [slot, gate, shared[1]],
        [VMEM_SPEC] * 2 + [ANY_SPEC],
        [(plan.cuts, plan.tokens, depth)] * 2 + [(plan.tokens, 1)],
        [],
        0,
        "picks",
        limit=4,
        dtypes=[BF16, BF16, F32],
    )
    outs = call(
        early_kernel,
        plan,
        [back_near, gates],
        [VMEM_SPEC, ANY_SPEC],
        [(SUB, C)] * half,
        [],
        0,
        "early",
        limit=4,
    )
    early = [outs[0]] + [to_source(outs[m], m) for m in range(1, half - 1)]
    (last,) = call(
        pass_kernel,
        plan,
        [outs[half - 1], early[1]],
        [VMEM_SPEC, ANY_SPEC],
        [(SUB, C)],
        [],
        0,
        "pass_on",
        limit=4,
    )
    early.append(to_source(last, half - 1))
    (total,) = call(
        gather_kernel,
        plan,
        [momentum] + columns_here + shared,
        [ANY_SPEC] + [VMEM_SPEC] * (2 * groups),
        [(share, F)],
        [
            pltpu.VMEM((3 * groups * rows, share), BF16),
            pltpu.VMEM((share, F), BF16),
            pltpu.SemaphoreType.DMA,
        ],
        0,
        "own_terms",
        dtypes=[F32],
    )
    def place(picks, got, placed, name):
        return call(
            unpack_kernel,
            plan,
            [picks, gates] + got + placed,
            [VMEM_SPEC] * (2 + half + len(placed)),
            [(plan.tokens, F), (plan.tokens, D)],
            [pltpu.VMEM((half, SUB, C), BF16), pltpu.SemaphoreType.DMA((half,))],
            0,
            name,
            limit=12,
        )

    placed = list(place(near_picks, early, [], "near_results"))
    outs = call(
        after_kernel,
        plan,
        [placement, payload, local, placed[0]],
        [SMEM_SPEC] + [VMEM_SPEC] * 2 + [ANY_SPEC],
        [(SUB, C)] * half + [(rows, F)],
        [],
        0,
        "after_swap",
        limit=8,
    )
    late = [outs[0]] + [to_source(outs[m], m) for m in range(1, half)]
    other_g = with_sisters(from_chips([outs[half]] * outer))

    new_weight, new_momentum = pl.pallas_call(
        functools.partial(update_kernel, plan),
        out_shape=[jax.ShapeDtypeStruct((1, share, F), BF16)] * 2,
        in_specs=[SMEM_SPEC] + [VMEM_SPEC] * 2 + [ANY_SPEC] * (groups + 1),
        out_specs=[ANY_SPEC] * 2,
        scratch_shapes=[
            pltpu.VMEM((half * SUB, C), BF16),
            pltpu.VMEM((groups, rows, F), BF16),
            pltpu.VMEM((share, F), BF16),
            pltpu.VMEM((share, F), BF16),
            pltpu.SemaphoreType.DMA((groups + 1,)),
            pltpu.SemaphoreType.DMA((share // LANES, 2)),
        ],
        compiler_params=pltpu.CompilerParams(vmem_limit_bytes=20 * MIB),
        cost_estimate=pl.CostEstimate(
            flops=2 * groups * rows * share * F, bytes_accessed=12 * share * F, transcendentals=0
        ),
        name="update",
    )(placement, total, old_weight, payload, *other_g)

    expert_out, token_grad = place(far_picks, late, placed, "far_results")
    return expert_out, token_grad, new_weight, new_momentum


def general(tokens, route_weight, cotangent, slot_ids, placement, weight, momentum):
    n_slots = lax.axis_size("expert")
    n_groups = lax.axis_size("dp")
    tok_count, D = tokens.shape
    F = cotangent.shape[1]
    capacity = tok_count * 9 // 8 // n_slots
    onehot = (slot_ids[:, None] == jnp.arange(n_slots, dtype=jnp.int32)[None, :]).astype(jnp.int32)
    ranks = jnp.sum((jnp.cumsum(onehot, axis=0) - 1) * onehot, axis=1)
    position = slot_ids * capacity + ranks
    send_rows = jnp.zeros((n_slots * capacity, D), BF16).at[position].set(tokens)
    scaled = (route_weight[:, None] * cotangent.astype(F32)).astype(BF16)
    send_grads = jnp.zeros((n_slots * capacity, F), BF16).at[position].set(scaled)
    matrix = weight[0]

    def exchange(rows):
        width = rows.shape[-1]
        return lax.all_to_all(
            rows.reshape(n_slots, capacity, width), "expert", split_axis=0, concat_axis=0, tiled=True
        ).reshape(-1, width)

    flat_x = exchange(send_rows)
    act, flat_grad = activate(dot(flat_x, matrix), exchange(send_grads))
    back = dot_nt(flat_grad, matrix).astype(BF16)
    act_rows = exchange(act)[position]
    expert_out = (route_weight[:, None] * act_rows.astype(F32)).astype(BF16)
    token_grad = exchange(back)[position]
    row_count = flat_x.shape[0]
    share = D // n_groups
    columns = lax.all_to_all(
        flat_x.reshape(1, row_count, n_groups, share), "dp", split_axis=2, concat_axis=0, tiled=True
    )
    columns = columns.reshape(n_groups, row_count, share)
    terms = jnp.einsum(
        "krd,krf->kdf",
        columns,
        lax.all_gather(flat_grad[None], "dp", axis=0, tiled=True),
        preferred_element_type=F32,
    )
    terms = lax.optimization_barrier(terms.astype(BF16)).astype(F32)
    reduced = jnp.sum(terms, axis=0).astype(BF16)
    half = n_slots // 2
    partner_grad = lax.ppermute(
        reduced, "expert", [(i, (i + half) % n_slots) for i in range(n_slots)]
    ).astype(F32)
    my_slot = lax.axis_index("expert")
    partner_slot = (my_slot + half) % n_slots
    same = placement[my_slot] == placement[partner_slot]
    total = reduced.astype(F32) + jnp.where(same, partner_grad, 0.0)
    new_momentum = (decay_rate * momentum[0].astype(F32) + total).astype(BF16)
    old = lax.dynamic_slice_in_dim(matrix, lax.axis_index("dp") * share, share, 0).astype(F32)
    new_weight = (old - learning_rate * new_momentum.astype(F32)).astype(BF16)
    return expert_out, token_grad, new_weight[None], new_momentum[None]


def solution(mesh):
    def shards(tokens, route_weight, cotangent, slot_ids, placement, weight, momentum):
        plan = Plan(
            mesh.shape["expert"],
            mesh.shape["dp"],
            tokens.shape[0],
            tokens.shape[1],
            cotangent.shape[1],
        )
        body = functools.partial(routed, plan) if plan.fits() else general
        return body(tokens, route_weight, cotangent, slot_ids, placement, weight, momentum)

    return jax.shard_map(
        shards,
        mesh=mesh,
        in_specs=(
            P(("dp", "expert"), None),
            P(("dp", "expert")),
            P(("dp", "expert"), None),
            P(("dp", "expert")),
            P(),
            P("expert", None, None),
            P("expert", "dp", None),
        ),
        out_specs=(
            P(("dp", "expert"), None),
            P(("dp", "expert"), None),
            P("expert", "dp", None),
            P("expert", "dp", None),
        ),
        check_vma=False,
    )
```

```python
import functools
import math

import jax
import jax.numpy as jnp
from jax import lax
from jax.experimental import pallas as pl
from jax.experimental.pallas import tpu as pltpu
from jax.sharding import PartitionSpec as P

learning_rate = 0.004
decay_rate = 0.9

BF16 = jnp.bfloat16
F32 = jnp.float32
SUB = 8
LANES = 128
INNER = 2


class Plan:
    def __init__(self, slots, groups, tokens, features, hidden):
        self.slots, self.groups, self.tokens = slots, groups, tokens
        self.D, self.F = features, hidden
        self.half = slots // 2
        self.cap = tokens * 9 // 8 // slots
        self.full, self.rest = divmod(self.cap, SUB)
        self.cuts = SUB // self.rest if self.rest else 1
        self.rows = self.half * self.cap
        self.back_order = [*range(0, self.half, 2), *range(1, self.half, 2)]
        self.far_order = [*range(0, self.half, 2), *range(1, self.half, 2)]
        self.share = features // groups
        self.DX = features * self.cap // SUB
        self.FG = hidden * self.cap // SUB
        self.C = self.DX + self.FG
        self.pieces = self.cap * groups // SUB
        self.outer = groups // INNER

    def group_at(self, group, step):
        chip, core = group // INNER, group % INNER
        if isinstance(group, int):
            return away(chip, step // INNER, self.outer) * INNER + (core ^ (step % INNER))
        return away_traced(chip, step // INNER, self.outer) * INNER + jnp.bitwise_xor(
            core, step % INNER
        )

    def group_from(self, step):
        chips = step // INNER
        if self.outer & (self.outer - 1):
            chips = (self.outer - chips) % self.outer
        return chips * INNER + step % INNER

    def fits(self):
        return (
            self.slots % 2 == 0
            and (self.rest == 0 or SUB % self.rest == 0)
            and self.D % (self.cuts * LANES) == 0
            and self.F % (self.cuts * LANES) == 0
            and self.D % (self.groups * LANES) == 0
            and self.groups % INNER == 0
            and (self.cap * self.groups) % SUB == 0
            and self.rows % SUB == 0
            and (self.half * self.rest) % SUB == 0
            and self.tokens % LANES == 0
        )


def away(place, step, count):
    if count & (count - 1) == 0:
        return place ^ step
    return (place + step) % count


def away_traced(place, step, count):
    if count & (count - 1) == 0:
        return jnp.bitwise_xor(place, step)
    return lax.rem(place + step, count)


def steps_between(first, second, count):
    if count & (count - 1) == 0:
        return jnp.bitwise_xor(first, second)
    return lax.rem(first - second + count, count)


def iota(shape, dim):
    return lax.broadcasted_iota(jnp.int32, shape, dim)


def dot(a, b):
    return jnp.dot(a, b, preferred_element_type=F32)


def dot_nt(a, b):
    return lax.dot_general(a, b, (((1,), (1,)), ((), ())), preferred_element_type=F32)


def dot_tn(a, b):
    return lax.dot_general(a, b, (((0,), (0,)), ((), ())), preferred_element_type=F32)


def picker(plan, cut):
    shape = (plan.half * plan.rest, plan.half * SUB)
    row, col = iota(shape, 0), iota(shape, 1)
    wanted = (row // plan.rest) * SUB + cut * plan.rest + row % plan.rest
    return (wanted == col).astype(BF16)


def unfold(plan, blocks, width):
    parts = [
        jnp.concatenate([b[:, i * width : (i + 1) * width] for b in blocks], axis=0)
        for i in range(plan.full)
    ]
    if plan.rest:
        piece = width // plan.cuts
        tail = jnp.concatenate([b[:, plan.full * width :] for b in blocks], axis=0).astype(BF16)
        parts.append(
            jnp.concatenate([dot(picker(plan, q), tail) for q in range(plan.cuts)], axis=1)
        )
    return jnp.concatenate(parts, axis=0).astype(BF16)


def fold(plan, rows):
    width = rows.shape[1]
    block = plan.half * SUB
    parts = [rows[i * block : (i + 1) * block] for i in range(plan.full)]
    if plan.rest:
        piece = width // plan.cuts
        tail = rows[plan.full * block :].astype(BF16)
        total = None
        for q in range(plan.cuts):
            term = dot_tn(picker(plan, q), tail[:, q * piece : (q + 1) * piece])
            total = term if total is None else total + term
        parts.append(total)
    return jnp.concatenate(parts, axis=1)


def is_hot(plan, placement_ref):
    me = lax.axis_index("expert")
    partner = lax.rem(me + plan.half, plan.slots)
    return placement_ref[me] == placement_ref[partner]


def token_places(plan, slot):
    me = lax.axis_index("expert")
    my_half = me // plan.half
    my_place = lax.rem(me, plan.half)
    upper = (slot >= plan.half).astype(jnp.int32)
    place = slot - plan.half * upper
    far = jnp.where(upper == my_half, 0, 1)
    step = steps_between(place, jnp.zeros_like(place) + my_place, plan.half)
    block = 2 * step + far
    count = plan.tokens
    onehot = (iota((2 * plan.half, count), 0) == block).astype(F32)
    upto = (iota((count, count), 0) <= iota((count, count), 1)).astype(BF16)
    seen = dot(onehot.astype(BF16), upto)
    rank = jnp.sum(onehot * (seen - 1.0), axis=0, keepdims=True).astype(jnp.int32)
    return block, rank


def row_targets(plan, block, rank):
    targets = []
    for i in range(plan.full):
        inside = (rank >= i * SUB) & (rank < (i + 1) * SUB)
        targets.append(jnp.where(inside, block * SUB + rank - i * SUB, -1))
    for q in range(plan.cuts if plan.rest else 0):
        inside = rank >= plan.full * SUB
        targets.append(
            jnp.where(inside, block * SUB + q * plan.rest + rank - plan.full * SUB, -1)
        )
    return targets


def to_column(row):
    n = row.shape[1]
    eye = (iota((n, n), 0) == iota((n, n), 1)).astype(F32)
    return jnp.sum(eye * row.astype(F32), axis=1, keepdims=True)


def pack_kernel(plan, slot_hbm, gate_hbm, tok_hbm, cot_hbm, *refs):
    half = plan.half
    near, far = refs[:half], refs[half : 2 * half]
    slot_ref, gate_ref, tok_ref, cot_ref, sems = refs[2 * half :]
    copies = [
        pltpu.make_async_copy(source, held, sems.at[i])
        for i, (source, held) in enumerate(
            ((slot_hbm, slot_ref), (tok_hbm, tok_ref), (gate_hbm, gate_ref), (cot_hbm, cot_ref))
        )
    ]
    for copy in copies:
        copy.start()
    copies[0].wait()
    block, rank = token_places(plan, slot_ref[...])
    targets = row_targets(plan, block, rank)
    height = 2 * half * SUB
    onehots = [(iota((height, plan.tokens), 0) == t).astype(BF16) for t in targets]

    def store(values, start):
        stop = start + values.shape[1]
        for m in range(half):
            low = 2 * m * SUB
            near[m][:, start:stop] = values[low : low + 2 * SUB].astype(BF16)
            far[m][:, start:stop] = values[low + SUB : low + 2 * SUB].astype(BF16)

    def place(data, base):
        width = data.shape[1]
        for i in range(plan.full):
            store(dot(onehots[i], data), base + i * width)
        if plan.rest:
            piece = width // plan.cuts
            total = None
            for q in range(plan.cuts):
                term = dot(onehots[plan.full + q], data[:, q * piece : (q + 1) * piece])
                total = term if total is None else total + term
            store(total, base + plan.full * width)

    copies[1].wait()
    place(tok_ref[...], 0)
    copies[2].wait()
    copies[3].wait()
    scaled = (to_column(gate_ref[...]) * cot_ref[...].astype(F32)).astype(BF16)
    place(scaled, plan.DX)


def hold_kernel(plan, weight_hbm, held, mine, sems):
    start = pl.multiple_of(lax.axis_index("dp") * plan.share, LANES)
    copies = [
        pltpu.make_async_copy(weight_hbm.at[0], held, sems.at[0]),
        pltpu.make_async_copy(weight_hbm.at[0, pl.ds(start, plan.share), :], mine, sems.at[1]),
    ]
    for copy in copies:
        copy.start()
    for copy in copies:
        copy.wait()


def blocks_of(refs, start, stop, low=0):
    return [r[:, start:stop].astype(F32)[low : low + SUB] for r in refs]


def columns_kernel(plan, *refs):
    near, outs, held = refs[: plan.half], refs[-plan.groups - 1 : -1], refs[-1]
    held[...] = unfold(plan, blocks_of(near, 0, plan.DX), plan.D)
    for m in range(plan.groups):
        start = pl.multiple_of(plan.group_at(lax.axis_index("dp"), m) * plan.share, LANES)
        outs[m][...] = held[:, pl.ds(start, plan.share)]


def activate(preact, scaled):
    sigma = jax.nn.sigmoid(preact)
    act = (preact * sigma).astype(BF16)
    grad_pre = (scaled.astype(F32) * sigma * (1.0 + preact * (1.0 - sigma))).astype(BF16)
    return act, grad_pre


def chip_columns(plan, rows, outs):
    width = INNER * plan.share
    chip = lax.axis_index("dp") // INNER
    for o in range(plan.outer):
        start = pl.multiple_of(away_traced(chip, o, plan.outer) * width, LANES)
        outs[o][:, :width] = rows[:, pl.ds(start, width)]


def near_kernel(plan, placement_ref, weight_ref, *refs):
    near = refs[: plan.half]
    back_near, local, folded_grad, grads, far_rows = refs[-5:]
    x_near = unfold(plan, blocks_of(near, 0, plan.DX), plan.D)
    x_far = unfold(plan, blocks_of(near, 0, plan.DX, SUB), plan.D)
    g_near = unfold(plan, blocks_of(near, plan.DX, plan.C), plan.F)
    g_far = unfold(plan, blocks_of(near, plan.DX, plan.C, SUB), plan.F)
    far_rows[...] = x_far
    x = jnp.concatenate([x_near.astype(F32), x_far.astype(F32)], axis=0).astype(BF16)
    g = jnp.concatenate([g_near.astype(F32), g_far.astype(F32)], axis=0).astype(BF16)
    act, grad_pre = activate(dot(x, weight_ref[...]), g)
    back = dot_nt(grad_pre, weight_ref[...])
    act, grad32 = act.astype(F32), grad_pre.astype(F32)
    back_near[:, : plan.DX] = fold(plan, back[: plan.rows]).astype(BF16)
    back_near[:, plan.DX :] = fold(plan, act[: plan.rows]).astype(BF16)
    local[:, : plan.DX] = fold(plan, back[plan.rows :]).astype(BF16)
    local[:, plan.DX :] = fold(plan, act[plan.rows :]).astype(BF16)
    grad_near = grad32[: plan.rows]
    grad_far = jnp.where(is_hot(plan, placement_ref), grad32[plan.rows :], 0.0)
    folded_grad[...] = fold(plan, grad_near).astype(BF16)
    grads[:, : plan.F] = grad_near.astype(BF16)
    grads[:, plan.F :] = grad_far.astype(BF16)


def payload_kernel(
    plan, placement_ref, weight_ref, folded_grad, near_grads, far_rows, *refs
):
    half, groups = plan.half, plan.groups
    far, refs = [refs[plan.far_order.index(m)] for m in range(half)], refs[half:]
    columns, refs = refs[:groups], refs[groups:]
    payload, refs = refs[0], refs[1:]
    shared, rows = refs[:groups], refs[groups]
    hot = is_hot(plan, placement_ref)
    x = unfold(plan, blocks_of(far, 0, plan.DX), plan.D)
    g = unfold(plan, blocks_of(far, plan.DX, plan.C), plan.F)
    rows[...] = x
    act, grad_pre = activate(dot(x, weight_ref[...]), g)

    @pl.when(jnp.logical_not(hot))
    def _():
        payload[:, : plan.DX] = fold(plan, dot_nt(grad_pre, weight_ref[...])).astype(BF16)
        payload[:, plan.DX :] = fold(plan, act.astype(F32)).astype(BF16)

    @pl.when(hot)
    def _():
        together = jnp.concatenate([c[...].astype(F32) for c in columns], axis=0)
        block = half * SUB
        for i in range(plan.pieces):
            payload[:, i * plan.share : (i + 1) * plan.share] = together[
                i * block : (i + 1) * block
            ].astype(BF16)
        payload[:, plan.DX :] = folded_grad[...]

    group = lax.axis_index("dp")
    width = plan.share
    for m in range(groups):
        start = pl.multiple_of(plan.group_at(group, m) * width, LANES)
        shared[m][:, :width] = far_rows[:, pl.ds(start, width)]
        shared[m][:, width : 2 * width] = rows[:, pl.ds(start, width)]
        shared[m][:, 2 * width : 2 * width + 2 * plan.F] = near_grads[...]
        shared[m][:, 2 * width + 2 * plan.F :] = grad_pre


def pass_kernel(plan, source, before, target):
    target[...] = source[...]


def early_kernel(plan, near_back, *refs):
    back = near_back[...].astype(F32)
    for m, out in enumerate(refs[-plan.half :]):
        out[...] = back[m * SUB : (m + 1) * SUB].astype(BF16)


def after_kernel(plan, placement_ref, payload, local, *refs):
    outs = refs[-plan.half - 1 :]
    hot = is_hot(plan, placement_ref)
    got = payload[...].astype(F32)
    chosen = jnp.where(hot, local[...].astype(F32), got)
    for m in range(plan.half):
        outs[m][...] = chosen[m * SUB : (m + 1) * SUB].astype(BF16)
    blocks = [got[m * SUB : (m + 1) * SUB, plan.DX :] for m in range(plan.half)]
    outs[plan.half][...] = jnp.where(hot, unfold(plan, blocks, plan.F).astype(F32), 0.0).astype(BF16)


def picks_kernel(plan, slot_ref, gate_ref, before, near, far, gate):
    block, rank = token_places(plan, slot_ref[...])
    width = plan.half * SUB
    for side, out in enumerate((near, far)):
        place = jnp.where(lax.rem(block, 2) == side, block // 2, -2)
        picks = []
        for target in row_targets(plan, place, rank):
            column = to_column(target).astype(jnp.int32)
            picks.append((iota((plan.tokens, width), 1) == column).astype(BF16))
        for q in range(plan.cuts):
            out[q] = jnp.concatenate(picks[: plan.full] + picks[plan.full + q :][:1], axis=1)
    gate[...] = to_column(gate_ref[...])


def unpack_kernel(plan, picks_ref, gate_ref, *refs):
    half = plan.half
    got, refs = refs[:half], refs[half:]
    before, refs = (refs[:-4], refs[-4:])
    out_ref, grad_ref, held, sems = refs
    copies = [
        pltpu.make_async_copy(source, held.at[m], sems.at[m])
        for m, source in zip(plan.back_order, got)
    ]
    for copy in copies:
        copy.start()
    for copy in copies:
        copy.wait()

    def gather(base, size, scale, placed, out):
        rows = [held[i, :, base : base + size * plan.cap // SUB].astype(F32) for i in range(half)]
        rows = jnp.concatenate(rows, axis=0).astype(BF16)
        piece = size // plan.cuts
        for q in range(plan.cuts):
            span = slice(q * piece, (q + 1) * piece)
            parts = []
            for i in range(plan.full):
                parts.append(rows[:, i * size + q * piece : i * size + (q + 1) * piece])
            if plan.rest:
                parts.append(rows[:, plan.full * size :])
            value = dot(picks_ref[q], jnp.concatenate(parts, axis=0))
            if scale is not None:
                value = scale * value
            if placed:
                value = value + placed[0][:, span].astype(F32)
            out[:, span] = value.astype(BF16)

    gather(0, plan.D, None, before[1:], grad_ref)
    gather(plan.DX, plan.F, gate_ref[...], before[:1], out_ref)


def rows_of(parts):
    return jnp.concatenate([p.astype(F32) for p in parts], axis=0).astype(BF16)


def gather_kernel(plan, momentum_hbm, *refs):
    groups, share, width = plan.groups, plan.share, plan.F
    columns, refs = refs[:groups], refs[groups:]
    shared, refs = refs[:groups], refs[groups:]
    total, x_all, momentum, sem = refs
    copy = pltpu.make_async_copy(momentum_hbm.at[0], momentum, sem)
    copy.start()
    base = 2 * share
    x_parts, g_parts = [], []
    for m in range(groups):
        x_parts.append(columns[m][...])
        x_parts += [shared[m][:, i * share : (i + 1) * share] for i in range(2)]
        g_parts += [shared[m][:, base + i * width : base + (i + 1) * width] for i in range(3)]
    x_all[...] = rows_of(x_parts)
    g_all = rows_of(g_parts)
    copy.wait()
    for i in range(share // LANES):
        span = slice(i * LANES, (i + 1) * LANES)
        before = decay_rate * momentum[span, :].astype(F32)
        total[span, :] = before + dot_tn(x_all[:, span], g_all)


def update_kernel(plan, placement_ref, total, old_weight, payload_hbm, *refs):
    groups, share = plan.groups, plan.share
    other_hbm, refs = refs[:groups], refs[groups:]
    new_weight, new_momentum, payload, other_g, weight, momentum, sems, out_sems = refs
    copies = [pltpu.make_async_copy(payload_hbm, payload, sems.at[groups])]
    for m in range(groups):
        copies.append(pltpu.make_async_copy(other_hbm[m], other_g.at[m], sems.at[m]))
    for copy in copies:
        copy.start()
    hot = is_hot(plan, placement_ref)
    for copy in copies:
        copy.wait()
    pieces = [payload[:, i * share : (i + 1) * share] for i in range(plan.pieces)]
    x = jnp.concatenate(pieces, axis=0)
    x = jnp.where(hot, x.astype(F32), 0.0).astype(BF16)
    g = rows_of([other_g[m] for m in range(groups)])
    done = []
    for i in range(share // LANES):
        span = pl.ds(i * LANES, LANES)
        value = total[span, :] + dot_tn(x[:, i * LANES : (i + 1) * LANES], g)
        value = value.astype(BF16)
        momentum[span, :] = value
        weight[span, :] = (
            old_weight[span, :].astype(F32) - learning_rate * value.astype(F32)
        ).astype(BF16)
        for j, (source, target) in enumerate(((momentum, new_momentum), (weight, new_weight))):
            copy = pltpu.make_async_copy(
                source.at[span, :], target.at[0, span, :], out_sems.at[i, j]
            )
            copy.start()
            done.append(copy)
    for copy in done:
        copy.wait()


MIB = 1024 * 1024
SMEM_SPEC = pl.BlockSpec(memory_space=pltpu.SMEM)
ANY_SPEC = pl.BlockSpec(memory_space=pl.ANY)
VMEM_SPEC = pl.BlockSpec(memory_space=pltpu.VMEM)


def call(kernel, plan, ins, specs, outs, scratch, flops, name, limit=16, dtypes=None):
    moved = sum(a.size * a.dtype.itemsize for a in ins) + sum(2 * math.prod(o) for o in outs)
    return pl.pallas_call(
        functools.partial(kernel, plan),
        out_shape=[
            jax.ShapeDtypeStruct(s, dtypes[i] if dtypes else BF16) for i, s in enumerate(outs)
        ],
        in_specs=specs,
        out_specs=[VMEM_SPEC] * len(outs),
        scratch_shapes=scratch,
        compiler_params=pltpu.CompilerParams(vmem_limit_bytes=limit * MIB),
        cost_estimate=pl.CostEstimate(
            flops=flops, bytes_accessed=moved if flops else 0, transcendentals=0
        ),
        name=name,
    )(*ins)


def routed(plan, tokens, route_weight, cotangent, slot_ids, placement, weight, momentum):
    half, groups, outer = plan.half, plan.groups, plan.outer
    D, F, C, rows, share = plan.D, plan.F, plan.C, plan.rows, plan.share
    slot = slot_ids.reshape(1, -1)
    gate = route_weight.reshape(1, -1)

    def to_slot(data, m, flip=0):
        pairs = []
        for e in range(plan.slots):
            h, k = divmod(e, half)
            pairs.append((e, (h ^ flip) * half + away(k, m, half)))
        return lax.ppermute(data, "expert", pairs)

    def to_source(data, m):
        pairs = []
        for e in range(plan.slots):
            h, k = divmod(e, half)
            pairs.append((h * half + away(k, m, half), e))
        return lax.ppermute(data, "expert", pairs)

    def to_partner(data):
        pairs = [(e, (e + half) % plan.slots) for e in range(plan.slots)]
        return lax.ppermute(data, "expert", pairs)

    def from_group(data, m):
        pairs = []
        for d in range(groups):
            pairs.append((plan.group_at(d, m), d))
        return lax.ppermute(data, "dp", pairs)

    def from_chips(per_chip):
        return [per_chip[0]] + [
            from_group(per_chip[plan.group_from(INNER * o) // INNER], INNER * o)
            for o in range(1, outer)
        ]

    def with_sisters(got):
        return [data for own in got for data in (own, from_group(own, 1))]

    def from_groups(per_group):
        return [per_group[0]] + [
            from_group(per_group[plan.group_from(m)], m) for m in range(1, groups)
        ]

    packed = call(
        pack_kernel,
        plan,
        [slot, gate, tokens, cotangent],
        [ANY_SPEC] * 4,
        [(2 * SUB, C)] * half + [(SUB, C)] * half,
        [
            pltpu.VMEM(slot.shape, slot.dtype),
            pltpu.VMEM(gate.shape, gate.dtype),
            pltpu.VMEM(tokens.shape, tokens.dtype),
            pltpu.VMEM(cotangent.shape, cotangent.dtype),
            pltpu.SemaphoreType.DMA((4,)),
        ],
        2 * 4 * half * SUB * plan.tokens * (D + F),
        "pack",
        limit=60,
    )
    near = [packed[0]] + [to_slot(packed[m], m) for m in range(1, half)]
    far = [to_slot(packed[half + m], m, 1) for m in range(half)]
    held, old_weight = call(
        hold_kernel,
        plan,
        [weight],
        [ANY_SPEC],
        [(D, F), (share, F)],
        [pltpu.SemaphoreType.DMA((2,))],
        0,
        "hold",
        limit=40,
    )
    columns = call(
        columns_kernel,
        plan,
        near,
        [VMEM_SPEC] * half,
        [(rows, share)] * groups,
        [pltpu.VMEM((rows, D), BF16)],
        0,
        "near_columns",
    )
    columns_here = from_groups(columns)
    back_near, local, folded_grad, grads, far_rows = call(
        near_kernel,
        plan,
        [placement, held] + near + [columns[0]],
        [SMEM_SPEC] + [VMEM_SPEC] * (1 + half) + [ANY_SPEC],
        [
            (half * SUB, C),
            (half * SUB, C),
            (half * SUB, plan.FG),
            (rows, 2 * F),
            (rows, D),
        ],
        [],
        8 * rows * D * F,
        "near_rows",
    )
    outs = call(
        payload_kernel,
        plan,
        [placement, held, folded_grad, grads, far_rows]
        + [far[m] for m in plan.far_order]
        + columns_here,
        [SMEM_SPEC] + [VMEM_SPEC] * (4 + half + groups),
        [(half * SUB, C)] + [(rows, 2 * share + 3 * F)] * groups,
        [pltpu.VMEM((rows, D), BF16)],
        4 * rows * D * F,
        "payload",
    )
    payload = to_partner(outs[0])
    shared = from_groups(outs[1:])
    depth = half * SUB * (plan.full + (1 if plan.rest else 0))
    near_picks, far_picks, gates = call(
        picks_kernel,
        plan,
        [slot, gate, shared[1]],
        [VMEM_SPEC] * 2 + [ANY_SPEC],
        [(plan.cuts, plan.tokens, depth)] * 2 + [(plan.tokens, 1)],
        [],
        0,
        "picks",
        limit=4,
        dtypes=[BF16, BF16, F32],
    )
    outs = call(
        early_kernel,
        plan,
        [back_near, gates],
        [VMEM_SPEC, ANY_SPEC],
        [(SUB, C)] * half,
        [],
        0,
        "early",
        limit=4,
    )
    early = [outs[0]] + [to_source(outs[m], m) for m in range(1, half - 1)]
    (last,) = call(
        pass_kernel,
        plan,
        [outs[half - 1], early[1]],
        [VMEM_SPEC, ANY_SPEC],
        [(SUB, C)],
        [],
        0,
        "pass_on",
        limit=4,
    )
    early.append(to_source(last, half - 1))
    (total,) = call(
        gather_kernel,
        plan,
        [momentum] + columns_here + shared,
        [ANY_SPEC] + [VMEM_SPEC] * (2 * groups),
        [(share, F)],
        [
            pltpu.VMEM((3 * groups * rows, share), BF16),
            pltpu.VMEM((share, F), BF16),
            pltpu.SemaphoreType.DMA,
        ],
        0,
        "own_terms",
        dtypes=[F32],
    )
    def place(picks, got, placed, name):
        return call(
            unpack_kernel,
            plan,
            [picks, gates] + [got[m] for m in plan.back_order] + placed,
            [VMEM_SPEC] * (2 + half + len(placed)),
            [(plan.tokens, F), (plan.tokens, D)],
            [pltpu.VMEM((half, SUB, C), BF16), pltpu.SemaphoreType.DMA((half,))],
            0,
            name,
            limit=12,
        )

    placed = list(place(near_picks, early, [], "near_results"))
    outs = call(
        after_kernel,
        plan,
        [placement, payload, local, placed[0]],
        [SMEM_SPEC] + [VMEM_SPEC] * 2 + [ANY_SPEC],
        [(SUB, C)] * half + [(rows, F)],
        [],
        0,
        "after_swap",
        limit=8,
    )
    late = [outs[0]] + [to_source(outs[m], m) for m in range(1, half)]
    other_g = with_sisters(from_chips([outs[half]] * outer))

    new_weight, new_momentum = pl.pallas_call(
        functools.partial(update_kernel, plan),
        out_shape=[jax.ShapeDtypeStruct((1, share, F), BF16)] * 2,
        in_specs=[SMEM_SPEC] + [VMEM_SPEC] * 2 + [ANY_SPEC] * (groups + 1),
        out_specs=[ANY_SPEC] * 2,
        scratch_shapes=[
            pltpu.VMEM((half * SUB, C), BF16),
            pltpu.VMEM((groups, rows, F), BF16),
            pltpu.VMEM((share, F), BF16),
            pltpu.VMEM((share, F), BF16),
            pltpu.SemaphoreType.DMA((groups + 1,)),
            pltpu.SemaphoreType.DMA((share // LANES, 2)),
        ],
        compiler_params=pltpu.CompilerParams(vmem_limit_bytes=20 * MIB),
        cost_estimate=pl.CostEstimate(
            flops=2 * groups * rows * share * F, bytes_accessed=12 * share * F, transcendentals=0
        ),
        name="update",
    )(placement, total, old_weight, payload, *other_g)

    expert_out, token_grad = place(far_picks, late, placed, "far_results")
    return expert_out, token_grad, new_weight, new_momentum


def general(tokens, route_weight, cotangent, slot_ids, placement, weight, momentum):
    n_slots = lax.axis_size("expert")
    n_groups = lax.axis_size("dp")
    tok_count, D = tokens.shape
    F = cotangent.shape[1]
    capacity = tok_count * 9 // 8 // n_slots
    onehot = (slot_ids[:, None] == jnp.arange(n_slots, dtype=jnp.int32)[None, :]).astype(jnp.int32)
    ranks = jnp.sum((jnp.cumsum(onehot, axis=0) - 1) * onehot, axis=1)
    position = slot_ids * capacity + ranks
    send_rows = jnp.zeros((n_slots * capacity, D), BF16).at[position].set(tokens)
    scaled = (route_weight[:, None] * cotangent.astype(F32)).astype(BF16)
    send_grads = jnp.zeros((n_slots * capacity, F), BF16).at[position].set(scaled)
    matrix = weight[0]

    def exchange(rows):
        width = rows.shape[-1]
        return lax.all_to_all(
            rows.reshape(n_slots, capacity, width), "expert", split_axis=0, concat_axis=0, tiled=True
        ).reshape(-1, width)

    flat_x = exchange(send_rows)
    act, flat_grad = activate(dot(flat_x, matrix), exchange(send_grads))
    back = dot_nt(flat_grad, matrix).astype(BF16)
    act_rows = exchange(act)[position]
    expert_out = (route_weight[:, None] * act_rows.astype(F32)).astype(BF16)
    token_grad = exchange(back)[position]
    row_count = flat_x.shape[0]
    share = D // n_groups
    columns = lax.all_to_all(
        flat_x.reshape(1, row_count, n_groups, share), "dp", split_axis=2, concat_axis=0, tiled=True
    )
    columns = columns.reshape(n_groups, row_count, share)
    terms = jnp.einsum(
        "krd,krf->kdf",
        columns,
        lax.all_gather(flat_grad[None], "dp", axis=0, tiled=True),
        preferred_element_type=F32,
    )
    terms = lax.optimization_barrier(terms.astype(BF16)).astype(F32)
    reduced = jnp.sum(terms, axis=0).astype(BF16)
    half = n_slots // 2
    partner_grad = lax.ppermute(
        reduced, "expert", [(i, (i + half) % n_slots) for i in range(n_slots)]
    ).astype(F32)
    my_slot = lax.axis_index("expert")
    partner_slot = (my_slot + half) % n_slots
    same = placement[my_slot] == placement[partner_slot]
    total = reduced.astype(F32) + jnp.where(same, partner_grad, 0.0)
    new_momentum = (decay_rate * momentum[0].astype(F32) + total).astype(BF16)
    old = lax.dynamic_slice_in_dim(matrix, lax.axis_index("dp") * share, share, 0).astype(F32)
    new_weight = (old - learning_rate * new_momentum.astype(F32)).astype(BF16)
    return expert_out, token_grad, new_weight[None], new_momentum[None]


def solution(mesh):
    def shards(tokens, route_weight, cotangent, slot_ids, placement, weight, momentum):
        plan = Plan(
            mesh.shape["expert"],
            mesh.shape["dp"],
            tokens.shape[0],
            tokens.shape[1],
            cotangent.shape[1],
        )
        body = functools.partial(routed, plan) if plan.fits() else general
        return body(tokens, route_weight, cotangent, slot_ids, placement, weight, momentum)

    return jax.shard_map(
        shards,
        mesh=mesh,
        in_specs=(
            P(("dp", "expert"), None),
            P(("dp", "expert")),
            P(("dp", "expert"), None),
            P(("dp", "expert")),
            P(),
            P("expert", None, None),
            P("expert", "dp", None),
        ),
        out_specs=(
            P(("dp", "expert"), None),
            P(("dp", "expert"), None),
            P("expert", "dp", None),
            P("expert", "dp", None),
        ),
        check_vma=False,
    )
```

```python
import functools
import math

import jax
import jax.numpy as jnp
from jax import lax
from jax.experimental import pallas as pl
from jax.experimental.pallas import tpu as pltpu
from jax.sharding import PartitionSpec as P

learning_rate = 0.004
decay_rate = 0.9

BF16 = jnp.bfloat16
F32 = jnp.float32
SUB = 8
LANES = 128
INNER = 2


class Plan:
    def __init__(self, slots, groups, tokens, features, hidden):
        self.slots, self.groups, self.tokens = slots, groups, tokens
        self.D, self.F = features, hidden
        self.half = slots // 2
        self.cap = tokens * 9 // 8 // slots
        self.full, self.rest = divmod(self.cap, SUB)
        self.cuts = SUB // self.rest if self.rest else 1
        self.rows = self.half * self.cap
        self.back_order = [*range(0, self.half, 2), *range(1, self.half, 2)]
        self.far_order = [*range(0, self.half, 2), *range(1, self.half, 2)]
        self.share = features // groups
        self.DX = features * self.cap // SUB
        self.FG = hidden * self.cap // SUB
        self.C = self.DX + self.FG
        self.pieces = self.cap * groups // SUB
        self.outer = groups // INNER

    def group_at(self, group, step):
        chip, core = group // INNER, group % INNER
        if isinstance(group, int):
            return away(chip, step // INNER, self.outer) * INNER + (core ^ (step % INNER))
        return away_traced(chip, step // INNER, self.outer) * INNER + jnp.bitwise_xor(
            core, step % INNER
        )

    def group_from(self, step):
        chips = step // INNER
        if self.outer & (self.outer - 1):
            chips = (self.outer - chips) % self.outer
        return chips * INNER + step % INNER

    def fits(self):
        return (
            self.slots % 2 == 0
            and (self.rest == 0 or SUB % self.rest == 0)
            and self.D % (self.cuts * LANES) == 0
            and self.F % (self.cuts * LANES) == 0
            and self.D % (self.groups * LANES) == 0
            and self.groups % INNER == 0
            and (self.cap * self.groups) % SUB == 0
            and self.rows % SUB == 0
            and (self.half * self.rest) % SUB == 0
            and self.tokens % LANES == 0
        )


def away(place, step, count):
    if count & (count - 1) == 0:
        return place ^ step
    return (place + step) % count


def away_traced(place, step, count):
    if count & (count - 1) == 0:
        return jnp.bitwise_xor(place, step)
    return lax.rem(place + step, count)


def steps_between(first, second, count):
    if count & (count - 1) == 0:
        return jnp.bitwise_xor(first, second)
    return lax.rem(first - second + count, count)


def iota(shape, dim):
    return lax.broadcasted_iota(jnp.int32, shape, dim)


def dot(a, b):
    return jnp.dot(a, b, preferred_element_type=F32)


def dot_nt(a, b):
    return lax.dot_general(a, b, (((1,), (1,)), ((), ())), preferred_element_type=F32)


def dot_tn(a, b):
    return lax.dot_general(a, b, (((0,), (0,)), ((), ())), preferred_element_type=F32)


def picker(plan, cut):
    shape = (plan.half * plan.rest, plan.half * SUB)
    row, col = iota(shape, 0), iota(shape, 1)
    wanted = (row // plan.rest) * SUB + cut * plan.rest + row % plan.rest
    return (wanted == col).astype(BF16)


def unfold(plan, blocks, width):
    parts = [
        jnp.concatenate([b[:, i * width : (i + 1) * width] for b in blocks], axis=0)
        for i in range(plan.full)
    ]
    if plan.rest:
        piece = width // plan.cuts
        tail = jnp.concatenate([b[:, plan.full * width :] for b in blocks], axis=0).astype(BF16)
        parts.append(
            jnp.concatenate([dot(picker(plan, q), tail) for q in range(plan.cuts)], axis=1)
        )
    return jnp.concatenate(parts, axis=0).astype(BF16)


def fold(plan, rows):
    width = rows.shape[1]
    block = plan.half * SUB
    parts = [rows[i * block : (i + 1) * block] for i in range(plan.full)]
    if plan.rest:
        piece = width // plan.cuts
        tail = rows[plan.full * block :].astype(BF16)
        total = None
        for q in range(plan.cuts):
            term = dot_tn(picker(plan, q), tail[:, q * piece : (q + 1) * piece])
            total = term if total is None else total + term
        parts.append(total)
    return jnp.concatenate(parts, axis=1)


def is_hot(plan, placement_ref):
    me = lax.axis_index("expert")
    partner = lax.rem(me + plan.half, plan.slots)
    return placement_ref[me] == placement_ref[partner]


def token_places(plan, slot):
    me = lax.axis_index("expert")
    my_half = me // plan.half
    my_place = lax.rem(me, plan.half)
    upper = (slot >= plan.half).astype(jnp.int32)
    place = slot - plan.half * upper
    far = jnp.where(upper == my_half, 0, 1)
    step = steps_between(place, jnp.zeros_like(place) + my_place, plan.half)
    block = 2 * step + far
    count = plan.tokens
    onehot = (iota((2 * plan.half, count), 0) == block).astype(F32)
    upto = (iota((count, count), 0) <= iota((count, count), 1)).astype(BF16)
    seen = dot(onehot.astype(BF16), upto)
    rank = jnp.sum(onehot * (seen - 1.0), axis=0, keepdims=True).astype(jnp.int32)
    return block, rank


def row_targets(plan, block, rank):
    targets = []
    for i in range(plan.full):
        inside = (rank >= i * SUB) & (rank < (i + 1) * SUB)
        targets.append(jnp.where(inside, block * SUB + rank - i * SUB, -1))
    for q in range(plan.cuts if plan.rest else 0):
        inside = rank >= plan.full * SUB
        targets.append(
            jnp.where(inside, block * SUB + q * plan.rest + rank - plan.full * SUB, -1)
        )
    return targets


def to_column(row):
    n = row.shape[1]
    eye = (iota((n, n), 0) == iota((n, n), 1)).astype(F32)
    return jnp.sum(eye * row.astype(F32), axis=1, keepdims=True)


def pack_kernel(plan, slot_hbm, gate_hbm, tok_hbm, cot_hbm, *refs):
    half = plan.half
    near, far = refs[:half], refs[half : 2 * half]
    slot_ref, gate_ref, tok_ref, cot_ref, sems = refs[2 * half :]
    copies = [
        pltpu.make_async_copy(source, held, sems.at[i])
        for i, (source, held) in enumerate(
            ((slot_hbm, slot_ref), (tok_hbm, tok_ref), (gate_hbm, gate_ref), (cot_hbm, cot_ref))
        )
    ]
    for copy in copies:
        copy.start()
    copies[0].wait()
    block, rank = token_places(plan, slot_ref[...])
    targets = row_targets(plan, block, rank)
    height = 2 * half * SUB
    onehots = [(iota((height, plan.tokens), 0) == t).astype(BF16) for t in targets]

    def store(values, start):
        stop = start + values.shape[1]
        for m in range(half):
            low = 2 * m * SUB
            near[m][:, start:stop] = values[low : low + 2 * SUB].astype(BF16)
            far[m][:, start:stop] = values[low + SUB : low + 2 * SUB].astype(BF16)

    def place(data, base):
        width = data.shape[1]
        for i in range(plan.full):
            store(dot(onehots[i], data), base + i * width)
        if plan.rest:
            piece = width // plan.cuts
            total = None
            for q in range(plan.cuts):
                term = dot(onehots[plan.full + q], data[:, q * piece : (q + 1) * piece])
                total = term if total is None else total + term
            store(total, base + plan.full * width)

    copies[1].wait()
    place(tok_ref[...], 0)
    copies[2].wait()
    copies[3].wait()
    scaled = (to_column(gate_ref[...]) * cot_ref[...].astype(F32)).astype(BF16)
    place(scaled, plan.DX)


def hold_kernel(plan, weight_hbm, held, mine, sems):
    start = pl.multiple_of(lax.axis_index("dp") * plan.share, LANES)
    copies = [
        pltpu.make_async_copy(weight_hbm.at[0], held, sems.at[0]),
        pltpu.make_async_copy(weight_hbm.at[0, pl.ds(start, plan.share), :], mine, sems.at[1]),
    ]
    for copy in copies:
        copy.start()
    for copy in copies:
        copy.wait()


def blocks_of(refs, start, stop, low=0):
    return [r[:, start:stop].astype(F32)[low : low + SUB] for r in refs]


def columns_kernel(plan, *refs):
    near, outs, held = refs[: plan.half], refs[-plan.groups - 1 : -1], refs[-1]
    held[...] = unfold(plan, blocks_of(near, 0, plan.DX), plan.D)
    for m in range(plan.groups):
        start = pl.multiple_of(plan.group_at(lax.axis_index("dp"), m) * plan.share, LANES)
        outs[m][...] = held[:, pl.ds(start, plan.share)]


def activate(preact, scaled):
    sigma = jax.nn.sigmoid(preact)
    act = (preact * sigma).astype(BF16)
    grad_pre = (scaled.astype(F32) * sigma * (1.0 + preact * (1.0 - sigma))).astype(BF16)
    return act, grad_pre


def chip_columns(plan, rows, outs):
    width = INNER * plan.share
    chip = lax.axis_index("dp") // INNER
    for o in range(plan.outer):
        start = pl.multiple_of(away_traced(chip, o, plan.outer) * width, LANES)
        outs[o][:, :width] = rows[:, pl.ds(start, width)]


def near_kernel(plan, placement_ref, weight_ref, *refs):
    near = refs[: plan.half]
    back_near, local, folded_grad, grads, far_rows = refs[-5:]
    x_near = unfold(plan, blocks_of(near, 0, plan.DX), plan.D)
    x_far = unfold(plan, blocks_of(near, 0, plan.DX, SUB), plan.D)
    g_near = unfold(plan, blocks_of(near, plan.DX, plan.C), plan.F)
    g_far = unfold(plan, blocks_of(near, plan.DX, plan.C, SUB), plan.F)
    far_rows[...] = x_far
    x = jnp.concatenate([x_near.astype(F32), x_far.astype(F32)], axis=0).astype(BF16)
    g = jnp.concatenate([g_near.astype(F32), g_far.astype(F32)], axis=0).astype(BF16)
    act, grad_pre = activate(dot(x, weight_ref[...]), g)
    back = dot_nt(grad_pre, weight_ref[...])
    act, grad32 = act.astype(F32), grad_pre.astype(F32)
    back_near[:, : plan.DX] = fold(plan, back[: plan.rows]).astype(BF16)
    back_near[:, plan.DX :] = fold(plan, act[: plan.rows]).astype(BF16)
    local[:, : plan.DX] = fold(plan, back[plan.rows :]).astype(BF16)
    local[:, plan.DX :] = fold(plan, act[plan.rows :]).astype(BF16)
    grad_near = grad32[: plan.rows]
    grad_far = jnp.where(is_hot(plan, placement_ref), grad32[plan.rows :], 0.0)
    folded_grad[...] = fold(plan, grad_near).astype(BF16)
    grads[:, : plan.F] = grad_near.astype(BF16)
    grads[:, plan.F :] = grad_far.astype(BF16)


def payload_kernel(
    plan, placement_ref, weight_ref, folded_grad, near_grads, far_rows, *refs
):
    half, groups = plan.half, plan.groups
    far, refs = [refs[plan.far_order.index(m)] for m in range(half)], refs[half:]
    columns, refs = refs[:groups], refs[groups:]
    payload, refs = refs[0], refs[1:]
    shared, rows = refs[:groups], refs[groups]
    hot = is_hot(plan, placement_ref)
    x = unfold(plan, blocks_of(far, 0, plan.DX), plan.D)
    g = unfold(plan, blocks_of(far, plan.DX, plan.C), plan.F)
    rows[...] = x
    act, grad_pre = activate(dot(x, weight_ref[...]), g)

    @pl.when(jnp.logical_not(hot))
    def _():
        payload[:, : plan.DX] = fold(plan, dot_nt(grad_pre, weight_ref[...])).astype(BF16)
        payload[:, plan.DX :] = fold(plan, act.astype(F32)).astype(BF16)

    @pl.when(hot)
    def _():
        together = jnp.concatenate([c[...].astype(F32) for c in columns], axis=0)
        block = half * SUB
        for i in range(plan.pieces):
            payload[:, i * plan.share : (i + 1) * plan.share] = together[
                i * block : (i + 1) * block
            ].astype(BF16)
        payload[:, plan.DX :] = folded_grad[...]

    group = lax.axis_index("dp")
    width = plan.share
    for m in range(groups):
        start = pl.multiple_of(plan.group_at(group, m) * width, LANES)
        shared[m][:, :width] = far_rows[:, pl.ds(start, width)]
        shared[m][:, width : 2 * width] = rows[:, pl.ds(start, width)]
        shared[m][:, 2 * width : 2 * width + 2 * plan.F] = near_grads[...]
        shared[m][:, 2 * width + 2 * plan.F :] = grad_pre


def pass_kernel(plan, source, before, target):
    target[...] = source[...]


def early_kernel(plan, near_back, *refs):
    back = near_back[...].astype(F32)
    for m, out in enumerate(refs[-plan.half :]):
        out[...] = back[m * SUB : (m + 1) * SUB].astype(BF16)


def after_kernel(plan, placement_ref, payload, local, *refs):
    outs = refs[-plan.half - 1 :]
    hot = is_hot(plan, placement_ref)
    got = payload[...].astype(F32)
    chosen = jnp.where(hot, local[...].astype(F32), got)
    for m in range(plan.half):
        outs[m][...] = chosen[m * SUB : (m + 1) * SUB].astype(BF16)
    blocks = [got[m * SUB : (m + 1) * SUB, plan.DX :] for m in range(plan.half)]
    outs[plan.half][...] = jnp.where(hot, unfold(plan, blocks, plan.F).astype(F32), 0.0).astype(BF16)


def picks_kernel(plan, slot_ref, gate_ref, before, near, far, gate):
    block, rank = token_places(plan, slot_ref[...])
    width = plan.half * SUB
    for side, out in enumerate((near, far)):
        place = jnp.where(lax.rem(block, 2) == side, block // 2, -2)
        picks = []
        for target in row_targets(plan, place, rank):
            column = to_column(target).astype(jnp.int32)
            picks.append((iota((plan.tokens, width), 1) == column).astype(BF16))
        for q in range(plan.cuts):
            out[q] = jnp.concatenate(picks[: plan.full] + picks[plan.full + q :][:1], axis=1)
    gate[...] = to_column(gate_ref[...])


def unpack_kernel(plan, picks_ref, gate_ref, *refs):
    half = plan.half
    got, refs = refs[:half], refs[half:]
    before, refs = refs[:-2], refs[-2:]
    out_ref, grad_ref = refs
    blocks = [got[plan.back_order.index(m)] for m in range(half)]

    def gather(base, size, scale, placed, out):
        rows = blocks_of(blocks, base, base + size * plan.cap // SUB)
        rows = jnp.concatenate(rows, axis=0).astype(BF16)
        piece = size // plan.cuts
        for q in range(plan.cuts):
            span = slice(q * piece, (q + 1) * piece)
            parts = []
            for i in range(plan.full):
                parts.append(rows[:, i * size + q * piece : i * size + (q + 1) * piece])
            if plan.rest:
                parts.append(rows[:, plan.full * size :])
            value = dot(picks_ref[q], jnp.concatenate(parts, axis=0))
            if scale is not None:
                value = scale * value
            if placed:
                value = value + placed[0][:, span].astype(F32)
            out[:, span] = value.astype(BF16)

    gather(0, plan.D, None, before[1:], grad_ref)
    gather(plan.DX, plan.F, gate_ref[...], before[:1], out_ref)


def rows_of(parts):
    return jnp.concatenate([p.astype(F32) for p in parts], axis=0).astype(BF16)


def gather_kernel(plan, momentum_hbm, *refs):
    groups, share, width = plan.groups, plan.share, plan.F
    columns, refs = refs[:groups], refs[groups:]
    shared, refs = refs[:groups], refs[groups:]
    total, x_all, momentum, sem = refs
    copy = pltpu.make_async_copy(momentum_hbm.at[0], momentum, sem)
    copy.start()
    base = 2 * share
    x_parts, g_parts = [], []
    for m in range(groups):
        x_parts.append(columns[m][...])
        x_parts += [shared[m][:, i * share : (i + 1) * share] for i in range(2)]
        g_parts += [shared[m][:, base + i * width : base + (i + 1) * width] for i in range(3)]
    x_all[...] = rows_of(x_parts)
    g_all = rows_of(g_parts)
    copy.wait()
    for i in range(share // LANES):
        span = slice(i * LANES, (i + 1) * LANES)
        before = decay_rate * momentum[span, :].astype(F32)
        total[span, :] = before + dot_tn(x_all[:, span], g_all)


def update_kernel(plan, placement_ref, total, old_weight, payload_hbm, *refs):
    groups, share = plan.groups, plan.share
    other_g, refs = refs[:groups], refs[groups:]
    new_weight, new_momentum, payload, weight, momentum, sem, out_sems = refs
    copy = pltpu.make_async_copy(payload_hbm, payload, sem)
    copy.start()
    hot = is_hot(plan, placement_ref)
    g = rows_of([data[...] for data in other_g])
    copy.wait()
    pieces = [payload[:, i * share : (i + 1) * share] for i in range(plan.pieces)]
    x = jnp.concatenate(pieces, axis=0)
    x = jnp.where(hot, x.astype(F32), 0.0).astype(BF16)
    done = []
    for i in range(share // LANES):
        span = pl.ds(i * LANES, LANES)
        value = total[span, :] + dot_tn(x[:, i * LANES : (i + 1) * LANES], g)
        value = value.astype(BF16)
        momentum[span, :] = value
        weight[span, :] = (
            old_weight[span, :].astype(F32) - learning_rate * value.astype(F32)
        ).astype(BF16)
        for j, (source, target) in enumerate(((momentum, new_momentum), (weight, new_weight))):
            copy = pltpu.make_async_copy(
                source.at[span, :], target.at[0, span, :], out_sems.at[i, j]
            )
            copy.start()
            done.append(copy)
    for copy in done:
        copy.wait()


MIB = 1024 * 1024
SMEM_SPEC = pl.BlockSpec(memory_space=pltpu.SMEM)
ANY_SPEC = pl.BlockSpec(memory_space=pl.ANY)
VMEM_SPEC = pl.BlockSpec(memory_space=pltpu.VMEM)


def call(kernel, plan, ins, specs, outs, scratch, flops, name, limit=16, dtypes=None):
    moved = sum(a.size * a.dtype.itemsize for a in ins) + sum(2 * math.prod(o) for o in outs)
    return pl.pallas_call(
        functools.partial(kernel, plan),
        out_shape=[
            jax.ShapeDtypeStruct(s, dtypes[i] if dtypes else BF16) for i, s in enumerate(outs)
        ],
        in_specs=specs,
        out_specs=[VMEM_SPEC] * len(outs),
        scratch_shapes=scratch,
        compiler_params=pltpu.CompilerParams(vmem_limit_bytes=limit * MIB),
        cost_estimate=pl.CostEstimate(
            flops=flops, bytes_accessed=moved if flops else 0, transcendentals=0
        ),
        name=name,
    )(*ins)


def routed(plan, tokens, route_weight, cotangent, slot_ids, placement, weight, momentum):
    half, groups, outer = plan.half, plan.groups, plan.outer
    D, F, C, rows, share = plan.D, plan.F, plan.C, plan.rows, plan.share
    slot = slot_ids.reshape(1, -1)
    gate = route_weight.reshape(1, -1)

    def to_slot(data, m, flip=0):
        pairs = []
        for e in range(plan.slots):
            h, k = divmod(e, half)
            pairs.append((e, (h ^ flip) * half + away(k, m, half)))
        return lax.ppermute(data, "expert", pairs)

    def to_source(data, m):
        pairs = []
        for e in range(plan.slots):
            h, k = divmod(e, half)
            pairs.append((h * half + away(k, m, half), e))
        return lax.ppermute(data, "expert", pairs)

    def to_partner(data):
        pairs = [(e, (e + half) % plan.slots) for e in range(plan.slots)]
        return lax.ppermute(data, "expert", pairs)

    def from_group(data, m):
        pairs = []
        for d in range(groups):
            pairs.append((plan.group_at(d, m), d))
        return lax.ppermute(data, "dp", pairs)

    def from_chips(per_chip):
        return [per_chip[0]] + [
            from_group(per_chip[plan.group_from(INNER * o) // INNER], INNER * o)
            for o in range(1, outer)
        ]

    def with_sisters(got):
        return [data for own in got for data in (own, from_group(own, 1))]

    def from_groups(per_group):
        return [per_group[0]] + [
            from_group(per_group[plan.group_from(m)], m) for m in range(1, groups)
        ]

    packed = call(
        pack_kernel,
        plan,
        [slot, gate, tokens, cotangent],
        [ANY_SPEC] * 4,
        [(2 * SUB, C)] * half + [(SUB, C)] * half,
        [
            pltpu.VMEM(slot.shape, slot.dtype),
            pltpu.VMEM(gate.shape, gate.dtype),
            pltpu.VMEM(tokens.shape, tokens.dtype),
            pltpu.VMEM(cotangent.shape, cotangent.dtype),
            pltpu.SemaphoreType.DMA((4,)),
        ],
        2 * 4 * half * SUB * plan.tokens * (D + F),
        "pack",
        limit=60,
    )
    near = [packed[0]] + [to_slot(packed[m], m) for m in range(1, half)]
    far = [to_slot(packed[half + m], m, 1) for m in range(half)]
    held, old_weight = call(
        hold_kernel,
        plan,
        [weight],
        [ANY_SPEC],
        [(D, F), (share, F)],
        [pltpu.SemaphoreType.DMA((2,))],
        0,
        "hold",
        limit=40,
    )
    columns = call(
        columns_kernel,
        plan,
        near,
        [VMEM_SPEC] * half,
        [(rows, share)] * groups,
        [pltpu.VMEM((rows, D), BF16)],
        0,
        "near_columns",
    )
    columns_here = from_groups(columns)
    back_near, local, folded_grad, grads, far_rows = call(
        near_kernel,
        plan,
        [placement, held] + near + [columns[0]],
        [SMEM_SPEC] + [VMEM_SPEC] * (1 + half) + [ANY_SPEC],
        [
            (half * SUB, C),
            (half * SUB, C),
            (half * SUB, plan.FG),
            (rows, 2 * F),
            (rows, D),
        ],
        [],
        8 * rows * D * F,
        "near_rows",
    )
    outs = call(
        payload_kernel,
        plan,
        [placement, held, folded_grad, grads, far_rows]
        + [far[m] for m in plan.far_order]
        + columns_here,
        [SMEM_SPEC] + [VMEM_SPEC] * (4 + half + groups),
        [(half * SUB, C)] + [(rows, 2 * share + 3 * F)] * groups,
        [pltpu.VMEM((rows, D), BF16)],
        4 * rows * D * F,
        "payload",
    )
    payload = to_partner(outs[0])
    shared = from_groups(outs[1:])
    depth = half * SUB * (plan.full + (1 if plan.rest else 0))
    near_picks, far_picks, gates = call(
        picks_kernel,
        plan,
        [slot, gate, shared[1]],
        [VMEM_SPEC] * 2 + [ANY_SPEC],
        [(plan.cuts, plan.tokens, depth)] * 2 + [(plan.tokens, 1)],
        [],
        0,
        "picks",
        limit=4,
        dtypes=[BF16, BF16, F32],
    )
    outs = call(
        early_kernel,
        plan,
        [back_near, gates],
        [VMEM_SPEC, ANY_SPEC],
        [(SUB, C)] * half,
        [],
        0,
        "early",
        limit=4,
    )
    early = [outs[0]] + [to_source(outs[m], m) for m in range(1, half - 1)]
    (last,) = call(
        pass_kernel,
        plan,
        [outs[half - 1], early[1]],
        [VMEM_SPEC, ANY_SPEC],
        [(SUB, C)],
        [],
        0,
        "pass_on",
        limit=4,
    )
    early.append(to_source(last, half - 1))
    (total,) = call(
        gather_kernel,
        plan,
        [momentum] + columns_here + shared,
        [ANY_SPEC] + [VMEM_SPEC] * (2 * groups),
        [(share, F)],
        [
            pltpu.VMEM((3 * groups * rows, share), BF16),
            pltpu.VMEM((share, F), BF16),
            pltpu.SemaphoreType.DMA,
        ],
        0,
        "own_terms",
        dtypes=[F32],
    )
    def place(picks, got, placed, name):
        return call(
            unpack_kernel,
            plan,
            [picks, gates] + [got[m] for m in plan.back_order] + placed,
            [VMEM_SPEC] * (2 + half + len(placed)),
            [(plan.tokens, F), (plan.tokens, D)],
            [],
            0,
            name,
            limit=12,
        )

    placed = list(place(near_picks, early, [], "near_results"))
    outs = call(
        after_kernel,
        plan,
        [placement, payload, local, placed[0]],
        [SMEM_SPEC] + [VMEM_SPEC] * 2 + [ANY_SPEC],
        [(SUB, C)] * half + [(rows, F)],
        [],
        0,
        "after_swap",
        limit=8,
    )
    late = [outs[0]] + [to_source(outs[m], m) for m in range(1, half)]
    other_g = with_sisters(from_chips([outs[half]] * outer))

    new_weight, new_momentum = pl.pallas_call(
        functools.partial(update_kernel, plan),
        out_shape=[jax.ShapeDtypeStruct((1, share, F), BF16)] * 2,
        in_specs=[SMEM_SPEC] + [VMEM_SPEC] * 2 + [ANY_SPEC] + [VMEM_SPEC] * groups,
        out_specs=[ANY_SPEC] * 2,
        scratch_shapes=[
            pltpu.VMEM((half * SUB, C), BF16),
            pltpu.VMEM((share, F), BF16),
            pltpu.VMEM((share, F), BF16),
            pltpu.SemaphoreType.DMA,
            pltpu.SemaphoreType.DMA((share // LANES, 2)),
        ],
        compiler_params=pltpu.CompilerParams(vmem_limit_bytes=20 * MIB),
        cost_estimate=pl.CostEstimate(
            flops=2 * groups * rows * share * F, bytes_accessed=12 * share * F, transcendentals=0
        ),
        name="update",
    )(placement, total, old_weight, payload, *other_g)

    expert_out, token_grad = place(far_picks, late, placed, "far_results")
    return expert_out, token_grad, new_weight, new_momentum


def general(tokens, route_weight, cotangent, slot_ids, placement, weight, momentum):
    n_slots = lax.axis_size("expert")
    n_groups = lax.axis_size("dp")
    tok_count, D = tokens.shape
    F = cotangent.shape[1]
    capacity = tok_count * 9 // 8 // n_slots
    onehot = (slot_ids[:, None] == jnp.arange(n_slots, dtype=jnp.int32)[None, :]).astype(jnp.int32)
    ranks = jnp.sum((jnp.cumsum(onehot, axis=0) - 1) * onehot, axis=1)
    position = slot_ids * capacity + ranks
    send_rows = jnp.zeros((n_slots * capacity, D), BF16).at[position].set(tokens)
    scaled = (route_weight[:, None] * cotangent.astype(F32)).astype(BF16)
    send_grads = jnp.zeros((n_slots * capacity, F), BF16).at[position].set(scaled)
    matrix = weight[0]

    def exchange(rows):
        width = rows.shape[-1]
        return lax.all_to_all(
            rows.reshape(n_slots, capacity, width), "expert", split_axis=0, concat_axis=0, tiled=True
        ).reshape(-1, width)

    flat_x = exchange(send_rows)
    act, flat_grad = activate(dot(flat_x, matrix), exchange(send_grads))
    back = dot_nt(flat_grad, matrix).astype(BF16)
    act_rows = exchange(act)[position]
    expert_out = (route_weight[:, None] * act_rows.astype(F32)).astype(BF16)
    token_grad = exchange(back)[position]
    row_count = flat_x.shape[0]
    share = D // n_groups
    columns = lax.all_to_all(
        flat_x.reshape(1, row_count, n_groups, share), "dp", split_axis=2, concat_axis=0, tiled=True
    )
    columns = columns.reshape(n_groups, row_count, share)
    terms = jnp.einsum(
        "krd,krf->kdf",
        columns,
        lax.all_gather(flat_grad[None], "dp", axis=0, tiled=True),
        preferred_element_type=F32,
    )
    terms = lax.optimization_barrier(terms.astype(BF16)).astype(F32)
    reduced = jnp.sum(terms, axis=0).astype(BF16)
    half = n_slots // 2
    partner_grad = lax.ppermute(
        reduced, "expert", [(i, (i + half) % n_slots) for i in range(n_slots)]
    ).astype(F32)
    my_slot = lax.axis_index("expert")
    partner_slot = (my_slot + half) % n_slots
    same = placement[my_slot] == placement[partner_slot]
    total = reduced.astype(F32) + jnp.where(same, partner_grad, 0.0)
    new_momentum = (decay_rate * momentum[0].astype(F32) + total).astype(BF16)
    old = lax.dynamic_slice_in_dim(matrix, lax.axis_index("dp") * share, share, 0).astype(F32)
    new_weight = (old - learning_rate * new_momentum.astype(F32)).astype(BF16)
    return expert_out, token_grad, new_weight[None], new_momentum[None]


def solution(mesh):
    def shards(tokens, route_weight, cotangent, slot_ids, placement, weight, momentum):
        plan = Plan(
            mesh.shape["expert"],
            mesh.shape["dp"],
            tokens.shape[0],
            tokens.shape[1],
            cotangent.shape[1],
        )
        body = functools.partial(routed, plan) if plan.fits() else general
        return body(tokens, route_weight, cotangent, slot_ids, placement, weight, momentum)

    return jax.shard_map(
        shards,
        mesh=mesh,
        in_specs=(
            P(("dp", "expert"), None),
            P(("dp", "expert")),
            P(("dp", "expert"), None),
            P(("dp", "expert")),
            P(),
            P("expert", None, None),
            P("expert", "dp", None),
        ),
        out_specs=(
            P(("dp", "expert"), None),
            P(("dp", "expert"), None),
            P("expert", "dp", None),
            P("expert", "dp", None),
        ),
        check_vma=False,
    )
```
